32 devices in a mesh: dp: 8 (over y, x, core), tm: 4 (over z).
Axes of the slice: x: 2, y: 2, z: 4, core: 2. Of those that a mesh axis runs over, the one named last changes fastest.
Arguments:
- feats: bfloat16 [24576, 512], P(('dp', 'tm')), may hold values from -40 to 40, as said below
- codes: int32 [8, 2, 1536], P('dp', None, 'tm'), may hold values from 0 to 1023, as said below
- conv_weight: bfloat16 [2048, 512], replicated, may hold values from -0.125 to 0.125
- conv_bias: float32 [512], replicated, may hold values from -3 to 3
- proj_weight: bfloat16 [512, 256], replicated, may hold values from -0.25 to 0.25
- codebooks: bfloat16 [2, 1024, 256], replicated, may hold values from -4.1875 to 4.1875
Outputs:
- feat_grad: bfloat16 [24576, 512], P(('dp', 'tm'))
- conv_grad: float32 [2048, 512], P(('dp', 'tm'))
- bias_grad: float32 [512], replicated
- proj_grad: float32 [512, 256], replicated
- code_means: bfloat16 [2, 1024, 256], P(None, 'tm')
- code_usage: float32 [2, 1024], P(None, 'tm')
The draws below stay inside these ranges and needn't reach their ends.
Inputs may be any that keep to these rules, and one draw needn't show every extreme that they name: `feats`: each clip has its own overall scale, and rows vary in scale within a clip. Codes are used with strongly unequal frequencies; on every level some codes occur in no frame.
All inputs are finite; a program needn't handle non-finite values.
Results may differ from the reference program's by a relative error of at most 0.0075.
Values may be sent and summed in bfloat16 or wider, within the bound.
No kernel may reach another device: no remote copies, remote signals or barrier semaphores. Data moves between devices by JAX's collectives and lax.ppermute only.
A program may use at most 64 MiB of HBM per device.

```python
import jax
import jax.numpy as jnp
from jax import lax

D = 512
DZ = 256
CODES = 1024
KW = 4
LEVELS = 2
CLIPS = 8
FRAMES = 1536
TOTAL = 12288
ROWS_IN = 24576


def draw_feats(key, part):
    key_base, key_clip, key_row = jax.random.split(jax.random.fold_in(key, 11), 3)
    row_total = CLIPS * 2 * FRAMES
    base = jax.random.normal(key_base, (row_total, D), jnp.float32)
    base = jnp.clip(base, -6.0, 6.0)
    clip_scale = jnp.exp(jax.random.uniform(key_clip, (CLIPS, 1), jnp.float32, 0.0, jnp.log(3.0)))
    row_scale = jnp.exp(jax.random.uniform(key_row, (row_total, 1), jnp.float32, -0.69, 0.69))
    scale = jnp.repeat(clip_scale, 2 * FRAMES, axis=0) * row_scale
    return (base * scale).astype(jnp.bfloat16)


def move_to(ranking, value, place):
    current = jnp.argmax(ranking == value).astype(jnp.int32)
    displaced = ranking[place]
    ranking = ranking.at[current].set(displaced)
    return ranking.at[place].set(value)


def draw_codes(key, part):
    living = CODES - CODES // 16
    key_order, key_ceiling, key_rank, key_place = jax.random.split(jax.random.fold_in(key, 23), 4)
    columns = []
    for level_index in range(LEVELS):
        ranking = jax.random.permutation(jax.random.fold_in(key_order, level_index), CODES).astype(jnp.int32)
        places = jax.random.randint(jax.random.fold_in(key_place, level_index), (2,), 0, living // 4).astype(jnp.int32)
        ranking = move_to(ranking, 0, places[0])
        ranking = move_to(ranking, CODES - 1, places[1] + living // 4)
        ceiling = jax.random.randint(jax.random.fold_in(key_ceiling, level_index), (CLIPS, FRAMES), 1, living + 1)
        rank_index = jax.random.randint(jax.random.fold_in(key_rank, level_index), (CLIPS, FRAMES), 0, ceiling)
        columns.append(ranking[rank_index])
    return jnp.stack(columns, 1).astype(jnp.int32)


def noise(stream_key, dims, width, bound, held_as=jnp.bfloat16):
    drawn = jax.random.normal(stream_key, dims, jnp.float32) * width
    return jnp.minimum(jnp.maximum(drawn, -bound), bound).astype(held_as)


def setup_inputs(seed: int = 0) -> dict:
    arg_keys = jax.random.split(jax.random.key(seed), 7)
    return {
        "feats": draw_feats(jax.random.fold_in(arg_keys[6], 71), 0),
        "codes": draw_codes(jax.random.fold_in(arg_keys[6], 71), 0),
        "conv_weight": noise(arg_keys[2], (KW * D, D), (KW * D) ** -0.5, 0.125),
        "conv_bias": noise(arg_keys[3], (D,), 0.5, 3.0, jnp.float32),
        "proj_weight": noise(arg_keys[4], (D, DZ), D ** -0.5, 0.25),
        "codebooks": noise(arg_keys[5], (LEVELS, CODES, DZ), 0.7, 4.1875),
    }


def clip_terms(running, inputs, conv_weight, conv_bias, proj_weight, codebooks):
    clip_feats, clip_codes = inputs
    frame_count = clip_feats.shape[0] // 2
    channels = clip_feats.shape[1]
    padded = jnp.concatenate([jnp.zeros((2, channels), clip_feats.dtype), clip_feats], 0)
    paired = padded.reshape(frame_count + 1, 2 * channels)
    unfold = jnp.concatenate([paired[:-1], paired[1:]], 1)
    conv_out = jnp.dot(unfold, conv_weight, preferred_element_type=jnp.float32) + conv_bias
    hidden = conv_out.astype(jnp.bfloat16)
    latent = jnp.dot(hidden, proj_weight, preferred_element_type=jnp.float32)
    residual = latent
    grad_total = jnp.zeros(latent.shape, jnp.float32)
    sums_list = []
    counts_list = []
    code_ids = jnp.arange(CODES, dtype=jnp.int32)
    for level_index in range(LEVELS):
        matches = clip_codes[level_index][:, None] == code_ids[None, :]
        onehot = matches.astype(jnp.float32)
        sums_list.append(jnp.dot(onehot.T, residual, precision=lax.Precision.HIGHEST))
        counts_list.append(jnp.sum(onehot, 0))
        chosen = jnp.dot(matches.astype(jnp.bfloat16), codebooks[level_index], preferred_element_type=jnp.float32)
        residual = residual - chosen
        grad_total = grad_total + residual
    latent_grad = grad_total.astype(jnp.bfloat16)
    proj_term = jnp.dot(hidden.T, latent_grad, preferred_element_type=jnp.float32)
    hidden_grad = jnp.dot(latent_grad, proj_weight.T, preferred_element_type=jnp.float32).astype(jnp.bfloat16)
    bias_term = jnp.sum(hidden_grad.astype(jnp.float32), 0)
    corr_term = jnp.dot(unfold.T, latent_grad, preferred_element_type=jnp.float32)
    grad_unfold = jnp.dot(hidden_grad, conv_weight.T, preferred_element_type=jnp.float32)
    first_half = grad_unfold[:, :2 * channels]
    second_half = grad_unfold[:, 2 * channels:]
    shifted = jnp.concatenate([first_half[1:], jnp.zeros((1, 2 * channels), jnp.float32)], 0)
    grad_paired = shifted + second_half
    grad_feats = grad_paired.reshape(2 * frame_count, channels).astype(jnp.bfloat16)
    corr_sum, proj_sum, bias_sum, code_sums, code_counts = running
    updated = (corr_sum + corr_term, proj_sum + proj_term, bias_sum + bias_term,
               code_sums + jnp.stack(sums_list), code_counts + jnp.stack(counts_list))
    return updated, grad_feats


def reference(feats, codes, conv_weight, conv_bias, proj_weight, codebooks):
    clip_rows = feats.reshape(CLIPS, 2 * FRAMES, D)
    init = (jnp.zeros((KW * D, DZ), jnp.float32), jnp.zeros((D, DZ), jnp.float32),
            jnp.zeros((D,), jnp.float32), jnp.zeros((LEVELS, CODES, DZ), jnp.float32),
            jnp.zeros((LEVELS, CODES), jnp.float32))

    def step_clip(running, inputs):
        return clip_terms(running, inputs, conv_weight, conv_bias, proj_weight, codebooks)

    running, grads = lax.scan(step_clip, init, (clip_rows, codes))
    corr_sum, proj_sum, bias_sum, code_sums, code_counts = running
    conv_grad = jnp.dot(corr_sum, proj_weight.astype(jnp.float32).T, precision=lax.Precision.HIGHEST) / TOTAL
    proj_grad = proj_sum / TOTAL
    bias_grad = bias_sum / TOTAL
    code_means = (code_sums / jnp.maximum(code_counts, 1.0)[:, :, None]).astype(jnp.bfloat16)
    code_usage = code_counts * (CODES / TOTAL)
    return grads.reshape(ROWS_IN, D), conv_grad, bias_grad, proj_grad, code_means, code_usage
```

```python
import functools

import jax
import jax.numpy as jnp
from jax import lax
from jax.experimental import pallas as pl
from jax.experimental.pallas import tpu as pltpu
from jax.sharding import PartitionSpec as P

BF16 = jnp.bfloat16
F32 = jnp.float32
LANES = 128
VMEM_LIMIT = 48 * 1024 * 1024


def log2(value):
    assert value & (value - 1) == 0
    return value.bit_length() - 1


def nn(a, b):
    return lax.dot_general(a, b, (((1,), (0,)), ((), ())), preferred_element_type=F32)


def nt(a, b):
    return lax.dot_general(a, b, (((1,), (1,)), ((), ())), preferred_element_type=F32)


def call(body, out_shape, args, scalars=0, scratch=(), aliases=None, flops=0):
    specs = [pl.BlockSpec(memory_space=pltpu.SMEM)] * scalars
    specs += [pl.BlockSpec(memory_space=pltpu.VMEM)] * (len(args) - scalars)
    many = isinstance(out_shape, (list, tuple))
    out_specs = [pl.BlockSpec(memory_space=pltpu.VMEM)] * len(out_shape) if many else pl.BlockSpec(
        memory_space=pltpu.VMEM)
    moved = sum(a.size * a.dtype.itemsize for a in args)
    return pl.pallas_call(
        body,
        out_shape=out_shape,
        in_specs=specs,
        out_specs=out_specs,
        scratch_shapes=list(scratch),
        input_output_aliases=aliases or {},
        compiler_params=pltpu.CompilerParams(vmem_limit_bytes=VMEM_LIMIT),
        cost_estimate=pl.CostEstimate(flops=flops, bytes_accessed=moved, transcendentals=0),
    )(*args)


def shape(dims, dtype):
    return jax.ShapeDtypeStruct(dims, dtype)


def digits_of(value):
    high = value.astype(BF16).astype(F32)
    rest = value - high
    middle = rest.astype(BF16).astype(F32)
    low = (rest - middle).astype(BF16).astype(F32)
    return high, middle, low


def one_hot(codes, axis_codes, first, count):
    frames = codes.shape[1 - axis_codes]
    dims = (count, frames) if axis_codes == 0 else (frames, count)
    places = lax.broadcasted_iota(jnp.int32, dims, axis_codes) + first
    return jnp.where(codes == places, 1.0, 0.0).astype(BF16)


def local_kernel(feats, weight, bias, codes, books, unfold, conv, chosen, wide):
    rows, channels = feats.shape
    frames = rows // 2
    for j in range(channels // LANES):
        wide[j, 0:8, :] = jnp.zeros((8, LANES), F32)
        wide[j, 8:, :] = feats[:, j * LANES:(j + 1) * LANES].astype(F32)
        for tap in range(4):
            start = tap * channels + j * LANES
            unfold[:, start:start + LANES] = wide[j, pl.ds(6 + tap, frames, stride=2), :].astype(BF16)
    conv[...] = nn(unfold[...], weight[...]) + bias[...]
    for level in range(books.shape[0]):
        matches = one_hot(codes[:, level:level + 1], 1, 0, books.shape[1])
        chosen[level] = nn(matches, books[level]).astype(BF16)


def pack_extras(block, values, stride):
    block[...] = jnp.zeros(block.shape, F32)
    for digit, part in enumerate(digits_of(values)):
        for j in range(values.shape[1] // LANES):
            block[digit * stride + j:digit * stride + j + 1, :] = part[:, j * LANES:(j + 1) * LANES]


def forward_kernel(split, place, halo, unfold_in, conv, chosen, weight, proj, codes,
                   unfold, latent_out, hidden_grad, send, keep, corr, block):
    frames, width = unfold.shape
    half = width // 2
    levels = chosen.shape[0]
    dz = proj.shape[1]
    row = lax.broadcasted_iota(jnp.int32, (16, half), 0)
    left = jnp.concatenate([halo[0:1, :], halo[1:2, :]], 1).astype(F32)
    head = jnp.where(row == 0, jnp.broadcast_to(left, (16, half)), 0.0)
    unfold[0:16, 0:half] = (unfold_in[0:16, 0:half].astype(F32) + head).astype(BF16)
    fix = nn(head.astype(BF16), weight[0:half, :])
    hidden = jnp.concatenate([conv[0:16, :] + fix, conv[16:, :]], 0).astype(BF16)
    latent = nn(hidden, proj[...])
    latent_out[0:frames, :] = latent.astype(BF16)
    residual = latent
    total = jnp.zeros_like(latent)
    for level in range(levels):
        residual = residual - chosen[level].astype(F32)
        total = total + residual
    latent_grad = total.astype(BF16)
    back = nt(latent_grad, proj[...]).astype(BF16)
    hidden_grad[...] = back
    flipped = jnp.transpose(latent_grad.astype(F32)).astype(BF16)
    pieces_a = width // LANES
    chunk = 512
    for start in range(0, width, chunk):
        product = nn(flipped, unfold[:, start:start + chunk])
        for j in range(chunk // LANES):
            corr[start // LANES + j] = product[:, j * LANES:(j + 1) * LANES]
    product = nn(flipped, hidden)
    pieces_c = hidden.shape[1] // LANES
    for j in range(pieces_c):
        corr[pieces_a + j] = product[:, j * LANES:(j + 1) * LANES]
    at = 0
    for first, count, bits, halved in place:
        shown = count // 2 if halved else count
        for position in range(shown):
            rest = 0
            others = bits[1:] if halved else bits
            for k, bit in enumerate(others):
                rest += ((position >> (len(others) - 1 - k)) & 1) << bit
            where_send = first + rest
            where_keep = first + rest
            if halved:
                where_send = where_send + (1 - split[0]) * (1 << bits[0])
                where_keep = where_keep + split[0] * (1 << bits[0])
            send[at * dz:(at + 1) * dz, :] = corr[where_send].astype(BF16)
            keep[at * dz:(at + 1) * dz, :] = corr[where_keep]
            at += 1
    extra = block.shape[0]
    pack_extras(block, jnp.sum(back.astype(F32), 0, keepdims=True), extra // 4)
    send[at * dz:at * dz + extra, :] = block[...].astype(BF16)
    keep[at * dz:at * dz + extra, :] = block[...]
    block_codes = codes[...]
    rows = []
    for level in range(levels):
        for part in (block_codes[level:level + 1] >> 8, block_codes[level:level + 1] & 255):
            for start in range(0, frames, dz):
                piece = part[:, start:start + dz].astype(F32)
                if piece.shape[1] < dz:
                    piece = jnp.concatenate([piece, jnp.zeros((1, dz - piece.shape[1]), F32)], 1)
                rows.append(piece)
    rows.append(jnp.zeros((latent_out.shape[0] - frames - len(rows), dz), F32))
    latent_out[frames:, :] = jnp.concatenate(rows, 0).astype(BF16)


def step_kernel(halves, extra, bit, got, kept, send, keep):
    at_in = 0
    at_out = 0
    for rows, halved in halves:
        if halved:
            half = rows // 2
            away = pl.multiple_of(at_in + (1 - bit[0]) * half, 16)
            home = pl.multiple_of(at_in + bit[0] * half, 16)
            send[at_out:at_out + half, :] = (
                kept[pl.ds(away, half), :] + got[pl.ds(away, half), :].astype(F32)).astype(BF16)
            keep[at_out:at_out + half, :] = kept[pl.ds(home, half), :] + got[pl.ds(home, half), :].astype(F32)
            at_out += half
        else:
            total = (kept[at_in:at_in + rows, :] + got[at_in:at_in + rows, :].astype(F32)).astype(BF16)
            send[at_out:at_out + rows, :] = total
            keep[at_out:at_out + rows, :] = total.astype(F32)
            at_out += rows
        at_in += rows
    stride = extra // 4
    mine = kept[at_in:at_in + extra, :]
    theirs = got[at_in:at_in + extra, :].astype(F32)
    value = ((mine[0:stride] + mine[stride:2 * stride]) + mine[2 * stride:3 * stride]) + (
        (theirs[0:stride] + theirs[stride:2 * stride]) + theirs[2 * stride:3 * stride])
    parts = digits_of(value)
    block = jnp.concatenate(list(parts) + [jnp.zeros_like(value)], 0)
    send[at_out:at_out + extra, :] = block.astype(BF16)
    keep[at_out:at_out + extra, :] = block


def feat_kernel(grad, after, weight, out, wide, inter):
    frames, channels = grad.shape
    half = weight.shape[0] // 2
    wide[0:frames, :] = grad[...].astype(F32)
    wide[frames:, :] = jnp.broadcast_to(after[0:1, :].astype(F32), (8, channels))
    ahead = wide[pl.ds(1, frames), :].astype(BF16)
    for parity in range(2):
        rows = pl.ds(parity * (half // 2), half // 2)
        rows_after = pl.ds(half + parity * (half // 2), half // 2)
        both = nt(ahead, weight[rows, :]) + nt(grad[...], weight[rows_after, :])
        for j in range(channels // LANES):
            inter[j, pl.ds(parity, frames, stride=2), :] = both[:, j * LANES:(j + 1) * LANES]
    for j in range(channels // LANES):
        out[:, j * LANES:(j + 1) * LANES] = inter[j].astype(BF16)


def sums_kernel(frames, count_blocks, info, *refs):
    blocks, books, send, keep = refs[:count_blocks], refs[-3], refs[-2], refs[-1]
    levels, size, dz = books.shape
    own = send.shape[0] - 16
    first = info[1]
    sums = [jnp.zeros((own, dz), F32) for _ in range(levels)]
    counts = [jnp.zeros((8, own), F32) for _ in range(levels)]
    pairs = {}
    per = -(-frames // dz)
    ones = jnp.ones((8, frames), BF16)
    for ref in blocks:
        digits = ref[frames:, :].astype(F32)
        latent = ref[0:frames, :]
        mine = []
        every = []
        for level in range(levels):
            parts = []
            for digit in range(2):
                base = (level * 2 + digit) * per
                row = jnp.concatenate([digits[base + j:base + j + 1, :] for j in range(per)], 1)[:, :frames]
                parts.append(row)
            codes = (parts[0] * 256.0 + parts[1]).astype(jnp.int32)
            mine.append(one_hot(codes, 0, first, own))
            every.append(one_hot(codes, 0, 0, size) if level < levels - 1 else None)
        for level in range(levels):
            sums[level] = sums[level] + nn(mine[level], latent)
            counts[level] = counts[level] + nt(ones, mine[level])
            for earlier in range(level):
                product = nt(mine[level], every[earlier])
                key = (level, earlier)
                pairs[key] = pairs[key] + product if key in pairs else product
    for (level, earlier), table in pairs.items():
        high = jnp.floor(table * (1.0 / 256.0)) * 256.0
        low = table - high
        sums[level] = sums[level] - nn(high.astype(BF16), books[earlier]) - nn(low.astype(BF16), books[earlier])
    bit = info[0]
    for out, chosen in ((send, 1 - bit), (keep, bit)):
        value = jnp.where(chosen == 1, sums[1], sums[0])
        count = jnp.where(chosen == 1, counts[1], counts[0])
        out[0:own, :] = value.astype(out.dtype)
        out[own:, :] = count_rows(count[0:1], dz).astype(out.dtype)


def count_rows(count, width):
    high = jnp.floor(count * (1.0 / 65536.0))
    rest = count - high * 65536.0
    middle = jnp.floor(rest * (1.0 / 256.0))
    low = rest - middle * 256.0
    block = jnp.concatenate([high, middle, low, jnp.zeros((13, count.shape[1]), F32)], 0)
    if count.shape[1] < width:
        block = jnp.concatenate([block, jnp.zeros((16, width - count.shape[1]), F32)], 1)
    return block


def count_of(block, own):
    return (block[0:1] * 65536.0 + block[1:2] * 256.0 + block[2:3])[:, :own]


def sums_step_kernel(got, kept, out):
    own = out.shape[0] - 16
    out[0:own, :] = (kept[0:own, :].astype(F32) + got[0:own, :].astype(F32)).astype(BF16)
    mine = kept[own:, :].astype(F32)
    theirs = got[own:, :].astype(F32)
    out[own:, :] = count_rows(count_of(mine, own) + count_of(theirs, own), out.shape[1]).astype(BF16)


def means_kernel(got, kept, out):
    own = out.shape[0] - 16
    mine = kept[own:, :].astype(F32)
    theirs = got[own:, :].astype(F32)
    count = count_of(mine, own) + count_of(theirs, own)
    square = (own, own)
    same = lax.broadcasted_iota(jnp.int32, square, 0) == lax.broadcasted_iota(jnp.int32, square, 1)
    tall = jnp.sum(jnp.where(same, jnp.broadcast_to(count, square), 0.0), 1, keepdims=True)
    total = kept[0:own, :].astype(F32) + got[0:own, :].astype(F32)
    out[0:own, :] = (total / jnp.maximum(tall, 1.0)).astype(BF16)
    out[own:, :] = count_rows(count, out.shape[1]).astype(BF16)


def means_out_kernel(scale, bit, mine, theirs, means, usage):
    own = mine.shape[0] - 16
    means[bit[0]] = mine[0:own, :]
    means[1 - bit[0]] = theirs[0:own, :]
    first = count_of(mine[own:, :].astype(F32), own) * scale
    second = count_of(theirs[own:, :].astype(F32), own) * scale
    swap = bit[0] == 1
    usage[0:1, :] = jnp.where(swap, second, first)
    usage[1:2, :] = jnp.where(swap, first, second)


def conv_out_kernel(total_frames, info, got, kept, proj, out, wide):
    rows = out.shape[0]
    corr = kept[...] + got[...].astype(F32)
    flipped = jnp.transpose(corr)
    high = flipped.astype(BF16)
    low = (flipped - high.astype(F32)).astype(BF16)
    wide[...] = (nt(high, proj[...]) + nt(low, proj[...])) * (1.0 / total_frames)
    start = info[0]
    if rows % 8 == 0:
        out[...] = wide[pl.ds(pl.multiple_of(start, 8), rows), :]
    else:
        taken = wide[0:rows, :]
        for other in range(rows, wide.shape[0], rows):
            taken = jnp.where(start == other, wide[other:other + rows, :], taken)
        out[...] = taken


def proj_out_kernel(total_frames, dz, order, refs_count, info, *refs):
    parts, out = refs[:refs_count], refs[-1]
    scale = 1.0 / total_frames
    for j, (ref, places) in enumerate(zip(parts, order)):
        for k, index in enumerate(places):
            start = pl.multiple_of(info[index] * LANES, LANES)
            out[pl.ds(start, LANES), :] = jnp.transpose(ref[k * dz:(k + 1) * dz, :].astype(F32)) * scale


def shifted(block, axis, distance):
    devices = range(lax.axis_size(axis))
    route = [(i - distance, i) for i in devices if i - distance in devices]
    return lax.ppermute(block, axis, route)


def swapped(block, axis, bit):
    route = [(i, i ^ (1 << bit)) for i in range(lax.axis_size(axis))]
    return lax.ppermute(block, axis, route)


def shards(feats, codes, conv_weight, conv_bias, proj_weight, codebooks):
    dp, tm = lax.axis_size("dp"), lax.axis_size("tm")
    rows_in, channels = feats.shape
    frames = rows_in // 2
    levels, book_size, dz = codebooks.shape
    width = conv_weight.shape[0]
    total_frames = frames * dp * tm
    per_shard = book_size // tm
    dp_bits, tm_bits = log2(dp), log2(tm)
    at_dp, at_tm = lax.axis_index("dp"), lax.axis_index("tm")
    me = at_dp * tm + at_tm

    exchanges = [("dp", b, b + tm_bits) for b in range(dp_bits)]
    exchanges += [("tm", b, b) for b in reversed(range(tm_bits))]
    owner_bits = dp_bits + tm_bits
    pieces_a = width // LANES
    under = max(owner_bits - log2(pieces_a), 0)
    pieces_c = channels // LANES
    c_bits = min(log2(pieces_c), 2, dp_bits)
    a_split = [bit - under if bit >= under else None for _, _, bit in exchanges]
    c_split = [log2(pieces_c) - 1 - k if k < c_bits else None for k in range(len(exchanges))]

    def order_of(split, count):
        used = [b for b in split if b is not None]
        rest = [b for b in reversed(range(log2(count))) if b not in used]
        return used + rest

    order_a, order_c = order_of(a_split, pieces_a), order_of(c_split, pieces_c)

    def bit_of(axis, b):
        return ((at_dp if axis == "dp" else at_tm) >> b) & 1

    def bits_array(*values):
        return jnp.stack([jnp.asarray(v, jnp.int32) for v in values])

    halo = shifted(feats[-2:], "tm", 1)
    codes = codes[0]
    codes_tall = codes.T
    unfold, conv, chosen = call(
        local_kernel,
        [shape((frames, width), BF16), shape((frames, channels), F32), shape((levels, frames, dz), BF16)],
        [feats, conv_weight, conv_bias[None, :], codes_tall, codebooks],
        scratch=[pltpu.VMEM((channels // LANES, rows_in + 8, LANES), F32)],
        flops=2 * frames * (width * channels + levels * book_size * dz),
    )

    extra = 4 * (-(-channels // LANES // 8) * 8)
    first_a = a_split[0] is not None
    first_c = c_split[0] is not None
    plan = [(0, pieces_a, order_a, first_a), (pieces_a, pieces_c, order_c, first_c)]
    now_a = pieces_a // 2 if first_a else pieces_a
    now_c = pieces_c // 2 if first_c else pieces_c
    sent_rows = (now_a + now_c) * dz + extra
    code_rows = -(-(levels * 2 * -(-frames // dz)) // 16) * 16
    axis, b, _ = exchanges[0]
    _, latent, hidden_grad, send, keep = call(
        lambda split, *refs: forward_kernel(split, plan, *refs),
        [shape((frames, width), BF16), shape((frames + code_rows, dz), BF16), shape((frames, channels), BF16),
         shape((sent_rows, LANES), BF16), shape((sent_rows, LANES), F32)],
        [bits_array(bit_of(axis, b)), halo, unfold, conv, chosen, conv_weight, proj_weight, codes],
        scalars=1,
        scratch=[pltpu.VMEM((pieces_a + pieces_c, dz, LANES), F32), pltpu.VMEM((extra, LANES), F32)],
        aliases={2: 0},
        flops=2 * frames * (width * dz + 3 * channels * dz),
    )

    got = swapped(send, axis, b)
    blocks = [latent]
    for distance in range(1, tm):
        blocks.append(lax.ppermute(latent, "tm", [(i, (i + distance) % tm) for i in range(tm)]))
    after = shifted(hidden_grad[:16], "tm", -1)
    feat_grad = call(
        feat_kernel,
        shape((rows_in, channels), BF16),
        [hidden_grad, after, conv_weight],
        scratch=[pltpu.VMEM((frames + 8, channels), F32), pltpu.VMEM((channels // LANES, rows_in, LANES), F32)],
        flops=2 * frames * width * channels,
    )

    for k in range(1, len(exchanges)):
        axis, b, _ = exchanges[k]
        halves = [(now_a * dz, a_split[k] is not None), (now_c * dz, c_split[k] is not None)]
        now_a = now_a // 2 if halves[0][1] else now_a
        now_c = now_c // 2 if halves[1][1] else now_c
        sent_rows = (now_a + now_c) * dz + extra
        send, keep = call(
            functools.partial(step_kernel, halves, extra),
            [shape((sent_rows, LANES), BF16), shape((sent_rows, LANES), F32)],
            [bits_array(bit_of(axis, b)), got, keep],
            scalars=1,
        )
        got = swapped(send, axis, b)
    assert now_a == 1
    mid_c = now_a * dz
    mid_x = mid_c + now_c * dz

    owner_rows = width // (dp * tm)
    conv_grad = call(
        functools.partial(conv_out_kernel, total_frames),
        shape((owner_rows, channels), F32),
        [bits_array((me * owner_rows) % LANES), got[:mid_c], keep[:mid_c], proj_weight],
        scalars=1,
        scratch=[pltpu.VMEM((LANES, channels), F32)],
    )
    parts = [(got[mid_c:mid_x].astype(F32) + keep[mid_c:mid_x]).astype(BF16)]
    value = got[mid_x:].astype(F32), keep[mid_x:]
    stride = extra // 4
    bias_sum = sum((v[:stride] + v[stride:2 * stride]) + v[2 * stride:3 * stride] for v in value)
    bias_grad = bias_sum[:channels // LANES].reshape(channels) / total_frames

    names = [[0]] if now_c == 1 else [list(range(now_c))]
    masks = [0]
    for k in reversed(range(c_bits)):
        axis, b, _ = exchanges[k]
        arrived = [swapped(part, axis, b) for part in parts]
        parts = parts + arrived
        masks = masks + [m | (1 << k) for m in masks]
    own_piece = 0
    for k in range(c_bits):
        axis, b, _ = exchanges[k]
        own_piece = own_piece + (bit_of(axis, b) << c_split[k])
    places, order = [], []
    for m in masks:
        flip = sum(1 << c_split[k] for k in range(c_bits) if m >> k & 1)
        group = []
        for inner in range(now_c):
            group.append(len(places))
            places.append((own_piece ^ flip) + inner)
        order.append(group)
    proj_grad = call(
        functools.partial(proj_out_kernel, total_frames, dz, order, len(parts)),
        shape((channels, dz), F32),
        [bits_array(*places)] + parts,
        scalars=1,
    )

    core = bit_of("dp", 0)
    send_sums, keep_sums = call(
        functools.partial(sums_kernel, frames, len(blocks)),
        [shape((per_shard + 16, dz), BF16), shape((per_shard + 16, dz), F32)],
        [bits_array(core, at_tm * per_shard)] + blocks + [codebooks],
        scalars=1,
        flops=2 * len(blocks) * frames * per_shard * (book_size + 2 * dz),
    )
    for b in range(dp_bits):
        got_sums = swapped(send_sums, "dp", b)
        last = b == dp_bits - 1
        send_sums = call(
            means_kernel if last else sums_step_kernel,
            shape((per_shard + 16, dz), BF16),
            [got_sums, keep_sums],
        )
        keep_sums = send_sums
    other = swapped(send_sums, "dp", 0)
    code_means, code_usage = call(
        functools.partial(means_out_kernel, book_size / total_frames),
        [shape((levels, per_shard, dz), BF16), shape((levels, per_shard), F32)],
        [bits_array(core), send_sums, other],
        scalars=1,
    )
    return feat_grad, conv_grad, bias_grad, proj_grad, code_means, code_usage


def solution(mesh):
    placed = (P(("dp", "tm"), None), P("dp", None, "tm"), P(), P(), P(), P())
    return jax.shard_map(
        shards,
        mesh=mesh,
        in_specs=placed,
        out_specs=(
            P(("dp", "tm"), None),
            P(("dp", "tm"), None),
            P(),
            P(),
            P(None, "tm", None),
            P(None, "tm"),
        ),
        check_vma=False,
    )
```

```python
import functools

import jax
import jax.numpy as jnp
from jax import lax
from jax.experimental import pallas as pl
from jax.experimental.pallas import tpu as pltpu
from jax.sharding import PartitionSpec as P

BF16 = jnp.bfloat16
F32 = jnp.float32
LANES = 128
VMEM_LIMIT = 16 * 1024 * 1024


def log2(value):
    assert value & (value - 1) == 0
    return value.bit_length() - 1


def nn(a, b):
    return lax.dot_general(a, b, (((1,), (0,)), ((), ())), preferred_element_type=F32)


def nt(a, b):
    return lax.dot_general(a, b, (((1,), (1,)), ((), ())), preferred_element_type=F32)


ANY = pl.ANY
VMEM = pltpu.VMEM


def call(body, out_shape, args, after=(), anywhere=(), scratch=(), aliases=None, flops=0):
    count = len(args)

    def kernel(*refs):
        body(*refs[:count], *refs[count + len(after):])

    specs = [pl.BlockSpec(memory_space=pltpu.SMEM)]
    specs += [pl.BlockSpec(memory_space=ANY if k in anywhere else VMEM) for k in range(1, count)]
    specs += [pl.BlockSpec(memory_space=ANY)] * len(after)
    moved = sum(a.size * a.dtype.itemsize for a in args)
    many = isinstance(out_shape, (list, tuple))
    return pl.pallas_call(
        kernel,
        out_shape=out_shape,
        in_specs=specs,
        out_specs=[pl.BlockSpec(memory_space=VMEM)] * len(out_shape) if many else pl.BlockSpec(memory_space=VMEM),
        scratch_shapes=list(scratch),
        input_output_aliases=aliases or {},
        compiler_params=pltpu.CompilerParams(vmem_limit_bytes=VMEM_LIMIT),
        cost_estimate=pl.CostEstimate(flops=flops, bytes_accessed=moved, transcendentals=0),
    )(*args, *after)


def shape(dims, dtype):
    return jax.ShapeDtypeStruct(dims, dtype)


def digits_of(value):
    high = value.astype(BF16).astype(F32)
    rest = value - high
    middle = rest.astype(BF16).astype(F32)
    low = (rest - middle).astype(BF16).astype(F32)
    return high, middle, low


def one_hot(codes, axis_codes, first, count):
    frames = codes.shape[1 - axis_codes]
    dims = (count, frames) if axis_codes == 0 else (frames, count)
    places = lax.broadcasted_iota(jnp.int32, dims, axis_codes) + first
    return jnp.where(codes == places, 1.0, 0.0).astype(BF16)


def local_kernel(info, feats_in, weight_in, bias, codes, books_in, proj_in,
                 unfold, conv, chosen, weight, proj, feats, books, wide, sems):
    loads = [pltpu.make_async_copy(src, dst, sems.at[k]) for k, (src, dst) in enumerate(
        [(feats_in, feats), (weight_in, weight), (books_in, books), (proj_in, proj)])]
    for load in loads:
        load.start()
    rows, channels = feats.shape
    frames = rows // 2
    loads[0].wait()
    for j in range(channels // LANES):
        wide[j, 0:8, :] = jnp.zeros((8, LANES), F32)
        wide[j, 8:, :] = feats[:, j * LANES:(j + 1) * LANES].astype(F32)
        for tap in range(4):
            start = tap * channels + j * LANES
            unfold[:, start:start + LANES] = wide[j, pl.ds(6 + tap, frames, stride=2), :].astype(BF16)
    loads[1].wait()
    conv[...] = nn(unfold[...], weight[...]) + bias[...]
    loads[2].wait()
    levels = books.shape[0]
    padded = jnp.concatenate([codes[...].astype(F32), jnp.zeros((8 - levels, frames), F32)], 0)
    tall = jnp.transpose(padded).astype(jnp.int32)
    for level in range(levels):
        matches = one_hot(tall[:, level:level + 1], 1, 0, books.shape[1])
        chosen[level] = nn(matches, books[level]).astype(BF16)
    loads[3].wait()


def walk(order, halved, count):
    others = order[1:] if halved else order
    shown = count // 2 if halved else count
    step = 2 if shown > 1 and others[-1] == 0 else 1
    for position in range(0, shown, step):
        piece = 0
        for k, bit in enumerate(others):
            piece += ((position >> (len(others) - 1 - k)) & 1) << bit
        yield position, piece, step


def correlate(flipped, sources, plan, bit, out):
    dz = flipped.shape[0]
    at = 0
    for source, (count, order, halved) in zip(sources, plan):
        shown = count // 2 if halved else count
        for position, piece, step in walk(order, halved, count):
            if halved:
                column = pl.multiple_of((piece + (bit << order[0])) * LANES, LANES)
                product = nn(flipped, source[:, pl.ds(column, step * LANES)])
            else:
                product = nn(flipped, source[:, piece * LANES:(piece + step) * LANES])
            for j in range(step):
                top = (at + position + j) * dz
                out[top:top + dz, :] = product[:, j * LANES:(j + 1) * LANES].astype(out.dtype)
        at += shown
    return at * dz


def code_digits(codes, dz, rows):
    parts = []
    for part in (codes >> 8, codes & 255):
        for start in range(0, codes.shape[1], dz):
            piece = part[:, start:start + dz].astype(F32)
            if piece.shape[1] < dz:
                piece = jnp.concatenate([piece, jnp.zeros((1, dz - piece.shape[1]), F32)], 1)
            parts.append(piece)
    parts.append(jnp.zeros((rows - len(parts), dz), F32))
    return jnp.concatenate(parts, 0).astype(BF16)


def codes_of(block, frames):
    dz = block.shape[1]
    per = -(-frames // dz)
    digits = block[...].astype(F32)
    parts = [jnp.concatenate([digits[k * per + j:k * per + j + 1, :] for j in range(per)], 1)[:, :frames]
             for k in range(2)]
    return (parts[0] * 256.0 + parts[1]).astype(jnp.int32)


def forward_kernel(plan, info, halo, unfold_in, conv, chosen, weight, proj, codes,
                   unfold, hidden, latent_grad, flipped, own, send):
    frames, width = unfold.shape
    half = width // 2
    dz = proj.shape[1]
    row = lax.broadcasted_iota(jnp.int32, (16, half), 0)
    left = jnp.concatenate([halo[0:1, :], halo[1:2, :]], 1).astype(F32)
    head = jnp.where(row == 0, jnp.broadcast_to(left, (16, half)), 0.0)
    unfold[0:16, 0:half] = (unfold_in[0:16, 0:half].astype(F32) + head).astype(BF16)
    fix = nn(head.astype(BF16), weight[0:half, :])
    hidden[...] = jnp.concatenate([conv[0:16, :] + fix, conv[16:, :]], 0).astype(BF16)
    latent = nn(hidden[...], proj[...])
    once = latent - chosen[0].astype(F32)
    total = once + (once - chosen[1].astype(F32))
    latent_grad[...] = total.astype(BF16)
    flipped[...] = jnp.transpose(latent_grad[...].astype(F32)).astype(BF16)
    bit = info[0]
    at = correlate(flipped[...], (unfold, hidden), plan, 1 - bit, send)
    code_rows = own.shape[0] - frames
    digits = [code_digits(codes[level:level + 1], dz, code_rows) for level in range(2)]
    own[0:frames, :] = jnp.where(bit == 1, once, latent).astype(BF16)
    own[frames:, :] = jnp.where(bit == 1, digits[1], digits[0])
    other = jnp.where(bit == 1, latent, once).astype(BF16)
    other_digits = jnp.where(bit == 1, digits[0], digits[1])
    for j in range(dz // LANES):
        send[at:at + frames, :] = other[:, j * LANES:(j + 1) * LANES]
        send[at + frames:at + frames + code_rows, :] = other_digits[:, j * LANES:(j + 1) * LANES]
        at += frames + code_rows


def rest_kernel(plan, info, flipped, unfold, hidden, latent_grad, proj, keep, hidden_grad, extras):
    correlate(flipped[...], (unfold, hidden), plan, info[0], keep)
    back = nt(latent_grad[...], proj[...]).astype(BF16)
    hidden_grad[...] = back
    stride = extras.shape[0] // 4
    extras[...] = jnp.zeros(extras.shape, F32)
    sums = jnp.sum(back.astype(F32), 0, keepdims=True)
    for digit, part in enumerate(digits_of(sums)):
        for j in range(sums.shape[1] // LANES):
            extras[digit * stride + j:digit * stride + j + 1, :] = part[:, j * LANES:(j + 1) * LANES]


def split_sum(halves, bit, got, kept, send, keep):
    at_in = 0
    at_out = 0
    for rows, halved in halves:
        if halved:
            half = rows // 2
            away = pl.multiple_of(at_in + (1 - bit) * half, 16)
            home = pl.multiple_of(at_in + bit * half, 16)
            send[at_out:at_out + half, :] = (
                kept[pl.ds(away, half), :] + got[pl.ds(away, half), :].astype(F32)).astype(BF16)
            keep[at_out:at_out + half, :] = kept[pl.ds(home, half), :] + got[pl.ds(home, half), :].astype(F32)
            at_out += half
        else:
            total = (kept[at_in:at_in + rows, :] + got[at_in:at_in + rows, :].astype(F32)).astype(BF16)
            send[at_out:at_out + rows, :] = total
            keep[at_out:at_out + rows, :] = total.astype(F32)
            at_out += rows
        at_in += rows
    return at_in, at_out


def add_digits(mine, theirs):
    stride = mine.shape[0] // 4
    return ((mine[0:stride] + mine[stride:2 * stride]) + mine[2 * stride:3 * stride]) + (
        (theirs[0:stride] + theirs[stride:2 * stride]) + theirs[2 * stride:3 * stride])


def digit_block(value):
    return jnp.concatenate(list(digits_of(value)) + [jnp.zeros_like(value)], 0)


def first_step_kernel(halves, place, info, got, kept, extras, send, keep):
    _, at = split_sum(halves, info[place], got, kept, send, keep)
    send[at:, :] = extras[...].astype(BF16)
    keep[at:, :] = extras[...]


def step_kernel(halves, place, info, got, kept, send, keep):
    at_in, at_out = split_sum(halves, info[place], got, kept, send, keep)
    block = digit_block(add_digits(kept[at_in:, :], got[at_in:, :].astype(F32)))
    send[at_out:, :] = block.astype(BF16)
    keep[at_out:, :] = block


def feat_kernel(info, grad, after, weight, out, wide, inter):
    frames, channels = grad.shape
    half = weight.shape[0] // 2
    wide[0:frames, :] = grad[...].astype(F32)
    wide[frames:, :] = jnp.broadcast_to(after[0:1, :].astype(F32), (8, channels))
    ahead = wide[pl.ds(1, frames), :].astype(BF16)
    for parity in range(2):
        rows = pl.ds(parity * (half // 2), half // 2)
        rows_after = pl.ds(half + parity * (half // 2), half // 2)
        both = nt(ahead, weight[rows, :]) + nt(grad[...], weight[rows_after, :])
        for j in range(channels // LANES):
            inter[j, pl.ds(parity, frames, stride=2), :] = both[:, j * LANES:(j + 1) * LANES]
    for j in range(channels // LANES):
        out[:, j * LANES:(j + 1) * LANES] = inter[j].astype(BF16)


def sums_kernel(first, place, info, got, own, hidden_grad, keep, *sends):
    row, sends = sends[-1], sends[:-1]
    row[...] = hidden_grad[0:16, :]
    rows, dz = own.shape
    theirs = jnp.concatenate([got[first + j * rows:first + (j + 1) * rows, :] for j in range(dz // LANES)], 1)
    frames = hidden_grad.shape[0]
    ones = jnp.ones((8, frames), BF16)
    parts = []
    for block in (own[...], theirs):
        parts.append((block[0:frames, :], codes_of(block[frames:, :], frames)))
    for shift, out in enumerate((keep,) + sends):
        count = out.shape[0] - 16
        total = jnp.zeros((count, dz), F32)
        counts = jnp.zeros((8, count), F32)
        for values, codes in parts:
            matches = one_hot(codes, 0, info[place + shift], count)
            total = total + nn(matches, values)
            counts = counts + nt(ones, matches)
        out[0:count, :] = total.astype(out.dtype)
        out[count:, :] = count_rows(counts[0:1], dz).astype(out.dtype)


def count_rows(count, width):
    high = jnp.floor(count * (1.0 / 65536.0))
    rest = count - high * 65536.0
    middle = jnp.floor(rest * (1.0 / 256.0))
    low = rest - middle * 256.0
    block = jnp.concatenate([high, middle, low, jnp.zeros((13, count.shape[1]), F32)], 0)
    if count.shape[1] < width:
        block = jnp.concatenate([block, jnp.zeros((16, width - count.shape[1]), F32)], 1)
    return block


def count_of(block, own):
    return (block[0:1] * 65536.0 + block[1:2] * 256.0 + block[2:3])[:, :own]


def sums_step_kernel(info, kept, *refs):
    gots, out = refs[:-1], refs[-1]
    own = out.shape[0] - 16
    total = kept[0:own, :].astype(F32)
    count = count_of(kept[own:, :].astype(F32), own)
    for got in gots:
        total = total + got[0:own, :].astype(F32)
        count = count + count_of(got[own:, :].astype(F32), own)
    out[0:own, :] = total.astype(BF16)
    out[own:, :] = count_rows(count, out.shape[1]).astype(BF16)


def means_kernel(info, kept, got, out):
    own = out.shape[0] - 16
    count = count_of(kept[own:, :].astype(F32), own) + count_of(got[own:, :].astype(F32), own)
    square = (own, own)
    same = lax.broadcasted_iota(jnp.int32, square, 0) == lax.broadcasted_iota(jnp.int32, square, 1)
    tall = jnp.sum(jnp.where(same, jnp.broadcast_to(count, square), 0.0), 1, keepdims=True)
    total = kept[0:own, :].astype(F32) + got[0:own, :].astype(F32)
    out[0:own, :] = (total / jnp.maximum(tall, 1.0)).astype(BF16)
    out[own:, :] = count_rows(count, out.shape[1]).astype(BF16)


def means_out_kernel(scale, info, mine, theirs, means, usage):
    own = mine.shape[0] - 16
    bit = info[0]
    means[bit] = mine[0:own, :]
    means[1 - bit] = theirs[0:own, :]
    first = count_of(mine[own:, :].astype(F32), own) * scale
    second = count_of(theirs[own:, :].astype(F32), own) * scale
    usage[0:1, :] = jnp.where(bit == 1, second, first)
    usage[1:2, :] = jnp.where(bit == 1, first, second)


def last_kernel(first, second, got, kept, pieces, extras):
    pieces[...] = (kept[first:second, :] + got[first:second, :].astype(F32)).astype(BF16)
    block = digit_block(add_digits(kept[second:, :], got[second:, :].astype(F32)))
    extras[0:second - first, :] = pieces[...]
    extras[second - first:, :] = block.astype(BF16)


def conv_out_kernel(total_frames, place, info, got, kept, proj, out, wide):
    rows = out.shape[0]
    corr = kept[0:proj.shape[1], :] + got[0:proj.shape[1], :].astype(F32)
    flipped = jnp.transpose(corr)
    high = flipped.astype(BF16)
    low = (flipped - high.astype(F32)).astype(BF16)
    wide[...] = (nt(high, proj[...]) + nt(low, proj[...])) * (1.0 / total_frames)
    start = info[place]
    if rows % 8 == 0:
        out[...] = wide[pl.ds(pl.multiple_of(start, 8), rows), :]
    else:
        taken = wide[0:rows, :]
        for other in range(rows, wide.shape[0], rows):
            taken = jnp.where(start == other, wide[other:other + rows, :], taken)
        out[...] = taken


def proj_out_kernel(total_frames, dz, place, inner, info, mine, *refs):
    parts, out, bias = refs[:-2], refs[-2], refs[-1]
    scale = 1.0 / total_frames
    for j, ref in enumerate(parts):
        for k in range(inner):
            start = pl.multiple_of((info[place + j] + k) * LANES, LANES)
            out[pl.ds(start, LANES), :] = jnp.transpose(ref[k * dz:(k + 1) * dz, :].astype(F32)) * scale
    top = inner * dz
    value = add_digits(mine[top:, :].astype(F32), parts[1][top:, :].astype(F32)) * scale
    for j in range(bias.shape[1] // LANES):
        bias[:, j * LANES:(j + 1) * LANES] = value[j:j + 1, :]


def shifted(block, axis, distance):
    devices = range(lax.axis_size(axis))
    route = [(i - distance, i) for i in devices if i - distance in devices]
    return lax.ppermute(block, axis, route)


def swapped(block, axis, mask):
    return lax.ppermute(block, axis, [(i, i ^ mask) for i in range(lax.axis_size(axis))])


def shards(feats, codes, conv_weight, conv_bias, proj_weight, codebooks):
    dp, tm = lax.axis_size("dp"), lax.axis_size("tm")
    rows_in, channels = feats.shape
    frames = rows_in // 2
    levels, book_size, dz = codebooks.shape
    assert levels == 2
    width = conv_weight.shape[0]
    total_frames = frames * dp * tm
    per_shard = book_size // tm
    dp_bits, tm_bits = log2(dp), log2(tm)
    owner_rows = width // (dp * tm)

    exchanges = [("dp", b, b + tm_bits) for b in range(dp_bits)]
    exchanges += [("tm", b, b) for b in reversed(range(tm_bits))]
    pieces_a, pieces_c = width // LANES, channels // LANES
    under = max(dp_bits + tm_bits - log2(pieces_a), 0)
    c_bits = min(log2(pieces_c), 2, dp_bits)
    a_split = [bit - under if bit >= under else None for _, _, bit in exchanges]
    c_split = [log2(pieces_c) - 1 - k if k < c_bits else None for k in range(len(exchanges))]

    def order_of(split, count):
        used = [b for b in split if b is not None]
        return used + [b for b in reversed(range(log2(count))) if b not in used]

    plan = [(pieces_a, order_of(a_split, pieces_a), a_split[0] is not None),
            (pieces_c, order_of(c_split, pieces_c), c_split[0] is not None)]
    now_a = pieces_a // 2 if plan[0][2] else pieces_a
    now_c = pieces_c // 2 if plan[1][2] else pieces_c

    at_dp, at_tm = lax.axis_index("dp"), lax.axis_index("tm")
    bits = [((at_dp if axis == "dp" else at_tm) >> b) & 1 for axis, b, _ in exchanges]
    masks = list(range(1 << c_bits))
    own_piece = sum((bits[k] << c_split[k]) for k in range(c_bits))
    flips = [sum(1 << c_split[k] for k in range(c_bits) if m >> k & 1) for m in masks]
    at_start = len(bits)
    at_codes = at_start + 1
    at_pieces = at_codes + tm
    info = jnp.stack(
        bits + [((at_dp * tm + at_tm) * owner_rows) & (LANES - 1)]
        + [((at_tm + shift) & (tm - 1)) * per_shard for shift in range(tm)]
        + [own_piece ^ flip for flip in flips]).astype(jnp.int32)

    halo = shifted(feats[-2:], "tm", 1)
    codes = codes[0]
    unfold, conv, chosen, weight, proj = call(
        local_kernel,
        [shape((frames, width), BF16), shape((frames, channels), F32), shape((levels, frames, dz), BF16),
         shape(conv_weight.shape, BF16), shape(proj_weight.shape, BF16)],
        [info, feats, conv_weight, conv_bias[None, :], codes, codebooks, proj_weight],
        anywhere=(1, 2, 5, 6),
        scratch=[VMEM((rows_in, channels), BF16), VMEM(codebooks.shape, BF16),
                 VMEM((channels // LANES, rows_in + 8, LANES), F32), pltpu.SemaphoreType.DMA((4,))],
        flops=2 * frames * (width * channels + levels * book_size * dz),
    )

    extra = 4 * (-(-channels // LANES // 8) * 8)
    code_rows = -(-(2 * -(-frames // dz)) // 16) * 16
    corr_rows = (now_a + now_c) * dz
    rows_b = frames + code_rows
    unfold, hidden, latent_grad, flipped, own, send = call(
        functools.partial(forward_kernel, plan),
        [shape((frames, width), BF16), shape((frames, channels), BF16), shape((frames, dz), BF16),
         shape((dz, frames), BF16), shape((rows_b, dz), BF16),
         shape((corr_rows + rows_b * (dz // LANES), LANES), BF16)],
        [info, halo, unfold, conv, chosen, weight, proj, codes],
        aliases={2: 0},
        flops=2 * frames * (width * dz + 3 * channels * dz),
    )
    got = swapped(send, "dp", 1)
    keep, hidden_grad, extras = call(
        functools.partial(rest_kernel, plan),
        [shape((corr_rows, LANES), F32), shape((frames, channels), BF16), shape((extra, LANES), F32)],
        [info, flipped, unfold, hidden, latent_grad, proj],
        after=[send],
        flops=2 * frames * (width * dz // 2 + channels * dz),
    )

    def step(k, body, args, after):
        nonlocal now_a, now_c
        halves = [(now_a * dz, a_split[k] is not None), (now_c * dz, c_split[k] is not None)]
        now_a = now_a // 2 if halves[0][1] else now_a
        now_c = now_c // 2 if halves[1][1] else now_c
        rows = (now_a + now_c) * dz + extra
        return call(
            functools.partial(body, halves, k),
            [shape((rows, LANES), BF16), shape((rows, LANES), F32)],
            [info] + args, after=after)

    def exchange(k, block):
        axis, b, _ = exchanges[k]
        return swapped(block, axis, 1 << b)

    send, keep = step(1, first_step_kernel, [got, keep, extras], [])
    got_x = exchange(1, send)
    sums = call(
        functools.partial(sums_kernel, corr_rows, at_codes),
        [shape((per_shard + 16, dz), F32)] + [shape((per_shard + 16, dz), BF16)] * (tm - 1)
        + [shape((16, channels), BF16)],
        [info, got, own, hidden_grad],
        after=[send],
        flops=4 * frames * book_size * dz,
    )
    ring = [lax.ppermute(sums[shift], "tm", [(i, (i + shift) % tm) for i in range(tm)]) for shift in range(1, tm)]
    after = shifted(sums[-1], "tm", -1)
    send, keep = step(2, step_kernel, [got_x, keep], [sums[0]])
    got = exchange(2, send)
    feat_grad = call(
        feat_kernel,
        shape((rows_in, channels), BF16),
        [info, hidden_grad, after, weight],
        after=[send],
        scratch=[VMEM((frames + 8, channels), F32), VMEM((channels // LANES, rows_in, LANES), F32)],
        flops=2 * frames * width * channels,
    )
    last = feat_grad
    sums_bits = list(range(1, dp_bits))
    sums_now = None
    for k in range(3, len(exchanges)):
        send, keep = step(k, step_kernel, [got, keep], [last])
        got = exchange(k, send)
        if sums_now is None:
            sums_now = call(sums_step_kernel, shape((per_shard + 16, dz), BF16),
                            [info, sums[0]] + ring, after=[send])
            last = sums_now
        elif len(sums_bits) > 1:
            sums_got = swapped(sums_now, "dp", 1 << sums_bits.pop(0))
            sums_now = call(sums_step_kernel, shape((per_shard + 16, dz), BF16),
                            [info, sums_now, sums_got], after=[send])
            last = sums_now
    assert now_a == 1
    first = now_a * dz
    second = first + now_c * dz

    piece, mine = call(
        lambda info, *refs: last_kernel(first, second, *refs),
        [shape((second - first, LANES), BF16), shape((second - first + extra, LANES), BF16)],
        [info, got, keep], after=[last])
    parts = [piece] + [swapped(mine if m == 1 else piece, "dp", m) for m in masks[1:]]
    conv_grad = call(
        functools.partial(conv_out_kernel, total_frames, at_start),
        shape((owner_rows, channels), F32),
        [info, got, keep, proj],
        after=[piece],
        scratch=[VMEM((LANES, channels), F32)],
    )
    while len(sums_bits) > 1:
        sums_got = swapped(sums_now, "dp", 1 << sums_bits.pop(0))
        sums_now = call(sums_step_kernel, shape((per_shard + 16, dz), BF16),
                        [info, sums_now, sums_got], after=[conv_grad])
    sums_got = swapped(sums_now, "dp", 1 << sums_bits.pop(0))
    means = call(means_kernel, shape((per_shard + 16, dz), BF16), [info, sums_now, sums_got], after=[conv_grad])
    other = swapped(means, "dp", 1)
    proj_grad, bias_grad = call(
        functools.partial(proj_out_kernel, total_frames, dz, at_pieces, now_c),
        [shape((channels, dz), F32), shape((1, channels), F32)],
        [info, mine] + parts,
        after=[means],
    )
    code_means, code_usage = call(
        functools.partial(means_out_kernel, book_size / total_frames),
        [shape((levels, per_shard, dz), BF16), shape((levels, per_shard), F32)],
        [info, means, other],
        after=[proj_grad],
    )
    return feat_grad, conv_grad, bias_grad[0], proj_grad, code_means, code_usage


def solution(mesh):
    placed = (P(("dp", "tm"), None), P("dp", None, "tm"), P(), P(), P(), P())
    return jax.shard_map(
        shards,
        mesh=mesh,
        in_specs=placed,
        out_specs=(
            P(("dp", "tm"), None),
            P(("dp", "tm"), None),
            P(),
            P(),
            P(None, "tm", None),
            P(None, "tm"),
        ),
        check_vma=False,
    )
```

```python
import functools

import jax
import jax.numpy as jnp
from jax import lax
from jax.experimental import pallas as pl
from jax.experimental.pallas import tpu as pltpu
from jax.sharding import PartitionSpec as P

BF16 = jnp.bfloat16
F32 = jnp.float32
LANES = 128
VMEM_LIMIT = 16 * 1024 * 1024


def log2(value):
    assert value & (value - 1) == 0
    return value.bit_length() - 1


def nn(a, b):
    return lax.dot_general(a, b, (((1,), (0,)), ((), ())), preferred_element_type=F32)


def nt(a, b):
    return lax.dot_general(a, b, (((1,), (1,)), ((), ())), preferred_element_type=F32)


VMEM = pltpu.VMEM


def call(body, out_shape, args, after=(), scratch=(), aliases=None, token=False, flops=0):
    count = len(args)
    many = isinstance(out_shape, (list, tuple))
    shapes = list(out_shape) if many else [out_shape]

    def kernel(*refs):
        ends = count + len(after)
        if token:
            refs[ends + len(shapes)][...] = jnp.zeros((8, LANES), F32)
            refs = refs[:ends + len(shapes)] + refs[ends + len(shapes) + 1:]
        body(*refs[:count], *refs[ends:])

    specs = [pl.BlockSpec(memory_space=pltpu.SMEM)]
    specs += [pl.BlockSpec(memory_space=VMEM)] * (count - 1)
    specs += [pl.BlockSpec(memory_space=pl.ANY)] * len(after)
    shown = shapes + [shape((8, LANES), F32)] * token
    outs = pl.pallas_call(
        kernel,
        out_shape=shown,
        in_specs=specs,
        out_specs=[pl.BlockSpec(memory_space=VMEM)] * len(shown),
        scratch_shapes=list(scratch),
        input_output_aliases=aliases or {},
        compiler_params=pltpu.CompilerParams(vmem_limit_bytes=VMEM_LIMIT),
        cost_estimate=pl.CostEstimate(flops=flops, bytes_accessed=0, transcendentals=0),
    )(*args, *after)
    return outs if len(shown) > 1 else outs[0]


def shape(dims, dtype):
    return jax.ShapeDtypeStruct(dims, dtype)


def digits_of(value):
    high = value.astype(BF16).astype(F32)
    rest = value - high
    middle = rest.astype(BF16).astype(F32)
    low = (rest - middle).astype(BF16).astype(F32)
    return high, middle, low


def one_hot(codes, axis_codes, first, count):
    frames = codes.shape[1 - axis_codes]
    dims = (count, frames) if axis_codes == 0 else (frames, count)
    places = lax.broadcasted_iota(jnp.int32, dims, axis_codes) + first
    return jnp.where(codes == places, 1.0, 0.0).astype(BF16)


def halo_kernel(info, feats, out):
    out[...] = feats[feats.shape[0] - out.shape[0]:, :]


def local_kernel(info, feats, weight, bias, codes, books, unfold, conv, chosen, wide):
    rows, channels = feats.shape
    frames = rows // 2
    for j in range(channels // LANES):
        wide[j, 0:8, :] = jnp.zeros((8, LANES), F32)
        wide[j, 8:, :] = feats[:, j * LANES:(j + 1) * LANES].astype(F32)
        for tap in range(4):
            start = tap * channels + j * LANES
            unfold[:, start:start + LANES] = wide[j, pl.ds(6 + tap, frames, stride=2), :].astype(BF16)
    conv[...] = nn(unfold[...], weight[...]) + bias[...]
    levels = books.shape[0]
    padded = jnp.concatenate([codes[...].astype(F32), jnp.zeros((8 - levels, frames), F32)], 0)
    tall = jnp.transpose(padded).astype(jnp.int32)
    for level in range(levels):
        matches = one_hot(tall[:, level:level + 1], 1, 0, books.shape[1])
        chosen[level] = nn(matches, books[level]).astype(BF16)


def walk(order, halved, count):
    others = order[1:] if halved else order
    shown = count // 2 if halved else count
    step = 2 if shown > 1 and others[-1] == 0 else 1
    for position in range(0, shown, step):
        piece = 0
        for k, bit in enumerate(others):
            piece += ((position >> (len(others) - 1 - k)) & 1) << bit
        yield position, piece, step


def correlate(flipped, sources, plan, bit, out):
    dz = flipped.shape[0]
    at = 0
    for source, (count, order, halved) in zip(sources, plan):
        shown = count // 2 if halved else count
        for position, piece, step in walk(order, halved, count):
            if halved:
                column = pl.multiple_of((piece + (bit << order[0])) * LANES, LANES)
                product = nn(flipped, source[:, pl.ds(column, step * LANES)])
            else:
                product = nn(flipped, source[:, piece * LANES:(piece + step) * LANES])
            for j in range(step):
                top = (at + position + j) * dz
                out[top:top + dz, :] = product[:, j * LANES:(j + 1) * LANES].astype(out.dtype)
        at += shown
    return at * dz


def code_digits(codes, dz, rows):
    parts = []
    for part in (codes >> 8, codes & 255):
        for start in range(0, codes.shape[1], dz):
            piece = part[:, start:start + dz].astype(F32)
            if piece.shape[1] < dz:
                piece = jnp.concatenate([piece, jnp.zeros((1, dz - piece.shape[1]), F32)], 1)
            parts.append(piece)
    parts.append(jnp.zeros((rows - len(parts), dz), F32))
    return jnp.concatenate(parts, 0).astype(BF16)


def codes_of(block, frames):
    dz = block.shape[1]
    per = -(-frames // dz)
    digits = block[...].astype(F32)
    parts = [jnp.concatenate([digits[k * per + j:k * per + j + 1, :] for j in range(per)], 1)[:, :frames]
             for k in range(2)]
    return (parts[0] * 256.0 + parts[1]).astype(jnp.int32)


def forward_kernel(plan, info, halo, unfold_in, conv, chosen, weight, proj, codes,
                   unfold, hidden, latent_grad, flipped, own, send):
    frames, width = unfold.shape
    half = width // 2
    dz = proj.shape[1]
    row = lax.broadcasted_iota(jnp.int32, (16, half), 0)
    last = halo[...].astype(F32)
    left = jnp.concatenate([last[14:15, :], last[15:16, :]], 1)
    head = jnp.where(row == 0, jnp.broadcast_to(left, (16, half)), 0.0)
    unfold[0:16, 0:half] = (unfold_in[0:16, 0:half].astype(F32) + head).astype(BF16)
    fix = nn(head.astype(BF16), weight[0:half, :])
    hidden[...] = jnp.concatenate([conv[0:16, :] + fix, conv[16:, :]], 0).astype(BF16)
    latent = nn(hidden[...], proj[...])
    once = latent - chosen[0].astype(F32)
    total = once + (once - chosen[1].astype(F32))
    latent_grad[...] = total.astype(BF16)
    flipped[...] = jnp.transpose(latent_grad[...].astype(F32)).astype(BF16)
    bit = info[0]
    at = correlate(flipped[...], (unfold, hidden), plan, 1 - bit, send)
    code_rows = own.shape[0] - frames
    digits = [code_digits(codes[level:level + 1], dz, code_rows) for level in range(2)]
    own[0:frames, :] = jnp.where(bit == 1, once, latent).astype(BF16)
    own[frames:, :] = jnp.where(bit == 1, digits[1], digits[0])
    other = jnp.where(bit == 1, latent, once).astype(BF16)
    other_digits = jnp.where(bit == 1, digits[0], digits[1])
    for j in range(dz // LANES):
        send[at:at + frames, :] = other[:, j * LANES:(j + 1) * LANES]
        send[at + frames:at + frames + code_rows, :] = other_digits[:, j * LANES:(j + 1) * LANES]
        at += frames + code_rows


def rest_kernel(plan, info, flipped, unfold, hidden, latent_grad, proj, keep, hidden_grad, extras, row):
    correlate(flipped[...], (unfold, hidden), plan, info[0], keep)
    back = nt(latent_grad[...], proj[...]).astype(BF16)
    hidden_grad[...] = back
    row[...] = back[0:16, :]
    stride = extras.shape[0] // 4
    extras[...] = jnp.zeros(extras.shape, F32)
    sums = jnp.sum(back.astype(F32), 0, keepdims=True)
    for digit, part in enumerate(digits_of(sums)):
        for j in range(sums.shape[1] // LANES):
            extras[digit * stride + j:digit * stride + j + 1, :] = part[:, j * LANES:(j + 1) * LANES]


def split_sum(halves, bit, got, kept, send, keep):
    at_in = 0
    at_out = 0
    for rows, halved in halves:
        if halved:
            half = rows // 2
            away = pl.multiple_of(at_in + (1 - bit) * half, 16)
            home = pl.multiple_of(at_in + bit * half, 16)
            send[at_out:at_out + half, :] = (
                kept[pl.ds(away, half), :] + got[pl.ds(away, half), :].astype(F32)).astype(BF16)
            keep[at_out:at_out + half, :] = kept[pl.ds(home, half), :] + got[pl.ds(home, half), :].astype(F32)
            at_out += half
        else:
            total = (kept[at_in:at_in + rows, :] + got[at_in:at_in + rows, :].astype(F32)).astype(BF16)
            send[at_out:at_out + rows, :] = total
            keep[at_out:at_out + rows, :] = total.astype(F32)
            at_out += rows
        at_in += rows
    return at_in, at_out


def add_digits(mine, theirs):
    stride = mine.shape[0] // 4
    return ((mine[0:stride] + mine[stride:2 * stride]) + mine[2 * stride:3 * stride]) + (
        (theirs[0:stride] + theirs[stride:2 * stride]) + theirs[2 * stride:3 * stride])


def digit_block(value):
    return jnp.concatenate(list(digits_of(value)) + [jnp.zeros_like(value)], 0)


def first_step_kernel(halves, place, info, got, kept, extras, send, keep):
    _, at = split_sum(halves, info[place], got, kept, send, keep)
    send[at:, :] = extras[...].astype(BF16)
    keep[at:, :] = extras[...]


def feat_kernel(info, grad, after, weight, out, wide, inter):
    frames, channels = grad.shape
    half = weight.shape[0] // 2
    wide[0:frames, :] = grad[...].astype(F32)
    wide[frames:, :] = jnp.broadcast_to(after[0:1, :].astype(F32), (8, channels))
    ahead = wide[pl.ds(1, frames), :].astype(BF16)
    for parity in range(2):
        rows = pl.ds(parity * (half // 2), half // 2)
        rows_after = pl.ds(half + parity * (half // 2), half // 2)
        both = nt(ahead, weight[rows, :]) + nt(grad[...], weight[rows_after, :])
        for j in range(channels // LANES):
            inter[j, pl.ds(parity, frames, stride=2), :] = both[:, j * LANES:(j + 1) * LANES]
    for j in range(channels // LANES):
        out[:, j * LANES:(j + 1) * LANES] = inter[j].astype(BF16)


def sums_kernel(first, frames, place, count, info, got, own, send, keep):
    rows, dz = own.shape
    theirs = jnp.concatenate([got[first + j * rows:first + (j + 1) * rows, :] for j in range(dz // LANES)], 1)
    ones = jnp.ones((8, frames), BF16)
    parts = []
    for block in (own[...], theirs):
        parts.append((block[0:frames, :], codes_of(block[frames:, :], frames)))
    size = count + 16
    for out in (send, keep):
        for top in range(0, out.shape[0], size):
            total = jnp.zeros((count, dz), F32)
            counts = jnp.zeros((8, count), F32)
            for values, codes in parts:
                matches = one_hot(codes, 0, info[place], count)
                total = total + nn(matches, values)
                counts = counts + nt(ones, matches)
            out[top:top + count, :] = total.astype(out.dtype)
            out[top + count:top + size, :] = count_rows(counts[0:1], dz).astype(out.dtype)
            place += 1


def count_rows(count, width):
    high = jnp.floor(count * (1.0 / 65536.0))
    rest = count - high * 65536.0
    middle = jnp.floor(rest * (1.0 / 256.0))
    low = rest - middle * 256.0
    block = jnp.concatenate([high, middle, low, jnp.zeros((13, count.shape[1]), F32)], 0)
    if count.shape[1] < width:
        block = jnp.concatenate([block, jnp.zeros((16, width - count.shape[1]), F32)], 1)
    return block


def count_of(block, own):
    return (block[0:1] * 65536.0 + block[1:2] * 256.0 + block[2:3])[:, :own]


def sums_step(halved, count, bit, got, kept, send, keep):
    size = count + 16
    dz = got.shape[1]
    half = kept.shape[0] // 2 if halved else 0
    outs = [(send, (1 - bit) * half), (keep, bit * half)] if halved else [(send, 0)]
    for out, start in outs:
        for top in range(0, out.shape[0], size):
            here = top + pl.multiple_of(start, 16) if halved else top
            sums = pl.ds(here, count)
            tail = pl.ds(here + count, 16)
            value = kept[sums, :].astype(F32) + got[sums, :].astype(F32)
            number = count_of(kept[tail, :].astype(F32), count) + count_of(got[tail, :].astype(F32), count)
            out[top:top + count, :] = value.astype(out.dtype)
            out[top + count:top + size, :] = count_rows(number, dz).astype(out.dtype)
    if not halved:
        keep[...] = send[...].astype(F32)


def window_kernel(halves, place, sums_halved, sums_count, sums_place, pass_on, info, got, kept, sums_got, sums_kept,
                  *refs):
    if pass_on:
        refs[-1][...] = refs[0][...]
        refs = refs[1:-1]
    send, keep, sums_send, sums_keep = refs
    at_in, at_out = split_sum(halves, info[place], got, kept, send, keep)
    block = digit_block(add_digits(kept[at_in:, :], got[at_in:, :].astype(F32)))
    send[at_out:, :] = block.astype(BF16)
    keep[at_out:, :] = block
    sums_step(sums_halved, sums_count, info[sums_place], sums_got, sums_kept, sums_send, sums_keep)


def last_kernel(first, second, count, info, got, kept, sums_got, sums_kept, pieces, mine):
    pieces[...] = (kept[first:second, :] + got[first:second, :].astype(F32)).astype(BF16)
    block = digit_block(add_digits(kept[second:, :], got[second:, :].astype(F32)))
    at = second - first
    mine[0:at, :] = pieces[...]
    mine[at:at + block.shape[0], :] = block.astype(BF16)
    at += block.shape[0]
    number = count_of(sums_kept[count:, :].astype(F32), count) + count_of(sums_got[count:, :].astype(F32), count)
    square = (count, count)
    same = lax.broadcasted_iota(jnp.int32, square, 0) == lax.broadcasted_iota(jnp.int32, square, 1)
    tall = jnp.sum(jnp.where(same, jnp.broadcast_to(number, square), 0.0), 1, keepdims=True)
    total = sums_kept[0:count, :].astype(F32) + sums_got[0:count, :].astype(F32)
    means = (total / jnp.maximum(tall, 1.0)).astype(BF16)
    digits = count_rows(number, means.shape[1]).astype(BF16)
    for j in range(means.shape[1] // LANES):
        mine[at:at + count, :] = means[:, j * LANES:(j + 1) * LANES]
        mine[at + count:at + count + 16, :] = digits[:, j * LANES:(j + 1) * LANES]
        at += count + 16


def conv_out_kernel(total_frames, place, info, got, kept, proj, out, wide):
    rows = out.shape[0]
    corr = kept[0:proj.shape[1], :] + got[0:proj.shape[1], :].astype(F32)
    flipped = jnp.transpose(corr)
    high = flipped.astype(BF16)
    low = (flipped - high.astype(F32)).astype(BF16)
    wide[...] = (nt(high, proj[...]) + nt(low, proj[...])) * (1.0 / total_frames)
    start = info[place]
    if rows % 8 == 0:
        out[...] = wide[pl.ds(pl.multiple_of(start, 8), rows), :]
    else:
        taken = wide[0:rows, :]
        for other in range(rows, wide.shape[0], rows):
            taken = jnp.where(start == other, wide[other:other + rows, :], taken)
        out[...] = taken


def out_kernel(total_frames, use_scale, count, dz, place, inner, extra, info, mine, *refs):
    parts, (out, bias, means, usage) = refs[:-4], refs[-4:]
    scale = 1.0 / total_frames
    for j, ref in enumerate(parts):
        for k in range(inner):
            start = pl.multiple_of((info[place + j] + k) * LANES, LANES)
            out[pl.ds(start, LANES), :] = jnp.transpose(ref[k * dz:(k + 1) * dz, :].astype(F32)) * scale
    theirs = parts[1]
    top = inner * dz
    value = add_digits(mine[top:top + extra, :].astype(F32), theirs[top:top + extra, :].astype(F32)) * scale
    for j in range(bias.shape[1] // LANES):
        bias[:, j * LANES:(j + 1) * LANES] = value[j:j + 1, :]
    bit = info[0]
    numbers = []
    for ref, level in ((mine, bit), (theirs, 1 - bit)):
        at = top + extra
        blocks = []
        for j in range(dz // LANES):
            blocks.append(ref[at:at + count + 16, :])
            at += count + 16
        whole = jnp.concatenate(blocks, 1)
        means[level] = whole[0:count, :]
        numbers.append(count_of(whole[count:, :].astype(F32), count) * use_scale)
    usage[0:1, :] = jnp.where(bit == 1, numbers[1], numbers[0])
    usage[1:2, :] = jnp.where(bit == 1, numbers[0], numbers[1])


def shifted(block, axis, distance):
    devices = range(lax.axis_size(axis))
    route = [(i - distance, i) for i in devices if i - distance in devices]
    return lax.ppermute(block, axis, route)


def swapped(block, axis, mask):
    return lax.ppermute(block, axis, [(i, i ^ mask) for i in range(lax.axis_size(axis))])


def shards(feats, codes, conv_weight, conv_bias, proj_weight, codebooks):
    dp, tm = lax.axis_size("dp"), lax.axis_size("tm")
    rows_in, channels = feats.shape
    frames = rows_in // 2
    levels, book_size, dz = codebooks.shape
    assert levels == 2
    width = conv_weight.shape[0]
    total_frames = frames * dp * tm
    per_shard = book_size // tm
    dp_bits, tm_bits = log2(dp), log2(tm)
    owner_rows = width // (dp * tm)

    exchanges = [("dp", b, b + tm_bits) for b in range(dp_bits)]
    exchanges += [("tm", b, b) for b in reversed(range(tm_bits))]
    pieces_a, pieces_c = width // LANES, channels // LANES
    under = max(dp_bits + tm_bits - log2(pieces_a), 0)
    c_bits = min(log2(pieces_c), 2, dp_bits)
    a_split = [bit - under if bit >= under else None for _, _, bit in exchanges]
    c_split = [log2(pieces_c) - 1 - k if k < c_bits else None for k in range(len(exchanges))]

    def order_of(split, count):
        used = [b for b in split if b is not None]
        return used + [b for b in reversed(range(log2(count))) if b not in used]

    plan = [(pieces_a, order_of(a_split, pieces_a), a_split[0] is not None),
            (pieces_c, order_of(c_split, pieces_c), c_split[0] is not None)]
    now_a = pieces_a // 2 if plan[0][2] else pieces_a
    now_c = pieces_c // 2 if plan[1][2] else pieces_c

    sums_exchanges = [("tm", b) for b in range(tm_bits)] + [("dp", b) for b in range(1, dp_bits)]

    at_dp, at_tm = lax.axis_index("dp"), lax.axis_index("tm")

    def bit_of(axis, b):
        return ((at_dp if axis == "dp" else at_tm) >> b) & 1

    bits = [bit_of(axis, b) for axis, b, _ in exchanges]
    sums_bits = [bit_of(axis, b) for axis, b in sums_exchanges]
    masks = list(range(1 << c_bits))
    own_piece = sum((bits[k] << c_split[k]) for k in range(c_bits))
    flips = [sum(1 << c_split[k] for k in range(c_bits) if m >> k & 1) for m in masks]
    quarters = [sum(((position >> (tm_bits - 1 - b)) & 1) << b for b in range(tm_bits)) for position in range(tm)]
    lead = at_tm & 1
    send_quarters = [(q | (1 - lead)) * per_shard for q in quarters[:tm // 2]]
    keep_quarters = [(q | lead) * per_shard for q in quarters[:tm // 2]]
    at_start = len(bits)
    at_codes = at_start + 1
    at_pieces = at_codes + tm
    at_sums = at_pieces + len(masks)
    info = jnp.stack(
        bits + [((at_dp * tm + at_tm) * owner_rows) & (LANES - 1)] + send_quarters + keep_quarters
        + [own_piece ^ flip for flip in flips] + sums_bits).astype(jnp.int32)

    halo = shifted(
        call(halo_kernel, shape((16, channels), BF16), [info, feats], flops=10 ** 11), "tm", 1)
    weight, proj, codes = conv_weight, proj_weight, codes[0]
    unfold, conv, chosen = call(
        local_kernel,
        [shape((frames, width), BF16), shape((frames, channels), F32), shape((levels, frames, dz), BF16)],
        [info, feats, weight, conv_bias[None, :], codes, codebooks],
        scratch=[VMEM((channels // LANES, rows_in + 8, LANES), F32)],
    )

    extra = 4 * (-(-channels // LANES // 8) * 8)
    code_rows = -(-(2 * -(-frames // dz)) // 16) * 16
    corr_rows = (now_a + now_c) * dz
    rows_b = frames + code_rows
    unfold, hidden, latent_grad, flipped, own, send = call(
        functools.partial(forward_kernel, plan),
        [shape((frames, width), BF16), shape((frames, channels), BF16), shape((frames, dz), BF16),
         shape((dz, frames), BF16), shape((rows_b, dz), BF16),
         shape((corr_rows + rows_b * (dz // LANES), LANES), BF16)],
        [info, halo, unfold, conv, chosen, weight, proj, codes],
        aliases={2: 0},
    )
    got = swapped(send, "dp", 1)
    keep, hidden_grad, extras, row = call(
        functools.partial(rest_kernel, plan),
        [shape((corr_rows, LANES), F32), shape((frames, channels), BF16), shape((extra, LANES), F32),
         shape((16, channels), BF16)],
        [info, flipped, unfold, hidden, latent_grad, proj],
        after=[send],
    )
    after = shifted(row, "tm", -1)

    def halves_at(k):
        nonlocal now_a, now_c
        halves = [(now_a * dz, a_split[k] is not None), (now_c * dz, c_split[k] is not None)]
        now_a = now_a // 2 if halves[0][1] else now_a
        now_c = now_c // 2 if halves[1][1] else now_c
        return halves, (now_a + now_c) * dz + extra

    halves, rows = halves_at(1)
    core_got = got
    send, keep = call(
        functools.partial(first_step_kernel, halves, 1),
        [shape((rows, LANES), BF16), shape((rows, LANES), F32)],
        [info, got, keep, extras])
    got = swapped(send, exchanges[1][0], 1 << exchanges[1][1])
    size = per_shard + 16
    sums_rows = size * (tm // 2)
    sums_send, sums_keep = call(
        functools.partial(sums_kernel, corr_rows, frames, at_codes, per_shard),
        [shape((sums_rows, dz), BF16), shape((sums_rows, dz), F32)],
        [info, core_got, own],
        after=[send])
    sums_got = swapped(sums_send, sums_exchanges[0][0], 1 << sums_exchanges[0][1])

    ordered = []
    for k in range(2, len(exchanges)):
        halves, rows = halves_at(k)
        halved = sums_exchanges[k - 1][0] == "tm"
        sums_rows = sums_rows // 2 if halved else sums_rows
        pass_on = k == 3
        outs = [shape((rows, LANES), BF16), shape((rows, LANES), F32),
                shape((sums_rows, dz), BF16), shape((sums_rows, dz), F32)]
        outs = call(
            functools.partial(window_kernel, halves, k, halved, per_shard, at_sums + k - 1, pass_on),
            outs + [shape((16, channels), BF16)] * pass_on,
            [info, got, keep, sums_got, sums_keep] + [after] * pass_on,
            after=ordered)
        send, keep, sums_send, sums_keep = outs[:4]
        after = outs[4] if pass_on else after
        got = swapped(send, exchanges[k][0], 1 << exchanges[k][1])
        sums_got = swapped(sums_send, sums_exchanges[k - 1][0], 1 << sums_exchanges[k - 1][1])
        if pass_on:
            feat_grad, *ordered = call(
                feat_kernel,
                shape((rows_in, channels), BF16),
                [info, hidden_grad, after, weight],
                after=[send],
                token=True,
                scratch=[VMEM((frames + 8, channels), F32), VMEM((channels // LANES, rows_in, LANES), F32)],
            )
    assert now_a == 1 and sums_rows == size

    first = now_a * dz
    second = first + now_c * dz
    piece, mine = call(
        functools.partial(last_kernel, first, second, per_shard),
        [shape((second - first, LANES), BF16),
         shape((second - first + extra + size * (dz // LANES), LANES), BF16)],
        [info, got, keep, sums_got, sums_keep])
    parts = [piece] + [swapped(mine if m == 1 else piece, "dp", m) for m in masks[1:]]
    conv_grad, last = call(
        functools.partial(conv_out_kernel, total_frames, at_start),
        shape((owner_rows, channels), F32),
        [info, got, keep, proj],
        after=[piece],
        token=True,
        scratch=[VMEM((LANES, channels), F32)],
    )
    proj_grad, bias_grad, code_means, code_usage = call(
        functools.partial(
            out_kernel, total_frames, book_size / total_frames, per_shard, dz, at_pieces, now_c, extra),
        [shape((channels, dz), F32), shape((1, channels), F32), shape((levels, per_shard, dz), BF16),
         shape((levels, per_shard), F32)],
        [info, mine] + parts,
        after=[last],
    )
    return feat_grad, conv_grad, bias_grad[0], proj_grad, code_means, code_usage


def solution(mesh):
    placed = (P(("dp", "tm"), None), P("dp", None, "tm"), P(), P(), P(), P())
    return jax.shard_map(
        shards,
        mesh=mesh,
        in_specs=placed,
        out_specs=(
            P(("dp", "tm"), None),
            P(("dp", "tm"), None),
            P(),
            P(),
            P(None, "tm", None),
            P(None, "tm"),
        ),
        check_vma=False,
    )
```

```python
import functools

import jax
import jax.numpy as jnp
from jax import lax
from jax.experimental import pallas as pl
from jax.experimental.pallas import tpu as pltpu
from jax.sharding import PartitionSpec as P

BF16 = jnp.bfloat16
F32 = jnp.float32
LANES = 128
VMEM_LIMIT = 16 * 1024 * 1024


def log2(value):
    assert value & (value - 1) == 0
    return value.bit_length() - 1


def nn(a, b):
    return lax.dot_general(a, b, (((1,), (0,)), ((), ())), preferred_element_type=F32)


def nt(a, b):
    return lax.dot_general(a, b, (((1,), (1,)), ((), ())), preferred_element_type=F32)


VMEM = pltpu.VMEM


def call(body, out_shape, args, after=(), scratch=(), aliases=None, token=False, flops=0):
    count = len(args)
    many = isinstance(out_shape, (list, tuple))
    shapes = list(out_shape) if many else [out_shape]

    def kernel(*refs):
        ends = count + len(after)
        if token:
            refs[ends + len(shapes)][...] = jnp.zeros((8, LANES), F32)
            refs = refs[:ends + len(shapes)] + refs[ends + len(shapes) + 1:]
        body(*refs[:count], *refs[ends:])

    specs = [pl.BlockSpec(memory_space=pltpu.SMEM)]
    specs += [pl.BlockSpec(memory_space=VMEM)] * (count - 1)
    specs += [pl.BlockSpec(memory_space=pl.ANY)] * len(after)
    shown = shapes + [shape((8, LANES), F32)] * token
    outs = pl.pallas_call(
        kernel,
        out_shape=shown,
        in_specs=specs,
        out_specs=[pl.BlockSpec(memory_space=VMEM)] * len(shown),
        scratch_shapes=list(scratch),
        input_output_aliases=aliases or {},
        compiler_params=pltpu.CompilerParams(vmem_limit_bytes=VMEM_LIMIT),
        cost_estimate=pl.CostEstimate(flops=flops, bytes_accessed=0, transcendentals=0),
    )(*args, *after)
    return outs if len(shown) > 1 else outs[0]


def shape(dims, dtype):
    return jax.ShapeDtypeStruct(dims, dtype)


def digits_of(value):
    high = value.astype(BF16).astype(F32)
    rest = value - high
    middle = rest.astype(BF16).astype(F32)
    low = (rest - middle).astype(BF16).astype(F32)
    return high, middle, low


def one_hot(codes, axis_codes, first, count):
    frames = codes.shape[1 - axis_codes]
    dims = (count, frames) if axis_codes == 0 else (frames, count)
    places = lax.broadcasted_iota(jnp.int32, dims, axis_codes) + first
    return jnp.where(codes == places, 1.0, 0.0).astype(BF16)


def halo_kernel(info, feats, out):
    out[...] = feats[feats.shape[0] - out.shape[0]:, :]


def local_kernel(info, feats, weight, bias, codes, books, unfold, conv, chosen, wide):
    rows, channels = feats.shape
    frames = rows // 2
    for j in range(channels // LANES):
        wide[j, 0:8, :] = jnp.zeros((8, LANES), F32)
        wide[j, 8:, :] = feats[:, j * LANES:(j + 1) * LANES].astype(F32)
        for tap in range(4):
            start = tap * channels + j * LANES
            unfold[:, start:start + LANES] = wide[j, pl.ds(6 + tap, frames, stride=2), :].astype(BF16)
    conv[...] = nn(unfold[...], weight[...]) + bias[...]
    levels = books.shape[0]
    padded = jnp.concatenate([codes[...].astype(F32), jnp.zeros((8 - levels, frames), F32)], 0)
    tall = jnp.transpose(padded).astype(jnp.int32)
    for level in range(levels):
        matches = one_hot(tall[:, level:level + 1], 1, 0, books.shape[1])
        chosen[level] = nn(matches, books[level]).astype(BF16)


def walk(order, halved, count):
    others = order[1:] if halved else order
    shown = count // 2 if halved else count
    step = 2 if shown > 1 and others[-1] == 0 else 1
    for position in range(0, shown, step):
        piece = 0
        for k, bit in enumerate(others):
            piece += ((position >> (len(others) - 1 - k)) & 1) << bit
        yield position, piece, step


def correlate(flipped, sources, plan, bit, out):
    dz = flipped.shape[0]
    at = 0
    for source, (count, order, halved) in zip(sources, plan):
        shown = count // 2 if halved else count
        for position, piece, step in walk(order, halved, count):
            if halved:
                column = pl.multiple_of((piece + (bit << order[0])) * LANES, LANES)
                product = nn(flipped, source[:, pl.ds(column, step * LANES)])
            else:
                product = nn(flipped, source[:, piece * LANES:(piece + step) * LANES])
            for j in range(step):
                top = (at + position + j) * dz
                out[top:top + dz, :] = product[:, j * LANES:(j + 1) * LANES].astype(out.dtype)
        at += shown
    return at * dz


def code_digits(codes, dz, rows):
    parts = []
    for part in (codes >> 8, codes & 255):
        for start in range(0, codes.shape[1], dz):
            piece = part[:, start:start + dz].astype(F32)
            if piece.shape[1] < dz:
                piece = jnp.concatenate([piece, jnp.zeros((1, dz - piece.shape[1]), F32)], 1)
            parts.append(piece)
    parts.append(jnp.zeros((rows - len(parts), dz), F32))
    return jnp.concatenate(parts, 0).astype(BF16)


def codes_of(block, frames):
    dz = block.shape[1]
    per = -(-frames // dz)
    digits = block[...].astype(F32)
    parts = [jnp.concatenate([digits[k * per + j:k * per + j + 1, :] for j in range(per)], 1)[:, :frames]
             for k in range(2)]
    return (parts[0] * 256.0 + parts[1]).astype(jnp.int32)


def forward_kernel(plan, info, halo, unfold_in, conv, chosen, weight, proj, codes,
                   unfold, hidden, latent_grad, flipped, own, send):
    frames, width = unfold.shape
    half = width // 2
    dz = proj.shape[1]
    row = lax.broadcasted_iota(jnp.int32, (16, half), 0)
    last = halo[...].astype(F32)
    left = jnp.concatenate([last[14:15, :], last[15:16, :]], 1)
    head = jnp.where(row == 0, jnp.broadcast_to(left, (16, half)), 0.0)
    unfold[0:16, 0:half] = (unfold_in[0:16, 0:half].astype(F32) + head).astype(BF16)
    fix = nn(head.astype(BF16), weight[0:half, :])
    hidden[...] = jnp.concatenate([conv[0:16, :] + fix, conv[16:, :]], 0).astype(BF16)
    latent = nn(hidden[...], proj[...])
    once = latent - chosen[0].astype(F32)
    total = once + (once - chosen[1].astype(F32))
    latent_grad[...] = total.astype(BF16)
    flipped[...] = jnp.transpose(latent_grad[...].astype(F32)).astype(BF16)
    bit = info[0]
    at = correlate(flipped[...], (unfold, hidden), plan, 1 - bit, send)
    code_rows = own.shape[0] - frames
    digits = [code_digits(codes[level:level + 1], dz, code_rows) for level in range(2)]
    own[0:frames, :] = jnp.where(bit == 1, once, latent).astype(BF16)
    own[frames:, :] = jnp.where(bit == 1, digits[1], digits[0])
    other = jnp.where(bit == 1, latent, once).astype(BF16)
    other_digits = jnp.where(bit == 1, digits[0], digits[1])
    for j in range(dz // LANES):
        send[at:at + frames, :] = other[:, j * LANES:(j + 1) * LANES]
        send[at + frames:at + frames + code_rows, :] = other_digits[:, j * LANES:(j + 1) * LANES]
        at += frames + code_rows


def rest_kernel(plan, info, flipped, unfold, hidden, latent_grad, proj, keep_a, keep_c, hidden_grad, extras, row):
    bit = info[0]
    correlate(flipped[...], (unfold,), plan[:1], bit, keep_a)
    correlate(flipped[...], (hidden,), plan[1:], bit, keep_c)
    back = nt(latent_grad[...], proj[...]).astype(BF16)
    hidden_grad[...] = back
    row[...] = back[0:16, :]
    stride = extras.shape[0] // 4
    extras[...] = jnp.zeros(extras.shape, F32)
    sums = jnp.sum(back.astype(F32), 0, keepdims=True)
    for digit, part in enumerate(digits_of(sums)):
        for j in range(sums.shape[1] // LANES):
            extras[digit * stride + j:digit * stride + j + 1, :] = part[:, j * LANES:(j + 1) * LANES]


def split_sum(halved, bit, got, at, kept, rows, send, to, keep):
    if halved:
        half = rows // 2
        away = pl.multiple_of((1 - bit) * half, 16)
        home = pl.multiple_of(bit * half, 16)
        send[to:to + half, :] = (kept[pl.ds(away, half), :] + got[pl.ds(at + away, half), :].astype(F32)).astype(BF16)
        keep[0:half, :] = kept[pl.ds(home, half), :] + got[pl.ds(at + home, half), :].astype(F32)
        return half
    total = (kept[0:rows, :] + got[at:at + rows, :].astype(F32)).astype(BF16)
    send[to:to + rows, :] = total
    keep[0:rows, :] = total.astype(F32)
    return rows


def add_digits(mine, theirs):
    stride = mine.shape[0] // 4
    return ((mine[0:stride] + mine[stride:2 * stride]) + mine[2 * stride:3 * stride]) + (
        (theirs[0:stride] + theirs[stride:2 * stride]) + theirs[2 * stride:3 * stride])


def digit_block(value):
    return jnp.concatenate(list(digits_of(value)) + [jnp.zeros_like(value)], 0)


def first_step_kernel(halves, place, info, got, kept_a, kept_c, extras, send, keep_a, keep_c):
    (rows_a, halved_a), (rows_c, halved_c) = halves
    to = split_sum(halved_a, info[place], got, 0, kept_a, rows_a, send, 0, keep_a)
    gone = split_sum(halved_c, info[place], got, rows_a, kept_c, rows_c, send, to, keep_c)
    send[to + gone:, :] = extras[...].astype(BF16)
    keep_c[gone:, :] = extras[...]


def feat_kernel(info, grad, after, weight, out, wide, inter):
    frames, channels = grad.shape
    half = weight.shape[0] // 2
    wide[0:frames, :] = grad[...].astype(F32)
    wide[frames:, :] = jnp.broadcast_to(after[0:1, :].astype(F32), (8, channels))
    ahead = wide[pl.ds(1, frames), :].astype(BF16)
    for parity in range(2):
        rows = pl.ds(parity * (half // 2), half // 2)
        rows_after = pl.ds(half + parity * (half // 2), half // 2)
        both = nt(ahead, weight[rows, :]) + nt(grad[...], weight[rows_after, :])
        for j in range(channels // LANES):
            inter[j, pl.ds(parity, frames, stride=2), :] = both[:, j * LANES:(j + 1) * LANES]
    for j in range(channels // LANES):
        out[:, j * LANES:(j + 1) * LANES] = inter[j].astype(BF16)


def put_row(out, row):
    wide = out.shape[1]
    parts = row.shape[1] // wide
    for j in range(parts):
        top = out.shape[0] - (parts - j) * row.shape[0]
        out[top:top + row.shape[0], :] = row[:, j * wide:(j + 1) * wide]


def get_row(block, parts):
    tall = 16
    tops = [block.shape[0] - (parts - j) * tall for j in range(parts)]
    return jnp.concatenate([block[top:top + tall, :] for top in tops], 1)


def sums_kernel(first, frames, place, count, info, got, own, row, send, keep):
    rows, dz = own.shape
    theirs = jnp.concatenate([got[first + j * rows:first + (j + 1) * rows, :] for j in range(dz // LANES)], 1)
    ones = jnp.ones((8, frames), BF16)
    parts = []
    for block in (own[...], theirs):
        parts.append((block[0:frames, :], codes_of(block[frames:, :], frames)))
    size = count + 16
    put_row(send, row[...])
    for out in (send, keep):
        for top in range(0, keep.shape[0], size):
            total = jnp.zeros((count, dz), F32)
            counts = jnp.zeros((8, count), F32)
            for values, codes in parts:
                matches = one_hot(codes, 0, info[place], count)
                total = total + nn(matches, values)
                counts = counts + nt(ones, matches)
            out[top:top + count, :] = total.astype(out.dtype)
            out[top + count:top + size, :] = count_rows(counts[0:1], dz).astype(out.dtype)
            place += 1


def count_rows(count, width):
    high = jnp.floor(count * (1.0 / 65536.0))
    rest = count - high * 65536.0
    middle = jnp.floor(rest * (1.0 / 256.0))
    low = rest - middle * 256.0
    block = jnp.concatenate([high, middle, low, jnp.zeros((13, count.shape[1]), F32)], 0)
    if count.shape[1] < width:
        block = jnp.concatenate([block, jnp.zeros((16, width - count.shape[1]), F32)], 1)
    return block


def count_of(block, own):
    return (block[0:1] * 65536.0 + block[1:2] * 256.0 + block[2:3])[:, :own]


def sums_step(halved, count, bit, got, kept, send, keep):
    size = count + 16
    dz = got.shape[1]
    half = kept.shape[0] // 2 if halved else 0
    outs = [(send, (1 - bit) * half), (keep, bit * half)] if halved else [(send, 0)]
    for out, start in outs:
        for top in range(0, keep.shape[0], size):
            here = top + pl.multiple_of(start, 16) if halved else top
            sums = pl.ds(here, count)
            tail = pl.ds(here + count, 16)
            value = kept[sums, :].astype(F32) + got[sums, :].astype(F32)
            number = count_of(kept[tail, :].astype(F32), count) + count_of(got[tail, :].astype(F32), count)
            out[top:top + count, :] = value.astype(out.dtype)
            out[top + count:top + size, :] = count_rows(number, dz).astype(out.dtype)
    if not halved:
        keep[...] = send[0:keep.shape[0], :].astype(F32)


def window_kernel(halves, at_c, place, apart, sums_plan, row_plan, info, got_a, got_c, kept_a, kept_c, sums_got,
                  sums_kept, *refs):
    (rows_a, halved_a), (rows_c, halved_c) = halves
    sums_halved, sums_count, sums_place = sums_plan
    row_step, row_parts, row_place = row_plan
    if row_step is not None:
        row = get_row(sums_got, row_parts)
        before = refs[0][...] if row_step else jnp.zeros_like(row)
        refs[-1][...] = jnp.where(info[row_place] == row_step, row, before)
        refs = refs[1 if row_step else 0:-1]
    if apart:
        send_a, send_c, keep_a, keep_c, sums_send, sums_keep = refs
    else:
        send_a, keep_a, keep_c, sums_send, sums_keep = refs
        send_c = send_a
    to = split_sum(halved_a, info[place], got_a, 0, kept_a, rows_a, send_a, 0, keep_a)
    to = 0 if apart else to
    gone = split_sum(halved_c, info[place], got_c, at_c, kept_c, rows_c, send_c, to, keep_c)
    block = digit_block(add_digits(kept_c[rows_c:, :], got_c[at_c + rows_c:, :].astype(F32)))
    send_c[to + gone:, :] = block.astype(BF16)
    keep_c[gone:, :] = block
    sums_step(sums_halved, sums_count, info[sums_place], sums_got, sums_kept, sums_send, sums_keep)
    if row_step is not None and sums_send.shape[0] > sums_keep.shape[0]:
        put_row(sums_send, row)


def last_kernel(rows, count, info, got_a, kept_a, got, kept, sums_got, sums_kept, corr, pieces, mine):
    corr[...] = kept_a[...] + got_a[...].astype(F32)
    pieces[...] = (kept[0:rows, :] + got[0:rows, :].astype(F32)).astype(BF16)
    block = digit_block(add_digits(kept[rows:, :], got[rows:, :].astype(F32)))
    at = rows
    mine[0:at, :] = pieces[...]
    mine[at:at + block.shape[0], :] = block.astype(BF16)
    at += block.shape[0]
    number = count_of(sums_kept[count:, :].astype(F32), count) + count_of(sums_got[count:, :].astype(F32), count)
    square = (count, count)
    same = lax.broadcasted_iota(jnp.int32, square, 0) == lax.broadcasted_iota(jnp.int32, square, 1)
    tall = jnp.sum(jnp.where(same, jnp.broadcast_to(number, square), 0.0), 1, keepdims=True)
    total = sums_kept[0:count, :].astype(F32) + sums_got[0:count, :].astype(F32)
    means = (total / jnp.maximum(tall, 1.0)).astype(BF16)
    digits = count_rows(number, means.shape[1]).astype(BF16)
    for j in range(means.shape[1] // LANES):
        mine[at:at + count, :] = means[:, j * LANES:(j + 1) * LANES]
        mine[at + count:at + count + 16, :] = digits[:, j * LANES:(j + 1) * LANES]
        at += count + 16


def conv_out_kernel(total_frames, place, info, corr, proj, out, wide):
    rows = out.shape[0]
    flipped = jnp.transpose(corr[...])
    high = flipped.astype(BF16)
    low = (flipped - high.astype(F32)).astype(BF16)
    wide[...] = (nt(high, proj[...]) + nt(low, proj[...])) * (1.0 / total_frames)
    start = info[place]
    if rows % 8 == 0:
        out[...] = wide[pl.ds(pl.multiple_of(start, 8), rows), :]
    else:
        taken = wide[0:rows, :]
        for other in range(rows, wide.shape[0], rows):
            taken = jnp.where(start == other, wide[other:other + rows, :], taken)
        out[...] = taken


def out_kernel(total_frames, use_scale, count, dz, place, inner, extra, info, mine, *refs):
    parts, (out, bias, means, usage) = refs[:-4], refs[-4:]
    scale = 1.0 / total_frames
    for j, ref in enumerate(parts):
        for k in range(inner):
            start = pl.multiple_of((info[place + j] + k) * LANES, LANES)
            out[pl.ds(start, LANES), :] = jnp.transpose(ref[k * dz:(k + 1) * dz, :].astype(F32)) * scale
    theirs = parts[1]
    top = inner * dz
    value = add_digits(mine[top:top + extra, :].astype(F32), theirs[top:top + extra, :].astype(F32)) * scale
    for j in range(bias.shape[1] // LANES):
        bias[:, j * LANES:(j + 1) * LANES] = value[j:j + 1, :]
    bit = info[0]
    numbers = []
    for ref, level in ((mine, bit), (theirs, 1 - bit)):
        at = top + extra
        blocks = []
        for j in range(dz // LANES):
            blocks.append(ref[at:at + count + 16, :])
            at += count + 16
        whole = jnp.concatenate(blocks, 1)
        means[level] = whole[0:count, :]
        numbers.append(count_of(whole[count:, :].astype(F32), count) * use_scale)
    usage[0:1, :] = jnp.where(bit == 1, numbers[1], numbers[0])
    usage[1:2, :] = jnp.where(bit == 1, numbers[0], numbers[1])


def shifted(block, axis, distance):
    devices = range(lax.axis_size(axis))
    route = [(i - distance, i) for i in devices if i - distance in devices]
    return lax.ppermute(block, axis, route)


def swapped(block, axis, mask):
    return lax.ppermute(block, axis, [(i, i ^ mask) for i in range(lax.axis_size(axis))])


def shards(feats, codes, conv_weight, conv_bias, proj_weight, codebooks):
    dp, tm = lax.axis_size("dp"), lax.axis_size("tm")
    rows_in, channels = feats.shape
    frames = rows_in // 2
    levels, book_size, dz = codebooks.shape
    assert levels == 2
    width = conv_weight.shape[0]
    total_frames = frames * dp * tm
    per_shard = book_size // tm
    dp_bits, tm_bits = log2(dp), log2(tm)
    owner_rows = width // (dp * tm)

    exchanges = [("dp", b, b + tm_bits) for b in range(dp_bits)]
    exchanges += [("tm", b, b) for b in reversed(range(tm_bits))]
    pieces_a, pieces_c = width // LANES, channels // LANES
    under = max(dp_bits + tm_bits - log2(pieces_a), 0)
    c_bits = min(log2(pieces_c), 2, dp_bits)
    a_split = [bit - under if bit >= under else None for _, _, bit in exchanges]
    c_split = [log2(pieces_c) - 1 - k if k < c_bits else None for k in range(len(exchanges))]

    def order_of(split, count):
        used = [b for b in split if b is not None]
        return used + [b for b in reversed(range(log2(count))) if b not in used]

    plan = [(pieces_a, order_of(a_split, pieces_a), a_split[0] is not None),
            (pieces_c, order_of(c_split, pieces_c), c_split[0] is not None)]
    now_a = pieces_a // 2 if plan[0][2] else pieces_a
    now_c = pieces_c // 2 if plan[1][2] else pieces_c

    sums_exchanges = [("tm", b) for b in range(tm_bits)] + [("dp", b) for b in range(1, dp_bits)]

    at_dp, at_tm = lax.axis_index("dp"), lax.axis_index("tm")

    def bit_of(axis, b):
        return ((at_dp if axis == "dp" else at_tm) >> b) & 1

    bits = [bit_of(axis, b) for axis, b, _ in exchanges]
    sums_bits = [bit_of(axis, b) for axis, b in sums_exchanges]
    masks = list(range(1 << c_bits))
    own_piece = sum((bits[k] << c_split[k]) for k in range(c_bits))
    flips = [sum(1 << c_split[k] for k in range(c_bits) if m >> k & 1) for m in masks]
    quarters = [sum(((position >> (tm_bits - 1 - b)) & 1) << b for b in range(tm_bits)) for position in range(tm)]
    lead = at_tm & 1
    send_quarters = [(q | (1 - lead)) * per_shard for q in quarters[:tm // 2]]
    keep_quarters = [(q | lead) * per_shard for q in quarters[:tm // 2]]
    at_start = len(bits)
    at_codes = at_start + 1
    at_pieces = at_codes + tm
    at_sums = at_pieces + len(masks)
    at_row = at_sums + len(sums_bits)
    ones_below = sum(((at_tm + 1) & ((1 << (b + 1)) - 1) == 0).astype(jnp.int32) for b in range(tm_bits))
    info = jnp.stack(
        bits + [((at_dp * tm + at_tm) * owner_rows) & (LANES - 1)] + send_quarters + keep_quarters
        + [own_piece ^ flip for flip in flips] + sums_bits + [ones_below]).astype(jnp.int32)

    halo = shifted(
        call(halo_kernel, shape((16, channels), BF16), [info, feats], flops=10 ** 11), "tm", 1)
    weight, proj, codes = conv_weight, proj_weight, codes[0]
    unfold, conv, chosen = call(
        local_kernel,
        [shape((frames, width), BF16), shape((frames, channels), F32), shape((levels, frames, dz), BF16)],
        [info, feats, weight, conv_bias[None, :], codes, codebooks],
        scratch=[VMEM((channels // LANES, rows_in + 8, LANES), F32)],
    )

    extra = 4 * (-(-channels // LANES // 8) * 8)
    code_rows = -(-(2 * -(-frames // dz)) // 16) * 16
    corr_rows = (now_a + now_c) * dz
    rows_b = frames + code_rows
    unfold, hidden, latent_grad, flipped, own, send = call(
        functools.partial(forward_kernel, plan),
        [shape((frames, width), BF16), shape((frames, channels), BF16), shape((frames, dz), BF16),
         shape((dz, frames), BF16), shape((rows_b, dz), BF16),
         shape((corr_rows + rows_b * (dz // LANES), LANES), BF16)],
        [info, halo, unfold, conv, chosen, weight, proj, codes],
        aliases={2: 0},
    )
    got = swapped(send, "dp", 1)
    keep_a, keep_c, hidden_grad, extras, row = call(
        functools.partial(rest_kernel, plan),
        [shape((now_a * dz, LANES), F32), shape((now_c * dz, LANES), F32), shape((frames, channels), BF16),
         shape((extra, LANES), F32), shape((16, channels), BF16)],
        [info, flipped, unfold, hidden, latent_grad, proj],
        after=[send],
    )

    def halves_at(k):
        nonlocal now_a, now_c
        halves = [(now_a * dz, a_split[k] is not None), (now_c * dz, c_split[k] is not None)]
        now_a = now_a // 2 if halves[0][1] else now_a
        now_c = now_c // 2 if halves[1][1] else now_c
        return halves, now_a * dz, now_c * dz + extra

    halves, rows_a, rows_c = halves_at(1)
    core_got = got
    send, keep_a, keep_c = call(
        functools.partial(first_step_kernel, halves, 1),
        [shape((rows_a + rows_c, LANES), BF16), shape((rows_a, LANES), F32), shape((rows_c, LANES), F32)],
        [info, got, keep_a, keep_c, extras])
    got_a = got_c = swapped(send, exchanges[1][0], 1 << exchanges[1][1])
    size = per_shard + 16
    row_parts = channels // dz
    sums_rows = size * (tm // 2)
    sums_send, sums_keep = call(
        functools.partial(sums_kernel, corr_rows, frames, at_codes, per_shard),
        [shape((sums_rows + 16 * row_parts, dz), BF16), shape((sums_rows, dz), F32)],
        [info, core_got, own, row],
        after=[send])
    sums_got = swapped(sums_send, sums_exchanges[0][0], 1 << sums_exchanges[0][1])
    after = None
    ordered = []
    for k in range(2, len(exchanges)):
        at_c = now_a * dz if got_a is got_c else 0
        halves, rows_a, rows_c = halves_at(k)
        apart = k >= dp_bits
        halved = sums_exchanges[k - 1][0] == "tm"
        sums_rows = sums_rows // 2 if halved else sums_rows
        row_step = k - 2 if k - 2 < tm_bits else None
        row_sent = 16 * row_parts * halved
        sends = [rows_a, rows_c] if apart else [rows_a + rows_c]
        outs = [shape((rows, LANES), BF16) for rows in sends] + [shape((rows, LANES), F32) for rows in (rows_a, rows_c)]
        outs += [shape((sums_rows + row_sent, dz), BF16), shape((sums_rows, dz), F32)]
        outs = call(
            functools.partial(window_kernel, halves, at_c, k, apart, (halved, per_shard, at_sums + k - 1),
                              (row_step, row_parts, at_row)),
            outs + [shape((16, channels), BF16)] * (row_step is not None),
            [info, got_a, got_c, keep_a, keep_c, sums_got, sums_keep] + [after] * bool(row_step),
            after=ordered)
        after = outs[-1] if row_step is not None else after
        got_a = got_c = swapped(outs[0], exchanges[k][0], 1 << exchanges[k][1])
        if apart:
            got_c = swapped(outs[1], "tm", 1 << (k - dp_bits))
        keep_a, keep_c, sums_send, sums_keep = outs[len(sends):len(sends) + 4]
        sums_got = swapped(sums_send, sums_exchanges[k - 1][0], 1 << sums_exchanges[k - 1][1])
        if k == tm_bits + 1:
            feat_grad, *ordered = call(
                feat_kernel,
                shape((rows_in, channels), BF16),
                [info, hidden_grad, after, weight],
                after=[outs[0]],
                token=True,
                scratch=[VMEM((frames + 8, channels), F32), VMEM((channels // LANES, rows_in, LANES), F32)],
            )
    assert now_a == 1 and sums_rows == size

    corr, piece, mine = call(
        functools.partial(last_kernel, rows_c - extra, per_shard),
        [shape((rows_a, LANES), F32), shape((rows_c - extra, LANES), BF16), shape((rows_c + size * (dz // LANES), LANES), BF16)],
        [info, got_a, keep_a, got_c, keep_c, sums_got, sums_keep],
        after=ordered)
    parts = [piece] + [swapped(mine if m == 1 else piece, "dp", m) for m in masks[1:]]
    conv_grad, last = call(
        functools.partial(conv_out_kernel, total_frames, at_start),
        shape((owner_rows, channels), F32),
        [info, corr, proj],
        after=[piece],
        token=True,
        scratch=[VMEM((LANES, channels), F32)],
    )
    proj_grad, bias_grad, code_means, code_usage = call(
        functools.partial(
            out_kernel, total_frames, book_size / total_frames, per_shard, dz, at_pieces, now_c, extra),
        [shape((channels, dz), F32), shape((1, channels), F32), shape((levels, per_shard, dz), BF16),
         shape((levels, per_shard), F32)],
        [info, mine] + parts,
        after=[last],
    )
    return feat_grad, conv_grad, bias_grad[0], proj_grad, code_means, code_usage


def solution(mesh):
    placed = (P(("dp", "tm"), None), P("dp", None, "tm"), P(), P(), P(), P())
    return jax.shard_map(
        shards,
        mesh=mesh,
        in_specs=placed,
        out_specs=(
            P(("dp", "tm"), None),
            P(("dp", "tm"), None),
            P(),
            P(),
            P(None, "tm", None),
            P(None, "tm"),
        ),
        check_vma=False,
    )
```

```python
import functools

import jax
import jax.numpy as jnp
from jax import lax
from jax.experimental import pallas as pl
from jax.experimental.pallas import tpu as pltpu
from jax.sharding import PartitionSpec as P

BF16 = jnp.bfloat16
F32 = jnp.float32
LANES = 128
VMEM_LIMIT = 16 * 1024 * 1024


def log2(value):
    assert value & (value - 1) == 0
    return value.bit_length() - 1


def nn(a, b):
    return lax.dot_general(a, b, (((1,), (0,)), ((), ())), preferred_element_type=F32)


def nt(a, b):
    return lax.dot_general(a, b, (((1,), (1,)), ((), ())), preferred_element_type=F32)


VMEM = pltpu.VMEM


def call(body, out_shape, args, after=(), scratch=(), aliases=None, token=False, flops=0):
    count = len(args)
    many = isinstance(out_shape, (list, tuple))
    shapes = list(out_shape) if many else [out_shape]

    def kernel(*refs):
        ends = count + len(after)
        if token:
            refs[ends + len(shapes)][...] = jnp.zeros((8, LANES), F32)
            refs = refs[:ends + len(shapes)] + refs[ends + len(shapes) + 1:]
        body(*refs[:count], *refs[ends:])

    specs = [pl.BlockSpec(memory_space=pltpu.SMEM)]
    specs += [pl.BlockSpec(memory_space=VMEM)] * (count - 1)
    specs += [pl.BlockSpec(memory_space=pl.ANY)] * len(after)
    shown = shapes + [shape((8, LANES), F32)] * token
    outs = pl.pallas_call(
        kernel,
        out_shape=shown,
        in_specs=specs,
        out_specs=[pl.BlockSpec(memory_space=VMEM)] * len(shown),
        scratch_shapes=list(scratch),
        input_output_aliases=aliases or {},
        compiler_params=pltpu.CompilerParams(vmem_limit_bytes=VMEM_LIMIT),
        cost_estimate=pl.CostEstimate(flops=flops, bytes_accessed=0, transcendentals=0),
    )(*args, *after)
    return outs if len(shown) > 1 else outs[0]


def shape(dims, dtype):
    return jax.ShapeDtypeStruct(dims, dtype)


def digits_of(value):
    high = value.astype(BF16).astype(F32)
    rest = value - high
    middle = rest.astype(BF16).astype(F32)
    low = (rest - middle).astype(BF16).astype(F32)
    return high, middle, low


def one_hot(codes, axis_codes, first, count):
    frames = codes.shape[1 - axis_codes]
    dims = (count, frames) if axis_codes == 0 else (frames, count)
    places = lax.broadcasted_iota(jnp.int16, dims, axis_codes)
    return jnp.where((codes - first).astype(jnp.int16) == places, jnp.ones((), BF16), jnp.zeros((), BF16))


def halo_kernel(info, feats, out):
    out[...] = feats[feats.shape[0] - out.shape[0]:, :]


def local_kernel(info, feats, weight, bias, codes, books, unfold, conv, chosen, wide):
    rows, channels = feats.shape
    frames = rows // 2
    for j in range(channels // LANES):
        wide[j, 0:8, :] = jnp.zeros((8, LANES), F32)
        wide[j, 8:, :] = feats[:, j * LANES:(j + 1) * LANES].astype(F32)
        for tap in range(4):
            start = tap * channels + j * LANES
            unfold[:, start:start + LANES] = wide[j, pl.ds(6 + tap, frames, stride=2), :].astype(BF16)
    conv[...] = nn(unfold[...], weight[...]) + bias[...]
    levels = books.shape[0]
    padded = jnp.concatenate([codes[...].astype(F32), jnp.zeros((8 - levels, frames), F32)], 0)
    tall = jnp.transpose(padded).astype(jnp.int32)
    for level in range(levels):
        matches = one_hot(tall[:, level:level + 1], 1, 0, books.shape[1])
        chosen[level] = nn(matches, books[level]).astype(BF16)


def walk(order, halved, count):
    others = order[1:] if halved else order
    shown = count // 2 if halved else count
    step = 2 if shown > 1 and others[-1] == 0 else 1
    for position in range(0, shown, step):
        piece = 0
        for k, bit in enumerate(others):
            piece += ((position >> (len(others) - 1 - k)) & 1) << bit
        yield position, piece, step


def correlate(flipped, sources, plan, bit, out):
    dz = flipped.shape[0]
    at = 0
    for source, (count, order, halved) in zip(sources, plan):
        shown = count // 2 if halved else count
        for position, piece, step in walk(order, halved, count):
            if halved:
                column = pl.multiple_of((piece + (bit << order[0])) * LANES, LANES)
                product = nn(flipped, source[:, pl.ds(column, step * LANES)])
            else:
                product = nn(flipped, source[:, piece * LANES:(piece + step) * LANES])
            for j in range(step):
                top = (at + position + j) * dz
                out[top:top + dz, :] = product[:, j * LANES:(j + 1) * LANES].astype(out.dtype)
        at += shown
    return at * dz


def code_digits(codes, dz, rows):
    parts = []
    for part in (codes >> 8, codes & 255):
        for start in range(0, codes.shape[1], dz):
            piece = part[:, start:start + dz].astype(F32)
            if piece.shape[1] < dz:
                piece = jnp.concatenate([piece, jnp.zeros((1, dz - piece.shape[1]), F32)], 1)
            parts.append(piece)
    parts.append(jnp.zeros((rows - len(parts), dz), F32))
    return jnp.concatenate(parts, 0).astype(BF16)


def codes_of(block, frames):
    dz = block.shape[1]
    per = -(-frames // dz)
    digits = block[...].astype(F32)
    parts = [jnp.concatenate([digits[k * per + j:k * per + j + 1, :] for j in range(per)], 1)[:, :frames]
             for k in range(2)]
    return (parts[0] * 256.0 + parts[1]).astype(jnp.int32)


def forward_kernel(plan, info, halo, unfold_in, conv, chosen, weight, proj, codes,
                   unfold, hidden, latent_grad, flipped, own, send):
    frames, width = unfold.shape
    half = width // 2
    dz = proj.shape[1]
    row = lax.broadcasted_iota(jnp.int32, (16, half), 0)
    last = halo[...].astype(F32)
    left = jnp.concatenate([last[14:15, :], last[15:16, :]], 1)
    head = jnp.where(row == 0, jnp.broadcast_to(left, (16, half)), 0.0)
    unfold[0:16, 0:half] = (unfold_in[0:16, 0:half].astype(F32) + head).astype(BF16)
    fix = nn(head.astype(BF16), weight[0:half, :])
    hidden[...] = jnp.concatenate([conv[0:16, :] + fix, conv[16:, :]], 0).astype(BF16)
    latent = nn(hidden[...], proj[...])
    once = latent - chosen[0].astype(F32)
    total = once + (once - chosen[1].astype(F32))
    latent_grad[...] = total.astype(BF16)
    flipped[...] = jnp.transpose(latent_grad[...].astype(F32)).astype(BF16)
    bit = info[0]
    at = correlate(flipped[...], (unfold, hidden), plan, 1 - bit, send)
    code_rows = own.shape[0] - frames
    digits = [code_digits(codes[level:level + 1], dz, code_rows) for level in range(2)]
    own[0:frames, :] = jnp.where(bit == 1, once, latent).astype(BF16)
    own[frames:, :] = jnp.where(bit == 1, digits[1], digits[0])
    other = jnp.where(bit == 1, latent, once).astype(BF16)
    other_digits = jnp.where(bit == 1, digits[0], digits[1])
    for j in range(dz // LANES):
        send[at:at + frames, :] = other[:, j * LANES:(j + 1) * LANES]
        send[at + frames:at + frames + code_rows, :] = other_digits[:, j * LANES:(j + 1) * LANES]
        at += frames + code_rows


def rest_kernel(plan, info, flipped, unfold, hidden, latent_grad, proj, keep_a, keep_c, hidden_grad, extras, row):
    bit = info[0]
    correlate(flipped[...], (unfold,), plan[:1], bit, keep_a)
    correlate(flipped[...], (hidden,), plan[1:], bit, keep_c)
    back = nt(latent_grad[...], proj[...]).astype(BF16)
    hidden_grad[...] = back
    row[...] = back[0:16, :]
    stride = extras.shape[0] // 6
    extras[...] = jnp.zeros(extras.shape, F32)
    sums = jnp.sum(back.astype(F32), 0, keepdims=True)
    for digit, part in enumerate(digits_of(sums)):
        for j in range(sums.shape[1] // LANES):
            extras[digit * stride + j:digit * stride + j + 1, :] = part[:, j * LANES:(j + 1) * LANES]


def split_sum(halved, bit, got, at, kept, rows, send, to, keep):
    if halved:
        half = rows // 2
        away = pl.multiple_of((1 - bit) * half, 16)
        home = pl.multiple_of(bit * half, 16)
        send[to:to + half, :] = (kept[pl.ds(away, half), :] + got[pl.ds(at + away, half), :].astype(F32)).astype(BF16)
        keep[0:half, :] = kept[pl.ds(home, half), :] + got[pl.ds(at + home, half), :].astype(F32)
        return half
    total = (kept[0:rows, :] + got[at:at + rows, :].astype(F32)).astype(BF16)
    send[to:to + rows, :] = total
    keep[0:rows, :] = total.astype(F32)
    return rows


def add_digits(mine, theirs):
    stride = mine.shape[0] // 6
    return ((mine[0:stride] + mine[stride:2 * stride]) + mine[2 * stride:3 * stride]) + (
        (theirs[0:stride] + theirs[stride:2 * stride]) + theirs[2 * stride:3 * stride])


def digit_block(value):
    return jnp.concatenate(list(digits_of(value)) + [jnp.zeros_like(value)] * 3, 0)


def first_step_kernel(halves, place, info, got, kept_a, kept_c, extras, send, keep_a, keep_c):
    (rows_a, halved_a), (rows_c, halved_c) = halves
    to = split_sum(halved_a, info[place], got, 0, kept_a, rows_a, send, 0, keep_a)
    gone = split_sum(halved_c, info[place], got, rows_a, kept_c, rows_c, send, to, keep_c)
    send[to + gone:, :] = extras[...].astype(BF16)
    keep_c[gone:, :] = extras[...]


def feat_kernel(info, grad, after, weight, out, wide, inter):
    frames, channels = grad.shape
    half = weight.shape[0] // 2
    wide[0:frames, :] = grad[...].astype(F32)
    wide[frames:, :] = jnp.broadcast_to(after[0:1, :].astype(F32), (8, channels))
    ahead = wide[pl.ds(1, frames), :].astype(BF16)
    for parity in range(2):
        rows = pl.ds(parity * (half // 2), half // 2)
        rows_after = pl.ds(half + parity * (half // 2), half // 2)
        both = nt(ahead, weight[rows, :]) + nt(grad[...], weight[rows_after, :])
        for j in range(channels // LANES):
            inter[j, pl.ds(parity, frames, stride=2), :] = both[:, j * LANES:(j + 1) * LANES]
    for j in range(channels // LANES):
        out[:, j * LANES:(j + 1) * LANES] = inter[j].astype(BF16)


def sums_kernel(first, frames, place, count, info, got, own, row, send, keep):
    rows, dz = own.shape
    theirs = jnp.concatenate([got[first + j * rows:first + (j + 1) * rows, :] for j in range(dz // LANES)], 1)
    ones = jnp.ones((8, frames), BF16)
    parts = []
    for block in (own[...], theirs):
        parts.append((block[0:frames, :], codes_of(block[frames:, :], frames)))
    size = count + 16
    riding = row[...].astype(F32)[0:1, :]
    for out in (send, keep):
        for top in range(0, keep.shape[0], size):
            total = jnp.zeros((count, dz), F32)
            counts = jnp.zeros((8, count), F32)
            for values, codes in parts:
                matches = one_hot(codes, 0, info[place], count)
                total = total + nn(matches, values)
                counts = counts + nt(ones, matches)
            out[top:top + count, :] = total.astype(out.dtype)
            out[top + count:top + size, :] = count_rows(counts[0:1], dz, riding).astype(out.dtype)
            place += 1


def count_rows(count, width, riding=None):
    high = jnp.floor(count * (1.0 / 65536.0))
    rest = count - high * 65536.0
    middle = jnp.floor(rest * (1.0 / 256.0))
    low = rest - middle * 256.0
    block = jnp.concatenate([high, middle, low], 0)
    if count.shape[1] < width:
        block = jnp.concatenate([block, jnp.zeros((3, width - count.shape[1]), F32)], 1)
    parts = [block]
    if riding is not None:
        parts += [riding[:, at:at + width] for at in range(0, riding.shape[1], width)]
    parts.append(jnp.zeros((16 - sum(part.shape[0] for part in parts), width), F32))
    return jnp.concatenate(parts, 0)


def riding_row(block, parts):
    return jnp.concatenate([block[3 + j:4 + j, :] for j in range(parts)], 1)


def count_of(block, own):
    return (block[0:1] * 65536.0 + block[1:2] * 256.0 + block[2:3])[:, :own]


def sums_step(halved, count, bit, riding, got, kept, send, keep):
    size = count + 16
    dz = got.shape[1]
    half = kept.shape[0] // 2 if halved else 0
    outs = [(send, (1 - bit) * half), (keep, bit * half)] if halved else [(send, 0)]
    for out, start in outs:
        for top in range(0, keep.shape[0], size):
            here = top + pl.multiple_of(start, 16) if halved else top
            sums = pl.ds(here, count)
            tail = pl.ds(here + count, 16)
            value = kept[sums, :].astype(F32) + got[sums, :].astype(F32)
            number = count_of(kept[tail, :].astype(F32), count) + count_of(got[tail, :].astype(F32), count)
            out[top:top + count, :] = value.astype(out.dtype)
            out[top + count:top + size, :] = count_rows(number, dz, riding).astype(out.dtype)
    if not halved:
        keep[...] = send[...].astype(F32)


def window_kernel(halves, at_c, place, apart, sums_plan, row_plan, info, got_a, got_c, kept_a, kept_c, sums_got,
                  sums_kept, *refs):
    (rows_a, halved_a), (rows_c, halved_c) = halves
    sums_halved, sums_count, sums_place = sums_plan
    row_step, row_parts, row_place = row_plan
    row = None
    if row_step is not None:
        row = riding_row(sums_got[sums_count:sums_count + 16, :].astype(F32), row_parts)
        wide = jnp.broadcast_to(row, refs[-1].shape)
        before = refs[0][...].astype(F32) if row_step else jnp.zeros_like(wide)
        refs[-1][...] = jnp.where(info[row_place] == row_step, wide, before).astype(BF16)
        refs = refs[1 if row_step else 0:-1]
    if apart:
        send_a, send_c, keep_a, keep_c, sums_send, sums_keep = refs
    else:
        send_a, keep_a, keep_c, sums_send, sums_keep = refs
        send_c = send_a
    to = split_sum(halved_a, info[place], got_a, 0, kept_a, rows_a, send_a, 0, keep_a)
    to = 0 if apart else to
    gone = split_sum(halved_c, info[place], got_c, at_c, kept_c, rows_c, send_c, to, keep_c)
    block = digit_block(add_digits(kept_c[rows_c:, :], got_c[at_c + rows_c:, :].astype(F32)))
    send_c[to + gone:, :] = block.astype(BF16)
    keep_c[gone:, :] = block
    sums_step(sums_halved, sums_count, info[sums_place], row, sums_got, sums_kept, sums_send, sums_keep)


def last_kernel(rows, at_c, count, info, got_a, kept_a, got, kept, sums_got, sums_kept, corr, pieces, mine):
    corr[...] = kept_a[...] + got_a[0:corr.shape[0], :].astype(F32)
    pieces[...] = (kept[0:rows, :] + got[at_c:at_c + rows, :].astype(F32)).astype(BF16)
    block = digit_block(add_digits(kept[rows:, :], got[at_c + rows:, :].astype(F32)))
    at = rows
    mine[0:at, :] = pieces[...]
    mine[at:at + block.shape[0], :] = block.astype(BF16)
    at += block.shape[0]
    number = count_of(sums_kept[count:, :].astype(F32), count) + count_of(sums_got[count:, :].astype(F32), count)
    square = (count, count)
    same = lax.broadcasted_iota(jnp.int32, square, 0) == lax.broadcasted_iota(jnp.int32, square, 1)
    tall = jnp.sum(jnp.where(same, jnp.broadcast_to(number, square), 0.0), 1, keepdims=True)
    total = sums_kept[0:count, :].astype(F32) + sums_got[0:count, :].astype(F32)
    means = (total / jnp.maximum(tall, 1.0)).astype(BF16)
    digits = count_rows(number, means.shape[1]).astype(BF16)
    for j in range(means.shape[1] // LANES):
        mine[at:at + count, :] = means[:, j * LANES:(j + 1) * LANES]
        mine[at + count:at + count + 16, :] = digits[:, j * LANES:(j + 1) * LANES]
        at += count + 16


def conv_out_kernel(total_frames, place, info, corr, proj, out, wide):
    rows = out.shape[0]
    flipped = jnp.transpose(corr[...])
    high = flipped.astype(BF16)
    low = (flipped - high.astype(F32)).astype(BF16)
    wide[...] = (nt(high, proj[...]) + nt(low, proj[...])) * (1.0 / total_frames)
    start = info[place]
    if rows % 8 == 0:
        out[...] = wide[pl.ds(pl.multiple_of(start, 8), rows), :]
    else:
        taken = wide[0:rows, :]
        for other in range(rows, wide.shape[0], rows):
            taken = jnp.where(start == other, wide[other:other + rows, :], taken)
        out[...] = taken


def means_out_kernel(total_frames, use_scale, count, dz, top, extra, info, mine, theirs, bias, means, usage):
    value = add_digits(mine[top:top + extra, :].astype(F32), theirs[top:top + extra, :].astype(F32)) * (
        1.0 / total_frames)
    for j in range(bias.shape[1] // LANES):
        bias[:, j * LANES:(j + 1) * LANES] = value[j:j + 1, :]
    bit = info[0]
    numbers = []
    for ref, level in ((mine, bit), (theirs, 1 - bit)):
        at = top + extra
        blocks = []
        for j in range(dz // LANES):
            blocks.append(ref[at:at + count + 16, :])
            at += count + 16
        whole = jnp.concatenate(blocks, 1)
        means[level] = whole[0:count, :]
        numbers.append(count_of(whole[count:, :].astype(F32), count) * use_scale)
    usage[0:1, :] = jnp.where(bit == 1, numbers[1], numbers[0])
    usage[1:2, :] = jnp.where(bit == 1, numbers[0], numbers[1])


def proj_out_kernel(total_frames, dz, place, inner, info, *refs):
    parts, out = refs[:-1], refs[-1]
    for j, ref in enumerate(parts):
        for k in range(inner):
            start = pl.multiple_of((info[place + j] + k) * LANES, LANES)
            turned = jnp.transpose(ref[k * dz:(k + 1) * dz, :])
            out[pl.ds(start, LANES), :] = turned.astype(F32) * (1.0 / total_frames)


def shifted(block, axis, distance):
    devices = range(lax.axis_size(axis))
    route = [(i - distance, i) for i in devices if i - distance in devices]
    return lax.ppermute(block, axis, route)


def swapped(block, axis, mask):
    return lax.ppermute(block, axis, [(i, i ^ mask) for i in range(lax.axis_size(axis))])


def shards(feats, codes, conv_weight, conv_bias, proj_weight, codebooks):
    dp, tm = lax.axis_size("dp"), lax.axis_size("tm")
    rows_in, channels = feats.shape
    frames = rows_in // 2
    levels, book_size, dz = codebooks.shape
    assert levels == 2
    width = conv_weight.shape[0]
    total_frames = frames * dp * tm
    per_shard = book_size // tm
    dp_bits, tm_bits = log2(dp), log2(tm)
    owner_rows = width // (dp * tm)

    exchanges = [("dp", b, b + tm_bits) for b in range(dp_bits)]
    exchanges += [("tm", b, b) for b in reversed(range(tm_bits))]
    pieces_a, pieces_c = width // LANES, channels // LANES
    under = max(dp_bits + tm_bits - log2(pieces_a), 0)
    c_bits = min(log2(pieces_c), 2, dp_bits)
    a_split = [bit - under if bit >= under else None for _, _, bit in exchanges]
    c_split = [log2(pieces_c) - 1 - k if k < c_bits else None for k in range(len(exchanges))]

    def order_of(split, count):
        used = [b for b in split if b is not None]
        return used + [b for b in reversed(range(log2(count))) if b not in used]

    plan = [(pieces_a, order_of(a_split, pieces_a), a_split[0] is not None),
            (pieces_c, order_of(c_split, pieces_c), c_split[0] is not None)]
    now_a = pieces_a // 2 if plan[0][2] else pieces_a
    now_c = pieces_c // 2 if plan[1][2] else pieces_c

    sums_exchanges = [("tm", b) for b in range(tm_bits)] + [("dp", b) for b in range(1, dp_bits)]

    at_dp, at_tm = lax.axis_index("dp"), lax.axis_index("tm")

    def bit_of(axis, b):
        return ((at_dp if axis == "dp" else at_tm) >> b) & 1

    bits = [bit_of(axis, b) for axis, b, _ in exchanges]
    sums_bits = [bit_of(axis, b) for axis, b in sums_exchanges]
    masks = list(range(1 << c_bits))
    own_piece = sum((bits[k] << c_split[k]) for k in range(c_bits))
    flips = [sum(1 << c_split[k] for k in range(c_bits) if m >> k & 1) for m in masks]
    quarters = [sum(((position >> (tm_bits - 1 - b)) & 1) << b for b in range(tm_bits)) for position in range(tm)]
    lead = at_tm & 1
    send_quarters = [(q | (1 - lead)) * per_shard for q in quarters[:tm // 2]]
    keep_quarters = [(q | lead) * per_shard for q in quarters[:tm // 2]]
    at_start = len(bits)
    at_codes = at_start + 1
    at_pieces = at_codes + tm
    at_sums = at_pieces + len(masks)
    at_row = at_sums + len(sums_bits)
    ones_below = sum(((at_tm + 1) & ((1 << (b + 1)) - 1) == 0).astype(jnp.int32) for b in range(tm_bits))
    info = jnp.stack(
        bits + [((at_dp * tm + at_tm) * owner_rows) & (LANES - 1)] + send_quarters + keep_quarters
        + [own_piece ^ flip for flip in flips] + sums_bits + [ones_below]).astype(jnp.int32)

    halo = shifted(
        call(halo_kernel, shape((16, channels), BF16), [info, feats], flops=10 ** 11), "tm", 1)
    weight, proj, codes = conv_weight, proj_weight, codes[0]
    unfold, conv, chosen = call(
        local_kernel,
        [shape((frames, width), BF16), shape((frames, channels), F32), shape((levels, frames, dz), BF16)],
        [info, feats, weight, conv_bias[None, :], codes, codebooks],
        scratch=[VMEM((channels // LANES, rows_in + 8, LANES), F32)],
    )

    extra = 6 * (-(-channels // LANES // 8) * 8)
    code_rows = -(-(2 * -(-frames // dz)) // 16) * 16
    corr_rows = (now_a + now_c) * dz
    rows_b = frames + code_rows
    unfold, hidden, latent_grad, flipped, own, send = call(
        functools.partial(forward_kernel, plan),
        [shape((frames, width), BF16), shape((frames, channels), BF16), shape((frames, dz), BF16),
         shape((dz, frames), BF16), shape((rows_b, dz), BF16),
         shape((corr_rows + rows_b * (dz // LANES), LANES), BF16)],
        [info, halo, unfold, conv, chosen, weight, proj, codes],
        aliases={2: 0},
    )
    got = swapped(send, "dp", 1)
    keep_a, keep_c, hidden_grad, extras, row = call(
        functools.partial(rest_kernel, plan),
        [shape((now_a * dz, LANES), F32), shape((now_c * dz, LANES), F32), shape((frames, channels), BF16),
         shape((extra, LANES), F32), shape((16, channels), BF16)],
        [info, flipped, unfold, hidden, latent_grad, proj],
        after=[send],
    )

    def halves_at(k):
        nonlocal now_a, now_c
        halves = [(now_a * dz, a_split[k] is not None), (now_c * dz, c_split[k] is not None)]
        now_a = now_a // 2 if halves[0][1] else now_a
        now_c = now_c // 2 if halves[1][1] else now_c
        return halves, now_a * dz, now_c * dz + extra

    halves, rows_a, rows_c = halves_at(1)
    core_got = got
    send, keep_a, keep_c = call(
        functools.partial(first_step_kernel, halves, 1),
        [shape((rows_a + rows_c, LANES), BF16), shape((rows_a, LANES), F32), shape((rows_c, LANES), F32)],
        [info, got, keep_a, keep_c, extras])
    got_a = got_c = swapped(send, exchanges[1][0], 1 << exchanges[1][1])
    size = per_shard + 16
    row_parts = channels // dz
    sums_rows = size * (tm // 2)
    sums_send, sums_keep = call(
        functools.partial(sums_kernel, corr_rows, frames, at_codes, per_shard),
        [shape((sums_rows, dz), BF16), shape((sums_rows, dz), F32)],
        [info, core_got, own, row],
        after=[send])
    sums_got = swapped(sums_send, sums_exchanges[0][0], 1 << sums_exchanges[0][1])
    after = None
    ordered = []
    for k in range(2, len(exchanges)):
        at_c = now_a * dz if got_a is got_c else 0
        halves, rows_a, rows_c = halves_at(k)
        apart = k <= tm_bits
        halved = sums_exchanges[k - 1][0] == "tm"
        sums_rows = sums_rows // 2 if halved else sums_rows
        row_step = k - 2 if k - 2 < tm_bits else None
        sends = [rows_a, rows_c] if apart else [rows_a + rows_c]
        outs = [shape((rows, LANES), BF16) for rows in sends] + [shape((rows, LANES), F32) for rows in (rows_a, rows_c)]
        outs += [shape((sums_rows, dz), BF16), shape((sums_rows, dz), F32)]
        outs = call(
            functools.partial(window_kernel, halves, at_c, k, apart, (halved, per_shard, at_sums + k - 1),
                              (row_step, row_parts, at_row)),
            outs + [shape((16, channels), BF16)] * (row_step is not None),
            [info, got_a, got_c, keep_a, keep_c, sums_got, sums_keep] + [after] * bool(row_step),
            after=ordered)
        after = outs[-1] if row_step is not None else after
        got_a = got_c = swapped(outs[0], exchanges[k][0], 1 << exchanges[k][1])
        if apart:
            got_c = swapped(outs[1], exchanges[k][0], 1 << exchanges[k][1])
        keep_a, keep_c, sums_send, sums_keep = outs[len(sends):len(sends) + 4]
        sums_got = swapped(sums_send, sums_exchanges[k - 1][0], 1 << sums_exchanges[k - 1][1])
        if k == tm_bits + 1:
            feat_grad, *ordered = call(
                feat_kernel,
                shape((rows_in, channels), BF16),
                [info, hidden_grad, after, weight],
                after=[outs[0]],
                token=True,
                scratch=[VMEM((frames + 8, channels), F32), VMEM((channels // LANES, rows_in, LANES), F32)],
            )
    assert now_a == 1 and sums_rows == size

    corr, piece, mine = call(
        functools.partial(last_kernel, rows_c - extra, rows_a if got_a is got_c else 0, per_shard),
        [shape((rows_a, LANES), F32), shape((rows_c - extra, LANES), BF16),
         shape((rows_c + size * (dz // LANES), LANES), BF16)],
        [info, got_a, keep_a, got_c, keep_c, sums_got, sums_keep],
        after=ordered)
    parts = [piece] + [swapped(mine if m == 1 else piece, "dp", m) for m in masks[1:]]
    conv_grad, last = call(
        functools.partial(conv_out_kernel, total_frames, at_start),
        shape((owner_rows, channels), F32),
        [info, corr, proj],
        after=[piece],
        token=True,
        scratch=[VMEM((LANES, channels), F32)],
    )
    bias_grad, code_means, code_usage, last = call(
        functools.partial(
            means_out_kernel, total_frames, book_size / total_frames, per_shard, dz, rows_c - extra, extra),
        [shape((1, channels), F32), shape((levels, per_shard, dz), BF16), shape((levels, per_shard), F32)],
        [info, mine, parts[1]],
        after=[last],
        token=True,
    )
    proj_grad = call(
        functools.partial(proj_out_kernel, total_frames, dz, at_pieces, now_c),
        shape((channels, dz), F32),
        [info] + parts,
        after=[last],
    )
    return feat_grad, conv_grad, bias_grad[0], proj_grad, code_means, code_usage


def solution(mesh):
    placed = (P(("dp", "tm"), None), P("dp", None, "tm"), P(), P(), P(), P())
    return jax.shard_map(
        shards,
        mesh=mesh,
        in_specs=placed,
        out_specs=(
            P(("dp", "tm"), None),
            P(("dp", "tm"), None),
            P(),
            P(),
            P(None, "tm", None),
            P(None, "tm"),
        ),
        check_vma=False,
    )
```

```python
import functools

import jax
import jax.numpy as jnp
from jax import lax
from jax.experimental import pallas as pl
from jax.experimental.pallas import tpu as pltpu
from jax.sharding import PartitionSpec as P

BF16 = jnp.bfloat16
F32 = jnp.float32
LANES = 128
VMEM_LIMIT = 16 * 1024 * 1024


def log2(value):
    assert value & (value - 1) == 0
    return value.bit_length() - 1


def nn(a, b):
    return lax.dot_general(a, b, (((1,), (0,)), ((), ())), preferred_element_type=F32)


def nt(a, b):
    return lax.dot_general(a, b, (((1,), (1,)), ((), ())), preferred_element_type=F32)


VMEM = pltpu.VMEM


def call(body, out_shape, args, after=(), scratch=(), aliases=None, token=False, flops=0):
    count = len(args)
    many = isinstance(out_shape, (list, tuple))
    shapes = list(out_shape) if many else [out_shape]

    def kernel(*refs):
        ends = count + len(after)
        if token:
            refs[ends + len(shapes)][...] = jnp.zeros((8, LANES), F32)
            refs = refs[:ends + len(shapes)] + refs[ends + len(shapes) + 1:]
        body(*refs[:count], *refs[ends:])

    specs = [pl.BlockSpec(memory_space=pltpu.SMEM)]
    specs += [pl.BlockSpec(memory_space=VMEM)] * (count - 1)
    specs += [pl.BlockSpec(memory_space=pl.ANY)] * len(after)
    shown = shapes + [shape((8, LANES), F32)] * token
    outs = pl.pallas_call(
        kernel,
        out_shape=shown,
        in_specs=specs,
        out_specs=[pl.BlockSpec(memory_space=VMEM)] * len(shown),
        scratch_shapes=list(scratch),
        input_output_aliases=aliases or {},
        compiler_params=pltpu.CompilerParams(vmem_limit_bytes=VMEM_LIMIT),
        cost_estimate=pl.CostEstimate(flops=flops, bytes_accessed=0, transcendentals=0),
    )(*args, *after)
    return outs if len(shown) > 1 else outs[0]


def shape(dims, dtype):
    return jax.ShapeDtypeStruct(dims, dtype)


def digits_of(value):
    high = value.astype(BF16).astype(F32)
    rest = value - high
    middle = rest.astype(BF16).astype(F32)
    low = (rest - middle).astype(BF16).astype(F32)
    return high, middle, low


def one_hot(codes, axis_codes, first, count):
    frames = codes.shape[1 - axis_codes]
    dims = (count, frames) if axis_codes == 0 else (frames, count)
    places = lax.broadcasted_iota(jnp.int32, dims, axis_codes) + first
    return jnp.where(codes == places, 1.0, 0.0).astype(BF16)


def halo_kernel(info, feats, out):
    out[...] = feats[feats.shape[0] - out.shape[0]:, :]


def local_kernel(info, feats, weight, bias, codes, books, unfold, conv, chosen, wide):
    rows, channels = feats.shape
    frames = rows // 2
    for j in range(channels // LANES):
        wide[j, 0:8, :] = jnp.zeros((8, LANES), F32)
        wide[j, 8:, :] = feats[:, j * LANES:(j + 1) * LANES].astype(F32)
        for tap in range(4):
            start = tap * channels + j * LANES
            unfold[:, start:start + LANES] = wide[j, pl.ds(6 + tap, frames, stride=2), :].astype(BF16)
    conv[...] = nn(unfold[...], weight[...]) + bias[...]
    levels = books.shape[0]
    padded = jnp.concatenate([codes[...].astype(F32), jnp.zeros((8 - levels, frames), F32)], 0)
    tall = jnp.transpose(padded).astype(jnp.int32)
    for level in range(levels):
        matches = one_hot(tall[:, level:level + 1], 1, 0, books.shape[1])
        chosen[level] = nn(matches, books[level]).astype(BF16)


def walk(order, halved, count):
    others = order[1:] if halved else order
    shown = count // 2 if halved else count
    step = 2 if shown > 1 and others[-1] == 0 else 1
    for position in range(0, shown, step):
        piece = 0
        for k, bit in enumerate(others):
            piece += ((position >> (len(others) - 1 - k)) & 1) << bit
        yield position, piece, step


def correlate(flipped, sources, plan, bit, out):
    dz = flipped.shape[0]
    at = 0
    for source, (count, order, halved) in zip(sources, plan):
        shown = count // 2 if halved else count
        for position, piece, step in walk(order, halved, count):
            if halved:
                column = pl.multiple_of((piece + (bit << order[0])) * LANES, LANES)
                product = nn(flipped, source[:, pl.ds(column, step * LANES)])
            else:
                product = nn(flipped, source[:, piece * LANES:(piece + step) * LANES])
            for j in range(step):
                top = (at + position + j) * dz
                out[top:top + dz, :] = product[:, j * LANES:(j + 1) * LANES].astype(out.dtype)
        at += shown
    return at * dz


def code_digits(codes, dz, rows):
    parts = []
    for part in (codes >> 8, codes & 255):
        for start in range(0, codes.shape[1], dz):
            piece = part[:, start:start + dz].astype(F32)
            if piece.shape[1] < dz:
                piece = jnp.concatenate([piece, jnp.zeros((1, dz - piece.shape[1]), F32)], 1)
            parts.append(piece)
    parts.append(jnp.zeros((rows - len(parts), dz), F32))
    return jnp.concatenate(parts, 0).astype(BF16)


def codes_of(block, frames):
    dz = block.shape[1]
    per = -(-frames // dz)
    digits = block[...].astype(F32)
    parts = [jnp.concatenate([digits[k * per + j:k * per + j + 1, :] for j in range(per)], 1)[:, :frames]
             for k in range(2)]
    return (parts[0] * 256.0 + parts[1]).astype(jnp.int32)


def forward_kernel(plan, info, halo, unfold_in, conv, chosen, weight, proj, codes,
                   unfold, hidden, latent_grad, flipped, own, send):
    frames, width = unfold.shape
    half = width // 2
    dz = proj.shape[1]
    row = lax.broadcasted_iota(jnp.int32, (16, half), 0)
    last = halo[...].astype(F32)
    left = jnp.concatenate([last[14:15, :], last[15:16, :]], 1)
    head = jnp.where(row == 0, jnp.broadcast_to(left, (16, half)), 0.0)
    unfold[0:16, 0:half] = (unfold_in[0:16, 0:half].astype(F32) + head).astype(BF16)
    fix = nn(head.astype(BF16), weight[0:half, :])
    hidden[...] = jnp.concatenate([conv[0:16, :] + fix, conv[16:, :]], 0).astype(BF16)
    latent = nn(hidden[...], proj[...])
    once = latent - chosen[0].astype(F32)
    total = once + (once - chosen[1].astype(F32))
    latent_grad[...] = total.astype(BF16)
    flipped[...] = jnp.transpose(latent_grad[...].astype(F32)).astype(BF16)
    bit = info[0]
    at = correlate(flipped[...], (unfold, hidden), plan, 1 - bit, send)
    code_rows = own.shape[0] - frames
    digits = [code_digits(codes[level:level + 1], dz, code_rows) for level in range(2)]
    own[0:frames, :] = jnp.where(bit == 1, once, latent).astype(BF16)
    own[frames:, :] = jnp.where(bit == 1, digits[1], digits[0])
    other = jnp.where(bit == 1, latent, once).astype(BF16)
    other_digits = jnp.where(bit == 1, digits[0], digits[1])
    for j in range(dz // LANES):
        send[at:at + frames, :] = other[:, j * LANES:(j + 1) * LANES]
        send[at + frames:at + frames + code_rows, :] = other_digits[:, j * LANES:(j + 1) * LANES]
        at += frames + code_rows


def rest_kernel(plan, info, flipped, unfold, hidden, latent_grad, proj, keep_a, keep_c, hidden_grad, extras, row):
    bit = info[0]
    correlate(flipped[...], (unfold,), plan[:1], bit, keep_a)
    correlate(flipped[...], (hidden,), plan[1:], bit, keep_c)
    back = nt(latent_grad[...], proj[...]).astype(BF16)
    hidden_grad[...] = back
    row[...] = back[0:16, :]
    stride = extras.shape[0] // 6
    extras[...] = jnp.zeros(extras.shape, F32)
    sums = jnp.sum(back.astype(F32), 0, keepdims=True)
    for digit, part in enumerate(digits_of(sums)):
        for j in range(sums.shape[1] // LANES):
            extras[digit * stride + j:digit * stride + j + 1, :] = part[:, j * LANES:(j + 1) * LANES]


def split_sum(halved, bit, got, at, kept, rows, send, to, keep):
    if halved:
        half = rows // 2
        away = pl.multiple_of((1 - bit) * half, 16)
        home = pl.multiple_of(bit * half, 16)
        send[to:to + half, :] = (kept[pl.ds(away, half), :] + got[pl.ds(at + away, half), :].astype(F32)).astype(BF16)
        keep[0:half, :] = kept[pl.ds(home, half), :] + got[pl.ds(at + home, half), :].astype(F32)
        return half
    total = (kept[0:rows, :] + got[at:at + rows, :].astype(F32)).astype(BF16)
    send[to:to + rows, :] = total
    keep[0:rows, :] = total.astype(F32)
    return rows


def add_digits(mine, theirs):
    stride = mine.shape[0] // 6
    return ((mine[0:stride] + mine[stride:2 * stride]) + mine[2 * stride:3 * stride]) + (
        (theirs[0:stride] + theirs[stride:2 * stride]) + theirs[2 * stride:3 * stride])


def digit_block(value):
    return jnp.concatenate(list(digits_of(value)) + [jnp.zeros_like(value)] * 3, 0)


def first_step_kernel(halves, place, info, got, kept_a, kept_c, extras, send, keep_a, keep_c):
    (rows_a, halved_a), (rows_c, halved_c) = halves
    to = split_sum(halved_a, info[place], got, 0, kept_a, rows_a, send, 0, keep_a)
    gone = split_sum(halved_c, info[place], got, rows_a, kept_c, rows_c, send, to, keep_c)
    send[to + gone:, :] = extras[...].astype(BF16)
    keep_c[gone:, :] = extras[...]


def feat_kernel(info, grad, after, weight, out, wide, inter):
    frames, channels = grad.shape
    half = weight.shape[0] // 2
    wide[0:frames, :] = grad[...].astype(F32)
    wide[frames:, :] = jnp.broadcast_to(after[0:1, :].astype(F32), (8, channels))
    ahead = wide[pl.ds(1, frames), :].astype(BF16)
    for parity in range(2):
        rows = pl.ds(parity * (half // 2), half // 2)
        rows_after = pl.ds(half + parity * (half // 2), half // 2)
        both = nt(ahead, weight[rows, :]) + nt(grad[...], weight[rows_after, :])
        for j in range(channels // LANES):
            inter[j, pl.ds(parity, frames, stride=2), :] = both[:, j * LANES:(j + 1) * LANES]
    for j in range(channels // LANES):
        out[:, j * LANES:(j + 1) * LANES] = inter[j].astype(BF16)


def sums_kernel(first, frames, info, got, own, row, send):
    rows, dz = own.shape
    theirs = jnp.concatenate([got[first + j * rows:first + (j + 1) * rows, :] for j in range(dz // LANES)], 1)
    ones = jnp.ones((8, frames), BF16)
    parts = []
    for block in (own[...], theirs):
        parts.append((block[0:frames, :], codes_of(block[frames:, :], frames)))
    count = send.shape[1] - 16
    riding = row[...].astype(F32)[0:1, :]
    for place in range(send.shape[0]):
        total = jnp.zeros((count, dz), F32)
        counts = jnp.zeros((8, count), F32)
        for values, codes in parts:
            matches = one_hot(codes, 0, place * count, count)
            total = total + nn(matches, values)
            counts = counts + nt(ones, matches)
        send[place, 0:count, :] = total.astype(BF16)
        send[place, count:, :] = count_rows(counts[0:1], dz, riding).astype(BF16)


def count_rows(count, width, riding=None):
    high = jnp.floor(count * (1.0 / 65536.0))
    rest = count - high * 65536.0
    middle = jnp.floor(rest * (1.0 / 256.0))
    low = rest - middle * 256.0
    block = jnp.concatenate([high, middle, low], 0)
    if count.shape[1] < width:
        block = jnp.concatenate([block, jnp.zeros((3, width - count.shape[1]), F32)], 1)
    parts = [block]
    if riding is not None:
        parts += [riding[:, at:at + width] for at in range(0, riding.shape[1], width)]
    parts.append(jnp.zeros((16 - sum(part.shape[0] for part in parts), width), F32))
    return jnp.concatenate(parts, 0)


def riding_row(block, parts):
    return jnp.concatenate([block[3 + j:4 + j, :] for j in range(parts)], 1)


def count_of(block, own):
    return (block[0:1] * 65536.0 + block[1:2] * 256.0 + block[2:3])[:, :own]


def sums_step(gots, kept, send, keep):
    count = keep.shape[0] - 16
    value = kept[0:count, :].astype(F32)
    number = count_of(kept[count:, :].astype(F32), count)
    for got in gots:
        value = value + got[0:count, :].astype(F32)
        number = number + count_of(got[count:, :].astype(F32), count)
    send[0:count, :] = value.astype(BF16)
    send[count:, :] = count_rows(number, send.shape[1]).astype(BF16)
    keep[...] = send[...].astype(F32)


def window_kernel(halves, place, at_tm, info, got, kept_a, kept_c, *refs):
    (rows_a, halved_a), (rows_c, halved_c) = halves
    if at_tm is not None:
        blocks = refs[0]
        after = refs[-1]
        refs = refs[1:-1]
        tm = blocks.shape[0]
        count = blocks.shape[1] - 16
        here = info[at_tm]
        following = blocks[jnp.minimum(here + 1, tm - 1), count:, :].astype(F32)
        row = riding_row(following, after.shape[1] // blocks.shape[2])
        row = jnp.where(here + 1 < tm, row, jnp.zeros_like(row))
        after[...] = jnp.broadcast_to(row, after.shape).astype(BF16)
        gots, sums_kept = [blocks.at[j] for j in range(1, tm)], blocks.at[0]
    elif len(refs) > 3:
        gots, sums_kept = [refs[0]], refs[1]
        refs = refs[2:]
    send, keep_a, keep_c = refs[:3]
    to = split_sum(halved_a, info[place], got, 0, kept_a, rows_a, send, 0, keep_a)
    gone = split_sum(halved_c, info[place], got, rows_a, kept_c, rows_c, send, to, keep_c)
    block = digit_block(add_digits(kept_c[rows_c:, :], got[rows_a + rows_c:, :].astype(F32)))
    send[to + gone:, :] = block.astype(BF16)
    keep_c[gone:, :] = block
    if len(refs) > 3:
        sums_step(gots, sums_kept, refs[3], refs[4])


def last_kernel(rows, at_c, count, info, got_a, kept_a, got, kept, sums_got, sums_kept, corr, pieces, mine):
    corr[...] = kept_a[...] + got_a[0:corr.shape[0], :].astype(F32)
    pieces[...] = (kept[0:rows, :] + got[at_c:at_c + rows, :].astype(F32)).astype(BF16)
    block = digit_block(add_digits(kept[rows:, :], got[at_c + rows:, :].astype(F32)))
    at = rows
    mine[0:at, :] = pieces[...]
    mine[at:at + block.shape[0], :] = block.astype(BF16)
    at += block.shape[0]
    number = count_of(sums_kept[count:, :].astype(F32), count) + count_of(sums_got[count:, :].astype(F32), count)
    square = (count, count)
    same = lax.broadcasted_iota(jnp.int32, square, 0) == lax.broadcasted_iota(jnp.int32, square, 1)
    tall = jnp.sum(jnp.where(same, jnp.broadcast_to(number, square), 0.0), 1, keepdims=True)
    total = sums_kept[0:count, :].astype(F32) + sums_got[0:count, :].astype(F32)
    means = (total / jnp.maximum(tall, 1.0)).astype(BF16)
    digits = count_rows(number, means.shape[1]).astype(BF16)
    for j in range(means.shape[1] // LANES):
        mine[at:at + count, :] = means[:, j * LANES:(j + 1) * LANES]
        mine[at + count:at + count + 16, :] = digits[:, j * LANES:(j + 1) * LANES]
        at += count + 16


def conv_out_kernel(total_frames, place, info, corr, proj, out, wide):
    rows = out.shape[0]
    flipped = jnp.transpose(corr[...])
    high = flipped.astype(BF16)
    low = (flipped - high.astype(F32)).astype(BF16)
    wide[...] = (nt(high, proj[...]) + nt(low, proj[...])) * (1.0 / total_frames)
    start = info[place]
    if rows % 8 == 0:
        out[...] = wide[pl.ds(pl.multiple_of(start, 8), rows), :]
    else:
        taken = wide[0:rows, :]
        for other in range(rows, wide.shape[0], rows):
            taken = jnp.where(start == other, wide[other:other + rows, :], taken)
        out[...] = taken


def means_out_kernel(total_frames, use_scale, count, dz, top, extra, info, mine, theirs, bias, means, usage):
    value = add_digits(mine[top:top + extra, :].astype(F32), theirs[top:top + extra, :].astype(F32)) * (
        1.0 / total_frames)
    for j in range(bias.shape[1] // LANES):
        bias[:, j * LANES:(j + 1) * LANES] = value[j:j + 1, :]
    bit = info[0]
    numbers = []
    for ref, level in ((mine, bit), (theirs, 1 - bit)):
        at = top + extra
        blocks = []
        for j in range(dz // LANES):
            blocks.append(ref[at:at + count + 16, :])
            at += count + 16
        whole = jnp.concatenate(blocks, 1)
        means[level] = whole[0:count, :]
        numbers.append(count_of(whole[count:, :].astype(F32), count) * use_scale)
    usage[0:1, :] = jnp.where(bit == 1, numbers[1], numbers[0])
    usage[1:2, :] = jnp.where(bit == 1, numbers[0], numbers[1])


def proj_out_kernel(total_frames, dz, place, inner, info, *refs):
    parts, out = refs[:-1], refs[-1]
    for j, ref in enumerate(parts):
        for k in range(inner):
            start = pl.multiple_of((info[place + j] + k) * LANES, LANES)
            turned = jnp.transpose(ref[k * dz:(k + 1) * dz, :])
            out[pl.ds(start, LANES), :] = turned.astype(F32) * (1.0 / total_frames)


def shifted(block, axis, distance):
    devices = range(lax.axis_size(axis))
    route = [(i - distance, i) for i in devices if i - distance in devices]
    return lax.ppermute(block, axis, route)


def swapped(block, axis, mask):
    return lax.ppermute(block, axis, [(i, i ^ mask) for i in range(lax.axis_size(axis))])


def shards(feats, codes, conv_weight, conv_bias, proj_weight, codebooks):
    dp, tm = lax.axis_size("dp"), lax.axis_size("tm")
    rows_in, channels = feats.shape
    frames = rows_in // 2
    levels, book_size, dz = codebooks.shape
    assert levels == 2
    width = conv_weight.shape[0]
    total_frames = frames * dp * tm
    per_shard = book_size // tm
    dp_bits, tm_bits = log2(dp), log2(tm)
    owner_rows = width // (dp * tm)

    exchanges = [("dp", b, b + tm_bits) for b in range(dp_bits)]
    exchanges += [("tm", b, b) for b in reversed(range(tm_bits))]
    pieces_a, pieces_c = width // LANES, channels // LANES
    under = max(dp_bits + tm_bits - log2(pieces_a), 0)
    c_bits = min(log2(pieces_c), 2, dp_bits)
    a_split = [bit - under if bit >= under else None for _, _, bit in exchanges]
    c_split = [log2(pieces_c) - 1 - k if k < c_bits else None for k in range(len(exchanges))]

    def order_of(split, count):
        used = [b for b in split if b is not None]
        return used + [b for b in reversed(range(log2(count))) if b not in used]

    plan = [(pieces_a, order_of(a_split, pieces_a), a_split[0] is not None),
            (pieces_c, order_of(c_split, pieces_c), c_split[0] is not None)]
    now_a = pieces_a // 2 if plan[0][2] else pieces_a
    now_c = pieces_c // 2 if plan[1][2] else pieces_c

    at_dp, at_tm = lax.axis_index("dp"), lax.axis_index("tm")

    def bit_of(axis, b):
        return ((at_dp if axis == "dp" else at_tm) >> b) & 1

    bits = [bit_of(axis, b) for axis, b, _ in exchanges]
    masks = list(range(1 << c_bits))
    own_piece = sum((bits[k] << c_split[k]) for k in range(c_bits))
    flips = [sum(1 << c_split[k] for k in range(c_bits) if m >> k & 1) for m in masks]
    at_start = len(bits)
    at_pieces = at_start + 1
    at_row = at_pieces + len(masks)
    info = jnp.stack(
        bits + [((at_dp * tm + at_tm) * owner_rows) & (LANES - 1)] + [own_piece ^ flip for flip in flips]
        + [at_tm]).astype(jnp.int32)

    halo = shifted(
        call(halo_kernel, shape((16, channels), BF16), [info, feats], flops=10 ** 11), "tm", 1)
    weight, proj, codes = conv_weight, proj_weight, codes[0]
    unfold, conv, chosen = call(
        local_kernel,
        [shape((frames, width), BF16), shape((frames, channels), F32), shape((levels, frames, dz), BF16)],
        [info, feats, weight, conv_bias[None, :], codes, codebooks],
        scratch=[VMEM((channels // LANES, rows_in + 8, LANES), F32)],
    )

    extra = 6 * (-(-channels // LANES // 8) * 8)
    code_rows = -(-(2 * -(-frames // dz)) // 16) * 16
    corr_rows = (now_a + now_c) * dz
    rows_b = frames + code_rows
    unfold, hidden, latent_grad, flipped, own, send = call(
        functools.partial(forward_kernel, plan),
        [shape((frames, width), BF16), shape((frames, channels), BF16), shape((frames, dz), BF16),
         shape((dz, frames), BF16), shape((rows_b, dz), BF16),
         shape((corr_rows + rows_b * (dz // LANES), LANES), BF16)],
        [info, halo, unfold, conv, chosen, weight, proj, codes],
        aliases={2: 0},
    )
    got = swapped(send, "dp", 1)
    keep_a, keep_c, hidden_grad, extras, row = call(
        functools.partial(rest_kernel, plan),
        [shape((now_a * dz, LANES), F32), shape((now_c * dz, LANES), F32), shape((frames, channels), BF16),
         shape((extra, LANES), F32), shape((16, channels), BF16)],
        [info, flipped, unfold, hidden, latent_grad, proj],
        after=[send],
    )

    def halves_at(k):
        nonlocal now_a, now_c
        halves = [(now_a * dz, a_split[k] is not None), (now_c * dz, c_split[k] is not None)]
        now_a = now_a // 2 if halves[0][1] else now_a
        now_c = now_c // 2 if halves[1][1] else now_c
        return halves, now_a * dz, now_c * dz + extra

    halves, rows_a, rows_c = halves_at(1)
    core_got = got
    send, keep_a, keep_c = call(
        functools.partial(first_step_kernel, halves, 1),
        [shape((rows_a + rows_c, LANES), BF16), shape((rows_a, LANES), F32), shape((rows_c, LANES), F32)],
        [info, got, keep_a, keep_c, extras])
    got = swapped(send, exchanges[1][0], 1 << exchanges[1][1])
    size = per_shard + 16
    sums_send = call(
        functools.partial(sums_kernel, corr_rows, frames),
        shape((tm, size, dz), BF16),
        [info, core_got, own, row],
        after=[send])
    blocks = lax.all_to_all(sums_send, "tm", 0, 0)
    sums_bits = list(range(1, dp_bits))
    ordered = []
    for k in range(2, len(exchanges)):
        halves, rows_a, rows_c = halves_at(k)
        outs = [shape((rows_a + rows_c, LANES), BF16), shape((rows_a, LANES), F32), shape((rows_c, LANES), F32)]
        args = [info, got, keep_a, keep_c]
        summed = len(exchanges) - k <= len(sums_bits)
        first_sum = summed and len(sums_bits) == dp_bits - 1
        if summed:
            outs += [shape((size, dz), BF16), shape((size, dz), F32)]
            args += [blocks] if first_sum else [sums_got, sums_keep]
        outs = call(
            functools.partial(window_kernel, halves, k, at_row if first_sum else None),
            outs + [shape((16, channels), BF16)] * first_sum,
            args,
            after=ordered)
        send, keep_a, keep_c = outs[:3]
        got = swapped(send, exchanges[k][0], 1 << exchanges[k][1])
        if summed:
            sums_send, sums_keep = outs[3:5]
            sums_got = swapped(sums_send, "dp", 1 << sums_bits.pop(0))
        if first_sum:
            feat_grad, *ordered = call(
                feat_kernel,
                shape((rows_in, channels), BF16),
                [info, hidden_grad, outs[5], weight],
                after=[send],
                token=True,
                scratch=[VMEM((frames + 8, channels), F32), VMEM((channels // LANES, rows_in, LANES), F32)],
            )
    assert now_a == 1 and not sums_bits

    corr, piece, mine = call(
        functools.partial(last_kernel, rows_c - extra, rows_a, per_shard),
        [shape((rows_a, LANES), F32), shape((rows_c - extra, LANES), BF16),
         shape((rows_c + size * (dz // LANES), LANES), BF16)],
        [info, got, keep_a, got, keep_c, sums_got, sums_keep],
        after=ordered)
    parts = [piece] + [swapped(mine if m == 1 else piece, "dp", m) for m in masks[1:]]
    conv_grad, last = call(
        functools.partial(conv_out_kernel, total_frames, at_start),
        shape((owner_rows, channels), F32),
        [info, corr, proj],
        after=[piece],
        token=True,
        scratch=[VMEM((LANES, channels), F32)],
    )
    bias_grad, code_means, code_usage, last = call(
        functools.partial(
            means_out_kernel, total_frames, book_size / total_frames, per_shard, dz, rows_c - extra, extra),
        [shape((1, channels), F32), shape((levels, per_shard, dz), BF16), shape((levels, per_shard), F32)],
        [info, mine, parts[1]],
        after=[last],
        token=True,
    )
    proj_grad = call(
        functools.partial(proj_out_kernel, total_frames, dz, at_pieces, now_c),
        shape((channels, dz), F32),
        [info] + parts,
        after=[last],
    )
    return feat_grad, conv_grad, bias_grad[0], proj_grad, code_means, code_usage


def solution(mesh):
    placed = (P(("dp", "tm"), None), P("dp", None, "tm"), P(), P(), P(), P())
    return jax.shard_map(
        shards,
        mesh=mesh,
        in_specs=placed,
        out_specs=(
            P(("dp", "tm"), None),
            P(("dp", "tm"), None),
            P(),
            P(),
            P(None, "tm", None),
            P(None, "tm"),
        ),
        check_vma=False,
    )
```

```python
import functools

import jax
import jax.numpy as jnp
from jax import lax
from jax.experimental import pallas as pl
from jax.experimental.pallas import tpu as pltpu
from jax.sharding import PartitionSpec as P

BF16 = jnp.bfloat16
F32 = jnp.float32
LANES = 128
VMEM_LIMIT = 16 * 1024 * 1024


def log2(value):
    assert value & (value - 1) == 0
    return value.bit_length() - 1


def nn(a, b):
    return lax.dot_general(a, b, (((1,), (0,)), ((), ())), preferred_element_type=F32)


def nt(a, b):
    return lax.dot_general(a, b, (((1,), (1,)), ((), ())), preferred_element_type=F32)


VMEM = pltpu.VMEM


def call(body, out_shape, args, after=(), scratch=(), aliases=None, token=False, flops=0):
    count = len(args)
    many = isinstance(out_shape, (list, tuple))
    shapes = list(out_shape) if many else [out_shape]

    def kernel(*refs):
        ends = count + len(after)
        if token:
            refs[ends + len(shapes)][...] = jnp.zeros((8, LANES), F32)
            refs = refs[:ends + len(shapes)] + refs[ends + len(shapes) + 1:]
        body(*refs[:count], *refs[ends:])

    specs = [pl.BlockSpec(memory_space=pltpu.SMEM)]
    specs += [pl.BlockSpec(memory_space=VMEM)] * (count - 1)
    specs += [pl.BlockSpec(memory_space=pl.ANY)] * len(after)
    shown = shapes + [shape((8, LANES), F32)] * token
    outs = pl.pallas_call(
        kernel,
        out_shape=shown,
        in_specs=specs,
        out_specs=[pl.BlockSpec(memory_space=VMEM)] * len(shown),
        scratch_shapes=list(scratch),
        input_output_aliases=aliases or {},
        compiler_params=pltpu.CompilerParams(vmem_limit_bytes=VMEM_LIMIT),
        cost_estimate=pl.CostEstimate(flops=flops, bytes_accessed=0, transcendentals=0),
    )(*args, *after)
    return outs if len(shown) > 1 else outs[0]


def shape(dims, dtype):
    return jax.ShapeDtypeStruct(dims, dtype)


def digits_of(value):
    high = value.astype(BF16).astype(F32)
    rest = value - high
    middle = rest.astype(BF16).astype(F32)
    low = (rest - middle).astype(BF16).astype(F32)
    return high, middle, low


def one_hot(codes, axis_codes, first, count):
    frames = codes.shape[1 - axis_codes]
    dims = (count, frames) if axis_codes == 0 else (frames, count)
    places = lax.broadcasted_iota(jnp.int32, dims, axis_codes) + first
    return jnp.where(codes == places, 1.0, 0.0).astype(BF16)


def halo_kernel(info, feats, out):
    out[...] = feats[feats.shape[0] - out.shape[0]:, :]


def local_kernel(info, feats, weight, bias, codes, books, unfold, conv, chosen, wide):
    rows, channels = feats.shape
    frames = rows // 2
    for j in range(channels // LANES):
        wide[j, 0:8, :] = jnp.zeros((8, LANES), F32)
        wide[j, 8:, :] = feats[:, j * LANES:(j + 1) * LANES].astype(F32)
        for tap in range(4):
            start = tap * channels + j * LANES
            unfold[:, start:start + LANES] = wide[j, pl.ds(6 + tap, frames, stride=2), :].astype(BF16)
    conv[...] = nn(unfold[...], weight[...]) + bias[...]
    levels = books.shape[0]
    padded = jnp.concatenate([codes[...].astype(F32), jnp.zeros((8 - levels, frames), F32)], 0)
    tall = jnp.transpose(padded).astype(jnp.int32)
    for level in range(levels):
        matches = one_hot(tall[:, level:level + 1], 1, 0, books.shape[1])
        chosen[level] = nn(matches, books[level]).astype(BF16)


def walk(orders, halved, count):
    start = 1 if halved else 0
    shown = count // 2 if halved else count
    bits = log2(shown)
    step = 2 if shown > 1 and all(order[-1] == 0 for order in orders) else 1
    for position in range(0, shown, step):
        yield position, [
            sum(((position >> (bits - 1 - k)) & 1) << bit for k, bit in enumerate(order[start:])) for order in orders
        ], step


def correlate(flipped, sources, plan, core, bit, out):
    dz = flipped.shape[0]
    at = 0
    for source, (count, orders, halved) in zip(sources, plan):
        for position, pieces, step in walk(orders, halved, count):
            column = pieces[0] + core * (pieces[1] - pieces[0])
            if halved:
                column = column + (bit << orders[0][0])
            column = pl.multiple_of(column * LANES, LANES)
            product = nn(flipped, source[:, pl.ds(column, step * LANES)])
            for j in range(step):
                top = (at + position + j) * dz
                out[top:top + dz, :] = product[:, j * LANES:(j + 1) * LANES].astype(out.dtype)
        at += count // 2 if halved else count
    return at * dz


def code_digits(codes, dz, rows):
    parts = []
    for part in (codes >> 8, codes & 255):
        for start in range(0, codes.shape[1], dz):
            piece = part[:, start:start + dz].astype(F32)
            if piece.shape[1] < dz:
                piece = jnp.concatenate([piece, jnp.zeros((1, dz - piece.shape[1]), F32)], 1)
            parts.append(piece)
    parts.append(jnp.zeros((rows - len(parts), dz), F32))
    return jnp.concatenate(parts, 0).astype(BF16)


def codes_of(block, frames):
    dz = block.shape[1]
    per = -(-frames // dz)
    digits = block[...].astype(F32)
    parts = [jnp.concatenate([digits[k * per + j:k * per + j + 1, :] for j in range(per)], 1)[:, :frames]
             for k in range(2)]
    return (parts[0] * 256.0 + parts[1]).astype(jnp.int32)


def forward_kernel(plan, info, halo, unfold_in, conv, chosen, weight, proj, codes,
                   unfold, hidden, latent_grad, flipped, own, send):
    frames, width = unfold.shape
    half = width // 2
    dz = proj.shape[1]
    row = lax.broadcasted_iota(jnp.int32, (16, half), 0)
    last = halo[...].astype(F32)
    left = jnp.concatenate([last[14:15, :], last[15:16, :]], 1)
    head = jnp.where(row == 0, jnp.broadcast_to(left, (16, half)), 0.0)
    unfold[0:16, 0:half] = (unfold_in[0:16, 0:half].astype(F32) + head).astype(BF16)
    fix = nn(head.astype(BF16), weight[0:half, :])
    hidden[...] = jnp.concatenate([conv[0:16, :] + fix, conv[16:, :]], 0).astype(BF16)
    latent = nn(hidden[...], proj[...])
    once = latent - chosen[0].astype(F32)
    total = once + (once - chosen[1].astype(F32))
    latent_grad[...] = total.astype(BF16)
    flipped[...] = jnp.transpose(latent_grad[...].astype(F32)).astype(BF16)
    bit = info[0]
    at = correlate(flipped[...], (unfold, hidden), plan, 1 - bit, 1 - bit, send)
    code_rows = own.shape[0] - frames
    digits = [code_digits(codes[level:level + 1], dz, code_rows) for level in range(2)]
    own[0:frames, :] = jnp.where(bit == 1, once, latent).astype(BF16)
    own[frames:, :] = jnp.where(bit == 1, digits[1], digits[0])
    other = jnp.where(bit == 1, latent, once).astype(BF16)
    other_digits = jnp.where(bit == 1, digits[0], digits[1])
    for j in range(dz // LANES):
        send[at:at + frames, :] = other[:, j * LANES:(j + 1) * LANES]
        send[at + frames:at + frames + code_rows, :] = other_digits[:, j * LANES:(j + 1) * LANES]
        at += frames + code_rows


def rest_kernel(plan, info, flipped, unfold, hidden, latent_grad, proj, keep_a, keep_c, hidden_grad, extras, row):
    bit = info[0]
    correlate(flipped[...], (unfold,), plan[:1], bit, bit, keep_a)
    correlate(flipped[...], (hidden,), plan[1:], bit, bit, keep_c)
    back = nt(latent_grad[...], proj[...]).astype(BF16)
    hidden_grad[...] = back
    row[...] = back[0:16, :]
    stride = extras.shape[0] // 6
    extras[...] = jnp.zeros(extras.shape, F32)
    sums = jnp.sum(back.astype(F32), 0, keepdims=True)
    for digit, part in enumerate(digits_of(sums)):
        for j in range(sums.shape[1] // LANES):
            extras[digit * stride + j:digit * stride + j + 1, :] = part[:, j * LANES:(j + 1) * LANES]


def split_sum(halved, bit, got, at, kept, rows, send, to, keep):
    if halved:
        half = rows // 2
        away = pl.multiple_of((1 - bit) * half, 16)
        home = pl.multiple_of(bit * half, 16)
        send[to:to + half, :] = (kept[pl.ds(away, half), :] + got[pl.ds(at + away, half), :].astype(F32)).astype(BF16)
        keep[0:half, :] = kept[pl.ds(home, half), :] + got[pl.ds(at + home, half), :].astype(F32)
        return half
    total = (kept[0:rows, :] + got[at:at + rows, :].astype(F32)).astype(BF16)
    send[to:to + rows, :] = total
    keep[0:rows, :] = total.astype(F32)
    return rows


def add_digits(mine, theirs):
    stride = mine.shape[0] // 6
    return ((mine[0:stride] + mine[stride:2 * stride]) + mine[2 * stride:3 * stride]) + (
        (theirs[0:stride] + theirs[stride:2 * stride]) + theirs[2 * stride:3 * stride])


def digit_block(value):
    return jnp.concatenate(list(digits_of(value)) + [jnp.zeros_like(value)] * 3, 0)


def first_step_kernel(halves, place, info, got, kept_a, kept_c, extras, send_a, send_c, keep_a, keep_c):
    (rows_a, halved_a), (rows_c, halved_c) = halves
    split_sum(halved_a, info[place], got, 0, kept_a, rows_a, send_a, 0, keep_a)
    gone = split_sum(halved_c, info[place], got, rows_a, kept_c, rows_c, send_c, 0, keep_c)
    send_c[gone:, :] = extras[...].astype(BF16)
    keep_c[gone:, :] = extras[...]


def feat_kernel(info, grad, after, weight, out, wide, inter):
    frames, channels = grad.shape
    half = weight.shape[0] // 2
    wide[0:frames, :] = grad[...].astype(F32)
    wide[frames:, :] = jnp.broadcast_to(after[0:1, :].astype(F32), (8, channels))
    ahead = wide[pl.ds(1, frames), :].astype(BF16)
    for parity in range(2):
        rows = pl.ds(parity * (half // 2), half // 2)
        rows_after = pl.ds(half + parity * (half // 2), half // 2)
        both = nt(ahead, weight[rows, :]) + nt(grad[...], weight[rows_after, :])
        for j in range(channels // LANES):
            inter[j, pl.ds(parity, frames, stride=2), :] = both[:, j * LANES:(j + 1) * LANES]
    for j in range(channels // LANES):
        out[:, j * LANES:(j + 1) * LANES] = inter[j].astype(BF16)


def sums_kernel(first, frames, place, count, info, got, own, row, out):
    rows, dz = own.shape
    theirs = jnp.concatenate([got[first + j * rows:first + (j + 1) * rows, :] for j in range(dz // LANES)], 1)
    ones = jnp.ones((8, frames), BF16)
    parts = []
    for block in (own[...], theirs):
        parts.append((block[0:frames, :], codes_of(block[frames:, :], frames)))
    size = count + 16
    riding = [row[...].astype(F32)[0:1, :]]
    for top in range(0, out.shape[0], size):
        total = jnp.zeros((count, dz), F32)
        counts = jnp.zeros((8, count), F32)
        for values, codes in parts:
            matches = one_hot(codes, 0, info[place], count)
            total = total + nn(matches, values)
            counts = counts + nt(ones, matches)
        out[top:top + count, :] = total.astype(out.dtype)
        out[top + count:top + size, :] = count_rows(counts[0:1], dz, riding).astype(out.dtype)
        place += 1


def count_rows(count, width, riding=()):
    high = jnp.floor(count * (1.0 / 65536.0))
    rest = count - high * 65536.0
    middle = jnp.floor(rest * (1.0 / 256.0))
    low = rest - middle * 256.0
    block = jnp.concatenate([high, middle, low], 0)
    if count.shape[1] < width:
        block = jnp.concatenate([block, jnp.zeros((3, width - count.shape[1]), F32)], 1)
    parts = [block]
    for row in riding:
        parts += [row[:, at:at + width] for at in range(0, row.shape[1], width)]
    left = 16 - sum(part.shape[0] for part in parts)
    return jnp.concatenate(parts + [jnp.zeros((left, width), F32)] * (left > 0), 0)


def riding_row(block, index, parts):
    return jnp.concatenate([block[3 + index * parts + j:4 + index * parts + j, :] for j in range(parts)], 1)


def count_of(block, own):
    return (block[0:1] * 65536.0 + block[1:2] * 256.0 + block[2:3])[:, :own]


def sums_step(halved, count, bit, riding, got, kept, send, keep):
    size = count + 16
    dz = got.shape[1]
    half = kept.shape[0] // 2 if halved else 0
    outs = [(send, (1 - bit) * half), (keep, bit * half)] if halved else [(send, 0)]
    for out, start in outs:
        for top in range(0, keep.shape[0], size):
            here = top + pl.multiple_of(start, 16) if halved else top
            sums = pl.ds(here, count)
            tail = pl.ds(here + count, 16)
            value = kept[sums, :].astype(F32) + got[sums, :].astype(F32)
            number = count_of(kept[tail, :].astype(F32), count) + count_of(got[tail, :].astype(F32), count)
            out[top:top + count, :] = value.astype(out.dtype)
            out[top + count:top + size, :] = count_rows(number, dz, riding).astype(out.dtype)
    if not halved:
        keep[...] = send[...].astype(F32)


def swap_halves(first, second, core):
    half = LANES // 2
    left = lax.broadcasted_iota(jnp.int32, first.shape, 1) < half
    turned_first, turned_second = pltpu.roll(first, half, 1), pltpu.roll(second, half, 1)
    swapped_first = jnp.where(left, first, turned_second)
    swapped_second = jnp.where(left, turned_first, second)
    return jnp.where(core == 1, swapped_first, first), jnp.where(core == 1, swapped_second, second)


def window_kernel(halves, at_c, place, apart, mixed, sums_plan, row_plan, info, got_a, got_c, kept_a, kept_c, sums_got,
                  sums_kept, *refs):
    (rows_a, halved_a), (rows_c, halved_c) = halves
    sums_halved, sums_count, sums_place = sums_plan
    row_step, row_place = row_plan
    riding = ()
    if row_step is not None:
        known, refs = refs[0][...].astype(F32), refs[1:]
        after, refs = refs[-1], refs[:-1]
        parts = known.shape[1] // sums_got.shape[1]
        block = sums_got[sums_count:sums_count + 16, :].astype(F32)
        rows = [known[j:j + 1, :] for j in range(1 << row_step)]
        rows += [riding_row(block, j, parts) for j in range(1 << row_step)]
        riding = rows if sums_halved else ()
        if sums_halved:
            total = rows + [jnp.zeros((16 - len(rows), known.shape[1]), F32)]
            after[...] = jnp.concatenate(total, 0).astype(BF16)
        else:
            wide = jnp.zeros(after.shape, F32)
            for j in range(1, len(rows)):
                wide = jnp.where(info[row_place] == j, jnp.broadcast_to(rows[j], after.shape), wide)
            after[...] = wide.astype(BF16)
    if apart:
        send_a, send_c, keep_a, keep_c, sums_send, sums_keep = refs
    else:
        send_a, keep_a, keep_c, sums_send, sums_keep = refs
        send_c = send_a
    if mixed:
        half = rows_a // 2
        total = kept_a[0:rows_a, :] + got_a[0:rows_a, :].astype(F32)
        first, second = swap_halves(total[0:half, :], total[half:, :], info[0])
        low = info[place] == 0
        send_a[0:half, :] = jnp.where(low, second, first).astype(BF16)
        keep_a[...] = jnp.where(low, first, second)
        to = half
    else:
        to = split_sum(halved_a, info[place], got_a, 0, kept_a, rows_a, send_a, 0, keep_a)
    to = 0 if apart else to
    gone = split_sum(halved_c, info[place], got_c, at_c, kept_c, rows_c, send_c, to, keep_c)
    block = digit_block(add_digits(kept_c[rows_c:, :], got_c[at_c + rows_c:, :].astype(F32)))
    send_c[to + gone:, :] = block.astype(BF16)
    keep_c[gone:, :] = block
    sums_step(sums_halved, sums_count, info[sums_place], riding, sums_got, sums_kept, sums_send, sums_keep)


def last_kernel(rows, at_c, count, info, got_a, kept_a, got, kept, sums_got, sums_kept, corr, pieces, mine):
    corr[...] = kept_a[...] + got_a[0:corr.shape[0], :].astype(F32)
    pieces[...] = (kept[0:rows, :] + got[at_c:at_c + rows, :].astype(F32)).astype(BF16)
    block = digit_block(add_digits(kept[rows:, :], got[at_c + rows:, :].astype(F32)))
    at = rows
    mine[0:at, :] = pieces[...]
    mine[at:at + block.shape[0], :] = block.astype(BF16)
    at += block.shape[0]
    number = count_of(sums_kept[count:, :].astype(F32), count) + count_of(sums_got[count:, :].astype(F32), count)
    square = (count, count)
    same = lax.broadcasted_iota(jnp.int32, square, 0) == lax.broadcasted_iota(jnp.int32, square, 1)
    tall = jnp.sum(jnp.where(same, jnp.broadcast_to(number, square), 0.0), 1, keepdims=True)
    total = sums_kept[0:count, :].astype(F32) + sums_got[0:count, :].astype(F32)
    means = (total / jnp.maximum(tall, 1.0)).astype(BF16)
    digits = count_rows(number, means.shape[1]).astype(BF16)
    for j in range(means.shape[1] // LANES):
        mine[at:at + count, :] = means[:, j * LANES:(j + 1) * LANES]
        mine[at + count:at + count + 16, :] = digits[:, j * LANES:(j + 1) * LANES]
        at += count + 16


def conv_out_kernel(total_frames, place, info, corr, proj, out, wide):
    rows = out.shape[0]
    flipped = jnp.transpose(corr[...])
    high = flipped.astype(BF16)
    low = (flipped - high.astype(F32)).astype(BF16)
    wide[...] = (nt(high, proj[...]) + nt(low, proj[...])) * (1.0 / total_frames)
    start = info[place]
    if rows % 8 == 0:
        out[...] = wide[pl.ds(pl.multiple_of(start, 8), rows), :]
    else:
        taken = wide[0:rows, :]
        for other in range(rows, wide.shape[0], rows):
            taken = jnp.where(start == other, wide[other:other + rows, :], taken)
        out[...] = taken


def means_out_kernel(total_frames, use_scale, count, dz, top, extra, info, mine, theirs, bias, means, usage):
    value = add_digits(mine[top:top + extra, :].astype(F32), theirs[top:top + extra, :].astype(F32)) * (
        1.0 / total_frames)
    for j in range(bias.shape[1] // LANES):
        bias[:, j * LANES:(j + 1) * LANES] = value[j:j + 1, :]
    bit = info[0]
    numbers = []
    for ref, level in ((mine, bit), (theirs, 1 - bit)):
        at = top + extra
        blocks = []
        for j in range(dz // LANES):
            blocks.append(ref[at:at + count + 16, :])
            at += count + 16
        whole = jnp.concatenate(blocks, 1)
        means[level] = whole[0:count, :]
        numbers.append(count_of(whole[count:, :].astype(F32), count) * use_scale)
    usage[0:1, :] = jnp.where(bit == 1, numbers[1], numbers[0])
    usage[1:2, :] = jnp.where(bit == 1, numbers[0], numbers[1])


def proj_out_kernel(total_frames, dz, place, inner, info, *refs):
    parts, out = refs[:-1], refs[-1]
    for j, ref in enumerate(parts):
        for k in range(inner):
            start = pl.multiple_of((info[place + j] + k) * LANES, LANES)
            turned = jnp.transpose(ref[k * dz:(k + 1) * dz, :])
            out[pl.ds(start, LANES), :] = turned.astype(F32) * (1.0 / total_frames)


def shifted(block, axis, distance):
    devices = range(lax.axis_size(axis))
    route = [(i - distance, i) for i in devices if i - distance in devices]
    return lax.ppermute(block, axis, route)


def swapped(block, steps):
    tm = lax.axis_size("tm")

    def partner(device):
        axis, bit = steps[(device // tm) & 1]
        return device ^ ((1 << bit) * (tm if axis == "dp" else 1))

    route = [(device, partner(device)) for device in range(lax.axis_size("dp") * tm)]
    return lax.ppermute(block, ("dp", "tm"), route)


def crossed(block, steps):
    tm = lax.axis_size("tm")

    def partner(device):
        axis, bit = steps[(device // tm) & 1]
        return device ^ tm ^ ((1 << bit) * (tm if axis == "dp" else 1))

    route = [(device, partner(device)) for device in range(lax.axis_size("dp") * tm)]
    return lax.ppermute(block, ("dp", "tm"), route)


def shards(feats, codes, conv_weight, conv_bias, proj_weight, codebooks):
    dp, tm = lax.axis_size("dp"), lax.axis_size("tm")
    rows_in, channels = feats.shape
    frames = rows_in // 2
    levels, book_size, dz = codebooks.shape
    assert levels == 2
    width = conv_weight.shape[0]
    total_frames = frames * dp * tm
    per_shard = book_size // tm
    dp_bits, tm_bits = log2(dp), log2(tm)
    owner_rows = width // (dp * tm)

    assert dp_bits >= 3 and 1 <= tm_bits <= 2
    pieces_a, pieces_c = width // LANES, channels // LANES
    under = max(dp_bits + tm_bits - log2(pieces_a), 0)
    c_bits = 2
    assert pieces_c >= 4
    whole_bits = [b for b in range(1, dp_bits) if b + tm_bits < under]
    piece_bits = [b for b in range(1, dp_bits) if b + tm_bits >= under]
    paths = [[("dp", b) for b in bits] for bits in (whole_bits + piece_bits, whole_bits[::-1] + piece_bits[::-1])]
    mixed = under == 1 and tm_bits == 2
    turned = mixed or under == 0 or under >= tm_bits
    up = [("tm", b) for b in range(tm_bits)]
    paths[0] += up[::-1]
    paths[1] += up if turned else up[::-1]
    exchanges = list(zip([("dp", 0)] + paths[0], [("dp", 0)] + paths[1]))
    sums_up = [("dp", b) for b in range(1, dp_bits)]
    sums_exchanges = list(zip(up + sums_up, up[::-1] + sums_up[::-1]))

    def piece_bit(step):
        axis, b = step
        bit = b + (tm_bits if axis == "dp" else 0)
        return bit - under if bit >= under else None

    a_split = [piece_bit(steps[0]) is not None for steps in exchanges]
    c_split = [log2(pieces_c) - 1 - k if k < c_bits else None for k in range(len(exchanges))]

    def order_of(split, count):
        used = [b for b in split if b is not None]
        return used + [b for b in reversed(range(log2(count))) if b not in used]

    orders = [order_of([piece_bit(steps[core]) for steps in exchanges], pieces_a) for core in range(2)]
    order_c = order_of(c_split, pieces_c)
    plan = [(pieces_a, orders, a_split[0]), (pieces_c, [order_c, order_c], True)]
    now_a = pieces_a // 2 if plan[0][2] else pieces_a
    now_c = pieces_c // 2

    at_dp, at_tm = lax.axis_index("dp"), lax.axis_index("tm")
    core = at_dp & 1

    def on_core(values):
        return values[0] + core * (values[1] - values[0])

    def bit_at(step):
        axis, b = step
        return ((at_dp if axis == "dp" else at_tm) >> b) & 1

    bits = [on_core([bit_at(step) for step in steps]) for steps in exchanges]
    sums_bits = [on_core([bit_at(step) for step in steps]) for steps in sums_exchanges]
    shared = [bit_at(step) for step in exchanges[1]]
    mine_c, other_c = on_core(shared), on_core(shared[::-1])
    places = [2 * core + mine_c, 2 * (1 - core) + other_c, 2 * core + 1 - mine_c, 2 * (1 - core) + 1 - other_c]
    places = [place << (log2(pieces_c) - c_bits) for place in places]
    lists = []
    for way in ([b for _, b in up], [b for _, b in up[::-1]]):
        lists.append([sum(((position >> (tm_bits - 1 - j)) & 1) << b for j, b in enumerate(way)) for position in range(tm)])
    first_bit = on_core([0, tm_bits - 1])
    lead = (at_tm >> first_bit) & 1
    quarters = [on_core([lists[0][j], lists[1][j]]) for j in range(tm // 2)]
    send_codes = [(q + ((1 - lead) << first_bit)) * per_shard for q in quarters]
    keep_codes = [(q + (lead << first_bit)) * per_shard for q in quarters]
    differ = at_tm ^ (at_tm + 1)
    ways = [sum(((differ >> b) & 1) << j for j, b in enumerate(way)) for way in (
        list(range(tm_bits)), list(reversed(range(tm_bits))))]
    row_code = jnp.where(at_tm + 1 < tm, on_core(ways), 0)
    if turned and not mixed:
        start = ((at_dp * tm + at_tm) * owner_rows) & (LANES - 1)
    else:
        start = on_core([(at_dp * tm + at_tm) * owner_rows, (at_tm >> 1) * owner_rows if mixed else (
            at_dp * tm + at_tm) * owner_rows]) & (LANES - 1)
    at_start = len(bits)
    at_codes = at_start + 1
    at_pieces = at_codes + tm
    at_sums = at_pieces + len(places)
    at_row = at_sums + len(sums_bits)
    info = jnp.stack(bits + [start] + send_codes + keep_codes + places + sums_bits + [row_code]).astype(jnp.int32)

    halo = shifted(
        call(halo_kernel, shape((16, channels), BF16), [info, feats], flops=10 ** 11), "tm", 1)
    weight, proj, codes = conv_weight, proj_weight, codes[0]
    unfold, conv, chosen = call(
        local_kernel,
        [shape((frames, width), BF16), shape((frames, channels), F32), shape((levels, frames, dz), BF16)],
        [info, feats, weight, conv_bias[None, :], codes, codebooks],
        scratch=[VMEM((channels // LANES, rows_in + 8, LANES), F32)],
    )

    extra = 6 * (-(-channels // LANES // 8) * 8)
    code_rows = -(-(2 * -(-frames // dz)) // 16) * 16
    corr_rows = (now_a + now_c) * dz
    rows_b = frames + code_rows
    unfold, hidden, latent_grad, flipped, own, send = call(
        functools.partial(forward_kernel, plan),
        [shape((frames, width), BF16), shape((frames, channels), BF16), shape((frames, dz), BF16),
         shape((dz, frames), BF16), shape((rows_b, dz), BF16),
         shape((corr_rows + rows_b * (dz // LANES), LANES), BF16)],
        [info, halo, unfold, conv, chosen, weight, proj, codes],
        aliases={2: 0},
    )
    got = swapped(send, exchanges[0])
    keep_a, keep_c, hidden_grad, extras, row = call(
        functools.partial(rest_kernel, plan),
        [shape((now_a * dz, LANES), F32), shape((now_c * dz, LANES), F32), shape((frames, channels), BF16),
         shape((extra, LANES), F32), shape((16, channels), BF16)],
        [info, flipped, unfold, hidden, latent_grad, proj],
        after=[send],
    )

    def halves_at(k):
        nonlocal now_a, now_c
        halves = [(now_a * dz, a_split[k]), (now_c * dz, c_split[k] is not None)]
        now_a = now_a // 2 if halves[0][1] else now_a
        now_c = now_c // 2 if halves[1][1] else now_c
        return halves, now_a * dz, now_c * dz + extra

    halves, rows_a, rows_c = halves_at(1)
    send_a, send_c, keep_a, keep_c = call(
        functools.partial(first_step_kernel, halves, 1),
        [shape((rows_a, LANES), BF16), shape((rows_c, LANES), BF16), shape((rows_a, LANES), F32),
         shape((rows_c, LANES), F32)],
        [info, got, keep_a, keep_c, extras])
    size = per_shard + 16
    sums_rows = size * (tm // 2)
    sums_send, sums_keep = [
        call(
            functools.partial(sums_kernel, corr_rows, frames, at_codes + first, per_shard),
            shape((sums_rows, dz), dtype),
            [info, got, own, row],
            after=[send_a])
        for first, dtype in ((0, BF16), (tm // 2, F32))]
    sums_got = swapped(sums_send, sums_exchanges[0])
    got_a, got_c = swapped(send_a, exchanges[1]), swapped(send_c, exchanges[1])
    known = row
    ordered = []
    for k in range(2, len(exchanges)):
        at_c = now_a * dz if got_a is got_c else 0
        halves, rows_a, rows_c = halves_at(k)
        apart = k <= tm_bits
        cut_mixed = mixed and k == dp_bits
        halved = sums_exchanges[k - 1][0][0] == "tm"
        sums_rows = sums_rows // 2 if halved else sums_rows
        row_step = k - 2 if k - 2 < tm_bits else None
        sends = [rows_a, rows_c] if apart else [rows_a + rows_c]
        outs = [shape((rows, LANES), BF16) for rows in sends] + [shape((rows, LANES), F32) for rows in (rows_a, rows_c)]
        outs += [shape((sums_rows, dz), BF16), shape((sums_rows, dz), F32)]
        outs = call(
            functools.partial(window_kernel, halves, at_c, k, apart, cut_mixed, (halved, per_shard, at_sums + k - 1),
                              (row_step, at_row)),
            outs + [shape((16, channels), BF16)] * (row_step is not None),
            [info, got_a, got_c, keep_a, keep_c, sums_got, sums_keep] + [known] * (row_step is not None),
            after=ordered)
        known = outs[-1] if row_step is not None else known
        got_a = got_c = swapped(outs[0], exchanges[k])
        if apart:
            got_c = swapped(outs[1], exchanges[k])
        keep_a, keep_c, sums_send, sums_keep = outs[len(sends):len(sends) + 4]
        sums_got = swapped(sums_send, sums_exchanges[k - 1])
        if k == tm_bits + 1:
            feat_grad, *ordered = call(
                feat_kernel,
                shape((rows_in, channels), BF16),
                [info, hidden_grad, known, weight],
                after=[outs[0]],
                token=True,
                scratch=[VMEM((frames + 8, channels), F32), VMEM((channels // LANES, rows_in, LANES), F32)],
            )
    assert now_a == 1 and sums_rows == size

    corr, piece, mine = call(
        functools.partial(last_kernel, rows_c - extra, rows_a if got_a is got_c else 0, per_shard),
        [shape((rows_a, LANES), F32), shape((rows_c - extra, LANES), BF16),
         shape((rows_c + size * (dz // LANES), LANES), BF16)],
        [info, got_a, keep_a, got_c, keep_c, sums_got, sums_keep],
        after=ordered)
    parts = [piece, swapped(mine, exchanges[0]), swapped(piece, exchanges[1]), crossed(piece, exchanges[1])]
    conv_grad, last = call(
        functools.partial(conv_out_kernel, total_frames, at_start),
        shape((owner_rows, channels), F32),
        [info, corr, proj],
        after=[piece],
        token=True,
        scratch=[VMEM((LANES, channels), F32)],
    )
    bias_grad, code_means, code_usage, last = call(
        functools.partial(
            means_out_kernel, total_frames, book_size / total_frames, per_shard, dz, rows_c - extra, extra),
        [shape((1, channels), F32), shape((levels, per_shard, dz), BF16), shape((levels, per_shard), F32)],
        [info, mine, parts[1]],
        after=[last],
        token=True,
    )
    proj_grad = call(
        functools.partial(proj_out_kernel, total_frames, dz, at_pieces, now_c),
        shape((channels, dz), F32),
        [info] + parts,
        after=[last],
    )
    return feat_grad, conv_grad, bias_grad[0], proj_grad, code_means, code_usage


def solution(mesh):
    placed = (P(("dp", "tm"), None), P("dp", None, "tm"), P(), P(), P(), P())
    return jax.shard_map(
        shards,
        mesh=mesh,
        in_specs=placed,
        out_specs=(
            P(("dp", "tm"), None),
            P(("dp", "tm"), None),
            P(),
            P(),
            P(None, "tm", None),
            P(None, "tm"),
        ),
        check_vma=False,
    )
```

```python
import functools

import jax
import jax.numpy as jnp
from jax import lax
from jax.experimental import pallas as pl
from jax.experimental.pallas import tpu as pltpu
from jax.sharding import PartitionSpec as P

BF16 = jnp.bfloat16
F32 = jnp.float32
LANES = 128
VMEM_LIMIT = 16 * 1024 * 1024


def log2(value):
    assert value & (value - 1) == 0
    return value.bit_length() - 1


def nn(a, b):
    return lax.dot_general(a, b, (((1,), (0,)), ((), ())), preferred_element_type=F32)


def nt(a, b):
    return lax.dot_general(a, b, (((1,), (1,)), ((), ())), preferred_element_type=F32)


VMEM = pltpu.VMEM


def call(body, out_shape, args, after=(), scratch=(), aliases=None, token=False, flops=0):
    count = len(args)
    many = isinstance(out_shape, (list, tuple))
    shapes = list(out_shape) if many else [out_shape]

    def kernel(*refs):
        ends = count + len(after)
        if token:
            refs[ends + len(shapes)][...] = jnp.zeros((8, LANES), F32)
            refs = refs[:ends + len(shapes)] + refs[ends + len(shapes) + 1:]
        body(*refs[:count], *refs[ends:])

    specs = [pl.BlockSpec(memory_space=pltpu.SMEM)]
    specs += [pl.BlockSpec(memory_space=VMEM)] * (count - 1)
    specs += [pl.BlockSpec(memory_space=pl.ANY)] * len(after)
    shown = shapes + [shape((8, LANES), F32)] * token
    outs = pl.pallas_call(
        kernel,
        out_shape=shown,
        in_specs=specs,
        out_specs=[pl.BlockSpec(memory_space=VMEM)] * len(shown),
        scratch_shapes=list(scratch),
        input_output_aliases=aliases or {},
        compiler_params=pltpu.CompilerParams(vmem_limit_bytes=VMEM_LIMIT),
        cost_estimate=pl.CostEstimate(flops=flops, bytes_accessed=0, transcendentals=0),
    )(*args, *after)
    return outs if len(shown) > 1 else outs[0]


def shape(dims, dtype):
    return jax.ShapeDtypeStruct(dims, dtype)


def digits_of(value):
    high = value.astype(BF16).astype(F32)
    rest = value - high
    middle = rest.astype(BF16).astype(F32)
    low = (rest - middle).astype(BF16).astype(F32)
    return high, middle, low


def one_hot(codes, axis_codes, first, count):
    frames = codes.shape[1 - axis_codes]
    dims = (count, frames) if axis_codes == 0 else (frames, count)
    places = lax.broadcasted_iota(jnp.int32, dims, axis_codes) + first
    return jnp.where(codes == places, 1.0, 0.0).astype(BF16)


def halo_kernel(info, feats, out):
    out[...] = feats[feats.shape[0] - out.shape[0]:, :]


def local_kernel(info, feats, weight, bias, codes, books, unfold, conv, chosen, wide):
    rows, channels = feats.shape
    frames = rows // 2
    for j in range(channels // LANES):
        wide[j, 0:8, :] = jnp.zeros((8, LANES), F32)
        wide[j, 8:, :] = feats[:, j * LANES:(j + 1) * LANES].astype(F32)
        for tap in range(4):
            start = tap * channels + j * LANES
            unfold[:, start:start + LANES] = wide[j, pl.ds(6 + tap, frames, stride=2), :].astype(BF16)
    conv[...] = nn(unfold[...], weight[...]) + bias[...]
    levels = books.shape[0]
    padded = jnp.concatenate([codes[...].astype(F32), jnp.zeros((8 - levels, frames), F32)], 0)
    tall = jnp.transpose(padded).astype(jnp.int32)
    for level in range(levels):
        matches = one_hot(tall[:, level:level + 1], 1, 0, books.shape[1])
        chosen[level] = nn(matches, books[level]).astype(BF16)


def walk(orders, halved, count):
    start = 1 if halved else 0
    shown = count // 2 if halved else count
    bits = log2(shown)
    step = 2 if shown > 1 and all(order[-1] == 0 for order in orders) else 1
    for position in range(0, shown, step):
        yield position, [
            sum(((position >> (bits - 1 - k)) & 1) << bit for k, bit in enumerate(order[start:])) for order in orders
        ], step


def correlate(flipped, sources, plan, core, bit, out):
    dz = flipped.shape[0]
    at = 0
    for source, (count, orders, halved) in zip(sources, plan):
        for position, pieces, step in walk(orders, halved, count):
            column = pieces[0] + core * (pieces[1] - pieces[0])
            if halved:
                column = column + (bit << orders[0][0])
            column = pl.multiple_of(column * LANES, LANES)
            product = nn(flipped, source[:, pl.ds(column, step * LANES)])
            for j in range(step):
                top = (at + position + j) * dz
                out[top:top + dz, :] = product[:, j * LANES:(j + 1) * LANES].astype(out.dtype)
        at += count // 2 if halved else count
    return at * dz


def code_digits(codes, dz, rows):
    parts = []
    for part in (codes >> 8, codes & 255):
        for start in range(0, codes.shape[1], dz):
            piece = part[:, start:start + dz].astype(F32)
            if piece.shape[1] < dz:
                piece = jnp.concatenate([piece, jnp.zeros((1, dz - piece.shape[1]), F32)], 1)
            parts.append(piece)
    parts.append(jnp.zeros((rows - len(parts), dz), F32))
    return jnp.concatenate(parts, 0).astype(BF16)


def codes_of(block, frames):
    dz = block.shape[1]
    per = -(-frames // dz)
    digits = block[...].astype(F32)
    parts = [jnp.concatenate([digits[k * per + j:k * per + j + 1, :] for j in range(per)], 1)[:, :frames]
             for k in range(2)]
    return (parts[0] * 256.0 + parts[1]).astype(jnp.int32)


def forward_kernel(plan, info, halo, unfold_in, conv, chosen, weight, proj, codes,
                   unfold, hidden, latent_grad, flipped, own, send):
    frames, width = unfold.shape
    half = width // 2
    dz = proj.shape[1]
    row = lax.broadcasted_iota(jnp.int32, (16, half), 0)
    last = halo[...].astype(F32)
    left = jnp.concatenate([last[14:15, :], last[15:16, :]], 1)
    head = jnp.where(row == 0, jnp.broadcast_to(left, (16, half)), 0.0)
    unfold[0:16, 0:half] = (unfold_in[0:16, 0:half].astype(F32) + head).astype(BF16)
    fix = nn(head.astype(BF16), weight[0:half, :])
    hidden[...] = jnp.concatenate([conv[0:16, :] + fix, conv[16:, :]], 0).astype(BF16)
    latent = nn(hidden[...], proj[...])
    once = latent - chosen[0].astype(F32)
    total = once + (once - chosen[1].astype(F32))
    latent_grad[...] = total.astype(BF16)
    flipped[...] = jnp.transpose(latent_grad[...].astype(F32)).astype(BF16)
    bit = info[0]
    at = correlate(flipped[...], (unfold, hidden), plan, 1 - bit, 1 - bit, send)
    code_rows = own.shape[0] - frames
    digits = [code_digits(codes[level:level + 1], dz, code_rows) for level in range(2)]
    own[0:frames, :] = jnp.where(bit == 1, once, latent).astype(BF16)
    own[frames:, :] = jnp.where(bit == 1, digits[1], digits[0])
    other = jnp.where(bit == 1, latent, once).astype(BF16)
    other_digits = jnp.where(bit == 1, digits[0], digits[1])
    for j in range(dz // LANES):
        send[at:at + frames, :] = other[:, j * LANES:(j + 1) * LANES]
        send[at + frames:at + frames + code_rows, :] = other_digits[:, j * LANES:(j + 1) * LANES]
        at += frames + code_rows


def rest_kernel(plan, info, flipped, unfold, hidden, latent_grad, proj, keep_a, keep_c, hidden_grad, extras, row):
    bit = info[0]
    correlate(flipped[...], (unfold,), plan[:1], bit, bit, keep_a)
    correlate(flipped[...], (hidden,), plan[1:], bit, bit, keep_c)
    back = nt(latent_grad[...], proj[...]).astype(BF16)
    hidden_grad[...] = back
    row[...] = back[0:16, :]
    stride = extras.shape[0] // 4
    extras[...] = jnp.zeros(extras.shape, F32)
    sums = jnp.sum(back.astype(F32), 0, keepdims=True)
    for digit, part in enumerate(digits_of(sums)):
        for j in range(sums.shape[1] // LANES):
            extras[digit * stride + j:digit * stride + j + 1, :] = part[:, j * LANES:(j + 1) * LANES]


def split_sum(halved, bit, got, at, kept, rows, send, to, keep):
    if halved:
        half = rows // 2
        away = pl.multiple_of((1 - bit) * half, 16)
        home = pl.multiple_of(bit * half, 16)
        send[to:to + half, :] = (kept[pl.ds(away, half), :] + got[pl.ds(at + away, half), :].astype(F32)).astype(BF16)
        keep[0:half, :] = kept[pl.ds(home, half), :] + got[pl.ds(at + home, half), :].astype(F32)
        return half
    total = (kept[0:rows, :] + got[at:at + rows, :].astype(F32)).astype(BF16)
    send[to:to + rows, :] = total
    keep[0:rows, :] = total.astype(F32)
    return rows


def add_digits(mine, theirs):
    stride = mine.shape[0] // 4
    return ((mine[0:stride] + mine[stride:2 * stride]) + mine[2 * stride:3 * stride]) + (
        (theirs[0:stride] + theirs[stride:2 * stride]) + theirs[2 * stride:3 * stride])


def digit_block(value):
    return jnp.concatenate(list(digits_of(value)) + [jnp.zeros_like(value)], 0)


def first_step_kernel(halves, place, info, got, kept_a, kept_c, extras, send, keep_a, keep_c):
    (rows_a, halved_a), (rows_c, halved_c) = halves
    to = split_sum(halved_a, info[place], got, 0, kept_a, rows_a, send, 0, keep_a)
    gone = split_sum(halved_c, info[place], got, rows_a, kept_c, rows_c, send, to, keep_c)
    send[to + gone:, :] = extras[...].astype(BF16)
    keep_c[gone:, :] = extras[...]


def feat_kernel(info, grad, after, weight, out, wide, inter):
    frames, channels = grad.shape
    half = weight.shape[0] // 2
    wide[0:frames, :] = grad[...].astype(F32)
    wide[frames:, :] = jnp.broadcast_to(after[0:1, :].astype(F32), (8, channels))
    ahead = wide[pl.ds(1, frames), :].astype(BF16)
    for parity in range(2):
        rows = pl.ds(parity * (half // 2), half // 2)
        rows_after = pl.ds(half + parity * (half // 2), half // 2)
        both = nt(ahead, weight[rows, :]) + nt(grad[...], weight[rows_after, :])
        for j in range(channels // LANES):
            inter[j, pl.ds(parity, frames, stride=2), :] = both[:, j * LANES:(j + 1) * LANES]
    for j in range(channels // LANES):
        out[:, j * LANES:(j + 1) * LANES] = inter[j].astype(BF16)


def sums_kernel(first, frames, place, count, info, got, own, row, out):
    rows, dz = own.shape
    theirs = jnp.concatenate([got[first + j * rows:first + (j + 1) * rows, :] for j in range(dz // LANES)], 1)
    ones = jnp.ones((8, frames), BF16)
    parts = []
    for block in (own[...], theirs):
        parts.append((block[0:frames, :], codes_of(block[frames:, :], frames)))
    size = count + 16
    riding = [row[...].astype(F32)[0:1, :]]
    for top in range(0, out.shape[0], size):
        total = jnp.zeros((count, dz), F32)
        counts = jnp.zeros((8, count), F32)
        for values, codes in parts:
            matches = one_hot(codes, 0, info[place], count)
            total = total + nn(matches, values)
            counts = counts + nt(ones, matches)
        out[top:top + count, :] = total.astype(out.dtype)
        out[top + count:top + size, :] = count_rows(counts[0:1], dz, riding).astype(out.dtype)
        place += 1


def count_rows(count, width, riding=()):
    high = jnp.floor(count * (1.0 / 65536.0))
    rest = count - high * 65536.0
    middle = jnp.floor(rest * (1.0 / 256.0))
    low = rest - middle * 256.0
    block = jnp.concatenate([high, middle, low], 0)
    if count.shape[1] < width:
        block = jnp.concatenate([block, jnp.zeros((3, width - count.shape[1]), F32)], 1)
    parts = [block]
    for row in riding:
        parts += [row[:, at:at + width] for at in range(0, row.shape[1], width)]
    left = 16 - sum(part.shape[0] for part in parts)
    return jnp.concatenate(parts + [jnp.zeros((left, width), F32)] * (left > 0), 0)


def riding_row(block, index, parts):
    return jnp.concatenate([block[3 + index * parts + j:4 + index * parts + j, :] for j in range(parts)], 1)


def count_of(block, own):
    return (block[0:1] * 65536.0 + block[1:2] * 256.0 + block[2:3])[:, :own]


def sums_step_kernel(halved, place, row_step, row_place, info, got, kept, *refs):
    riding = ()
    if row_step is not None:
        known, refs = refs[0][...].astype(F32), refs[1:]
        after, refs = refs[-1], refs[:-1]
        parts = known.shape[1] // got.shape[1]
        block = got[row_place[0]:row_place[0] + 16, :].astype(F32)
        rows = [known[j:j + 1, :] for j in range(1 << row_step)]
        rows += [riding_row(block, j, parts) for j in range(1 << row_step)]
        if halved:
            riding = rows
            total = rows + [jnp.zeros((16 - len(rows), known.shape[1]), F32)]
            after[...] = jnp.concatenate(total, 0).astype(BF16)
        else:
            wide = jnp.zeros(after.shape, F32)
            for j in range(1, len(rows)):
                wide = jnp.where(info[row_place[1]] == j, jnp.broadcast_to(rows[j], after.shape), wide)
            after[...] = wide.astype(BF16)
    send, keep = refs
    dz = got.shape[1]
    bit = info[place]
    half = kept.shape[0] // 2 if halved else 0
    outs = [(send, (1 - bit) * half), (keep, bit * half)] if halved else [(send, 0)]
    count = row_place[0]
    size = count + 16
    for out, start in outs:
        for top in range(0, keep.shape[0], size):
            here = top + pl.multiple_of(start, 16) if halved else top
            sums = pl.ds(here, count)
            tail = pl.ds(here + count, 16)
            value = kept[sums, :].astype(F32) + got[sums, :].astype(F32)
            number = count_of(kept[tail, :].astype(F32), count) + count_of(got[tail, :].astype(F32), count)
            out[top:top + count, :] = value.astype(out.dtype)
            out[top + count:top + size, :] = count_rows(number, dz, riding).astype(out.dtype)
    if not halved:
        keep[...] = send[0:keep.shape[0], :].astype(F32)


def swap_halves(first, second, core):
    half = LANES // 2
    left = lax.broadcasted_iota(jnp.int32, first.shape, 1) < half
    turned_first, turned_second = pltpu.roll(first, half, 1), pltpu.roll(second, half, 1)
    swapped_first = jnp.where(left, first, turned_second)
    swapped_second = jnp.where(left, turned_first, second)
    return jnp.where(core == 1, swapped_first, first), jnp.where(core == 1, swapped_second, second)


def step_kernel(halves, place, mixed, info, got, kept_a, kept_c, send, keep_a, keep_c):
    (rows_a, halved_a), (rows_c, halved_c) = halves
    if mixed:
        to = rows_a // 2
        total = kept_a[0:rows_a, :] + got[0:rows_a, :].astype(F32)
        first, second = swap_halves(total[0:to, :], total[to:, :], info[0])
        low = info[place] == 0
        send[0:to, :] = jnp.where(low, second, first).astype(BF16)
        keep_a[...] = jnp.where(low, first, second)
    else:
        to = split_sum(halved_a, info[place], got, 0, kept_a, rows_a, send, 0, keep_a)
    gone = split_sum(halved_c, info[place], got, rows_a, kept_c, rows_c, send, to, keep_c)
    block = digit_block(add_digits(kept_c[rows_c:, :], got[rows_a + rows_c:, :].astype(F32)))
    send[to + gone:, :] = block.astype(BF16)
    keep_c[gone:, :] = block


def last_kernel(rows_a, rows, info, got, kept_a, kept_c, sums_got, sums_kept, corr, pieces, mine):
    corr[...] = kept_a[...] + got[0:rows_a, :].astype(F32)
    pieces[...] = (kept_c[0:rows, :] + got[rows_a:rows_a + rows, :].astype(F32)).astype(BF16)
    block = digit_block(add_digits(kept_c[rows:, :], got[rows_a + rows:, :].astype(F32)))
    mine[0:rows, :] = pieces[...]
    mine[rows:kept_c.shape[0], :] = block.astype(BF16)
    at = kept_c.shape[0]
    count = sums_kept.shape[0] - 16
    number = count_of(sums_kept[count:, :].astype(F32), count) + count_of(sums_got[count:, :].astype(F32), count)
    square = (count, count)
    same = lax.broadcasted_iota(jnp.int32, square, 0) == lax.broadcasted_iota(jnp.int32, square, 1)
    tall = jnp.sum(jnp.where(same, jnp.broadcast_to(number, square), 0.0), 1, keepdims=True)
    total = sums_kept[0:count, :].astype(F32) + sums_got[0:count, :].astype(F32)
    means = (total / jnp.maximum(tall, 1.0)).astype(BF16)
    digits = count_rows(number, means.shape[1]).astype(BF16)
    for j in range(means.shape[1] // LANES):
        mine[at:at + count, :] = means[:, j * LANES:(j + 1) * LANES]
        mine[at + count:at + count + 16, :] = digits[:, j * LANES:(j + 1) * LANES]
        at += count + 16


def conv_out_kernel(total_frames, place, info, corr, proj, out, wide):
    rows = out.shape[0]
    flipped = jnp.transpose(corr[...])
    high = flipped.astype(BF16)
    low = (flipped - high.astype(F32)).astype(BF16)
    wide[...] = (nt(high, proj[...]) + nt(low, proj[...])) * (1.0 / total_frames)
    start = info[place]
    if rows % 8 == 0:
        out[...] = wide[pl.ds(pl.multiple_of(start, 8), rows), :]
    else:
        taken = wide[0:rows, :]
        for other in range(rows, wide.shape[0], rows):
            taken = jnp.where(start == other, wide[other:other + rows, :], taken)
        out[...] = taken


def out_kernel(total_frames, use_scale, dz, place, inner, extra, info, mine, *refs):
    parts, (out, bias, means, usage) = refs[:-4], refs[-4:]
    theirs = parts[1]
    scale = 1.0 / total_frames
    top = inner * dz
    value = add_digits(mine[top:top + extra, :].astype(F32), theirs[top:top + extra, :].astype(F32)) * scale
    for j in range(bias.shape[1] // LANES):
        bias[:, j * LANES:(j + 1) * LANES] = value[j:j + 1, :]
    bit = info[0]
    count = means.shape[1]
    numbers = []
    for ref, level in ((mine, bit), (theirs, 1 - bit)):
        at = top + extra
        blocks = []
        for j in range(dz // LANES):
            blocks.append(ref[at:at + count + 16, :])
            at += count + 16
        whole = jnp.concatenate(blocks, 1)
        means[level] = whole[0:count, :]
        numbers.append(count_of(whole[count:, :].astype(F32), count) * use_scale)
    usage[0:1, :] = jnp.where(bit == 1, numbers[1], numbers[0])
    usage[1:2, :] = jnp.where(bit == 1, numbers[0], numbers[1])
    for j, ref in enumerate(parts):
        for k in range(inner):
            start = pl.multiple_of((info[place + j] + k) * LANES, LANES)
            turned = jnp.transpose(ref[k * dz:(k + 1) * dz, :])
            out[pl.ds(start, LANES), :] = turned.astype(F32) * scale


def shifted(block, axis, distance):
    devices = range(lax.axis_size(axis))
    route = [(i - distance, i) for i in devices if i - distance in devices]
    return lax.ppermute(block, axis, route)


def swapped(block, steps):
    tm = lax.axis_size("tm")

    def partner(device):
        axis, bit = steps[(device // tm) & 1]
        return device ^ ((1 << bit) * (tm if axis == "dp" else 1))

    route = [(device, partner(device)) for device in range(lax.axis_size("dp") * tm)]
    return lax.ppermute(block, ("dp", "tm"), route)


def crossed(block, steps):
    tm = lax.axis_size("tm")

    def partner(device):
        axis, bit = steps[(device // tm) & 1]
        return device ^ tm ^ ((1 << bit) * (tm if axis == "dp" else 1))

    route = [(device, partner(device)) for device in range(lax.axis_size("dp") * tm)]
    return lax.ppermute(block, ("dp", "tm"), route)


def shards(feats, codes, conv_weight, conv_bias, proj_weight, codebooks):
    dp, tm = lax.axis_size("dp"), lax.axis_size("tm")
    rows_in, channels = feats.shape
    frames = rows_in // 2
    levels, book_size, dz = codebooks.shape
    assert levels == 2
    width = conv_weight.shape[0]
    total_frames = frames * dp * tm
    per_shard = book_size // tm
    dp_bits, tm_bits = log2(dp), log2(tm)
    owner_rows = width // (dp * tm)

    assert dp_bits >= 3 and 1 <= tm_bits <= 2
    pieces_a, pieces_c = width // LANES, channels // LANES
    under = max(dp_bits + tm_bits - log2(pieces_a), 0)
    c_bits = 2
    assert pieces_c >= 4
    whole_bits = [b for b in range(1, dp_bits) if b + tm_bits < under]
    piece_bits = [b for b in range(1, dp_bits) if b + tm_bits >= under]
    paths = [[("dp", b) for b in bits] for bits in (whole_bits + piece_bits, whole_bits[::-1] + piece_bits[::-1])]
    mixed = under == 1 and tm_bits == 2
    turned = mixed or under == 0 or under >= tm_bits
    up = [("tm", b) for b in range(tm_bits)]
    paths[0] += up[::-1]
    paths[1] += up if turned else up[::-1]
    exchanges = list(zip([("dp", 0)] + paths[0], [("dp", 0)] + paths[1]))
    sums_up = [("dp", b) for b in range(1, dp_bits)]
    sums_exchanges = list(zip(up + sums_up, up[::-1] + sums_up[::-1]))

    def piece_bit(step):
        axis, b = step
        bit = b + (tm_bits if axis == "dp" else 0)
        return bit - under if bit >= under else None

    a_split = [piece_bit(steps[0]) is not None for steps in exchanges]
    c_split = [log2(pieces_c) - 1 - k if k < c_bits else None for k in range(len(exchanges))]

    def order_of(split, count):
        used = [b for b in split if b is not None]
        return used + [b for b in reversed(range(log2(count))) if b not in used]

    orders = [order_of([piece_bit(steps[core]) for steps in exchanges], pieces_a) for core in range(2)]
    order_c = order_of(c_split, pieces_c)
    plan = [(pieces_a, orders, a_split[0]), (pieces_c, [order_c, order_c], True)]
    now_a = pieces_a // 2 if plan[0][2] else pieces_a
    now_c = pieces_c // 2

    at_dp, at_tm = lax.axis_index("dp"), lax.axis_index("tm")
    core = at_dp & 1

    def on_core(values):
        return values[0] + core * (values[1] - values[0])

    def bit_at(step):
        axis, b = step
        return ((at_dp if axis == "dp" else at_tm) >> b) & 1

    bits = [on_core([bit_at(step) for step in steps]) for steps in exchanges]
    sums_bits = [on_core([bit_at(step) for step in steps]) for steps in sums_exchanges]
    shared = [bit_at(step) for step in exchanges[1]]
    mine_c, other_c = on_core(shared), on_core(shared[::-1])
    places = [2 * core + mine_c, 2 * (1 - core) + other_c, 2 * core + 1 - mine_c, 2 * (1 - core) + 1 - other_c]
    places = [place << (log2(pieces_c) - c_bits) for place in places]
    lists = []
    for way in ([b for _, b in up], [b for _, b in up[::-1]]):
        lists.append([sum(((position >> (tm_bits - 1 - j)) & 1) << b for j, b in enumerate(way)) for position in range(tm)])
    first_bit = on_core([0, tm_bits - 1])
    lead = (at_tm >> first_bit) & 1
    quarters = [on_core([lists[0][j], lists[1][j]]) for j in range(tm // 2)]
    send_codes = [(q + ((1 - lead) << first_bit)) * per_shard for q in quarters]
    keep_codes = [(q + (lead << first_bit)) * per_shard for q in quarters]
    differ = at_tm ^ (at_tm + 1)
    ways = [sum(((differ >> b) & 1) << j for j, b in enumerate(way)) for way in (
        list(range(tm_bits)), list(reversed(range(tm_bits))))]
    row_code = jnp.where(at_tm + 1 < tm, on_core(ways), 0)
    if turned and not mixed:
        start = ((at_dp * tm + at_tm) * owner_rows) & (LANES - 1)
    else:
        start = on_core([(at_dp * tm + at_tm) * owner_rows, (at_tm >> 1) * owner_rows if mixed else (
            at_dp * tm + at_tm) * owner_rows]) & (LANES - 1)
    at_start = len(bits)
    at_codes = at_start + 1
    at_pieces = at_codes + tm
    at_sums = at_pieces + len(places)
    at_row = at_sums + len(sums_bits)
    info = jnp.stack(bits + [start] + send_codes + keep_codes + places + sums_bits + [row_code]).astype(jnp.int32)

    halo = shifted(
        call(halo_kernel, shape((16, channels), BF16), [info, feats], flops=10 ** 11), "tm", 1)
    weight, proj, codes = conv_weight, proj_weight, codes[0]
    unfold, conv, chosen = call(
        local_kernel,
        [shape((frames, width), BF16), shape((frames, channels), F32), shape((levels, frames, dz), BF16)],
        [info, feats, weight, conv_bias[None, :], codes, codebooks],
        scratch=[VMEM((channels // LANES, rows_in + 8, LANES), F32)],
    )

    extra = 4 * (-(-channels // LANES // 8) * 8)
    code_rows = -(-(2 * -(-frames // dz)) // 16) * 16
    corr_rows = (now_a + now_c) * dz
    rows_b = frames + code_rows
    unfold, hidden, latent_grad, flipped, own, send = call(
        functools.partial(forward_kernel, plan),
        [shape((frames, width), BF16), shape((frames, channels), BF16), shape((frames, dz), BF16),
         shape((dz, frames), BF16), shape((rows_b, dz), BF16),
         shape((corr_rows + rows_b * (dz // LANES), LANES), BF16)],
        [info, halo, unfold, conv, chosen, weight, proj, codes],
        aliases={2: 0},
    )
    got = swapped(send, exchanges[0])
    keep_a, keep_c, hidden_grad, extras, row = call(
        functools.partial(rest_kernel, plan),
        [shape((now_a * dz, LANES), F32), shape((now_c * dz, LANES), F32), shape((frames, channels), BF16),
         shape((extra, LANES), F32), shape((16, channels), BF16)],
        [info, flipped, unfold, hidden, latent_grad, proj],
        after=[send],
    )

    def halves_at(k):
        nonlocal now_a, now_c
        halves = [(now_a * dz, a_split[k]), (now_c * dz, c_split[k] is not None)]
        now_a = now_a // 2 if halves[0][1] else now_a
        now_c = now_c // 2 if halves[1][1] else now_c
        return halves, now_a * dz, now_c * dz + extra

    halves, rows_a, rows_c = halves_at(1)
    send, keep_a, keep_c = call(
        functools.partial(first_step_kernel, halves, 1),
        [shape((rows_a + rows_c, LANES), BF16), shape((rows_a, LANES), F32), shape((rows_c, LANES), F32)],
        [info, got, keep_a, keep_c, extras])
    size = per_shard + 16
    sums_rows = size * (tm // 2)
    sums_send = call(
        functools.partial(sums_kernel, corr_rows, frames, at_codes, per_shard),
        shape((sums_rows, dz), BF16),
        [info, got, own, row],
        after=[send])
    sums_keep = call(
        functools.partial(sums_kernel, corr_rows, frames, at_codes + tm // 2, per_shard),
        shape((sums_rows, dz), F32),
        [info, got, own, row],
        after=[sums_send])
    sums_got = swapped(sums_send, sums_exchanges[0])
    got = swapped(send, exchanges[1])
    known = row
    ordered = [sums_keep]
    for k in range(2, len(exchanges)):
        halves, rows_a, rows_c = halves_at(k)
        send, keep_a, keep_c = call(
            functools.partial(step_kernel, halves, k, mixed and k == dp_bits),
            [shape((rows_a + rows_c, LANES), BF16), shape((rows_a, LANES), F32), shape((rows_c, LANES), F32)],
            [info, got, keep_a, keep_c],
            after=ordered)
        got = swapped(send, exchanges[k])
        halved = sums_exchanges[k - 1][0][0] == "tm"
        sums_rows = sums_rows // 2 if halved else sums_rows
        row_step = k - 2 if k - 2 < tm_bits else None
        outs = call(
            functools.partial(sums_step_kernel, halved, at_sums + k - 1, row_step, (per_shard, at_row)),
            [shape((sums_rows, dz), BF16), shape((sums_rows, dz), F32)]
            + [shape((16, channels), BF16)] * (row_step is not None),
            [info, sums_got, sums_keep] + [known] * (row_step is not None),
            after=[send])
        sums_send, sums_keep = outs[:2]
        known = outs[2] if row_step is not None else known
        sums_got = swapped(sums_send, sums_exchanges[k - 1])
        ordered = [sums_send]
        if k == tm_bits + 1:
            feat_grad, *ordered = call(
                feat_kernel,
                shape((rows_in, channels), BF16),
                [info, hidden_grad, known, weight],
                after=[sums_send],
                token=True,
                scratch=[VMEM((frames + 8, channels), F32), VMEM((channels // LANES, rows_in, LANES), F32)],
            )
    assert now_a == 1 and sums_rows == size

    corr, piece, mine = call(
        functools.partial(last_kernel, rows_a, rows_c - extra),
        [shape((rows_a, LANES), F32), shape((rows_c - extra, LANES), BF16),
         shape((rows_c + size * (dz // LANES), LANES), BF16)],
        [info, got, keep_a, keep_c, sums_got, sums_keep],
        after=ordered)
    parts = [piece, swapped(mine, exchanges[0]), swapped(piece, exchanges[1]), crossed(piece, exchanges[1])]
    conv_grad, last = call(
        functools.partial(conv_out_kernel, total_frames, at_start),
        shape((owner_rows, channels), F32),
        [info, corr, proj],
        after=[piece],
        token=True,
        scratch=[VMEM((LANES, channels), F32)],
    )
    proj_grad, bias_grad, code_means, code_usage = call(
        functools.partial(out_kernel, total_frames, book_size / total_frames, dz, at_pieces, now_c, extra),
        [shape((channels, dz), F32), shape((1, channels), F32), shape((levels, per_shard, dz), BF16),
         shape((levels, per_shard), F32)],
        [info, mine] + parts,
        after=[last],
    )
    return feat_grad, conv_grad, bias_grad[0], proj_grad, code_means, code_usage


def solution(mesh):
    placed = (P(("dp", "tm"), None), P("dp", None, "tm"), P(), P(), P(), P())
    return jax.shard_map(
        shards,
        mesh=mesh,
        in_specs=placed,
        out_specs=(
            P(("dp", "tm"), None),
            P(("dp", "tm"), None),
            P(),
            P(),
            P(None, "tm", None),
            P(None, "tm"),
        ),
        check_vma=False,
    )
```

```python
import functools

import jax
import jax.numpy as jnp
from jax import lax
from jax.experimental import pallas as pl
from jax.experimental.pallas import tpu as pltpu
from jax.sharding import PartitionSpec as P

BF16 = jnp.bfloat16
F32 = jnp.float32
LANES = 128
VMEM_LIMIT = 16 * 1024 * 1024


def log2(value):
    assert value & (value - 1) == 0
    return value.bit_length() - 1


def nn(a, b):
    return lax.dot_general(a, b, (((1,), (0,)), ((), ())), preferred_element_type=F32)


def nt(a, b):
    return lax.dot_general(a, b, (((1,), (1,)), ((), ())), preferred_element_type=F32)


VMEM = pltpu.VMEM


def call(body, out_shape, args, after=(), scratch=(), aliases=None, token=False, flops=0):
    count = len(args)
    many = isinstance(out_shape, (list, tuple))
    shapes = list(out_shape) if many else [out_shape]

    def kernel(*refs):
        ends = count + len(after)
        if token:
            refs[ends + len(shapes)][...] = jnp.zeros((8, LANES), F32)
            refs = refs[:ends + len(shapes)] + refs[ends + len(shapes) + 1:]
        body(*refs[:count], *refs[ends:])

    specs = [pl.BlockSpec(memory_space=pltpu.SMEM)]
    specs += [pl.BlockSpec(memory_space=VMEM)] * (count - 1)
    specs += [pl.BlockSpec(memory_space=pl.ANY)] * len(after)
    shown = shapes + [shape((8, LANES), F32)] * token
    outs = pl.pallas_call(
        kernel,
        out_shape=shown,
        in_specs=specs,
        out_specs=[pl.BlockSpec(memory_space=VMEM)] * len(shown),
        scratch_shapes=list(scratch),
        input_output_aliases=aliases or {},
        compiler_params=pltpu.CompilerParams(vmem_limit_bytes=VMEM_LIMIT),
        cost_estimate=pl.CostEstimate(flops=flops, bytes_accessed=0, transcendentals=0),
    )(*args, *after)
    return outs if len(shown) > 1 else outs[0]


def shape(dims, dtype):
    return jax.ShapeDtypeStruct(dims, dtype)


def digits_of(value):
    high = value.astype(BF16).astype(F32)
    rest = value - high
    middle = rest.astype(BF16).astype(F32)
    low = (rest - middle).astype(BF16).astype(F32)
    return high, middle, low


def one_hot(codes, axis_codes, first, count):
    frames = codes.shape[1 - axis_codes]
    dims = (count, frames) if axis_codes == 0 else (frames, count)
    places = lax.broadcasted_iota(jnp.int32, dims, axis_codes) + first
    return jnp.where(codes == places, 1.0, 0.0).astype(BF16)


def halo_kernel(info, feats, out):
    out[...] = feats[feats.shape[0] - out.shape[0]:, :]


def local_kernel(info, feats, weight, bias, codes, books, unfold, conv, chosen, wide):
    rows, channels = feats.shape
    frames = rows // 2
    for j in range(channels // LANES):
        wide[j, 0:8, :] = jnp.zeros((8, LANES), F32)
        wide[j, 8:, :] = feats[:, j * LANES:(j + 1) * LANES].astype(F32)
        for tap in range(4):
            start = tap * channels + j * LANES
            unfold[:, start:start + LANES] = wide[j, pl.ds(6 + tap, frames, stride=2), :].astype(BF16)
    conv[...] = nn(unfold[...], weight[...]) + bias[...]
    levels = books.shape[0]
    padded = jnp.concatenate([codes[...].astype(F32), jnp.zeros((8 - levels, frames), F32)], 0)
    tall = jnp.transpose(padded).astype(jnp.int32)
    for level in range(levels):
        matches = one_hot(tall[:, level:level + 1], 1, 0, books.shape[1])
        chosen[level] = nn(matches, books[level]).astype(BF16)


def walk(orders, halved, count):
    start = 1 if halved else 0
    shown = count // 2 if halved else count
    bits = log2(shown)
    step = 2 if shown > 1 and all(order[-1] == 0 for order in orders) else 1
    for position in range(0, shown, step):
        yield position, [
            sum(((position >> (bits - 1 - k)) & 1) << bit for k, bit in enumerate(order[start:])) for order in orders
        ], step


def correlate(flipped, sources, plan, core, bit, out):
    dz = flipped.shape[0]
    at = 0
    for source, (count, orders, halved) in zip(sources, plan):
        for position, pieces, step in walk(orders, halved, count):
            column = pieces[0] + core * (pieces[1] - pieces[0])
            if halved:
                column = column + (bit << orders[0][0])
            column = pl.multiple_of(column * LANES, LANES)
            product = nn(flipped, source[:, pl.ds(column, step * LANES)])
            for j in range(step):
                top = (at + position + j) * dz
                out[top:top + dz, :] = product[:, j * LANES:(j + 1) * LANES].astype(out.dtype)
        at += count // 2 if halved else count
    return at * dz


def code_digits(codes, dz, rows):
    parts = []
    for part in (codes >> 8, codes & 255):
        for start in range(0, codes.shape[1], dz):
            piece = part[:, start:start + dz].astype(F32)
            if piece.shape[1] < dz:
                piece = jnp.concatenate([piece, jnp.zeros((1, dz - piece.shape[1]), F32)], 1)
            parts.append(piece)
    parts.append(jnp.zeros((rows - len(parts), dz), F32))
    return jnp.concatenate(parts, 0).astype(BF16)


def codes_of(block, frames):
    dz = block.shape[1]
    per = -(-frames // dz)
    digits = block[...].astype(F32)
    parts = [jnp.concatenate([digits[k * per + j:k * per + j + 1, :] for j in range(per)], 1)[:, :frames]
             for k in range(2)]
    return (parts[0] * 256.0 + parts[1]).astype(jnp.int32)


def forward_kernel(plan, info, halo, unfold_in, conv, chosen, weight, proj, codes,
                   unfold, hidden, latent_grad, flipped, own, send):
    frames, width = unfold.shape
    half = width // 2
    dz = proj.shape[1]
    row = lax.broadcasted_iota(jnp.int32, (16, half), 0)
    last = halo[...].astype(F32)
    left = jnp.concatenate([last[14:15, :], last[15:16, :]], 1)
    head = jnp.where(row == 0, jnp.broadcast_to(left, (16, half)), 0.0)
    unfold[0:16, 0:half] = (unfold_in[0:16, 0:half].astype(F32) + head).astype(BF16)
    fix = nn(head.astype(BF16), weight[0:half, :])
    hidden[...] = jnp.concatenate([conv[0:16, :] + fix, conv[16:, :]], 0).astype(BF16)
    latent = nn(hidden[...], proj[...])
    once = latent - chosen[0].astype(F32)
    total = once + (once - chosen[1].astype(F32))
    latent_grad[...] = total.astype(BF16)
    flipped[...] = jnp.transpose(latent_grad[...].astype(F32)).astype(BF16)
    bit = info[0]
    at = correlate(flipped[...], (unfold, hidden), plan, 1 - bit, 1 - bit, send)
    code_rows = own.shape[0] - frames
    digits = [code_digits(codes[level:level + 1], dz, code_rows) for level in range(2)]
    own[0:frames, :] = jnp.where(bit == 1, once, latent).astype(BF16)
    own[frames:, :] = jnp.where(bit == 1, digits[1], digits[0])
    other = jnp.where(bit == 1, latent, once).astype(BF16)
    other_digits = jnp.where(bit == 1, digits[0], digits[1])
    for j in range(dz // LANES):
        send[at:at + frames, :] = other[:, j * LANES:(j + 1) * LANES]
        send[at + frames:at + frames + code_rows, :] = other_digits[:, j * LANES:(j + 1) * LANES]
        at += frames + code_rows


def rest_kernel(plan, info, flipped, unfold, hidden, latent_grad, proj, keep_a, keep_c, hidden_grad, extras, row):
    bit = info[0]
    correlate(flipped[...], (unfold,), plan[:1], bit, bit, keep_a)
    correlate(flipped[...], (hidden,), plan[1:], bit, bit, keep_c)
    back = nt(latent_grad[...], proj[...]).astype(BF16)
    hidden_grad[...] = back
    row[...] = back[0:16, :]
    stride = extras.shape[0] // 4
    extras[...] = jnp.zeros(extras.shape, F32)
    sums = jnp.sum(back.astype(F32), 0, keepdims=True)
    for digit, part in enumerate(digits_of(sums)):
        for j in range(sums.shape[1] // LANES):
            extras[digit * stride + j:digit * stride + j + 1, :] = part[:, j * LANES:(j + 1) * LANES]


def split_sum(halved, bit, got, at, kept, rows, send, to, keep):
    if halved:
        half = rows // 2
        away = pl.multiple_of((1 - bit) * half, 16)
        home = pl.multiple_of(bit * half, 16)
        send[to:to + half, :] = (kept[pl.ds(away, half), :] + got[pl.ds(at + away, half), :].astype(F32)).astype(BF16)
        keep[0:half, :] = kept[pl.ds(home, half), :] + got[pl.ds(at + home, half), :].astype(F32)
        return half
    total = (kept[0:rows, :] + got[at:at + rows, :].astype(F32)).astype(BF16)
    send[to:to + rows, :] = total
    keep[0:rows, :] = total.astype(F32)
    return rows


def add_digits(mine, theirs):
    stride = mine.shape[0] // 4
    return ((mine[0:stride] + mine[stride:2 * stride]) + mine[2 * stride:3 * stride]) + (
        (theirs[0:stride] + theirs[stride:2 * stride]) + theirs[2 * stride:3 * stride])


def digit_block(value):
    return jnp.concatenate(list(digits_of(value)) + [jnp.zeros_like(value)], 0)


def first_step_kernel(halves, place, info, got, kept_a, kept_c, extras, send, keep_a, keep_c):
    (rows_a, halved_a), (rows_c, halved_c) = halves
    to = split_sum(halved_a, info[place], got, 0, kept_a, rows_a, send, 0, keep_a)
    gone = split_sum(halved_c, info[place], got, rows_a, kept_c, rows_c, send, to, keep_c)
    send[to + gone:, :] = extras[...].astype(BF16)
    keep_c[gone:, :] = extras[...]


def feat_kernel(info, grad, after, weight, out, wide, inter):
    frames, channels = grad.shape
    half = weight.shape[0] // 2
    wide[0:frames, :] = grad[...].astype(F32)
    wide[frames:, :] = jnp.broadcast_to(after[0:1, :].astype(F32), (8, channels))
    ahead = wide[pl.ds(1, frames), :].astype(BF16)
    for parity in range(2):
        rows = pl.ds(parity * (half // 2), half // 2)
        rows_after = pl.ds(half + parity * (half // 2), half // 2)
        both = nt(ahead, weight[rows, :]) + nt(grad[...], weight[rows_after, :])
        for j in range(channels // LANES):
            inter[j, pl.ds(parity, frames, stride=2), :] = both[:, j * LANES:(j + 1) * LANES]
    for j in range(channels // LANES):
        out[:, j * LANES:(j + 1) * LANES] = inter[j].astype(BF16)


def sums_kernel(first, frames, place, count, info, got, own, row, out):
    rows, dz = own.shape
    theirs = jnp.concatenate([got[first + j * rows:first + (j + 1) * rows, :] for j in range(dz // LANES)], 1)
    ones = jnp.ones((8, frames), BF16)
    parts = []
    for block in (own[...], theirs):
        parts.append((block[0:frames, :], codes_of(block[frames:, :], frames)))
    size = count + 16
    riding = [row[...].astype(F32)[0:1, :]]
    for top in range(0, out.shape[0], size):
        total = jnp.zeros((count, dz), F32)
        counts = jnp.zeros((8, count), F32)
        for values, codes in parts:
            matches = one_hot(codes, 0, info[place], count)
            total = total + nn(matches, values)
            counts = counts + nt(ones, matches)
        out[top:top + count, :] = total.astype(out.dtype)
        out[top + count:top + size, :] = count_rows(counts[0:1], dz, riding).astype(out.dtype)
        place += 1


def count_rows(count, width, riding=()):
    high = jnp.floor(count * (1.0 / 65536.0))
    rest = count - high * 65536.0
    middle = jnp.floor(rest * (1.0 / 256.0))
    low = rest - middle * 256.0
    block = jnp.concatenate([high, middle, low], 0)
    if count.shape[1] < width:
        block = jnp.concatenate([block, jnp.zeros((3, width - count.shape[1]), F32)], 1)
    parts = [block]
    for row in riding:
        parts += [row[:, at:at + width] for at in range(0, row.shape[1], width)]
    left = 16 - sum(part.shape[0] for part in parts)
    return jnp.concatenate(parts + [jnp.zeros((left, width), F32)] * (left > 0), 0)


def riding_row(block, index, parts):
    return jnp.concatenate([block[3 + index * parts + j:4 + index * parts + j, :] for j in range(parts)], 1)


def count_of(block, own):
    return (block[0:1] * 65536.0 + block[1:2] * 256.0 + block[2:3])[:, :own]


def sums_step_kernel(halved, place, row_step, row_place, info, got, kept, *refs):
    riding = ()
    if row_step is not None:
        known, refs = refs[0][...].astype(F32), refs[1:]
        after, refs = refs[-1], refs[:-1]
        parts = known.shape[1] // got.shape[1]
        block = got[row_place[0]:row_place[0] + 16, :].astype(F32)
        rows = [known[j:j + 1, :] for j in range(1 << row_step)]
        rows += [riding_row(block, j, parts) for j in range(1 << row_step)]
        if halved:
            riding = rows
            total = rows + [jnp.zeros((16 - len(rows), known.shape[1]), F32)]
            after[...] = jnp.concatenate(total, 0).astype(BF16)
        else:
            wide = jnp.zeros(after.shape, F32)
            for j in range(1, len(rows)):
                wide = jnp.where(info[row_place[1]] == j, jnp.broadcast_to(rows[j], after.shape), wide)
            after[...] = wide.astype(BF16)
    send, keep = refs
    dz = got.shape[1]
    bit = info[place]
    half = kept.shape[0] // 2 if halved else 0
    outs = [(send, (1 - bit) * half), (keep, bit * half)] if halved else [(send, 0)]
    count = row_place[0]
    size = count + 16
    for out, start in outs:
        for top in range(0, keep.shape[0], size):
            here = top + pl.multiple_of(start, 16) if halved else top
            sums = pl.ds(here, count)
            tail = pl.ds(here + count, 16)
            value = kept[sums, :].astype(F32) + got[sums, :].astype(F32)
            number = count_of(kept[tail, :].astype(F32), count) + count_of(got[tail, :].astype(F32), count)
            out[top:top + count, :] = value.astype(out.dtype)
            out[top + count:top + size, :] = count_rows(number, dz, riding).astype(out.dtype)
    if not halved:
        keep[...] = send[0:keep.shape[0], :].astype(F32)


def swap_halves(first, second, core):
    half = LANES // 2
    left = lax.broadcasted_iota(jnp.int32, first.shape, 1) < half
    turned_first, turned_second = pltpu.roll(first, half, 1), pltpu.roll(second, half, 1)
    swapped_first = jnp.where(left, first, turned_second)
    swapped_second = jnp.where(left, turned_first, second)
    return jnp.where(core == 1, swapped_first, first), jnp.where(core == 1, swapped_second, second)


def step_kernel(halves, place, mixed, info, got, kept_a, kept_c, send, keep_a, keep_c):
    (rows_a, halved_a), (rows_c, halved_c) = halves
    if mixed:
        to = rows_a // 2
        total = kept_a[0:rows_a, :] + got[0:rows_a, :].astype(F32)
        first, second = swap_halves(total[0:to, :], total[to:, :], info[0])
        low = info[place] == 0
        send[0:to, :] = jnp.where(low, second, first).astype(BF16)
        keep_a[...] = jnp.where(low, first, second)
    else:
        to = split_sum(halved_a, info[place], got, 0, kept_a, rows_a, send, 0, keep_a)
    gone = split_sum(halved_c, info[place], got, rows_a, kept_c, rows_c, send, to, keep_c)
    block = digit_block(add_digits(kept_c[rows_c:, :], got[rows_a + rows_c:, :].astype(F32)))
    keep_c[gone:, :] = block
    to += gone
    send[to:to + block.shape[0], :] = block.astype(BF16)
    to += block.shape[0]
    if to < send.shape[0]:
        send[to:, :] = jnp.zeros((send.shape[0] - to, LANES), BF16)


def last_kernel(rows_a, rows, info, got, kept_a, kept_c, sums_got, sums_kept, corr, pieces, mine):
    corr[...] = kept_a[...] + got[0:rows_a, :].astype(F32)
    pieces[...] = (kept_c[0:rows, :] + got[rows_a:rows_a + rows, :].astype(F32)).astype(BF16)
    block = digit_block(add_digits(kept_c[rows:, :], got[rows_a + rows:rows_a + kept_c.shape[0], :].astype(F32)))
    mine[0:rows, :] = pieces[...]
    mine[rows:kept_c.shape[0], :] = block.astype(BF16)
    at = kept_c.shape[0]
    count = sums_kept.shape[0] - 16
    number = count_of(sums_kept[count:, :].astype(F32), count) + count_of(sums_got[count:, :].astype(F32), count)
    square = (count, count)
    same = lax.broadcasted_iota(jnp.int32, square, 0) == lax.broadcasted_iota(jnp.int32, square, 1)
    tall = jnp.sum(jnp.where(same, jnp.broadcast_to(number, square), 0.0), 1, keepdims=True)
    total = sums_kept[0:count, :].astype(F32) + sums_got[0:count, :].astype(F32)
    means = (total / jnp.maximum(tall, 1.0)).astype(BF16)
    digits = count_rows(number, means.shape[1]).astype(BF16)
    for j in range(means.shape[1] // LANES):
        mine[at:at + count, :] = means[:, j * LANES:(j + 1) * LANES]
        mine[at + count:at + count + 16, :] = digits[:, j * LANES:(j + 1) * LANES]
        at += count + 16


def conv_out_kernel(total_frames, place, info, corr, proj, out, wide):
    rows = out.shape[0]
    flipped = jnp.transpose(corr[...])
    high = flipped.astype(BF16)
    low = (flipped - high.astype(F32)).astype(BF16)
    wide[...] = (nt(high, proj[...]) + nt(low, proj[...])) * (1.0 / total_frames)
    start = info[place]
    if rows % 8 == 0:
        out[...] = wide[pl.ds(pl.multiple_of(start, 8), rows), :]
    else:
        taken = wide[0:rows, :]
        for other in range(rows, wide.shape[0], rows):
            taken = jnp.where(start == other, wide[other:other + rows, :], taken)
        out[...] = taken


def out_kernel(total_frames, use_scale, dz, place, inner, extra, info, mine, *refs):
    parts, (out, bias, means, usage) = refs[:-4], refs[-4:]
    theirs = parts[1]
    scale = 1.0 / total_frames
    top = inner * dz
    value = add_digits(mine[top:top + extra, :].astype(F32), theirs[top:top + extra, :].astype(F32)) * scale
    for j in range(bias.shape[1] // LANES):
        bias[:, j * LANES:(j + 1) * LANES] = value[j:j + 1, :]
    bit = info[0]
    count = means.shape[1]
    numbers = []
    for ref, level in ((mine, bit), (theirs, 1 - bit)):
        at = top + extra
        blocks = []
        for j in range(dz // LANES):
            blocks.append(ref[at:at + count + 16, :])
            at += count + 16
        whole = jnp.concatenate(blocks, 1)
        means[level] = whole[0:count, :]
        numbers.append(count_of(whole[count:, :].astype(F32), count) * use_scale)
    usage[0:1, :] = jnp.where(bit == 1, numbers[1], numbers[0])
    usage[1:2, :] = jnp.where(bit == 1, numbers[0], numbers[1])
    for j, ref in enumerate(parts):
        for k in range(inner):
            start = pl.multiple_of((info[place + j] + k) * LANES, LANES)
            turned = jnp.transpose(ref[k * dz:(k + 1) * dz, :])
            out[pl.ds(start, LANES), :] = turned.astype(F32) * scale


def shifted(block, axis, distance):
    devices = range(lax.axis_size(axis))
    route = [(i - distance, i) for i in devices if i - distance in devices]
    return lax.ppermute(block, axis, route)


def swapped(block, steps):
    tm = lax.axis_size("tm")

    def partner(device):
        axis, bit = steps[(device // tm) & 1]
        return device ^ ((1 << bit) * (tm if axis == "dp" else 1))

    route = [(device, partner(device)) for device in range(lax.axis_size("dp") * tm)]
    return lax.ppermute(block, ("dp", "tm"), route)


def crossed(block, steps):
    tm = lax.axis_size("tm")

    def partner(device):
        axis, bit = steps[(device // tm) & 1]
        return device ^ tm ^ ((1 << bit) * (tm if axis == "dp" else 1))

    route = [(device, partner(device)) for device in range(lax.axis_size("dp") * tm)]
    return lax.ppermute(block, ("dp", "tm"), route)


def shards(feats, codes, conv_weight, conv_bias, proj_weight, codebooks):
    dp, tm = lax.axis_size("dp"), lax.axis_size("tm")
    rows_in, channels = feats.shape
    frames = rows_in // 2
    levels, book_size, dz = codebooks.shape
    assert levels == 2
    width = conv_weight.shape[0]
    total_frames = frames * dp * tm
    per_shard = book_size // tm
    dp_bits, tm_bits = log2(dp), log2(tm)
    owner_rows = width // (dp * tm)

    assert dp_bits >= 3 and 1 <= tm_bits <= 2
    pieces_a, pieces_c = width // LANES, channels // LANES
    under = max(dp_bits + tm_bits - log2(pieces_a), 0)
    c_bits = 2
    assert pieces_c >= 4
    whole_bits = [b for b in range(1, dp_bits) if b + tm_bits < under]
    piece_bits = [b for b in range(1, dp_bits) if b + tm_bits >= under]
    paths = [[("dp", b) for b in bits] for bits in (whole_bits + piece_bits, whole_bits[::-1] + piece_bits[::-1])]
    mixed = under == 1 and tm_bits == 2
    turned = mixed or under == 0 or under >= tm_bits
    up = [("tm", b) for b in range(tm_bits)]
    paths[0] += up[::-1]
    paths[1] += up if turned else up[::-1]
    exchanges = list(zip([("dp", 0)] + paths[0], [("dp", 0)] + paths[1]))
    sums_up = [("dp", b) for b in range(1, dp_bits)]
    sums_exchanges = list(zip(up + sums_up, up[::-1] + sums_up[::-1]))

    def piece_bit(step):
        axis, b = step
        bit = b + (tm_bits if axis == "dp" else 0)
        return bit - under if bit >= under else None

    a_split = [piece_bit(steps[0]) is not None for steps in exchanges]
    c_split = [log2(pieces_c) - 1 - k if k < c_bits else None for k in range(len(exchanges))]

    def order_of(split, count):
        used = [b for b in split if b is not None]
        return used + [b for b in reversed(range(log2(count))) if b not in used]

    orders = [order_of([piece_bit(steps[core]) for steps in exchanges], pieces_a) for core in range(2)]
    order_c = order_of(c_split, pieces_c)
    plan = [(pieces_a, orders, a_split[0]), (pieces_c, [order_c, order_c], True)]
    now_a = pieces_a // 2 if plan[0][2] else pieces_a
    now_c = pieces_c // 2

    at_dp, at_tm = lax.axis_index("dp"), lax.axis_index("tm")
    core = at_dp & 1

    def on_core(values):
        return values[0] + core * (values[1] - values[0])

    def bit_at(step):
        axis, b = step
        return ((at_dp if axis == "dp" else at_tm) >> b) & 1

    bits = [on_core([bit_at(step) for step in steps]) for steps in exchanges]
    sums_bits = [on_core([bit_at(step) for step in steps]) for steps in sums_exchanges]
    shared = [bit_at(step) for step in exchanges[1]]
    mine_c, other_c = on_core(shared), on_core(shared[::-1])
    places = [2 * core + mine_c, 2 * (1 - core) + other_c, 2 * core + 1 - mine_c, 2 * (1 - core) + 1 - other_c]
    places = [place << (log2(pieces_c) - c_bits) for place in places]
    lists = []
    for way in ([b for _, b in up], [b for _, b in up[::-1]]):
        lists.append([sum(((position >> (tm_bits - 1 - j)) & 1) << b for j, b in enumerate(way)) for position in range(tm)])
    first_bit = on_core([0, tm_bits - 1])
    lead = (at_tm >> first_bit) & 1
    quarters = [on_core([lists[0][j], lists[1][j]]) for j in range(tm // 2)]
    send_codes = [(q + ((1 - lead) << first_bit)) * per_shard for q in quarters]
    keep_codes = [(q + (lead << first_bit)) * per_shard for q in quarters]
    differ = at_tm ^ (at_tm + 1)
    ways = [sum(((differ >> b) & 1) << j for j, b in enumerate(way)) for way in (
        list(range(tm_bits)), list(reversed(range(tm_bits))))]
    row_code = jnp.where(at_tm + 1 < tm, on_core(ways), 0)
    if turned and not mixed:
        start = ((at_dp * tm + at_tm) * owner_rows) & (LANES - 1)
    else:
        start = on_core([(at_dp * tm + at_tm) * owner_rows, (at_tm >> 1) * owner_rows if mixed else (
            at_dp * tm + at_tm) * owner_rows]) & (LANES - 1)
    at_start = len(bits)
    at_codes = at_start + 1
    at_pieces = at_codes + tm
    at_sums = at_pieces + len(places)
    at_row = at_sums + len(sums_bits)
    info = jnp.stack(bits + [start] + send_codes + keep_codes + places + sums_bits + [row_code]).astype(jnp.int32)

    halo = shifted(
        call(halo_kernel, shape((16, channels), BF16), [info, feats], flops=10 ** 11), "tm", 1)
    weight, proj, codes = conv_weight, proj_weight, codes[0]
    unfold, conv, chosen = call(
        local_kernel,
        [shape((frames, width), BF16), shape((frames, channels), F32), shape((levels, frames, dz), BF16)],
        [info, feats, weight, conv_bias[None, :], codes, codebooks],
        scratch=[VMEM((channels // LANES, rows_in + 8, LANES), F32)],
    )

    extra = 4 * (-(-channels // LANES // 8) * 8)
    code_rows = -(-(2 * -(-frames // dz)) // 16) * 16
    corr_rows = (now_a + now_c) * dz
    rows_b = frames + code_rows
    unfold, hidden, latent_grad, flipped, own, send = call(
        functools.partial(forward_kernel, plan),
        [shape((frames, width), BF16), shape((frames, channels), BF16), shape((frames, dz), BF16),
         shape((dz, frames), BF16), shape((rows_b, dz), BF16),
         shape((corr_rows + rows_b * (dz // LANES), LANES), BF16)],
        [info, halo, unfold, conv, chosen, weight, proj, codes],
        aliases={2: 0},
    )
    got = swapped(send, exchanges[0])
    keep_a, keep_c, hidden_grad, extras, row = call(
        functools.partial(rest_kernel, plan),
        [shape((now_a * dz, LANES), F32), shape((now_c * dz, LANES), F32), shape((frames, channels), BF16),
         shape((extra, LANES), F32), shape((16, channels), BF16)],
        [info, flipped, unfold, hidden, latent_grad, proj],
        after=[send],
    )

    def halves_at(k):
        nonlocal now_a, now_c
        halves = [(now_a * dz, a_split[k]), (now_c * dz, c_split[k] is not None)]
        now_a = now_a // 2 if halves[0][1] else now_a
        now_c = now_c // 2 if halves[1][1] else now_c
        return halves, now_a * dz, now_c * dz + extra

    halves, rows_a, rows_c = halves_at(1)
    send, keep_a, keep_c = call(
        functools.partial(first_step_kernel, halves, 1),
        [shape((rows_a + rows_c, LANES), BF16), shape((rows_a, LANES), F32), shape((rows_c, LANES), F32)],
        [info, got, keep_a, keep_c, extras])
    size = per_shard + 16
    sums_rows = size * (tm // 2)
    sums_send = call(
        functools.partial(sums_kernel, corr_rows, frames, at_codes, per_shard),
        shape((sums_rows, dz), BF16),
        [info, got, own, row],
        after=[send])
    sums_keep = call(
        functools.partial(sums_kernel, corr_rows, frames, at_codes + tm // 2, per_shard),
        shape((sums_rows, dz), F32),
        [info, got, own, row],
        after=[sums_send])
    sums_got = swapped(sums_send, sums_exchanges[0])
    got = swapped(send, exchanges[1])
    known = row
    ordered = [sums_keep]
    for k in range(2, len(exchanges)):
        halves, rows_a, rows_c = halves_at(k)
        spare = 16 * (k == len(exchanges) - 1)
        send, keep_a, keep_c = call(
            functools.partial(step_kernel, halves, k, mixed and k == dp_bits),
            [shape((rows_a + rows_c + spare, LANES), BF16), shape((rows_a, LANES), F32), shape((rows_c, LANES), F32)],
            [info, got, keep_a, keep_c],
            after=ordered)
        got = swapped(send, exchanges[k])
        halved = sums_exchanges[k - 1][0][0] == "tm"
        sums_rows = sums_rows // 2 if halved else sums_rows
        row_step = k - 2 if k - 2 < tm_bits else None
        outs = call(
            functools.partial(sums_step_kernel, halved, at_sums + k - 1, row_step, (per_shard, at_row)),
            [shape((sums_rows, dz), BF16), shape((sums_rows, dz), F32)]
            + [shape((16, channels), BF16)] * (row_step is not None),
            [info, sums_got, sums_keep] + [known] * (row_step is not None),
            after=[send])
        sums_send, sums_keep = outs[:2]
        known = outs[2] if row_step is not None else known
        sums_got = swapped(sums_send, sums_exchanges[k - 1])
        ordered = [sums_send]
    assert now_a == 1 and sums_rows == size
    feat_grad, last = call(
        feat_kernel,
        shape((rows_in, channels), BF16),
        [info, hidden_grad, known, weight],
        after=[sums_send],
        token=True,
        scratch=[VMEM((frames + 8, channels), F32), VMEM((channels // LANES, rows_in, LANES), F32)],
    )

    corr, piece, mine = call(
        functools.partial(last_kernel, rows_a, rows_c - extra),
        [shape((rows_a, LANES), F32), shape((rows_c - extra, LANES), BF16),
         shape((rows_c + size * (dz // LANES), LANES), BF16)],
        [info, got, keep_a, keep_c, sums_got, sums_keep],
        after=[last])
    parts = [piece, swapped(mine, exchanges[0]), swapped(piece, exchanges[1]), crossed(piece, exchanges[1])]
    conv_grad, last = call(
        functools.partial(conv_out_kernel, total_frames, at_start),
        shape((owner_rows, channels), F32),
        [info, corr, proj],
        after=[piece],
        token=True,
        scratch=[VMEM((LANES, channels), F32)],
    )
    proj_grad, bias_grad, code_means, code_usage = call(
        functools.partial(out_kernel, total_frames, book_size / total_frames, dz, at_pieces, now_c, extra),
        [shape((channels, dz), F32), shape((1, channels), F32), shape((levels, per_shard, dz), BF16),
         shape((levels, per_shard), F32)],
        [info, mine] + parts,
        after=[last],
    )
    return feat_grad, conv_grad, bias_grad[0], proj_grad, code_means, code_usage


def solution(mesh):
    placed = (P(("dp", "tm"), None), P("dp", None, "tm"), P(), P(), P(), P())
    return jax.shard_map(
        shards,
        mesh=mesh,
        in_specs=placed,
        out_specs=(
            P(("dp", "tm"), None),
            P(("dp", "tm"), None),
            P(),
            P(),
            P(None, "tm", None),
            P(None, "tm"),
        ),
        check_vma=False,
    )
```

```python
import functools

import jax
import jax.numpy as jnp
from jax import lax
from jax.experimental import pallas as pl
from jax.experimental.pallas import tpu as pltpu
from jax.sharding import PartitionSpec as P

BF16 = jnp.bfloat16
F32 = jnp.float32
LANES = 128
VMEM_LIMIT = 16 * 1024 * 1024


def log2(value):
    assert value & (value - 1) == 0
    return value.bit_length() - 1


def nn(a, b):
    return lax.dot_general(a, b, (((1,), (0,)), ((), ())), preferred_element_type=F32)


def nt(a, b):
    return lax.dot_general(a, b, (((1,), (1,)), ((), ())), preferred_element_type=F32)


VMEM = pltpu.VMEM


def call(body, out_shape, args, after=(), scratch=(), aliases=None, token=False, flops=0):
    count = len(args)
    many = isinstance(out_shape, (list, tuple))
    shapes = list(out_shape) if many else [out_shape]

    def kernel(*refs):
        ends = count + len(after)
        if token:
            refs[ends + len(shapes)][...] = jnp.zeros((8, LANES), F32)
            refs = refs[:ends + len(shapes)] + refs[ends + len(shapes) + 1:]
        body(*refs[:count], *refs[ends:])

    specs = [pl.BlockSpec(memory_space=pltpu.SMEM)]
    specs += [pl.BlockSpec(memory_space=VMEM)] * (count - 1)
    specs += [pl.BlockSpec(memory_space=pl.ANY)] * len(after)
    shown = shapes + [shape((8, LANES), F32)] * token
    outs = pl.pallas_call(
        kernel,
        out_shape=shown,
        in_specs=specs,
        out_specs=[pl.BlockSpec(memory_space=VMEM)] * len(shown),
        scratch_shapes=list(scratch),
        input_output_aliases=aliases or {},
        compiler_params=pltpu.CompilerParams(vmem_limit_bytes=VMEM_LIMIT),
        cost_estimate=pl.CostEstimate(flops=flops, bytes_accessed=0, transcendentals=0),
    )(*args, *after)
    return outs if len(shown) > 1 else outs[0]


def shape(dims, dtype):
    return jax.ShapeDtypeStruct(dims, dtype)


def digits_of(value):
    high = value.astype(BF16).astype(F32)
    rest = value - high
    middle = rest.astype(BF16).astype(F32)
    low = (rest - middle).astype(BF16).astype(F32)
    return high, middle, low


def one_hot(codes, axis_codes, first, count):
    frames = codes.shape[1 - axis_codes]
    dims = (count, frames) if axis_codes == 0 else (frames, count)
    places = lax.broadcasted_iota(jnp.int32, dims, axis_codes) + first
    return jnp.where(codes == places, 1.0, 0.0).astype(BF16)


def halo_kernel(info, feats, out):
    out[...] = feats[feats.shape[0] - out.shape[0]:, :]


def local_kernel(info, feats, weight, bias, codes, books, unfold, conv, chosen, wide):
    rows, channels = feats.shape
    frames = rows // 2
    for j in range(channels // LANES):
        wide[j, 0:8, :] = jnp.zeros((8, LANES), F32)
        wide[j, 8:, :] = feats[:, j * LANES:(j + 1) * LANES].astype(F32)
        for tap in range(4):
            start = tap * channels + j * LANES
            unfold[:, start:start + LANES] = wide[j, pl.ds(6 + tap, frames, stride=2), :].astype(BF16)
    conv[...] = nn(unfold[...], weight[...]) + bias[...]
    levels = books.shape[0]
    padded = jnp.concatenate([codes[...].astype(F32), jnp.zeros((8 - levels, frames), F32)], 0)
    tall = jnp.transpose(padded).astype(jnp.int32)
    for level in range(levels):
        matches = one_hot(tall[:, level:level + 1], 1, 0, books.shape[1])
        chosen[level] = nn(matches, books[level]).astype(BF16)


def walk(orders, halved, count):
    start = 1 if halved else 0
    shown = count // 2 if halved else count
    bits = log2(shown)
    step = 2 if shown > 1 and all(order[-1] == 0 for order in orders) else 1
    for position in range(0, shown, step):
        yield position, [
            sum(((position >> (bits - 1 - k)) & 1) << bit for k, bit in enumerate(order[start:])) for order in orders
        ], step


def correlate(flipped, sources, plan, core, bit, out):
    dz = flipped.shape[0]
    at = 0
    for source, (count, orders, halved) in zip(sources, plan):
        for position, pieces, step in walk(orders, halved, count):
            column = pieces[0] + core * (pieces[1] - pieces[0])
            if halved:
                column = column + (bit << orders[0][0])
            column = pl.multiple_of(column * LANES, LANES)
            product = nn(flipped, source[:, pl.ds(column, step * LANES)])
            for j in range(step):
                top = (at + position + j) * dz
                out[top:top + dz, :] = product[:, j * LANES:(j + 1) * LANES].astype(out.dtype)
        at += count // 2 if halved else count
    return at * dz


def code_digits(codes, dz, rows):
    parts = []
    for part in (codes >> 8, codes & 255):
        for start in range(0, codes.shape[1], dz):
            piece = part[:, start:start + dz].astype(F32)
            if piece.shape[1] < dz:
                piece = jnp.concatenate([piece, jnp.zeros((1, dz - piece.shape[1]), F32)], 1)
            parts.append(piece)
    parts.append(jnp.zeros((rows - len(parts), dz), F32))
    return jnp.concatenate(parts, 0).astype(BF16)


def codes_of(block, frames):
    dz = block.shape[1]
    per = -(-frames // dz)
    digits = block[...].astype(F32)
    parts = [jnp.concatenate([digits[k * per + j:k * per + j + 1, :] for j in range(per)], 1)[:, :frames]
             for k in range(2)]
    return (parts[0] * 256.0 + parts[1]).astype(jnp.int32)


def forward_kernel(plan, info, halo, unfold_in, conv, chosen, weight, proj, codes,
                   unfold, hidden, latent_grad, flipped, own, send):
    frames, width = unfold.shape
    half = width // 2
    dz = proj.shape[1]
    row = lax.broadcasted_iota(jnp.int32, (16, half), 0)
    last = halo[...].astype(F32)
    left = jnp.concatenate([last[14:15, :], last[15:16, :]], 1)
    head = jnp.where(row == 0, jnp.broadcast_to(left, (16, half)), 0.0)
    unfold[0:16, 0:half] = (unfold_in[0:16, 0:half].astype(F32) + head).astype(BF16)
    fix = nn(head.astype(BF16), weight[0:half, :])
    hidden[...] = jnp.concatenate([conv[0:16, :] + fix, conv[16:, :]], 0).astype(BF16)
    latent = nn(hidden[...], proj[...])
    once = latent - chosen[0].astype(F32)
    total = once + (once - chosen[1].astype(F32))
    latent_grad[...] = total.astype(BF16)
    flipped[...] = jnp.transpose(latent_grad[...].astype(F32)).astype(BF16)
    bit = info[0]
    at = correlate(flipped[...], (unfold, hidden), plan, 1 - bit, 1 - bit, send)
    code_rows = own.shape[0] - frames
    digits = [code_digits(codes[level:level + 1], dz, code_rows) for level in range(2)]
    own[0:frames, :] = jnp.where(bit == 1, once, latent).astype(BF16)
    own[frames:, :] = jnp.where(bit == 1, digits[1], digits[0])
    other = jnp.where(bit == 1, latent, once).astype(BF16)
    other_digits = jnp.where(bit == 1, digits[0], digits[1])
    for j in range(dz // LANES):
        send[at:at + frames, :] = other[:, j * LANES:(j + 1) * LANES]
        send[at + frames:at + frames + code_rows, :] = other_digits[:, j * LANES:(j + 1) * LANES]
        at += frames + code_rows


def rest_kernel(plan, info, flipped, unfold, hidden, latent_grad, proj, keep_a, keep_c, hidden_grad, extras, row):
    bit = info[0]
    correlate(flipped[...], (unfold,), plan[:1], bit, bit, keep_a)
    correlate(flipped[...], (hidden,), plan[1:], bit, bit, keep_c)
    back = nt(latent_grad[...], proj[...]).astype(BF16)
    hidden_grad[...] = back
    row[...] = back[0:16, :]
    stride = extras.shape[0] // 4
    extras[...] = jnp.zeros(extras.shape, F32)
    sums = jnp.sum(back.astype(F32), 0, keepdims=True)
    for digit, part in enumerate(digits_of(sums)):
        for j in range(sums.shape[1] // LANES):
            extras[digit * stride + j:digit * stride + j + 1, :] = part[:, j * LANES:(j + 1) * LANES]


def split_sum(halved, bit, got, at, kept, rows, send, to, keep):
    if halved:
        half = rows // 2
        away = pl.multiple_of((1 - bit) * half, 16)
        home = pl.multiple_of(bit * half, 16)
        send[to:to + half, :] = (kept[pl.ds(away, half), :] + got[pl.ds(at + away, half), :].astype(F32)).astype(BF16)
        keep[0:half, :] = kept[pl.ds(home, half), :] + got[pl.ds(at + home, half), :].astype(F32)
        return half
    total = (kept[0:rows, :] + got[at:at + rows, :].astype(F32)).astype(BF16)
    send[to:to + rows, :] = total
    keep[0:rows, :] = total.astype(F32)
    return rows


def add_digits(mine, theirs):
    stride = mine.shape[0] // 4
    return ((mine[0:stride] + mine[stride:2 * stride]) + mine[2 * stride:3 * stride]) + (
        (theirs[0:stride] + theirs[stride:2 * stride]) + theirs[2 * stride:3 * stride])


def digit_block(value):
    return jnp.concatenate(list(digits_of(value)) + [jnp.zeros_like(value)], 0)


def first_step_kernel(halves, place, info, got, kept_a, kept_c, extras, send, keep_a, keep_c):
    (rows_a, halved_a), (rows_c, halved_c) = halves
    to = split_sum(halved_a, info[place], got, 0, kept_a, rows_a, send, 0, keep_a)
    gone = split_sum(halved_c, info[place], got, rows_a, kept_c, rows_c, send, to, keep_c)
    send[to + gone:, :] = extras[...].astype(BF16)
    keep_c[gone:, :] = extras[...]


def feat_kernel(info, grad, after, weight, out, wide, inter):
    frames, channels = grad.shape
    half = weight.shape[0] // 2
    wide[0:frames, :] = grad[...].astype(F32)
    wide[frames:, :] = jnp.broadcast_to(after[0:1, :].astype(F32), (8, channels))
    ahead = wide[pl.ds(1, frames), :].astype(BF16)
    for parity in range(2):
        rows = pl.ds(parity * (half // 2), half // 2)
        rows_after = pl.ds(half + parity * (half // 2), half // 2)
        both = nt(ahead, weight[rows, :]) + nt(grad[...], weight[rows_after, :])
        for j in range(channels // LANES):
            inter[j, pl.ds(parity, frames, stride=2), :] = both[:, j * LANES:(j + 1) * LANES]
    for j in range(channels // LANES):
        out[:, j * LANES:(j + 1) * LANES] = inter[j].astype(BF16)


def sums_kernel(first, frames, place, count, info, got, own, row, out):
    rows, dz = own.shape
    theirs = jnp.concatenate([got[first + j * rows:first + (j + 1) * rows, :] for j in range(dz // LANES)], 1)
    ones = jnp.ones((8, frames), BF16)
    parts = []
    for block in (own[...], theirs):
        parts.append((block[0:frames, :], codes_of(block[frames:, :], frames)))
    size = count + 16
    riding = [row[...].astype(F32)[0:1, :]]
    for top in range(0, out.shape[0], size):
        total = jnp.zeros((count, dz), F32)
        counts = jnp.zeros((8, count), F32)
        for values, codes in parts:
            matches = one_hot(codes, 0, info[place], count)
            total = total + nn(matches, values)
            counts = counts + nt(ones, matches)
        out[top:top + count, :] = total.astype(out.dtype)
        out[top + count:top + size, :] = count_rows(counts[0:1], dz, riding).astype(out.dtype)
        place += 1


def count_rows(count, width, riding=()):
    high = jnp.floor(count * (1.0 / 65536.0))
    rest = count - high * 65536.0
    middle = jnp.floor(rest * (1.0 / 256.0))
    low = rest - middle * 256.0
    block = jnp.concatenate([high, middle, low], 0)
    if count.shape[1] < width:
        block = jnp.concatenate([block, jnp.zeros((3, width - count.shape[1]), F32)], 1)
    parts = [block]
    for row in riding:
        parts += [row[:, at:at + width] for at in range(0, row.shape[1], width)]
    left = 16 - sum(part.shape[0] for part in parts)
    return jnp.concatenate(parts + [jnp.zeros((left, width), F32)] * (left > 0), 0)


def riding_row(block, index, parts):
    return jnp.concatenate([block[3 + index * parts + j:4 + index * parts + j, :] for j in range(parts)], 1)


def count_of(block, own):
    return (block[0:1] * 65536.0 + block[1:2] * 256.0 + block[2:3])[:, :own]


def sums_step_kernel(halved, place, row_step, row_place, info, got, kept, *refs):
    riding = ()
    if row_step is not None:
        known, refs = refs[0][...].astype(F32), refs[1:]
        after, refs = refs[-1], refs[:-1]
        parts = known.shape[1] // got.shape[1]
        block = got[row_place[0]:row_place[0] + 16, :].astype(F32)
        rows = [known[j:j + 1, :] for j in range(1 << row_step)]
        rows += [riding_row(block, j, parts) for j in range(1 << row_step)]
        if halved:
            riding = rows
            total = rows + [jnp.zeros((16 - len(rows), known.shape[1]), F32)]
            after[...] = jnp.concatenate(total, 0).astype(BF16)
        else:
            wide = jnp.zeros(after.shape, F32)
            for j in range(1, len(rows)):
                wide = jnp.where(info[row_place[1]] == j, jnp.broadcast_to(rows[j], after.shape), wide)
            after[...] = wide.astype(BF16)
    send, keep = refs
    dz = got.shape[1]
    bit = info[place]
    half = kept.shape[0] // 2 if halved else 0
    outs = [(send, (1 - bit) * half), (keep, bit * half)] if halved else [(send, 0)]
    count = row_place[0]
    size = count + 16
    for out, start in outs:
        for top in range(0, keep.shape[0], size):
            here = top + pl.multiple_of(start, 16) if halved else top
            sums = pl.ds(here, count)
            tail = pl.ds(here + count, 16)
            value = kept[sums, :].astype(F32) + got[sums, :].astype(F32)
            number = count_of(kept[tail, :].astype(F32), count) + count_of(got[tail, :].astype(F32), count)
            out[top:top + count, :] = value.astype(out.dtype)
            out[top + count:top + size, :] = count_rows(number, dz, riding).astype(out.dtype)
    if not halved:
        keep[...] = send[0:keep.shape[0], :].astype(F32)


def swap_halves(first, second, core):
    half = LANES // 2
    left = lax.broadcasted_iota(jnp.int32, first.shape, 1) < half
    turned_first, turned_second = pltpu.roll(first, half, 1), pltpu.roll(second, half, 1)
    swapped_first = jnp.where(left, first, turned_second)
    swapped_second = jnp.where(left, turned_first, second)
    return jnp.where(core == 1, swapped_first, first), jnp.where(core == 1, swapped_second, second)


def step_kernel(halves, place, mixed, info, got, kept_a, kept_c, send, keep_a, keep_c):
    (rows_a, halved_a), (rows_c, halved_c) = halves
    if mixed:
        to = rows_a // 2
        total = kept_a[0:rows_a, :] + got[0:rows_a, :].astype(F32)
        first, second = swap_halves(total[0:to, :], total[to:, :], info[0])
        low = info[place] == 0
        send[0:to, :] = jnp.where(low, second, first).astype(BF16)
        keep_a[...] = jnp.where(low, first, second)
    else:
        to = split_sum(halved_a, info[place], got, 0, kept_a, rows_a, send, 0, keep_a)
    gone = split_sum(halved_c, info[place], got, rows_a, kept_c, rows_c, send, to, keep_c)
    block = digit_block(add_digits(kept_c[rows_c:, :], got[rows_a + rows_c:, :].astype(F32)))
    keep_c[gone:, :] = block
    to += gone
    send[to:to + block.shape[0], :] = block.astype(BF16)
    to += block.shape[0]
    if to < send.shape[0]:
        send[to:, :] = jnp.zeros((send.shape[0] - to, LANES), BF16)


def last_kernel(rows_a, rows, info, got, kept_a, kept_c, sums_got, sums_kept, corr, pieces, mine):
    corr[...] = kept_a[...] + got[0:rows_a, :].astype(F32)
    pieces[...] = (kept_c[0:rows, :] + got[rows_a:rows_a + rows, :].astype(F32)).astype(BF16)
    block = digit_block(add_digits(kept_c[rows:, :], got[rows_a + rows:rows_a + kept_c.shape[0], :].astype(F32)))
    mine[0:rows, :] = pieces[...]
    mine[rows:kept_c.shape[0], :] = block.astype(BF16)
    at = kept_c.shape[0]
    count = sums_kept.shape[0] - 16
    number = count_of(sums_kept[count:, :].astype(F32), count) + count_of(sums_got[count:, :].astype(F32), count)
    square = (count, count)
    same = lax.broadcasted_iota(jnp.int32, square, 0) == lax.broadcasted_iota(jnp.int32, square, 1)
    tall = jnp.sum(jnp.where(same, jnp.broadcast_to(number, square), 0.0), 1, keepdims=True)
    total = sums_kept[0:count, :].astype(F32) + sums_got[0:count, :].astype(F32)
    means = (total / jnp.maximum(tall, 1.0)).astype(BF16)
    digits = count_rows(number, means.shape[1]).astype(BF16)
    for j in range(means.shape[1] // LANES):
        mine[at:at + count, :] = means[:, j * LANES:(j + 1) * LANES]
        mine[at + count:at + count + 16, :] = digits[:, j * LANES:(j + 1) * LANES]
        at += count + 16


def conv_out_kernel(total_frames, place, info, corr, proj, out, wide):
    rows = out.shape[0]
    flipped = jnp.transpose(corr[...])
    high = flipped.astype(BF16)
    low = (flipped - high.astype(F32)).astype(BF16)
    wide[...] = (nt(high, proj[...]) + nt(low, proj[...])) * (1.0 / total_frames)
    start = info[place]
    if rows % 8 == 0:
        out[...] = wide[pl.ds(pl.multiple_of(start, 8), rows), :]
    else:
        taken = wide[0:rows, :]
        for other in range(rows, wide.shape[0], rows):
            taken = jnp.where(start == other, wide[other:other + rows, :], taken)
        out[...] = taken


def out_kernel(total_frames, use_scale, dz, place, inner, extra, info, mine, *refs):
    parts, (out, bias, means, usage) = refs[:-4], refs[-4:]
    theirs = parts[1]
    scale = 1.0 / total_frames
    top = inner * dz
    value = add_digits(mine[top:top + extra, :].astype(F32), theirs[top:top + extra, :].astype(F32)) * scale
    for j in range(bias.shape[1] // LANES):
        bias[:, j * LANES:(j + 1) * LANES] = value[j:j + 1, :]
    bit = info[0]
    count = means.shape[1]
    numbers = []
    for ref, level in ((mine, bit), (theirs, 1 - bit)):
        at = top + extra
        blocks = []
        for j in range(dz // LANES):
            blocks.append(ref[at:at + count + 16, :])
            at += count + 16
        whole = jnp.concatenate(blocks, 1)
        means[level] = whole[0:count, :]
        numbers.append(count_of(whole[count:, :].astype(F32), count) * use_scale)
    usage[0:1, :] = jnp.where(bit == 1, numbers[1], numbers[0])
    usage[1:2, :] = jnp.where(bit == 1, numbers[0], numbers[1])
    for j, ref in enumerate(parts):
        for k in range(inner):
            start = pl.multiple_of((info[place + j] + k) * LANES, LANES)
            turned = jnp.transpose(ref[k * dz:(k + 1) * dz, :])
            out[pl.ds(start, LANES), :] = turned.astype(F32) * scale


def shifted(block, axis, distance):
    devices = range(lax.axis_size(axis))
    route = [(i - distance, i) for i in devices if i - distance in devices]
    return lax.ppermute(block, axis, route)


def swapped(block, steps):
    tm = lax.axis_size("tm")

    def partner(device):
        axis, bit = steps[(device // tm) & 1]
        return device ^ ((1 << bit) * (tm if axis == "dp" else 1))

    route = [(device, partner(device)) for device in range(lax.axis_size("dp") * tm)]
    return lax.ppermute(block, ("dp", "tm"), route)


def crossed(block, steps):
    tm = lax.axis_size("tm")

    def partner(device):
        axis, bit = steps[(device // tm) & 1]
        return device ^ tm ^ ((1 << bit) * (tm if axis == "dp" else 1))

    route = [(device, partner(device)) for device in range(lax.axis_size("dp") * tm)]
    return lax.ppermute(block, ("dp", "tm"), route)


def shards(feats, codes, conv_weight, conv_bias, proj_weight, codebooks):
    dp, tm = lax.axis_size("dp"), lax.axis_size("tm")
    rows_in, channels = feats.shape
    frames = rows_in // 2
    levels, book_size, dz = codebooks.shape
    assert levels == 2
    width = conv_weight.shape[0]
    total_frames = frames * dp * tm
    per_shard = book_size // tm
    dp_bits, tm_bits = log2(dp), log2(tm)
    owner_rows = width // (dp * tm)

    assert dp_bits >= 3 and 1 <= tm_bits <= 2
    pieces_a, pieces_c = width // LANES, channels // LANES
    under = max(dp_bits + tm_bits - log2(pieces_a), 0)
    c_bits = 2
    assert pieces_c >= 4
    whole_bits = [b for b in range(1, dp_bits) if b + tm_bits < under]
    piece_bits = [b for b in range(1, dp_bits) if b + tm_bits >= under]
    paths = [[("dp", b) for b in bits] for bits in (whole_bits + piece_bits, whole_bits[::-1] + piece_bits[::-1])]
    mixed = under == 1 and tm_bits == 2
    turned = mixed or under == 0 or under >= tm_bits
    up = [("tm", b) for b in range(tm_bits)]
    paths[0] += up[::-1]
    paths[1] += up if turned else up[::-1]
    exchanges = list(zip([("dp", 0)] + paths[0], [("dp", 0)] + paths[1]))
    sums_up = [("dp", b) for b in range(1, dp_bits)]
    sums_exchanges = list(zip(up[::-1] + sums_up, up + sums_up[::-1]))

    def piece_bit(step):
        axis, b = step
        bit = b + (tm_bits if axis == "dp" else 0)
        return bit - under if bit >= under else None

    a_split = [piece_bit(steps[0]) is not None for steps in exchanges]
    c_split = [log2(pieces_c) - 1 - k if k < c_bits else None for k in range(len(exchanges))]

    def order_of(split, count):
        used = [b for b in split if b is not None]
        return used + [b for b in reversed(range(log2(count))) if b not in used]

    orders = [order_of([piece_bit(steps[core]) for steps in exchanges], pieces_a) for core in range(2)]
    order_c = order_of(c_split, pieces_c)
    plan = [(pieces_a, orders, a_split[0]), (pieces_c, [order_c, order_c], True)]
    now_a = pieces_a // 2 if plan[0][2] else pieces_a
    now_c = pieces_c // 2

    at_dp, at_tm = lax.axis_index("dp"), lax.axis_index("tm")
    core = at_dp & 1

    def on_core(values):
        return values[0] + core * (values[1] - values[0])

    def bit_at(step):
        axis, b = step
        return ((at_dp if axis == "dp" else at_tm) >> b) & 1

    bits = [on_core([bit_at(step) for step in steps]) for steps in exchanges]
    sums_bits = [on_core([bit_at(step) for step in steps]) for steps in sums_exchanges]
    shared = [bit_at(step) for step in exchanges[1]]
    mine_c, other_c = on_core(shared), on_core(shared[::-1])
    places = [2 * core + mine_c, 2 * (1 - core) + other_c, 2 * core + 1 - mine_c, 2 * (1 - core) + 1 - other_c]
    places = [place << (log2(pieces_c) - c_bits) for place in places]
    lists = []
    for way in ([b for _, b in up[::-1]], [b for _, b in up]):
        lists.append([sum(((position >> (tm_bits - 1 - j)) & 1) << b for j, b in enumerate(way)) for position in range(tm)])
    first_bit = on_core([tm_bits - 1, 0])
    lead = (at_tm >> first_bit) & 1
    quarters = [on_core([lists[0][j], lists[1][j]]) for j in range(tm // 2)]
    send_codes = [(q + ((1 - lead) << first_bit)) * per_shard for q in quarters]
    keep_codes = [(q + (lead << first_bit)) * per_shard for q in quarters]
    differ = at_tm ^ (at_tm + 1)
    ways = [sum(((differ >> b) & 1) << j for j, b in enumerate(way)) for way in (
        list(reversed(range(tm_bits))), list(range(tm_bits)))]
    row_code = jnp.where(at_tm + 1 < tm, on_core(ways), 0)
    if turned and not mixed:
        start = ((at_dp * tm + at_tm) * owner_rows) & (LANES - 1)
    else:
        start = on_core([(at_dp * tm + at_tm) * owner_rows, (at_tm >> 1) * owner_rows if mixed else (
            at_dp * tm + at_tm) * owner_rows]) & (LANES - 1)
    at_start = len(bits)
    at_codes = at_start + 1
    at_pieces = at_codes + tm
    at_sums = at_pieces + len(places)
    at_row = at_sums + len(sums_bits)
    info = jnp.stack(bits + [start] + send_codes + keep_codes + places + sums_bits + [row_code]).astype(jnp.int32)

    halo = shifted(
        call(halo_kernel, shape((16, channels), BF16), [info, feats], flops=10 ** 11), "tm", 1)
    weight, proj, codes = conv_weight, proj_weight, codes[0]
    unfold, conv, chosen = call(
        local_kernel,
        [shape((frames, width), BF16), shape((frames, channels), F32), shape((levels, frames, dz), BF16)],
        [info, feats, weight, conv_bias[None, :], codes, codebooks],
        scratch=[VMEM((channels // LANES, rows_in + 8, LANES), F32)],
    )

    extra = 4 * (-(-channels // LANES // 8) * 8)
    code_rows = -(-(2 * -(-frames // dz)) // 16) * 16
    corr_rows = (now_a + now_c) * dz
    rows_b = frames + code_rows
    unfold, hidden, latent_grad, flipped, own, send = call(
        functools.partial(forward_kernel, plan),
        [shape((frames, width), BF16), shape((frames, channels), BF16), shape((frames, dz), BF16),
         shape((dz, frames), BF16), shape((rows_b, dz), BF16),
         shape((corr_rows + rows_b * (dz // LANES), LANES), BF16)],
        [info, halo, unfold, conv, chosen, weight, proj, codes],
        aliases={2: 0},
    )
    got = swapped(send, exchanges[0])
    keep_a, keep_c, hidden_grad, extras, row = call(
        functools.partial(rest_kernel, plan),
        [shape((now_a * dz, LANES), F32), shape((now_c * dz, LANES), F32), shape((frames, channels), BF16),
         shape((extra, LANES), F32), shape((16, channels), BF16)],
        [info, flipped, unfold, hidden, latent_grad, proj],
        after=[send],
    )

    def halves_at(k):
        nonlocal now_a, now_c
        halves = [(now_a * dz, a_split[k]), (now_c * dz, c_split[k] is not None)]
        now_a = now_a // 2 if halves[0][1] else now_a
        now_c = now_c // 2 if halves[1][1] else now_c
        return halves, now_a * dz, now_c * dz + extra

    halves, rows_a, rows_c = halves_at(1)
    send, keep_a, keep_c = call(
        functools.partial(first_step_kernel, halves, 1),
        [shape((rows_a + rows_c, LANES), BF16), shape((rows_a, LANES), F32), shape((rows_c, LANES), F32)],
        [info, got, keep_a, keep_c, extras])
    size = per_shard + 16
    sums_rows = size * (tm // 2)
    sums_send = call(
        functools.partial(sums_kernel, corr_rows, frames, at_codes, per_shard),
        shape((sums_rows, dz), BF16),
        [info, got, own, row],
        after=[send])
    sums_keep = call(
        functools.partial(sums_kernel, corr_rows, frames, at_codes + tm // 2, per_shard),
        shape((sums_rows, dz), F32),
        [info, got, own, row],
        after=[sums_send])
    sums_got = swapped(sums_send, sums_exchanges[0])
    got = swapped(send, exchanges[1])
    known = row
    ordered = [sums_keep]
    for k in range(2, len(exchanges)):
        halves, rows_a, rows_c = halves_at(k)
        spare = 16 * (k == len(exchanges) - 1)
        send, keep_a, keep_c = call(
            functools.partial(step_kernel, halves, k, mixed and k == dp_bits),
            [shape((rows_a + rows_c + spare, LANES), BF16), shape((rows_a, LANES), F32), shape((rows_c, LANES), F32)],
            [info, got, keep_a, keep_c],
            after=ordered)
        got = swapped(send, exchanges[k])
        halved = sums_exchanges[k - 1][0][0] == "tm"
        sums_rows = sums_rows // 2 if halved else sums_rows
        row_step = k - 2 if k - 2 < tm_bits else None
        outs = call(
            functools.partial(sums_step_kernel, halved, at_sums + k - 1, row_step, (per_shard, at_row)),
            [shape((sums_rows, dz), BF16), shape((sums_rows, dz), F32)]
            + [shape((16, channels), BF16)] * (row_step is not None),
            [info, sums_got, sums_keep] + [known] * (row_step is not None),
            after=[send])
        sums_send, sums_keep = outs[:2]
        known = outs[2] if row_step is not None else known
        sums_got = swapped(sums_send, sums_exchanges[k - 1])
        ordered = [sums_send]
    assert now_a == 1 and sums_rows == size
    feat_grad, last = call(
        feat_kernel,
        shape((rows_in, channels), BF16),
        [info, hidden_grad, known, weight],
        after=[sums_send],
        token=True,
        scratch=[VMEM((frames + 8, channels), F32), VMEM((channels // LANES, rows_in, LANES), F32)],
    )

    corr, piece, mine = call(
        functools.partial(last_kernel, rows_a, rows_c - extra),
        [shape((rows_a, LANES), F32), shape((rows_c - extra, LANES), BF16),
         shape((rows_c + size * (dz // LANES), LANES), BF16)],
        [info, got, keep_a, keep_c, sums_got, sums_keep],
        after=[last])
    parts = [piece, swapped(mine, exchanges[0]), swapped(piece, exchanges[1]), crossed(piece, exchanges[1])]
    conv_grad, last = call(
        functools.partial(conv_out_kernel, total_frames, at_start),
        shape((owner_rows, channels), F32),
        [info, corr, proj],
        after=[piece],
        token=True,
        scratch=[VMEM((LANES, channels), F32)],
    )
    proj_grad, bias_grad, code_means, code_usage = call(
        functools.partial(out_kernel, total_frames, book_size / total_frames, dz, at_pieces, now_c, extra),
        [shape((channels, dz), F32), shape((1, channels), F32), shape((levels, per_shard, dz), BF16),
         shape((levels, per_shard), F32)],
        [info, mine] + parts,
        after=[last],
    )
    return feat_grad, conv_grad, bias_grad[0], proj_grad, code_means, code_usage


def solution(mesh):
    placed = (P(("dp", "tm"), None), P("dp", None, "tm"), P(), P(), P(), P())
    return jax.shard_map(
        shards,
        mesh=mesh,
        in_specs=placed,
        out_specs=(
            P(("dp", "tm"), None),
            P(("dp", "tm"), None),
            P(),
            P(),
            P(None, "tm", None),
            P(None, "tm"),
        ),
        check_vma=False,
    )
```

```python
import functools

import jax
import jax.numpy as jnp
from jax import lax
from jax.experimental import pallas as pl
from jax.experimental.pallas import tpu as pltpu
from jax.sharding import PartitionSpec as P

BF16 = jnp.bfloat16
F32 = jnp.float32
LANES = 128
VMEM_LIMIT = 16 * 1024 * 1024


def log2(value):
    assert value & (value - 1) == 0
    return value.bit_length() - 1


def nn(a, b):
    return lax.dot_general(a, b, (((1,), (0,)), ((), ())), preferred_element_type=F32)


def nt(a, b):
    return lax.dot_general(a, b, (((1,), (1,)), ((), ())), preferred_element_type=F32)


VMEM = pltpu.VMEM


def call(body, out_shape, args, after=(), scratch=(), aliases=None, token=False, flops=0):
    count = len(args)
    many = isinstance(out_shape, (list, tuple))
    shapes = list(out_shape) if many else [out_shape]

    def kernel(*refs):
        ends = count + len(after)
        if token:
            refs[ends + len(shapes)][...] = jnp.zeros((8, LANES), F32)
            refs = refs[:ends + len(shapes)] + refs[ends + len(shapes) + 1:]
        body(*refs[:count], *refs[ends:])

    specs = [pl.BlockSpec(memory_space=pltpu.SMEM)]
    specs += [pl.BlockSpec(memory_space=VMEM)] * (count - 1)
    specs += [pl.BlockSpec(memory_space=pl.ANY)] * len(after)
    shown = shapes + [shape((8, LANES), F32)] * token
    outs = pl.pallas_call(
        kernel,
        out_shape=shown,
        in_specs=specs,
        out_specs=[pl.BlockSpec(memory_space=VMEM)] * len(shown),
        scratch_shapes=list(scratch),
        input_output_aliases=aliases or {},
        compiler_params=pltpu.CompilerParams(vmem_limit_bytes=VMEM_LIMIT),
        cost_estimate=pl.CostEstimate(flops=flops, bytes_accessed=0, transcendentals=0),
    )(*args, *after)
    return outs if len(shown) > 1 else outs[0]


def shape(dims, dtype):
    return jax.ShapeDtypeStruct(dims, dtype)


def digits_of(value):
    high = value.astype(BF16).astype(F32)
    rest = value - high
    middle = rest.astype(BF16).astype(F32)
    low = (rest - middle).astype(BF16).astype(F32)
    return high, middle, low


def one_hot(codes, axis_codes, first, count):
    frames = codes.shape[1 - axis_codes]
    dims = (count, frames) if axis_codes == 0 else (frames, count)
    places = lax.broadcasted_iota(jnp.int32, dims, axis_codes) + first
    return jnp.where(codes == places, 1.0, 0.0).astype(BF16)


def idle_kernel(info, out):
    out[...] = jnp.zeros(out.shape, F32)


def local_kernel(info, feats, weight, bias, codes, books, unfold, conv, chosen, wide):
    rows, channels = feats.shape
    frames = rows // 2
    for j in range(channels // LANES):
        wide[j, 0:8, :] = jnp.zeros((8, LANES), F32)
        wide[j, 8:, :] = feats[:, j * LANES:(j + 1) * LANES].astype(F32)
        for tap in range(4):
            start = tap * channels + j * LANES
            unfold[:, start:start + LANES] = wide[j, pl.ds(6 + tap, frames, stride=2), :].astype(BF16)
    conv[...] = nn(unfold[...], weight[...]) + bias[...]
    levels = books.shape[0]
    padded = jnp.concatenate([codes[...].astype(F32), jnp.zeros((8 - levels, frames), F32)], 0)
    tall = jnp.transpose(padded).astype(jnp.int32)
    for level in range(levels):
        matches = one_hot(tall[:, level:level + 1], 1, 0, books.shape[1])
        chosen[level] = nn(matches, books[level]).astype(BF16)


def walk(orders, halved, count):
    start = 1 if halved else 0
    shown = count // 2 if halved else count
    bits = log2(shown)
    step = 2 if shown > 1 and all(order[-1] == 0 for order in orders) else 1
    for position in range(0, shown, step):
        yield position, [
            sum(((position >> (bits - 1 - k)) & 1) << bit for k, bit in enumerate(order[start:])) for order in orders
        ], step


def correlate(flipped, sources, plan, core, bit, out):
    dz = flipped.shape[0]
    at = 0
    for source, (count, orders, halved) in zip(sources, plan):
        for position, pieces, step in walk(orders, halved, count):
            column = pieces[0] + core * (pieces[1] - pieces[0])
            if halved:
                column = column + (bit << orders[0][0])
            column = pl.multiple_of(column * LANES, LANES)
            product = nn(flipped, source[:, pl.ds(column, step * LANES)])
            for j in range(step):
                top = (at + position + j) * dz
                out[top:top + dz, :] = product[:, j * LANES:(j + 1) * LANES].astype(out.dtype)
        at += count // 2 if halved else count
    return at * dz


def code_digits(codes, dz, rows):
    parts = []
    for part in (codes >> 8, codes & 255):
        for start in range(0, codes.shape[1], dz):
            piece = part[:, start:start + dz].astype(F32)
            if piece.shape[1] < dz:
                piece = jnp.concatenate([piece, jnp.zeros((1, dz - piece.shape[1]), F32)], 1)
            parts.append(piece)
    parts.append(jnp.zeros((rows - len(parts), dz), F32))
    return jnp.concatenate(parts, 0).astype(BF16)


def codes_of(block, frames):
    dz = block.shape[1]
    per = -(-frames // dz)
    digits = block[...].astype(F32)
    parts = [jnp.concatenate([digits[k * per + j:k * per + j + 1, :] for j in range(per)], 1)[:, :frames]
             for k in range(2)]
    return (parts[0] * 256.0 + parts[1]).astype(jnp.int32)


def forward_kernel(plan, info, halo, unfold_in, conv, chosen, weight, proj, codes,
                   unfold, hidden, latent_grad, flipped, own, send):
    frames, width = unfold.shape
    half = width // 2
    dz = proj.shape[1]
    row = lax.broadcasted_iota(jnp.int32, (16, half), 0)
    left = jnp.concatenate([halo[0:1, :], halo[1:2, :]], 1).astype(F32)
    head = jnp.where(row == 0, jnp.broadcast_to(left, (16, half)), 0.0)
    unfold[0:16, 0:half] = (unfold_in[0:16, 0:half].astype(F32) + head).astype(BF16)
    fix = nn(head.astype(BF16), weight[0:half, :])
    hidden[...] = jnp.concatenate([conv[0:16, :] + fix, conv[16:, :]], 0).astype(BF16)
    latent = nn(hidden[...], proj[...])
    once = latent - chosen[0].astype(F32)
    total = once + (once - chosen[1].astype(F32))
    latent_grad[...] = total.astype(BF16)
    flipped[...] = jnp.transpose(latent_grad[...].astype(F32)).astype(BF16)
    bit = info[0]
    at = correlate(flipped[...], (unfold, hidden), plan, 1 - bit, 1 - bit, send)
    code_rows = own.shape[0] - frames
    digits = [code_digits(codes[level:level + 1], dz, code_rows) for level in range(2)]
    own[0:frames, :] = jnp.where(bit == 1, once, latent).astype(BF16)
    own[frames:, :] = jnp.where(bit == 1, digits[1], digits[0])
    other = jnp.where(bit == 1, latent, once).astype(BF16)
    other_digits = jnp.where(bit == 1, digits[0], digits[1])
    for j in range(dz // LANES):
        send[at:at + frames, :] = other[:, j * LANES:(j + 1) * LANES]
        send[at + frames:at + frames + code_rows, :] = other_digits[:, j * LANES:(j + 1) * LANES]
        at += frames + code_rows


def rest_kernel(plan, info, flipped, unfold, hidden, latent_grad, proj, keep_a, keep_c, hidden_grad, extras, row):
    bit = info[0]
    correlate(flipped[...], (unfold,), plan[:1], bit, bit, keep_a)
    correlate(flipped[...], (hidden,), plan[1:], bit, bit, keep_c)
    back = nt(latent_grad[...], proj[...]).astype(BF16)
    hidden_grad[...] = back
    row[...] = back[0:16, :]
    stride = extras.shape[0] // 4
    extras[...] = jnp.zeros(extras.shape, F32)
    sums = jnp.sum(back.astype(F32), 0, keepdims=True)
    for digit, part in enumerate(digits_of(sums)):
        for j in range(sums.shape[1] // LANES):
            extras[digit * stride + j:digit * stride + j + 1, :] = part[:, j * LANES:(j + 1) * LANES]


def split_sum(halved, bit, got, at, kept, rows, send, to, keep):
    if halved:
        half = rows // 2
        away = pl.multiple_of((1 - bit) * half, 16)
        home = pl.multiple_of(bit * half, 16)
        send[to:to + half, :] = (kept[pl.ds(away, half), :] + got[pl.ds(at + away, half), :].astype(F32)).astype(BF16)
        keep[0:half, :] = kept[pl.ds(home, half), :] + got[pl.ds(at + home, half), :].astype(F32)
        return half
    total = (kept[0:rows, :] + got[at:at + rows, :].astype(F32)).astype(BF16)
    send[to:to + rows, :] = total
    keep[0:rows, :] = total.astype(F32)
    return rows


def add_digits(mine, theirs):
    stride = mine.shape[0] // 4
    return ((mine[0:stride] + mine[stride:2 * stride]) + mine[2 * stride:3 * stride]) + (
        (theirs[0:stride] + theirs[stride:2 * stride]) + theirs[2 * stride:3 * stride])


def digit_block(value):
    return jnp.concatenate(list(digits_of(value)) + [jnp.zeros_like(value)], 0)


def first_step_kernel(halves, place, info, got, kept_a, kept_c, extras, send, keep_a, keep_c):
    (rows_a, halved_a), (rows_c, halved_c) = halves
    to = split_sum(halved_a, info[place], got, 0, kept_a, rows_a, send, 0, keep_a)
    gone = split_sum(halved_c, info[place], got, rows_a, kept_c, rows_c, send, to, keep_c)
    send[to + gone:, :] = extras[...].astype(BF16)
    keep_c[gone:, :] = extras[...]


def feat_kernel(info, grad, after, weight, out, wide, inter):
    frames, channels = grad.shape
    half = weight.shape[0] // 2
    wide[0:frames, :] = grad[...].astype(F32)
    wide[frames:, :] = jnp.broadcast_to(after[0:1, :].astype(F32), (8, channels))
    ahead = wide[pl.ds(1, frames), :].astype(BF16)
    for parity in range(2):
        rows = pl.ds(parity * (half // 2), half // 2)
        rows_after = pl.ds(half + parity * (half // 2), half // 2)
        both = nt(ahead, weight[rows, :]) + nt(grad[...], weight[rows_after, :])
        for j in range(channels // LANES):
            inter[j, pl.ds(parity, frames, stride=2), :] = both[:, j * LANES:(j + 1) * LANES]
    for j in range(channels // LANES):
        out[:, j * LANES:(j + 1) * LANES] = inter[j].astype(BF16)


def sums_kernel(first, frames, place, count, info, got, own, row, out):
    rows, dz = own.shape
    theirs = jnp.concatenate([got[first + j * rows:first + (j + 1) * rows, :] for j in range(dz // LANES)], 1)
    ones = jnp.ones((8, frames), BF16)
    parts = []
    for block in (own[...], theirs):
        parts.append((block[0:frames, :], codes_of(block[frames:, :], frames)))
    size = count + 16
    riding = [row[...].astype(F32)[0:1, :]]
    for top in range(0, out.shape[0], size):
        total = jnp.zeros((count, dz), F32)
        counts = jnp.zeros((8, count), F32)
        for values, codes in parts:
            matches = one_hot(codes, 0, info[place], count)
            total = total + nn(matches, values)
            counts = counts + nt(ones, matches)
        out[top:top + count, :] = total.astype(out.dtype)
        out[top + count:top + size, :] = count_rows(counts[0:1], dz, riding).astype(out.dtype)
        place += 1


def count_rows(count, width, riding=()):
    high = jnp.floor(count * (1.0 / 65536.0))
    rest = count - high * 65536.0
    middle = jnp.floor(rest * (1.0 / 256.0))
    low = rest - middle * 256.0
    block = jnp.concatenate([high, middle, low], 0)
    if count.shape[1] < width:
        block = jnp.concatenate([block, jnp.zeros((3, width - count.shape[1]), F32)], 1)
    parts = [block]
    for row in riding:
        parts += [row[:, at:at + width] for at in range(0, row.shape[1], width)]
    left = 16 - sum(part.shape[0] for part in parts)
    return jnp.concatenate(parts + [jnp.zeros((left, width), F32)] * (left > 0), 0)


def riding_row(block, index, parts):
    return jnp.concatenate([block[3 + index * parts + j:4 + index * parts + j, :] for j in range(parts)], 1)


def count_of(block, own):
    return (block[0:1] * 65536.0 + block[1:2] * 256.0 + block[2:3])[:, :own]


def sums_step_kernel(halved, place, row_step, row_place, info, got, kept, *refs):
    riding = ()
    if row_step is not None:
        known, refs = refs[0][...].astype(F32), refs[1:]
        after, refs = refs[-1], refs[:-1]
        parts = known.shape[1] // got.shape[1]
        block = got[row_place[0]:row_place[0] + 16, :].astype(F32)
        rows = [known[j:j + 1, :] for j in range(1 << row_step)]
        rows += [riding_row(block, j, parts) for j in range(1 << row_step)]
        if halved:
            riding = rows
            total = rows + [jnp.zeros((16 - len(rows), known.shape[1]), F32)]
            after[...] = jnp.concatenate(total, 0).astype(BF16)
        else:
            wide = jnp.zeros(after.shape, F32)
            for j in range(1, len(rows)):
                wide = jnp.where(info[row_place[1]] == j, jnp.broadcast_to(rows[j], after.shape), wide)
            after[...] = wide.astype(BF16)
    send, keep = refs
    dz = got.shape[1]
    bit = info[place]
    half = kept.shape[0] // 2 if halved else 0
    outs = [(send, (1 - bit) * half), (keep, bit * half)] if halved else [(send, 0)]
    count = row_place[0]
    size = count + 16
    for out, start in outs:
        for top in range(0, keep.shape[0], size):
            here = top + pl.multiple_of(start, 16) if halved else top
            sums = pl.ds(here, count)
            tail = pl.ds(here + count, 16)
            value = kept[sums, :].astype(F32) + got[sums, :].astype(F32)
            number = count_of(kept[tail, :].astype(F32), count) + count_of(got[tail, :].astype(F32), count)
            out[top:top + count, :] = value.astype(out.dtype)
            out[top + count:top + size, :] = count_rows(number, dz, riding).astype(out.dtype)
    if not halved:
        keep[...] = send[0:keep.shape[0], :].astype(F32)


def swap_halves(first, second, core):
    half = LANES // 2
    left = lax.broadcasted_iota(jnp.int32, first.shape, 1) < half
    turned_first, turned_second = pltpu.roll(first, half, 1), pltpu.roll(second, half, 1)
    swapped_first = jnp.where(left, first, turned_second)
    swapped_second = jnp.where(left, turned_first, second)
    return jnp.where(core == 1, swapped_first, first), jnp.where(core == 1, swapped_second, second)


def step_kernel(halves, place, mixed, info, got, kept_a, kept_c, send, keep_a, keep_c):
    (rows_a, halved_a), (rows_c, halved_c) = halves
    if mixed:
        to = rows_a // 2
        total = kept_a[0:rows_a, :] + got[0:rows_a, :].astype(F32)
        first, second = swap_halves(total[0:to, :], total[to:, :], info[0])
        low = info[place] == 0
        send[0:to, :] = jnp.where(low, second, first).astype(BF16)
        keep_a[...] = jnp.where(low, first, second)
    else:
        to = split_sum(halved_a, info[place], got, 0, kept_a, rows_a, send, 0, keep_a)
    gone = split_sum(halved_c, info[place], got, rows_a, kept_c, rows_c, send, to, keep_c)
    block = digit_block(add_digits(kept_c[rows_c:, :], got[rows_a + rows_c:, :].astype(F32)))
    keep_c[gone:, :] = block
    to += gone
    send[to:to + block.shape[0], :] = block.astype(BF16)
    to += block.shape[0]
    if to < send.shape[0]:
        send[to:, :] = jnp.zeros((send.shape[0] - to, LANES), BF16)


def last_kernel(rows_a, rows, info, got, kept_a, kept_c, sums_got, sums_kept, corr, pieces, mine):
    corr[...] = kept_a[...] + got[0:rows_a, :].astype(F32)
    pieces[...] = (kept_c[0:rows, :] + got[rows_a:rows_a + rows, :].astype(F32)).astype(BF16)
    block = digit_block(add_digits(kept_c[rows:, :], got[rows_a + rows:rows_a + kept_c.shape[0], :].astype(F32)))
    mine[0:rows, :] = pieces[...]
    mine[rows:kept_c.shape[0], :] = block.astype(BF16)
    at = kept_c.shape[0]
    count = sums_kept.shape[0] - 16
    number = count_of(sums_kept[count:, :].astype(F32), count) + count_of(sums_got[count:, :].astype(F32), count)
    square = (count, count)
    same = lax.broadcasted_iota(jnp.int32, square, 0) == lax.broadcasted_iota(jnp.int32, square, 1)
    tall = jnp.sum(jnp.where(same, jnp.broadcast_to(number, square), 0.0), 1, keepdims=True)
    total = sums_kept[0:count, :].astype(F32) + sums_got[0:count, :].astype(F32)
    means = (total / jnp.maximum(tall, 1.0)).astype(BF16)
    digits = count_rows(number, means.shape[1]).astype(BF16)
    for j in range(means.shape[1] // LANES):
        mine[at:at + count, :] = means[:, j * LANES:(j + 1) * LANES]
        mine[at + count:at + count + 16, :] = digits[:, j * LANES:(j + 1) * LANES]
        at += count + 16


def conv_out_kernel(total_frames, place, info, corr, proj, out, wide):
    rows = out.shape[0]
    flipped = jnp.transpose(corr[...])
    high = flipped.astype(BF16)
    low = (flipped - high.astype(F32)).astype(BF16)
    wide[...] = (nt(high, proj[...]) + nt(low, proj[...])) * (1.0 / total_frames)
    start = info[place]
    if rows % 8 == 0:
        out[...] = wide[pl.ds(pl.multiple_of(start, 8), rows), :]
    else:
        taken = wide[0:rows, :]
        for other in range(rows, wide.shape[0], rows):
            taken = jnp.where(start == other, wide[other:other + rows, :], taken)
        out[...] = taken


def out_kernel(total_frames, use_scale, dz, place, inner, extra, info, mine, *refs):
    parts, (out, bias, means, usage) = refs[:-4], refs[-4:]
    theirs = parts[1]
    scale = 1.0 / total_frames
    top = inner * dz
    value = add_digits(mine[top:top + extra, :].astype(F32), theirs[top:top + extra, :].astype(F32)) * scale
    for j in range(bias.shape[1] // LANES):
        bias[:, j * LANES:(j + 1) * LANES] = value[j:j + 1, :]
    bit = info[0]
    count = means.shape[1]
    numbers = []
    for ref, level in ((mine, bit), (theirs, 1 - bit)):
        at = top + extra
        blocks = []
        for j in range(dz // LANES):
            blocks.append(ref[at:at + count + 16, :])
            at += count + 16
        whole = jnp.concatenate(blocks, 1)
        means[level] = whole[0:count, :]
        numbers.append(count_of(whole[count:, :].astype(F32), count) * use_scale)
    usage[0:1, :] = jnp.where(bit == 1, numbers[1], numbers[0])
    usage[1:2, :] = jnp.where(bit == 1, numbers[0], numbers[1])
    for j, ref in enumerate(parts):
        for k in range(inner):
            start = pl.multiple_of((info[place + j] + k) * LANES, LANES)
            turned = jnp.transpose(ref[k * dz:(k + 1) * dz, :])
            out[pl.ds(start, LANES), :] = turned.astype(F32) * scale


def shifted(block, axis, distance):
    devices = range(lax.axis_size(axis))
    route = [(i - distance, i) for i in devices if i - distance in devices]
    return lax.ppermute(block, axis, route)


def swapped(block, steps):
    tm = lax.axis_size("tm")

    def partner(device):
        axis, bit = steps[(device // tm) & 1]
        return device ^ ((1 << bit) * (tm if axis == "dp" else 1))

    route = [(device, partner(device)) for device in range(lax.axis_size("dp") * tm)]
    return lax.ppermute(block, ("dp", "tm"), route)


def crossed(block, steps):
    tm = lax.axis_size("tm")

    def partner(device):
        axis, bit = steps[(device // tm) & 1]
        return device ^ tm ^ ((1 << bit) * (tm if axis == "dp" else 1))

    route = [(device, partner(device)) for device in range(lax.axis_size("dp") * tm)]
    return lax.ppermute(block, ("dp", "tm"), route)


def shards(feats, codes, conv_weight, conv_bias, proj_weight, codebooks):
    dp, tm = lax.axis_size("dp"), lax.axis_size("tm")
    rows_in, channels = feats.shape
    frames = rows_in // 2
    levels, book_size, dz = codebooks.shape
    assert levels == 2
    width = conv_weight.shape[0]
    total_frames = frames * dp * tm
    per_shard = book_size // tm
    dp_bits, tm_bits = log2(dp), log2(tm)
    owner_rows = width // (dp * tm)

    assert dp_bits >= 3 and 1 <= tm_bits <= 2
    pieces_a, pieces_c = width // LANES, channels // LANES
    under = max(dp_bits + tm_bits - log2(pieces_a), 0)
    c_bits = 2
    assert pieces_c >= 4
    whole_bits = [b for b in range(1, dp_bits) if b + tm_bits < under]
    piece_bits = [b for b in range(1, dp_bits) if b + tm_bits >= under]
    paths = [[("dp", b) for b in bits] for bits in (whole_bits + piece_bits, whole_bits[::-1] + piece_bits[::-1])]
    mixed = under == 1 and tm_bits == 2
    turned = mixed or under == 0 or under >= tm_bits
    up = [("tm", b) for b in range(tm_bits)]
    paths[0] += up[::-1]
    paths[1] += up if turned else up[::-1]
    exchanges = list(zip([("dp", 0)] + paths[0], [("dp", 0)] + paths[1]))
    sums_up = [("dp", b) for b in range(1, dp_bits)]
    sums_exchanges = list(zip(up + sums_up, up[::-1] + sums_up[::-1]))

    def piece_bit(step):
        axis, b = step
        bit = b + (tm_bits if axis == "dp" else 0)
        return bit - under if bit >= under else None

    a_split = [piece_bit(steps[0]) is not None for steps in exchanges]
    c_split = [log2(pieces_c) - 1 - k if k < c_bits else None for k in range(len(exchanges))]

    def order_of(split, count):
        used = [b for b in split if b is not None]
        return used + [b for b in reversed(range(log2(count))) if b not in used]

    orders = [order_of([piece_bit(steps[core]) for steps in exchanges], pieces_a) for core in range(2)]
    order_c = order_of(c_split, pieces_c)
    plan = [(pieces_a, orders, a_split[0]), (pieces_c, [order_c, order_c], True)]
    now_a = pieces_a // 2 if plan[0][2] else pieces_a
    now_c = pieces_c // 2

    at_dp, at_tm = lax.axis_index("dp"), lax.axis_index("tm")
    core = at_dp & 1

    def on_core(values):
        return values[0] + core * (values[1] - values[0])

    def bit_at(step):
        axis, b = step
        return ((at_dp if axis == "dp" else at_tm) >> b) & 1

    bits = [on_core([bit_at(step) for step in steps]) for steps in exchanges]
    sums_bits = [on_core([bit_at(step) for step in steps]) for steps in sums_exchanges]
    shared = [bit_at(step) for step in exchanges[1]]
    mine_c, other_c = on_core(shared), on_core(shared[::-1])
    places = [2 * core + mine_c, 2 * (1 - core) + other_c, 2 * core + 1 - mine_c, 2 * (1 - core) + 1 - other_c]
    places = [place << (log2(pieces_c) - c_bits) for place in places]
    lists = []
    for way in ([b for _, b in up], [b for _, b in up[::-1]]):
        lists.append([sum(((position >> (tm_bits - 1 - j)) & 1) << b for j, b in enumerate(way)) for position in range(tm)])
    first_bit = on_core([0, tm_bits - 1])
    lead = (at_tm >> first_bit) & 1
    quarters = [on_core([lists[0][j], lists[1][j]]) for j in range(tm // 2)]
    send_codes = [(q + ((1 - lead) << first_bit)) * per_shard for q in quarters]
    keep_codes = [(q + (lead << first_bit)) * per_shard for q in quarters]
    differ = at_tm ^ (at_tm + 1)
    ways = [sum(((differ >> b) & 1) << j for j, b in enumerate(way)) for way in (
        list(range(tm_bits)), list(reversed(range(tm_bits))))]
    row_code = jnp.where(at_tm + 1 < tm, on_core(ways), 0)
    if turned and not mixed:
        start = ((at_dp * tm + at_tm) * owner_rows) & (LANES - 1)
    else:
        start = on_core([(at_dp * tm + at_tm) * owner_rows, (at_tm >> 1) * owner_rows if mixed else (
            at_dp * tm + at_tm) * owner_rows]) & (LANES - 1)
    at_start = len(bits)
    at_codes = at_start + 1
    at_pieces = at_codes + tm
    at_sums = at_pieces + len(places)
    at_row = at_sums + len(sums_bits)
    info = jnp.stack(bits + [start] + send_codes + keep_codes + places + sums_bits + [row_code]).astype(jnp.int32)

    halo = shifted(feats[-2:], "tm", 1)
    idle = call(idle_kernel, shape((8, LANES), F32), [info], flops=10 ** 11)
    weight, proj, codes = conv_weight, proj_weight, codes[0]
    unfold, conv, chosen = call(
        local_kernel,
        [shape((frames, width), BF16), shape((frames, channels), F32), shape((levels, frames, dz), BF16)],
        [info, feats, weight, conv_bias[None, :], codes, codebooks],
        after=[idle],
        scratch=[VMEM((channels // LANES, rows_in + 8, LANES), F32)],
    )

    extra = 4 * (-(-channels // LANES // 8) * 8)
    code_rows = -(-(2 * -(-frames // dz)) // 16) * 16
    corr_rows = (now_a + now_c) * dz
    rows_b = frames + code_rows
    unfold, hidden, latent_grad, flipped, own, send = call(
        functools.partial(forward_kernel, plan),
        [shape((frames, width), BF16), shape((frames, channels), BF16), shape((frames, dz), BF16),
         shape((dz, frames), BF16), shape((rows_b, dz), BF16),
         shape((corr_rows + rows_b * (dz // LANES), LANES), BF16)],
        [info, halo, unfold, conv, chosen, weight, proj, codes],
        aliases={2: 0},
    )
    got = swapped(send, exchanges[0])
    keep_a, keep_c, hidden_grad, extras, row = call(
        functools.partial(rest_kernel, plan),
        [shape((now_a * dz, LANES), F32), shape((now_c * dz, LANES), F32), shape((frames, channels), BF16),
         shape((extra, LANES), F32), shape((16, channels), BF16)],
        [info, flipped, unfold, hidden, latent_grad, proj],
        after=[send],
    )

    def halves_at(k):
        nonlocal now_a, now_c
        halves = [(now_a * dz, a_split[k]), (now_c * dz, c_split[k] is not None)]
        now_a = now_a // 2 if halves[0][1] else now_a
        now_c = now_c // 2 if halves[1][1] else now_c
        return halves, now_a * dz, now_c * dz + extra

    halves, rows_a, rows_c = halves_at(1)
    send, keep_a, keep_c = call(
        functools.partial(first_step_kernel, halves, 1),
        [shape((rows_a + rows_c, LANES), BF16), shape((rows_a, LANES), F32), shape((rows_c, LANES), F32)],
        [info, got, keep_a, keep_c, extras])
    size = per_shard + 16
    sums_rows = size * (tm // 2)
    sums_send = call(
        functools.partial(sums_kernel, corr_rows, frames, at_codes, per_shard),
        shape((sums_rows, dz), BF16),
        [info, got, own, row],
        after=[send])
    sums_keep = call(
        functools.partial(sums_kernel, corr_rows, frames, at_codes + tm // 2, per_shard),
        shape((sums_rows, dz), F32),
        [info, got, own, row],
        after=[sums_send])
    sums_got = swapped(sums_send, sums_exchanges[0])
    got = swapped(send, exchanges[1])
    known = row
    ordered = [sums_keep]
    for k in range(2, len(exchanges)):
        halves, rows_a, rows_c = halves_at(k)
        spare = 16 * (k == len(exchanges) - 1)
        send, keep_a, keep_c = call(
            functools.partial(step_kernel, halves, k, mixed and k == dp_bits),
            [shape((rows_a + rows_c + spare, LANES), BF16), shape((rows_a, LANES), F32), shape((rows_c, LANES), F32)],
            [info, got, keep_a, keep_c],
            after=ordered)
        got = swapped(send, exchanges[k])
        halved = sums_exchanges[k - 1][0][0] == "tm"
        sums_rows = sums_rows // 2 if halved else sums_rows
        row_step = k - 2 if k - 2 < tm_bits else None
        outs = call(
            functools.partial(sums_step_kernel, halved, at_sums + k - 1, row_step, (per_shard, at_row)),
            [shape((sums_rows, dz), BF16), shape((sums_rows, dz), F32)]
            + [shape((16, channels), BF16)] * (row_step is not None),
            [info, sums_got, sums_keep] + [known] * (row_step is not None),
            after=[send])
        sums_send, sums_keep = outs[:2]
        known = outs[2] if row_step is not None else known
        sums_got = swapped(sums_send, sums_exchanges[k - 1])
        ordered = [sums_send]
    assert now_a == 1 and sums_rows == size
    feat_grad, last = call(
        feat_kernel,
        shape((rows_in, channels), BF16),
        [info, hidden_grad, known, weight],
        after=[sums_send],
        token=True,
        scratch=[VMEM((frames + 8, channels), F32), VMEM((channels // LANES, rows_in, LANES), F32)],
    )

    corr, piece, mine = call(
        functools.partial(last_kernel, rows_a, rows_c - extra),
        [shape((rows_a, LANES), F32), shape((rows_c - extra, LANES), BF16),
         shape((rows_c + size * (dz // LANES), LANES), BF16)],
        [info, got, keep_a, keep_c, sums_got, sums_keep],
        after=[last])
    parts = [piece, swapped(mine, exchanges[0]), swapped(piece, exchanges[1]), crossed(piece, exchanges[1])]
    conv_grad, last = call(
        functools.partial(conv_out_kernel, total_frames, at_start),
        shape((owner_rows, channels), F32),
        [info, corr, proj],
        after=[piece],
        token=True,
        scratch=[VMEM((LANES, channels), F32)],
    )
    proj_grad, bias_grad, code_means, code_usage = call(
        functools.partial(out_kernel, total_frames, book_size / total_frames, dz, at_pieces, now_c, extra),
        [shape((channels, dz), F32), shape((1, channels), F32), shape((levels, per_shard, dz), BF16),
         shape((levels, per_shard), F32)],
        [info, mine] + parts,
        after=[last],
    )
    return feat_grad, conv_grad, bias_grad[0], proj_grad, code_means, code_usage


def solution(mesh):
    placed = (P(("dp", "tm"), None), P("dp", None, "tm"), P(), P(), P(), P())
    return jax.shard_map(
        shards,
        mesh=mesh,
        in_specs=placed,
        out_specs=(
            P(("dp", "tm"), None),
            P(("dp", "tm"), None),
            P(),
            P(),
            P(None, "tm", None),
            P(None, "tm"),
        ),
        check_vma=False,
    )
```

```python
import functools

import jax
import jax.numpy as jnp
from jax import lax
from jax.experimental import pallas as pl
from jax.experimental.pallas import tpu as pltpu
from jax.sharding import PartitionSpec as P

BF16 = jnp.bfloat16
F32 = jnp.float32
LANES = 128
VMEM_LIMIT = 16 * 1024 * 1024


def log2(value):
    assert value & (value - 1) == 0
    return value.bit_length() - 1


def nn(a, b):
    return lax.dot_general(a, b, (((1,), (0,)), ((), ())), preferred_element_type=F32)


def nt(a, b):
    return lax.dot_general(a, b, (((1,), (1,)), ((), ())), preferred_element_type=F32)


VMEM = pltpu.VMEM


def call(body, out_shape, args, after=(), scratch=(), aliases=None, token=False, flops=0):
    count = len(args)
    many = isinstance(out_shape, (list, tuple))
    shapes = list(out_shape) if many else [out_shape]

    def kernel(*refs):
        ends = count + len(after)
        if token:
            refs[ends + len(shapes)][...] = jnp.zeros((8, LANES), F32)
            refs = refs[:ends + len(shapes)] + refs[ends + len(shapes) + 1:]
        body(*refs[:count], *refs[ends:])

    specs = [pl.BlockSpec(memory_space=pltpu.SMEM)]
    specs += [pl.BlockSpec(memory_space=VMEM)] * (count - 1)
    specs += [pl.BlockSpec(memory_space=pl.ANY)] * len(after)
    shown = shapes + [shape((8, LANES), F32)] * token
    outs = pl.pallas_call(
        kernel,
        out_shape=shown,
        in_specs=specs,
        out_specs=[pl.BlockSpec(memory_space=VMEM)] * len(shown),
        scratch_shapes=list(scratch),
        input_output_aliases=aliases or {},
        compiler_params=pltpu.CompilerParams(vmem_limit_bytes=VMEM_LIMIT),
        cost_estimate=pl.CostEstimate(flops=flops, bytes_accessed=0, transcendentals=0),
    )(*args, *after)
    return outs if len(shown) > 1 else outs[0]


def shape(dims, dtype):
    return jax.ShapeDtypeStruct(dims, dtype)


def digits_of(value):
    high = value.astype(BF16).astype(F32)
    rest = value - high
    middle = rest.astype(BF16).astype(F32)
    low = (rest - middle).astype(BF16).astype(F32)
    return high, middle, low


def one_hot(codes, axis_codes, first, count):
    frames = codes.shape[1 - axis_codes]
    dims = (count, frames) if axis_codes == 0 else (frames, count)
    places = lax.broadcasted_iota(jnp.int32, dims, axis_codes) + first
    return jnp.where(codes == places, 1.0, 0.0).astype(BF16)


def halo_kernel(info, rows, out):
    out[...] = rows[...]


def local_kernel(info, feats, weight, bias, codes, books, unfold, conv, chosen, wide):
    rows, channels = feats.shape
    frames = rows // 2
    for j in range(channels // LANES):
        wide[j, 0:8, :] = jnp.zeros((8, LANES), F32)
        wide[j, 8:, :] = feats[:, j * LANES:(j + 1) * LANES].astype(F32)
        for tap in range(4):
            start = tap * channels + j * LANES
            unfold[:, start:start + LANES] = wide[j, pl.ds(6 + tap, frames, stride=2), :].astype(BF16)
    conv[...] = nn(unfold[...], weight[...]) + bias[...]
    levels = books.shape[0]
    padded = jnp.concatenate([codes[...].astype(F32), jnp.zeros((8 - levels, frames), F32)], 0)
    tall = jnp.transpose(padded).astype(jnp.int32)
    for level in range(levels):
        matches = one_hot(tall[:, level:level + 1], 1, 0, books.shape[1])
        chosen[level] = nn(matches, books[level]).astype(BF16)


def walk(orders, halved, count):
    start = 1 if halved else 0
    shown = count // 2 if halved else count
    bits = log2(shown)
    step = 2 if shown > 1 and all(order[-1] == 0 for order in orders) else 1
    for position in range(0, shown, step):
        yield position, [
            sum(((position >> (bits - 1 - k)) & 1) << bit for k, bit in enumerate(order[start:])) for order in orders
        ], step


def correlate(flipped, sources, plan, core, bit, out):
    dz = flipped.shape[0]
    at = 0
    for source, (count, orders, halved) in zip(sources, plan):
        for position, pieces, step in walk(orders, halved, count):
            column = pieces[0] + core * (pieces[1] - pieces[0])
            if halved:
                column = column + (bit << orders[0][0])
            column = pl.multiple_of(column * LANES, LANES)
            product = nn(flipped, source[:, pl.ds(column, step * LANES)])
            for j in range(step):
                top = (at + position + j) * dz
                out[top:top + dz, :] = product[:, j * LANES:(j + 1) * LANES].astype(out.dtype)
        at += count // 2 if halved else count
    return at * dz


def code_digits(codes, dz, rows):
    parts = []
    for part in (codes >> 8, codes & 255):
        for start in range(0, codes.shape[1], dz):
            piece = part[:, start:start + dz].astype(F32)
            if piece.shape[1] < dz:
                piece = jnp.concatenate([piece, jnp.zeros((1, dz - piece.shape[1]), F32)], 1)
            parts.append(piece)
    parts.append(jnp.zeros((rows - len(parts), dz), F32))
    return jnp.concatenate(parts, 0).astype(BF16)


def codes_of(block, frames):
    dz = block.shape[1]
    per = -(-frames // dz)
    digits = block[...].astype(F32)
    parts = [jnp.concatenate([digits[k * per + j:k * per + j + 1, :] for j in range(per)], 1)[:, :frames]
             for k in range(2)]
    return (parts[0] * 256.0 + parts[1]).astype(jnp.int32)


def forward_kernel(plan, info, halo, unfold_in, conv, chosen, weight, proj, codes,
                   unfold, hidden, latent_grad, flipped, own, send):
    frames, width = unfold.shape
    half = width // 2
    dz = proj.shape[1]
    row = lax.broadcasted_iota(jnp.int32, (16, half), 0)
    left = jnp.concatenate([halo[0:1, :], halo[1:2, :]], 1).astype(F32)
    head = jnp.where(row == 0, jnp.broadcast_to(left, (16, half)), 0.0)
    unfold[0:16, 0:half] = (unfold_in[0:16, 0:half].astype(F32) + head).astype(BF16)
    fix = nn(head.astype(BF16), weight[0:half, :])
    hidden[...] = jnp.concatenate([conv[0:16, :] + fix, conv[16:, :]], 0).astype(BF16)
    latent = nn(hidden[...], proj[...])
    once = latent - chosen[0].astype(F32)
    total = once + (once - chosen[1].astype(F32))
    latent_grad[...] = total.astype(BF16)
    flipped[...] = jnp.transpose(latent_grad[...].astype(F32)).astype(BF16)
    bit = info[0]
    at = correlate(flipped[...], (unfold, hidden), plan, 1 - bit, 1 - bit, send)
    code_rows = own.shape[0] - frames
    digits = [code_digits(codes[level:level + 1], dz, code_rows) for level in range(2)]
    own[0:frames, :] = jnp.where(bit == 1, once, latent).astype(BF16)
    own[frames:, :] = jnp.where(bit == 1, digits[1], digits[0])
    other = jnp.where(bit == 1, latent, once).astype(BF16)
    other_digits = jnp.where(bit == 1, digits[0], digits[1])
    for j in range(dz // LANES):
        send[at:at + frames, :] = other[:, j * LANES:(j + 1) * LANES]
        send[at + frames:at + frames + code_rows, :] = other_digits[:, j * LANES:(j + 1) * LANES]
        at += frames + code_rows


def rest_kernel(plan, info, flipped, unfold, hidden, latent_grad, proj, keep_a, keep_c, hidden_grad, extras, row):
    bit = info[0]
    correlate(flipped[...], (unfold,), plan[:1], bit, bit, keep_a)
    correlate(flipped[...], (hidden,), plan[1:], bit, bit, keep_c)
    back = nt(latent_grad[...], proj[...]).astype(BF16)
    hidden_grad[...] = back
    row[...] = back[0:16, :]
    stride = extras.shape[0] // 4
    extras[...] = jnp.zeros(extras.shape, F32)
    sums = jnp.sum(back.astype(F32), 0, keepdims=True)
    for digit, part in enumerate(digits_of(sums)):
        for j in range(sums.shape[1] // LANES):
            extras[digit * stride + j:digit * stride + j + 1, :] = part[:, j * LANES:(j + 1) * LANES]


def split_sum(halved, bit, got, at, kept, rows, send, to, keep):
    if halved:
        half = rows // 2
        away = pl.multiple_of((1 - bit) * half, 16)
        home = pl.multiple_of(bit * half, 16)
        send[to:to + half, :] = (kept[pl.ds(away, half), :] + got[pl.ds(at + away, half), :].astype(F32)).astype(BF16)
        keep[0:half, :] = kept[pl.ds(home, half), :] + got[pl.ds(at + home, half), :].astype(F32)
        return half
    total = (kept[0:rows, :] + got[at:at + rows, :].astype(F32)).astype(BF16)
    send[to:to + rows, :] = total
    keep[0:rows, :] = total.astype(F32)
    return rows


def add_digits(mine, theirs):
    stride = mine.shape[0] // 4
    return ((mine[0:stride] + mine[stride:2 * stride]) + mine[2 * stride:3 * stride]) + (
        (theirs[0:stride] + theirs[stride:2 * stride]) + theirs[2 * stride:3 * stride])


def digit_block(value):
    return jnp.concatenate(list(digits_of(value)) + [jnp.zeros_like(value)], 0)


def first_step_kernel(halves, place, info, got, kept_a, kept_c, extras, send, keep_a, keep_c):
    (rows_a, halved_a), (rows_c, halved_c) = halves
    to = split_sum(halved_a, info[place], got, 0, kept_a, rows_a, send, 0, keep_a)
    gone = split_sum(halved_c, info[place], got, rows_a, kept_c, rows_c, send, to, keep_c)
    send[to + gone:, :] = extras[...].astype(BF16)
    keep_c[gone:, :] = extras[...]


def feat_kernel(info, grad, after, weight, out, wide, inter):
    frames, channels = grad.shape
    half = weight.shape[0] // 2
    wide[0:frames, :] = grad[...].astype(F32)
    wide[frames:, :] = jnp.broadcast_to(after[0:1, :].astype(F32), (8, channels))
    ahead = wide[pl.ds(1, frames), :].astype(BF16)
    for parity in range(2):
        rows = pl.ds(parity * (half // 2), half // 2)
        rows_after = pl.ds(half + parity * (half // 2), half // 2)
        both = nt(ahead, weight[rows, :]) + nt(grad[...], weight[rows_after, :])
        for j in range(channels // LANES):
            inter[j, pl.ds(parity, frames, stride=2), :] = both[:, j * LANES:(j + 1) * LANES]
    for j in range(channels // LANES):
        out[:, j * LANES:(j + 1) * LANES] = inter[j].astype(BF16)


def sums_kernel(first, frames, place, count, info, got, own, row, out):
    rows, dz = own.shape
    theirs = jnp.concatenate([got[first + j * rows:first + (j + 1) * rows, :] for j in range(dz // LANES)], 1)
    ones = jnp.ones((8, frames), BF16)
    parts = []
    for block in (own[...], theirs):
        parts.append((block[0:frames, :], codes_of(block[frames:, :], frames)))
    size = count + 16
    riding = [row[...].astype(F32)[0:1, :]]
    for top in range(0, out.shape[0], size):
        total = jnp.zeros((count, dz), F32)
        counts = jnp.zeros((8, count), F32)
        for values, codes in parts:
            matches = one_hot(codes, 0, info[place], count)
            total = total + nn(matches, values)
            counts = counts + nt(ones, matches)
        out[top:top + count, :] = total.astype(out.dtype)
        out[top + count:top + size, :] = count_rows(counts[0:1], dz, riding).astype(out.dtype)
        place += 1


def count_rows(count, width, riding=()):
    high = jnp.floor(count * (1.0 / 65536.0))
    rest = count - high * 65536.0
    middle = jnp.floor(rest * (1.0 / 256.0))
    low = rest - middle * 256.0
    block = jnp.concatenate([high, middle, low], 0)
    if count.shape[1] < width:
        block = jnp.concatenate([block, jnp.zeros((3, width - count.shape[1]), F32)], 1)
    parts = [block]
    for row in riding:
        parts += [row[:, at:at + width] for at in range(0, row.shape[1], width)]
    left = 16 - sum(part.shape[0] for part in parts)
    return jnp.concatenate(parts + [jnp.zeros((left, width), F32)] * (left > 0), 0)


def riding_row(block, index, parts):
    return jnp.concatenate([block[3 + index * parts + j:4 + index * parts + j, :] for j in range(parts)], 1)


def count_of(block, own):
    return (block[0:1] * 65536.0 + block[1:2] * 256.0 + block[2:3])[:, :own]


def sums_step_kernel(halved, place, row_step, row_place, info, got, kept, *refs):
    riding = ()
    if row_step is not None:
        known, refs = refs[0][...].astype(F32), refs[1:]
        after, refs = refs[-1], refs[:-1]
        parts = known.shape[1] // got.shape[1]
        block = got[row_place[0]:row_place[0] + 16, :].astype(F32)
        rows = [known[j:j + 1, :] for j in range(1 << row_step)]
        rows += [riding_row(block, j, parts) for j in range(1 << row_step)]
        if halved:
            riding = rows
            total = rows + [jnp.zeros((16 - len(rows), known.shape[1]), F32)]
            after[...] = jnp.concatenate(total, 0).astype(BF16)
        else:
            wide = jnp.zeros(after.shape, F32)
            for j in range(1, len(rows)):
                wide = jnp.where(info[row_place[1]] == j, jnp.broadcast_to(rows[j], after.shape), wide)
            after[...] = wide.astype(BF16)
    send, keep = refs
    dz = got.shape[1]
    bit = info[place]
    half = kept.shape[0] // 2 if halved else 0
    outs = [(send, (1 - bit) * half), (keep, bit * half)] if halved else [(send, 0)]
    count = row_place[0]
    size = count + 16
    for out, start in outs:
        for top in range(0, keep.shape[0], size):
            here = top + pl.multiple_of(start, 16) if halved else top
            sums = pl.ds(here, count)
            tail = pl.ds(here + count, 16)
            value = kept[sums, :].astype(F32) + got[sums, :].astype(F32)
            number = count_of(kept[tail, :].astype(F32), count) + count_of(got[tail, :].astype(F32), count)
            out[top:top + count, :] = value.astype(out.dtype)
            out[top + count:top + size, :] = count_rows(number, dz, riding).astype(out.dtype)
    if not halved:
        keep[...] = send[0:keep.shape[0], :].astype(F32)


def swap_halves(first, second, core):
    half = LANES // 2
    left = lax.broadcasted_iota(jnp.int32, first.shape, 1) < half
    turned_first, turned_second = pltpu.roll(first, half, 1), pltpu.roll(second, half, 1)
    swapped_first = jnp.where(left, first, turned_second)
    swapped_second = jnp.where(left, turned_first, second)
    return jnp.where(core == 1, swapped_first, first), jnp.where(core == 1, swapped_second, second)


def step_kernel(halves, place, mixed, info, got, kept_a, kept_c, send, keep_a, keep_c):
    (rows_a, halved_a), (rows_c, halved_c) = halves
    if mixed:
        to = rows_a // 2
        total = kept_a[0:rows_a, :] + got[0:rows_a, :].astype(F32)
        first, second = swap_halves(total[0:to, :], total[to:, :], info[0])
        low = info[place] == 0
        send[0:to, :] = jnp.where(low, second, first).astype(BF16)
        keep_a[...] = jnp.where(low, first, second)
    else:
        to = split_sum(halved_a, info[place], got, 0, kept_a, rows_a, send, 0, keep_a)
    gone = split_sum(halved_c, info[place], got, rows_a, kept_c, rows_c, send, to, keep_c)
    block = digit_block(add_digits(kept_c[rows_c:, :], got[rows_a + rows_c:, :].astype(F32)))
    keep_c[gone:, :] = block
    to += gone
    send[to:to + block.shape[0], :] = block.astype(BF16)
    to += block.shape[0]
    if to < send.shape[0]:
        send[to:, :] = jnp.zeros((send.shape[0] - to, LANES), BF16)


def last_kernel(rows_a, rows, info, got, kept_a, kept_c, sums_got, sums_kept, corr, pieces, mine):
    corr[...] = kept_a[...] + got[0:rows_a, :].astype(F32)
    pieces[...] = (kept_c[0:rows, :] + got[rows_a:rows_a + rows, :].astype(F32)).astype(BF16)
    block = digit_block(add_digits(kept_c[rows:, :], got[rows_a + rows:rows_a + kept_c.shape[0], :].astype(F32)))
    mine[0:rows, :] = pieces[...]
    mine[rows:kept_c.shape[0], :] = block.astype(BF16)
    at = kept_c.shape[0]
    count = sums_kept.shape[0] - 16
    number = count_of(sums_kept[count:, :].astype(F32), count) + count_of(sums_got[count:, :].astype(F32), count)
    square = (count, count)
    same = lax.broadcasted_iota(jnp.int32, square, 0) == lax.broadcasted_iota(jnp.int32, square, 1)
    tall = jnp.sum(jnp.where(same, jnp.broadcast_to(number, square), 0.0), 1, keepdims=True)
    total = sums_kept[0:count, :].astype(F32) + sums_got[0:count, :].astype(F32)
    means = (total / jnp.maximum(tall, 1.0)).astype(BF16)
    digits = count_rows(number, means.shape[1]).astype(BF16)
    for j in range(means.shape[1] // LANES):
        mine[at:at + count, :] = means[:, j * LANES:(j + 1) * LANES]
        mine[at + count:at + count + 16, :] = digits[:, j * LANES:(j + 1) * LANES]
        at += count + 16


def conv_out_kernel(total_frames, place, info, corr, proj, out, wide):
    rows = out.shape[0]
    flipped = jnp.transpose(corr[...])
    high = flipped.astype(BF16)
    low = (flipped - high.astype(F32)).astype(BF16)
    wide[...] = (nt(high, proj[...]) + nt(low, proj[...])) * (1.0 / total_frames)
    start = info[place]
    if rows % 8 == 0:
        out[...] = wide[pl.ds(pl.multiple_of(start, 8), rows), :]
    else:
        taken = wide[0:rows, :]
        for other in range(rows, wide.shape[0], rows):
            taken = jnp.where(start == other, wide[other:other + rows, :], taken)
        out[...] = taken


def out_kernel(total_frames, use_scale, dz, place, inner, extra, info, mine, *refs):
    parts, (out, bias, means, usage) = refs[:-4], refs[-4:]
    theirs = parts[1]
    scale = 1.0 / total_frames
    top = inner * dz
    value = add_digits(mine[top:top + extra, :].astype(F32), theirs[top:top + extra, :].astype(F32)) * scale
    for j in range(bias.shape[1] // LANES):
        bias[:, j * LANES:(j + 1) * LANES] = value[j:j + 1, :]
    bit = info[0]
    count = means.shape[1]
    numbers = []
    for ref, level in ((mine, bit), (theirs, 1 - bit)):
        at = top + extra
        blocks = []
        for j in range(dz // LANES):
            blocks.append(ref[at:at + count + 16, :])
            at += count + 16
        whole = jnp.concatenate(blocks, 1)
        means[level] = whole[0:count, :]
        numbers.append(count_of(whole[count:, :].astype(F32), count) * use_scale)
    usage[0:1, :] = jnp.where(bit == 1, numbers[1], numbers[0])
    usage[1:2, :] = jnp.where(bit == 1, numbers[0], numbers[1])
    for j, ref in enumerate(parts):
        for k in range(inner):
            start = pl.multiple_of((info[place + j] + k) * LANES, LANES)
            turned = jnp.transpose(ref[k * dz:(k + 1) * dz, :])
            out[pl.ds(start, LANES), :] = turned.astype(F32) * scale


def shifted(block, axis, distance):
    devices = range(lax.axis_size(axis))
    route = [(i - distance, i) for i in devices if i - distance in devices]
    return lax.ppermute(block, axis, route)


def swapped(block, steps):
    tm = lax.axis_size("tm")

    def partner(device):
        axis, bit = steps[(device // tm) & 1]
        return device ^ ((1 << bit) * (tm if axis == "dp" else 1))

    route = [(device, partner(device)) for device in range(lax.axis_size("dp") * tm)]
    return lax.ppermute(block, ("dp", "tm"), route)


def crossed(block, steps):
    tm = lax.axis_size("tm")

    def partner(device):
        axis, bit = steps[(device // tm) & 1]
        return device ^ tm ^ ((1 << bit) * (tm if axis == "dp" else 1))

    route = [(device, partner(device)) for device in range(lax.axis_size("dp") * tm)]
    return lax.ppermute(block, ("dp", "tm"), route)


def shards(feats, codes, conv_weight, conv_bias, proj_weight, codebooks):
    dp, tm = lax.axis_size("dp"), lax.axis_size("tm")
    rows_in, channels = feats.shape
    frames = rows_in // 2
    levels, book_size, dz = codebooks.shape
    assert levels == 2
    width = conv_weight.shape[0]
    total_frames = frames * dp * tm
    per_shard = book_size // tm
    dp_bits, tm_bits = log2(dp), log2(tm)
    owner_rows = width // (dp * tm)

    assert dp_bits >= 3 and 1 <= tm_bits <= 2
    pieces_a, pieces_c = width // LANES, channels // LANES
    under = max(dp_bits + tm_bits - log2(pieces_a), 0)
    c_bits = 2
    assert pieces_c >= 4
    whole_bits = [b for b in range(1, dp_bits) if b + tm_bits < under]
    piece_bits = [b for b in range(1, dp_bits) if b + tm_bits >= under]
    paths = [[("dp", b) for b in bits] for bits in (whole_bits + piece_bits, whole_bits[::-1] + piece_bits[::-1])]
    mixed = under == 1 and tm_bits == 2
    turned = mixed or under == 0 or under >= tm_bits
    up = [("tm", b) for b in range(tm_bits)]
    paths[0] += up[::-1]
    paths[1] += up if turned else up[::-1]
    exchanges = list(zip([("dp", 0)] + paths[0], [("dp", 0)] + paths[1]))
    sums_up = [("dp", b) for b in range(1, dp_bits)]
    sums_exchanges = list(zip(up + sums_up, up[::-1] + sums_up[::-1]))

    def piece_bit(step):
        axis, b = step
        bit = b + (tm_bits if axis == "dp" else 0)
        return bit - under if bit >= under else None

    a_split = [piece_bit(steps[0]) is not None for steps in exchanges]
    c_split = [log2(pieces_c) - 1 - k if k < c_bits else None for k in range(len(exchanges))]

    def order_of(split, count):
        used = [b for b in split if b is not None]
        return used + [b for b in reversed(range(log2(count))) if b not in used]

    orders = [order_of([piece_bit(steps[core]) for steps in exchanges], pieces_a) for core in range(2)]
    order_c = order_of(c_split, pieces_c)
    plan = [(pieces_a, orders, a_split[0]), (pieces_c, [order_c, order_c], True)]
    now_a = pieces_a // 2 if plan[0][2] else pieces_a
    now_c = pieces_c // 2

    at_dp, at_tm = lax.axis_index("dp"), lax.axis_index("tm")
    core = at_dp & 1

    def on_core(values):
        return values[0] + core * (values[1] - values[0])

    def bit_at(step):
        axis, b = step
        return ((at_dp if axis == "dp" else at_tm) >> b) & 1

    bits = [on_core([bit_at(step) for step in steps]) for steps in exchanges]
    sums_bits = [on_core([bit_at(step) for step in steps]) for steps in sums_exchanges]
    shared = [bit_at(step) for step in exchanges[1]]
    mine_c, other_c = on_core(shared), on_core(shared[::-1])
    places = [2 * core + mine_c, 2 * (1 - core) + other_c, 2 * core + 1 - mine_c, 2 * (1 - core) + 1 - other_c]
    places = [place << (log2(pieces_c) - c_bits) for place in places]
    lists = []
    for way in ([b for _, b in up], [b for _, b in up[::-1]]):
        lists.append([sum(((position >> (tm_bits - 1 - j)) & 1) << b for j, b in enumerate(way)) for position in range(tm)])
    first_bit = on_core([0, tm_bits - 1])
    lead = (at_tm >> first_bit) & 1
    quarters = [on_core([lists[0][j], lists[1][j]]) for j in range(tm // 2)]
    send_codes = [(q + ((1 - lead) << first_bit)) * per_shard for q in quarters]
    keep_codes = [(q + (lead << first_bit)) * per_shard for q in quarters]
    differ = at_tm ^ (at_tm + 1)
    ways = [sum(((differ >> b) & 1) << j for j, b in enumerate(way)) for way in (
        list(range(tm_bits)), list(reversed(range(tm_bits))))]
    row_code = jnp.where(at_tm + 1 < tm, on_core(ways), 0)
    if turned and not mixed:
        start = ((at_dp * tm + at_tm) * owner_rows) & (LANES - 1)
    else:
        start = on_core([(at_dp * tm + at_tm) * owner_rows, (at_tm >> 1) * owner_rows if mixed else (
            at_dp * tm + at_tm) * owner_rows]) & (LANES - 1)
    at_start = len(bits)
    at_codes = at_start + 1
    at_pieces = at_codes + tm
    at_sums = at_pieces + len(places)
    at_row = at_sums + len(sums_bits)
    info = jnp.stack(bits + [start] + send_codes + keep_codes + places + sums_bits + [row_code]).astype(jnp.int32)

    halo = shifted(call(halo_kernel, shape((2, channels), BF16), [info, feats[-2:]], flops=10 ** 11), "tm", 1)
    weight, proj, codes = conv_weight, proj_weight, codes[0]
    unfold, conv, chosen = call(
        local_kernel,
        [shape((frames, width), BF16), shape((frames, channels), F32), shape((levels, frames, dz), BF16)],
        [info, feats, weight, conv_bias[None, :], codes, codebooks],
        scratch=[VMEM((channels // LANES, rows_in + 8, LANES), F32)],
    )

    extra = 4 * (-(-channels // LANES // 8) * 8)
    code_rows = -(-(2 * -(-frames // dz)) // 16) * 16
    corr_rows = (now_a + now_c) * dz
    rows_b = frames + code_rows
    unfold, hidden, latent_grad, flipped, own, send = call(
        functools.partial(forward_kernel, plan),
        [shape((frames, width), BF16), shape((frames, channels), BF16), shape((frames, dz), BF16),
         shape((dz, frames), BF16), shape((rows_b, dz), BF16),
         shape((corr_rows + rows_b * (dz // LANES), LANES), BF16)],
        [info, halo, unfold, conv, chosen, weight, proj, codes],
        aliases={2: 0},
    )
    got = swapped(send, exchanges[0])
    keep_a, keep_c, hidden_grad, extras, row = call(
        functools.partial(rest_kernel, plan),
        [shape((now_a * dz, LANES), F32), shape((now_c * dz, LANES), F32), shape((frames, channels), BF16),
         shape((extra, LANES), F32), shape((16, channels), BF16)],
        [info, flipped, unfold, hidden, latent_grad, proj],
        after=[send],
    )

    def halves_at(k):
        nonlocal now_a, now_c
        halves = [(now_a * dz, a_split[k]), (now_c * dz, c_split[k] is not None)]
        now_a = now_a // 2 if halves[0][1] else now_a
        now_c = now_c // 2 if halves[1][1] else now_c
        return halves, now_a * dz, now_c * dz + extra

    halves, rows_a, rows_c = halves_at(1)
    send, keep_a, keep_c = call(
        functools.partial(first_step_kernel, halves, 1),
        [shape((rows_a + rows_c, LANES), BF16), shape((rows_a, LANES), F32), shape((rows_c, LANES), F32)],
        [info, got, keep_a, keep_c, extras])
    size = per_shard + 16
    sums_rows = size * (tm // 2)
    sums_send = call(
        functools.partial(sums_kernel, corr_rows, frames, at_codes, per_shard),
        shape((sums_rows, dz), BF16),
        [info, got, own, row],
        after=[send])
    sums_keep = call(
        functools.partial(sums_kernel, corr_rows, frames, at_codes + tm // 2, per_shard),
        shape((sums_rows, dz), F32),
        [info, got, own, row],
        after=[sums_send])
    sums_got = swapped(sums_send, sums_exchanges[0])
    got = swapped(send, exchanges[1])
    known = row
    ordered = [sums_keep]
    for k in range(2, len(exchanges)):
        halves, rows_a, rows_c = halves_at(k)
        spare = 16 * (k == len(exchanges) - 1)
        send, keep_a, keep_c = call(
            functools.partial(step_kernel, halves, k, mixed and k == dp_bits),
            [shape((rows_a + rows_c + spare, LANES), BF16), shape((rows_a, LANES), F32), shape((rows_c, LANES), F32)],
            [info, got, keep_a, keep_c],
            after=ordered)
        got = swapped(send, exchanges[k])
        halved = sums_exchanges[k - 1][0][0] == "tm"
        sums_rows = sums_rows // 2 if halved else sums_rows
        row_step = k - 2 if k - 2 < tm_bits else None
        outs = call(
            functools.partial(sums_step_kernel, halved, at_sums + k - 1, row_step, (per_shard, at_row)),
            [shape((sums_rows, dz), BF16), shape((sums_rows, dz), F32)]
            + [shape((16, channels), BF16)] * (row_step is not None),
            [info, sums_got, sums_keep] + [known] * (row_step is not None),
            after=[send])
        sums_send, sums_keep = outs[:2]
        known = outs[2] if row_step is not None else known
        sums_got = swapped(sums_send, sums_exchanges[k - 1])
        ordered = [sums_send]
    assert now_a == 1 and sums_rows == size
    feat_grad, last = call(
        feat_kernel,
        shape((rows_in, channels), BF16),
        [info, hidden_grad, known, weight],
        after=[sums_send],
        token=True,
        scratch=[VMEM((frames + 8, channels), F32), VMEM((channels // LANES, rows_in, LANES), F32)],
    )

    corr, piece, mine = call(
        functools.partial(last_kernel, rows_a, rows_c - extra),
        [shape((rows_a, LANES), F32), shape((rows_c - extra, LANES), BF16),
         shape((rows_c + size * (dz // LANES), LANES), BF16)],
        [info, got, keep_a, keep_c, sums_got, sums_keep],
        after=[last])
    parts = [piece, swapped(mine, exchanges[0]), swapped(piece, exchanges[1]), crossed(piece, exchanges[1])]
    conv_grad, last = call(
        functools.partial(conv_out_kernel, total_frames, at_start),
        shape((owner_rows, channels), F32),
        [info, corr, proj],
        after=[piece],
        token=True,
        scratch=[VMEM((LANES, channels), F32)],
    )
    proj_grad, bias_grad, code_means, code_usage = call(
        functools.partial(out_kernel, total_frames, book_size / total_frames, dz, at_pieces, now_c, extra),
        [shape((channels, dz), F32), shape((1, channels), F32), shape((levels, per_shard, dz), BF16),
         shape((levels, per_shard), F32)],
        [info, mine] + parts,
        after=[last],
    )
    return feat_grad, conv_grad, bias_grad[0], proj_grad, code_means, code_usage


def solution(mesh):
    placed = (P(("dp", "tm"), None), P("dp", None, "tm"), P(), P(), P(), P())
    return jax.shard_map(
        shards,
        mesh=mesh,
        in_specs=placed,
        out_specs=(
            P(("dp", "tm"), None),
            P(("dp", "tm"), None),
            P(),
            P(),
            P(None, "tm", None),
            P(None, "tm"),
        ),
        check_vma=False,
    )
```

```python
import functools

import jax
import jax.numpy as jnp
from jax import lax
from jax.experimental import pallas as pl
from jax.experimental.pallas import tpu as pltpu
from jax.sharding import PartitionSpec as P

BF16 = jnp.bfloat16
F32 = jnp.float32
LANES = 128
VMEM_LIMIT = 16 * 1024 * 1024


def log2(value):
    assert value & (value - 1) == 0
    return value.bit_length() - 1


def nn(a, b):
    return lax.dot_general(a, b, (((1,), (0,)), ((), ())), preferred_element_type=F32)


def nt(a, b):
    return lax.dot_general(a, b, (((1,), (1,)), ((), ())), preferred_element_type=F32)


VMEM = pltpu.VMEM


def call(body, out_shape, args, after=(), scratch=(), aliases=None, token=False, flops=0):
    count = len(args)
    many = isinstance(out_shape, (list, tuple))
    shapes = list(out_shape) if many else [out_shape]

    def kernel(*refs):
        ends = count + len(after)
        if token:
            refs[ends + len(shapes)][...] = jnp.zeros((8, LANES), F32)
            refs = refs[:ends + len(shapes)] + refs[ends + len(shapes) + 1:]
        body(*refs[:count], *refs[ends:])

    specs = [pl.BlockSpec(memory_space=pltpu.SMEM)]
    specs += [pl.BlockSpec(memory_space=VMEM)] * (count - 1)
    specs += [pl.BlockSpec(memory_space=pl.ANY)] * len(after)
    shown = shapes + [shape((8, LANES), F32)] * token
    outs = pl.pallas_call(
        kernel,
        out_shape=shown,
        in_specs=specs,
        out_specs=[pl.BlockSpec(memory_space=VMEM)] * len(shown),
        scratch_shapes=list(scratch),
        input_output_aliases=aliases or {},
        compiler_params=pltpu.CompilerParams(vmem_limit_bytes=VMEM_LIMIT),
        cost_estimate=pl.CostEstimate(flops=flops, bytes_accessed=0, transcendentals=0),
    )(*args, *after)
    return outs if len(shown) > 1 else outs[0]


def shape(dims, dtype):
    return jax.ShapeDtypeStruct(dims, dtype)


def digits_of(value):
    high = value.astype(BF16).astype(F32)
    rest = value - high
    middle = rest.astype(BF16).astype(F32)
    low = (rest - middle).astype(BF16).astype(F32)
    return high, middle, low


def one_hot(codes, axis_codes, first, count):
    frames = codes.shape[1 - axis_codes]
    dims = (count, frames) if axis_codes == 0 else (frames, count)
    places = lax.broadcasted_iota(jnp.int32, dims, axis_codes) + first
    return jnp.where(codes == places, 1.0, 0.0).astype(BF16)


def halo_kernel(info, rows, out):
    out[...] = rows[...]


def local_kernel(info, feats, weight, bias, codes, books, unfold, conv, chosen, wide):
    rows, channels = feats.shape
    frames = rows // 2
    for j in range(channels // LANES):
        wide[j, 0:8, :] = jnp.zeros((8, LANES), F32)
        wide[j, 8:, :] = feats[:, j * LANES:(j + 1) * LANES].astype(F32)
        for tap in range(4):
            start = tap * channels + j * LANES
            unfold[:, start:start + LANES] = wide[j, pl.ds(6 + tap, frames, stride=2), :].astype(BF16)
    conv[...] = nn(unfold[...], weight[...]) + bias[...]
    levels = books.shape[0]
    padded = jnp.concatenate([codes[...].astype(F32), jnp.zeros((8 - levels, frames), F32)], 0)
    tall = jnp.transpose(padded).astype(jnp.int32)
    for level in range(levels):
        matches = one_hot(tall[:, level:level + 1], 1, 0, books.shape[1])
        chosen[level] = nn(matches, books[level]).astype(BF16)


def walk(orders, halved, count):
    start = 1 if halved else 0
    shown = count // 2 if halved else count
    bits = log2(shown)
    step = 2 if shown > 1 and all(order[-1] == 0 for order in orders) else 1
    for position in range(0, shown, step):
        yield position, [
            sum(((position >> (bits - 1 - k)) & 1) << bit for k, bit in enumerate(order[start:])) for order in orders
        ], step


def correlate(flipped, sources, plan, core, bit, out):
    dz = flipped.shape[0]
    at = 0
    for source, (count, orders, halved) in zip(sources, plan):
        for position, pieces, step in walk(orders, halved, count):
            column = pieces[0] + core * (pieces[1] - pieces[0])
            if halved:
                column = column + (bit << orders[0][0])
            column = pl.multiple_of(column * LANES, LANES)
            product = nn(flipped, source[:, pl.ds(column, step * LANES)])
            for j in range(step):
                top = (at + position + j) * dz
                out[top:top + dz, :] = product[:, j * LANES:(j + 1) * LANES].astype(out.dtype)
        at += count // 2 if halved else count
    return at * dz


def code_digits(codes, dz, rows):
    parts = []
    for part in (codes >> 8, codes & 255):
        for start in range(0, codes.shape[1], dz):
            piece = part[:, start:start + dz].astype(F32)
            if piece.shape[1] < dz:
                piece = jnp.concatenate([piece, jnp.zeros((1, dz - piece.shape[1]), F32)], 1)
            parts.append(piece)
    parts.append(jnp.zeros((rows - len(parts), dz), F32))
    return jnp.concatenate(parts, 0).astype(BF16)


def codes_of(block, frames):
    dz = block.shape[1]
    per = -(-frames // dz)
    digits = block[...].astype(F32)
    parts = [jnp.concatenate([digits[k * per + j:k * per + j + 1, :] for j in range(per)], 1)[:, :frames]
             for k in range(2)]
    return (parts[0] * 256.0 + parts[1]).astype(jnp.int32)


def forward_kernel(plan, info, halo, unfold_in, conv, chosen, weight, proj, codes,
                   unfold, hidden, latent_grad, flipped, own, send):
    frames, width = unfold.shape
    half = width // 2
    dz = proj.shape[1]
    row = lax.broadcasted_iota(jnp.int32, (16, half), 0)
    left = jnp.concatenate([halo[0:1, :], halo[1:2, :]], 1).astype(F32)
    head = jnp.where(row == 0, jnp.broadcast_to(left, (16, half)), 0.0)
    unfold[0:16, 0:half] = (unfold_in[0:16, 0:half].astype(F32) + head).astype(BF16)
    fix = nn(head.astype(BF16), weight[0:half, :])
    hidden[...] = jnp.concatenate([conv[0:16, :] + fix, conv[16:, :]], 0).astype(BF16)
    latent = nn(hidden[...], proj[...])
    once = latent - chosen[0].astype(F32)
    total = once + (once - chosen[1].astype(F32))
    latent_grad[...] = total.astype(BF16)
    flipped[...] = jnp.transpose(latent_grad[...].astype(F32)).astype(BF16)
    bit = info[0]
    at = correlate(flipped[...], (unfold, hidden), plan, 1 - bit, 1 - bit, send)
    code_rows = own.shape[0] - frames
    digits = [code_digits(codes[level:level + 1], dz, code_rows) for level in range(2)]
    own[0:frames, :] = jnp.where(bit == 1, once, latent).astype(BF16)
    own[frames:, :] = jnp.where(bit == 1, digits[1], digits[0])
    other = jnp.where(bit == 1, latent, once).astype(BF16)
    other_digits = jnp.where(bit == 1, digits[0], digits[1])
    for j in range(dz // LANES):
        send[at:at + frames, :] = other[:, j * LANES:(j + 1) * LANES]
        send[at + frames:at + frames + code_rows, :] = other_digits[:, j * LANES:(j + 1) * LANES]
        at += frames + code_rows


def rest_kernel(plan, info, flipped, unfold, hidden, latent_grad, proj, keep_a, keep_c, hidden_grad, extras, row):
    bit = info[0]
    correlate(flipped[...], (unfold,), plan[:1], bit, bit, keep_a)
    correlate(flipped[...], (hidden,), plan[1:], bit, bit, keep_c)
    back = nt(latent_grad[...], proj[...]).astype(BF16)
    hidden_grad[...] = back
    row[...] = back[0:16, :]
    stride = extras.shape[0] // 4
    extras[...] = jnp.zeros(extras.shape, F32)
    sums = jnp.sum(back.astype(F32), 0, keepdims=True)
    for digit, part in enumerate(digits_of(sums)):
        for j in range(sums.shape[1] // LANES):
            extras[digit * stride + j:digit * stride + j + 1, :] = part[:, j * LANES:(j + 1) * LANES]


def split_sum(halved, bit, got, at, kept, rows, send, to, keep):
    if halved:
        half = rows // 2
        away = pl.multiple_of((1 - bit) * half, 16)
        home = pl.multiple_of(bit * half, 16)
        send[to:to + half, :] = (kept[pl.ds(away, half), :] + got[pl.ds(at + away, half), :].astype(F32)).astype(BF16)
        keep[0:half, :] = kept[pl.ds(home, half), :] + got[pl.ds(at + home, half), :].astype(F32)
        return half
    total = (kept[0:rows, :] + got[at:at + rows, :].astype(F32)).astype(BF16)
    send[to:to + rows, :] = total
    keep[0:rows, :] = total.astype(F32)
    return rows


def add_digits(mine, theirs):
    stride = mine.shape[0] // 4
    return ((mine[0:stride] + mine[stride:2 * stride]) + mine[2 * stride:3 * stride]) + (
        (theirs[0:stride] + theirs[stride:2 * stride]) + theirs[2 * stride:3 * stride])


def digit_block(value):
    return jnp.concatenate(list(digits_of(value)) + [jnp.zeros_like(value)], 0)


def first_step_kernel(halves, place, info, got, kept_a, kept_c, extras, send, keep_a, keep_c):
    (rows_a, halved_a), (rows_c, halved_c) = halves
    to = split_sum(halved_a, info[place], got, 0, kept_a, rows_a, send, 0, keep_a)
    gone = split_sum(halved_c, info[place], got, rows_a, kept_c, rows_c, send, to, keep_c)
    send[to + gone:, :] = extras[...].astype(BF16)
    keep_c[gone:, :] = extras[...]


def feat_kernel(info, grad, after, weight, out, wide, inter):
    frames, channels = grad.shape
    half = weight.shape[0] // 2
    wide[0:frames, :] = grad[...].astype(F32)
    wide[frames:, :] = jnp.broadcast_to(after[0:1, :].astype(F32), (8, channels))
    ahead = wide[pl.ds(1, frames), :].astype(BF16)
    for parity in range(2):
        rows = pl.ds(parity * (half // 2), half // 2)
        rows_after = pl.ds(half + parity * (half // 2), half // 2)
        both = nt(ahead, weight[rows, :]) + nt(grad[...], weight[rows_after, :])
        for j in range(channels // LANES):
            inter[j, pl.ds(parity, frames, stride=2), :] = both[:, j * LANES:(j + 1) * LANES]
    for j in range(channels // LANES):
        out[:, j * LANES:(j + 1) * LANES] = inter[j].astype(BF16)


def sums_kernel(first, frames, place, count, info, got, own, row, out):
    rows, dz = own.shape
    theirs = jnp.concatenate([got[first + j * rows:first + (j + 1) * rows, :] for j in range(dz // LANES)], 1)
    ones = jnp.ones((8, frames), BF16)
    parts = []
    for block in (own[...], theirs):
        parts.append((block[0:frames, :], codes_of(block[frames:, :], frames)))
    size = count + 16
    riding = [row[...].astype(F32)[0:1, :]]
    for top in range(0, out.shape[0], size):
        total = jnp.zeros((count, dz), F32)
        counts = jnp.zeros((8, count), F32)
        for values, codes in parts:
            matches = one_hot(codes, 0, info[place], count)
            total = total + nn(matches, values)
            counts = counts + nt(ones, matches)
        out[top:top + count, :] = total.astype(out.dtype)
        out[top + count:top + size, :] = count_rows(counts[0:1], dz, riding).astype(out.dtype)
        place += 1


def count_rows(count, width, riding=()):
    high = jnp.floor(count * (1.0 / 65536.0))
    rest = count - high * 65536.0
    middle = jnp.floor(rest * (1.0 / 256.0))
    low = rest - middle * 256.0
    block = jnp.concatenate([high, middle, low], 0)
    if count.shape[1] < width:
        block = jnp.concatenate([block, jnp.zeros((3, width - count.shape[1]), F32)], 1)
    parts = [block]
    for row in riding:
        parts += [row[:, at:at + width] for at in range(0, row.shape[1], width)]
    left = 16 - sum(part.shape[0] for part in parts)
    return jnp.concatenate(parts + [jnp.zeros((left, width), F32)] * (left > 0), 0)


def riding_row(block, index, parts):
    return jnp.concatenate([block[3 + index * parts + j:4 + index * parts + j, :] for j in range(parts)], 1)


def count_of(block, own):
    return (block[0:1] * 65536.0 + block[1:2] * 256.0 + block[2:3])[:, :own]


def sums_step_kernel(halved, place, row_step, row_place, info, got, kept, *refs):
    riding = ()
    if row_step is not None:
        known, refs = refs[0][...].astype(F32), refs[1:]
        after, refs = refs[-1], refs[:-1]
        parts = known.shape[1] // got.shape[1]
        block = got[row_place[0]:row_place[0] + 16, :].astype(F32)
        rows = [known[j:j + 1, :] for j in range(1 << row_step)]
        rows += [riding_row(block, j, parts) for j in range(1 << row_step)]
        if halved:
            riding = rows
            total = rows + [jnp.zeros((16 - len(rows), known.shape[1]), F32)]
            after[...] = jnp.concatenate(total, 0).astype(BF16)
        else:
            wide = jnp.zeros(after.shape, F32)
            for j in range(1, len(rows)):
                wide = jnp.where(info[row_place[1]] == j, jnp.broadcast_to(rows[j], after.shape), wide)
            after[...] = wide.astype(BF16)
    send, keep = refs
    dz = got.shape[1]
    bit = info[place]
    half = kept.shape[0] // 2 if halved else 0
    outs = [(send, (1 - bit) * half), (keep, bit * half)] if halved else [(send, 0)]
    count = row_place[0]
    size = count + 16
    for out, start in outs:
        for top in range(0, keep.shape[0], size):
            here = top + pl.multiple_of(start, 16) if halved else top
            sums = pl.ds(here, count)
            tail = pl.ds(here + count, 16)
            value = kept[sums, :].astype(F32) + got[sums, :].astype(F32)
            number = count_of(kept[tail, :].astype(F32), count) + count_of(got[tail, :].astype(F32), count)
            out[top:top + count, :] = value.astype(out.dtype)
            out[top + count:top + size, :] = count_rows(number, dz, riding).astype(out.dtype)
    if not halved:
        keep[...] = send[0:keep.shape[0], :].astype(F32)


def swap_halves(first, second, core):
    half = LANES // 2
    left = lax.broadcasted_iota(jnp.int32, first.shape, 1) < half
    turned_first, turned_second = pltpu.roll(first, half, 1), pltpu.roll(second, half, 1)
    swapped_first = jnp.where(left, first, turned_second)
    swapped_second = jnp.where(left, turned_first, second)
    return jnp.where(core == 0, swapped_first, first), jnp.where(core == 0, swapped_second, second)


def step_kernel(halves, place, mixed, info, got, kept_a, kept_c, send, keep_a, keep_c):
    (rows_a, halved_a), (rows_c, halved_c) = halves
    if mixed:
        to = rows_a // 2
        total = kept_a[0:rows_a, :] + got[0:rows_a, :].astype(F32)
        first, second = swap_halves(total[0:to, :], total[to:, :], info[0])
        low = info[place] == 0
        send[0:to, :] = jnp.where(low, second, first).astype(BF16)
        keep_a[...] = jnp.where(low, first, second)
    else:
        to = split_sum(halved_a, info[place], got, 0, kept_a, rows_a, send, 0, keep_a)
    gone = split_sum(halved_c, info[place], got, rows_a, kept_c, rows_c, send, to, keep_c)
    block = digit_block(add_digits(kept_c[rows_c:, :], got[rows_a + rows_c:, :].astype(F32)))
    keep_c[gone:, :] = block
    to += gone
    send[to:to + block.shape[0], :] = block.astype(BF16)
    to += block.shape[0]
    if to < send.shape[0]:
        send[to:, :] = jnp.zeros((send.shape[0] - to, LANES), BF16)


def last_kernel(rows_a, rows, info, got, kept_a, kept_c, sums_got, sums_kept, corr, pieces, mine):
    corr[...] = kept_a[...] + got[0:rows_a, :].astype(F32)
    pieces[...] = (kept_c[0:rows, :] + got[rows_a:rows_a + rows, :].astype(F32)).astype(BF16)
    block = digit_block(add_digits(kept_c[rows:, :], got[rows_a + rows:rows_a + kept_c.shape[0], :].astype(F32)))
    mine[0:rows, :] = pieces[...]
    mine[rows:kept_c.shape[0], :] = block.astype(BF16)
    at = kept_c.shape[0]
    count = sums_kept.shape[0] - 16
    number = count_of(sums_kept[count:, :].astype(F32), count) + count_of(sums_got[count:, :].astype(F32), count)
    square = (count, count)
    same = lax.broadcasted_iota(jnp.int32, square, 0) == lax.broadcasted_iota(jnp.int32, square, 1)
    tall = jnp.sum(jnp.where(same, jnp.broadcast_to(number, square), 0.0), 1, keepdims=True)
    total = sums_kept[0:count, :].astype(F32) + sums_got[0:count, :].astype(F32)
    means = (total / jnp.maximum(tall, 1.0)).astype(BF16)
    digits = count_rows(number, means.shape[1]).astype(BF16)
    for j in range(means.shape[1] // LANES):
        mine[at:at + count, :] = means[:, j * LANES:(j + 1) * LANES]
        mine[at + count:at + count + 16, :] = digits[:, j * LANES:(j + 1) * LANES]
        at += count + 16


def conv_out_kernel(total_frames, place, info, corr, proj, out, wide):
    rows = out.shape[0]
    flipped = jnp.transpose(corr[...])
    high = flipped.astype(BF16)
    low = (flipped - high.astype(F32)).astype(BF16)
    wide[...] = (nt(high, proj[...]) + nt(low, proj[...])) * (1.0 / total_frames)
    start = info[place]
    if rows % 8 == 0:
        out[...] = wide[pl.ds(pl.multiple_of(start, 8), rows), :]
    else:
        taken = wide[0:rows, :]
        for other in range(rows, wide.shape[0], rows):
            taken = jnp.where(start == other, wide[other:other + rows, :], taken)
        out[...] = taken


def out_kernel(total_frames, use_scale, dz, place, inner, extra, info, mine, *refs):
    parts, (out, bias, means, usage) = refs[:-4], refs[-4:]
    theirs = parts[1]
    scale = 1.0 / total_frames
    top = inner * dz
    value = add_digits(mine[top:top + extra, :].astype(F32), theirs[top:top + extra, :].astype(F32)) * scale
    for j in range(bias.shape[1] // LANES):
        bias[:, j * LANES:(j + 1) * LANES] = value[j:j + 1, :]
    bit = info[0]
    count = means.shape[1]
    numbers = []
    for ref, level in ((mine, bit), (theirs, 1 - bit)):
        at = top + extra
        blocks = []
        for j in range(dz // LANES):
            blocks.append(ref[at:at + count + 16, :])
            at += count + 16
        whole = jnp.concatenate(blocks, 1)
        means[level] = whole[0:count, :]
        numbers.append(count_of(whole[count:, :].astype(F32), count) * use_scale)
    usage[0:1, :] = jnp.where(bit == 1, numbers[1], numbers[0])
    usage[1:2, :] = jnp.where(bit == 1, numbers[0], numbers[1])
    for j, ref in enumerate(parts):
        for k in range(inner):
            start = pl.multiple_of((info[place + j] + k) * LANES, LANES)
            turned = jnp.transpose(ref[k * dz:(k + 1) * dz, :])
            out[pl.ds(start, LANES), :] = turned.astype(F32) * scale


def shifted(block, axis, distance):
    devices = range(lax.axis_size(axis))
    route = [(i - distance, i) for i in devices if i - distance in devices]
    return lax.ppermute(block, axis, route)


def swapped(block, steps):
    tm = lax.axis_size("tm")

    def partner(device):
        axis, bit = steps[(device // tm) & 1]
        return device ^ ((1 << bit) * (tm if axis == "dp" else 1))

    route = [(device, partner(device)) for device in range(lax.axis_size("dp") * tm)]
    return lax.ppermute(block, ("dp", "tm"), route)


def crossed(block, steps):
    tm = lax.axis_size("tm")

    def partner(device):
        axis, bit = steps[(device // tm) & 1]
        return device ^ tm ^ ((1 << bit) * (tm if axis == "dp" else 1))

    route = [(device, partner(device)) for device in range(lax.axis_size("dp") * tm)]
    return lax.ppermute(block, ("dp", "tm"), route)


def shards(feats, codes, conv_weight, conv_bias, proj_weight, codebooks):
    dp, tm = lax.axis_size("dp"), lax.axis_size("tm")
    rows_in, channels = feats.shape
    frames = rows_in // 2
    levels, book_size, dz = codebooks.shape
    assert levels == 2
    width = conv_weight.shape[0]
    total_frames = frames * dp * tm
    per_shard = book_size // tm
    dp_bits, tm_bits = log2(dp), log2(tm)
    owner_rows = width // (dp * tm)

    assert dp_bits >= 3 and 1 <= tm_bits <= 2
    pieces_a, pieces_c = width // LANES, channels // LANES
    under = max(dp_bits + tm_bits - log2(pieces_a), 0)
    c_bits = 2
    assert pieces_c >= 4
    whole_bits = [b for b in range(1, dp_bits) if b + tm_bits < under]
    piece_bits = [b for b in range(1, dp_bits) if b + tm_bits >= under]
    paths = [[("dp", b) for b in bits] for bits in (whole_bits + piece_bits, whole_bits[::-1] + piece_bits[::-1])]
    mixed = under == 1 and tm_bits == 2
    turned = mixed or under == 0 or under >= tm_bits
    up = [("tm", b) for b in range(tm_bits)]
    paths[0] += up if turned else up[::-1]
    paths[1] += up[::-1]
    exchanges = list(zip([("dp", 0)] + paths[0], [("dp", 0)] + paths[1]))
    sums_up = [("dp", b) for b in range(1, dp_bits)]
    sums_exchanges = list(zip(up + sums_up, up[::-1] + sums_up[::-1]))

    def piece_bit(step):
        axis, b = step
        bit = b + (tm_bits if axis == "dp" else 0)
        return bit - under if bit >= under else None

    a_split = [piece_bit(steps[1]) is not None for steps in exchanges]
    c_split = [log2(pieces_c) - 1 - k if k < c_bits else None for k in range(len(exchanges))]

    def order_of(split, count):
        used = [b for b in split if b is not None]
        return used + [b for b in reversed(range(log2(count))) if b not in used]

    orders = [order_of([piece_bit(steps[core]) for steps in exchanges], pieces_a) for core in range(2)]
    order_c = order_of(c_split, pieces_c)
    plan = [(pieces_a, orders, a_split[0]), (pieces_c, [order_c, order_c], True)]
    now_a = pieces_a // 2 if plan[0][2] else pieces_a
    now_c = pieces_c // 2

    at_dp, at_tm = lax.axis_index("dp"), lax.axis_index("tm")
    core = at_dp & 1

    def on_core(values):
        return values[0] + core * (values[1] - values[0])

    def bit_at(step):
        axis, b = step
        return ((at_dp if axis == "dp" else at_tm) >> b) & 1

    bits = [on_core([bit_at(step) for step in steps]) for steps in exchanges]
    sums_bits = [on_core([bit_at(step) for step in steps]) for steps in sums_exchanges]
    shared = [bit_at(step) for step in exchanges[1]]
    mine_c, other_c = on_core(shared), on_core(shared[::-1])
    places = [2 * core + mine_c, 2 * (1 - core) + other_c, 2 * core + 1 - mine_c, 2 * (1 - core) + 1 - other_c]
    places = [place << (log2(pieces_c) - c_bits) for place in places]
    lists = []
    for way in ([b for _, b in up], [b for _, b in up[::-1]]):
        lists.append([sum(((position >> (tm_bits - 1 - j)) & 1) << b for j, b in enumerate(way)) for position in range(tm)])
    first_bit = on_core([0, tm_bits - 1])
    lead = (at_tm >> first_bit) & 1
    quarters = [on_core([lists[0][j], lists[1][j]]) for j in range(tm // 2)]
    send_codes = [(q + ((1 - lead) << first_bit)) * per_shard for q in quarters]
    keep_codes = [(q + (lead << first_bit)) * per_shard for q in quarters]
    differ = at_tm ^ (at_tm + 1)
    ways = [sum(((differ >> b) & 1) << j for j, b in enumerate(way)) for way in (
        list(range(tm_bits)), list(reversed(range(tm_bits))))]
    row_code = jnp.where(at_tm + 1 < tm, on_core(ways), 0)
    if turned and not mixed:
        start = ((at_dp * tm + at_tm) * owner_rows) & (LANES - 1)
    else:
        start = on_core([(at_tm >> 1) * owner_rows if mixed else (at_dp * tm + at_tm) * owner_rows,
                         (at_dp * tm + at_tm) * owner_rows]) & (LANES - 1)
    at_start = len(bits)
    at_codes = at_start + 1
    at_pieces = at_codes + tm
    at_sums = at_pieces + len(places)
    at_row = at_sums + len(sums_bits)
    info = jnp.stack(bits + [start] + send_codes + keep_codes + places + sums_bits + [row_code]).astype(jnp.int32)

    halo = shifted(call(halo_kernel, shape((2, channels), BF16), [info, feats[-2:]], flops=10 ** 11), "tm", 1)
    weight, proj, codes = conv_weight, proj_weight, codes[0]
    unfold, conv, chosen = call(
        local_kernel,
        [shape((frames, width), BF16), shape((frames, channels), F32), shape((levels, frames, dz), BF16)],
        [info, feats, weight, conv_bias[None, :], codes, codebooks],
        scratch=[VMEM((channels // LANES, rows_in + 8, LANES), F32)],
    )

    extra = 4 * (-(-channels // LANES // 8) * 8)
    code_rows = -(-(2 * -(-frames // dz)) // 16) * 16
    corr_rows = (now_a + now_c) * dz
    rows_b = frames + code_rows
    unfold, hidden, latent_grad, flipped, own, send = call(
        functools.partial(forward_kernel, plan),
        [shape((frames, width), BF16), shape((frames, channels), BF16), shape((frames, dz), BF16),
         shape((dz, frames), BF16), shape((rows_b, dz), BF16),
         shape((corr_rows + rows_b * (dz // LANES), LANES), BF16)],
        [info, halo, unfold, conv, chosen, weight, proj, codes],
        aliases={2: 0},
    )
    got = swapped(send, exchanges[0])
    keep_a, keep_c, hidden_grad, extras, row = call(
        functools.partial(rest_kernel, plan),
        [shape((now_a * dz, LANES), F32), shape((now_c * dz, LANES), F32), shape((frames, channels), BF16),
         shape((extra, LANES), F32), shape((16, channels), BF16)],
        [info, flipped, unfold, hidden, latent_grad, proj],
        after=[send],
    )

    def halves_at(k):
        nonlocal now_a, now_c
        halves = [(now_a * dz, a_split[k]), (now_c * dz, c_split[k] is not None)]
        now_a = now_a // 2 if halves[0][1] else now_a
        now_c = now_c // 2 if halves[1][1] else now_c
        return halves, now_a * dz, now_c * dz + extra

    halves, rows_a, rows_c = halves_at(1)
    send, keep_a, keep_c = call(
        functools.partial(first_step_kernel, halves, 1),
        [shape((rows_a + rows_c, LANES), BF16), shape((rows_a, LANES), F32), shape((rows_c, LANES), F32)],
        [info, got, keep_a, keep_c, extras])
    size = per_shard + 16
    sums_rows = size * (tm // 2)
    sums_send = call(
        functools.partial(sums_kernel, corr_rows, frames, at_codes, per_shard),
        shape((sums_rows, dz), BF16),
        [info, got, own, row],
        after=[send])
    sums_keep = call(
        functools.partial(sums_kernel, corr_rows, frames, at_codes + tm // 2, per_shard),
        shape((sums_rows, dz), F32),
        [info, got, own, row],
        after=[sums_send])
    sums_got = swapped(sums_send, sums_exchanges[0])
    got = swapped(send, exchanges[1])
    known = row
    ordered = [sums_keep]
    for k in range(2, len(exchanges)):
        halves, rows_a, rows_c = halves_at(k)
        spare = 16 * (k == len(exchanges) - 1)
        send, keep_a, keep_c = call(
            functools.partial(step_kernel, halves, k, mixed and k == dp_bits),
            [shape((rows_a + rows_c + spare, LANES), BF16), shape((rows_a, LANES), F32), shape((rows_c, LANES), F32)],
            [info, got, keep_a, keep_c],
            after=ordered)
        got = swapped(send, exchanges[k])
        halved = sums_exchanges[k - 1][0][0] == "tm"
        sums_rows = sums_rows // 2 if halved else sums_rows
        row_step = k - 2 if k - 2 < tm_bits else None
        outs = call(
            functools.partial(sums_step_kernel, halved, at_sums + k - 1, row_step, (per_shard, at_row)),
            [shape((sums_rows, dz), BF16), shape((sums_rows, dz), F32)]
            + [shape((16, channels), BF16)] * (row_step is not None),
            [info, sums_got, sums_keep] + [known] * (row_step is not None),
            after=[send])
        sums_send, sums_keep = outs[:2]
        known = outs[2] if row_step is not None else known
        sums_got = swapped(sums_send, sums_exchanges[k - 1])
        ordered = [sums_send]
    assert now_a == 1 and sums_rows == size
    feat_grad, last = call(
        feat_kernel,
        shape((rows_in, channels), BF16),
        [info, hidden_grad, known, weight],
        after=[sums_send],
        token=True,
        scratch=[VMEM((frames + 8, channels), F32), VMEM((channels // LANES, rows_in, LANES), F32)],
    )

    corr, piece, mine = call(
        functools.partial(last_kernel, rows_a, rows_c - extra),
        [shape((rows_a, LANES), F32), shape((rows_c - extra, LANES), BF16),
         shape((rows_c + size * (dz // LANES), LANES), BF16)],
        [info, got, keep_a, keep_c, sums_got, sums_keep],
        after=[last])
    parts = [piece, swapped(mine, exchanges[0]), swapped(piece, exchanges[1]), crossed(piece, exchanges[1])]
    conv_grad, last = call(
        functools.partial(conv_out_kernel, total_frames, at_start),
        shape((owner_rows, channels), F32),
        [info, corr, proj],
        after=[piece],
        token=True,
        scratch=[VMEM((LANES, channels), F32)],
    )
    proj_grad, bias_grad, code_means, code_usage = call(
        functools.partial(out_kernel, total_frames, book_size / total_frames, dz, at_pieces, now_c, extra),
        [shape((channels, dz), F32), shape((1, channels), F32), shape((levels, per_shard, dz), BF16),
         shape((levels, per_shard), F32)],
        [info, mine] + parts,
        after=[last],
    )
    return feat_grad, conv_grad, bias_grad[0], proj_grad, code_means, code_usage


def solution(mesh):
    placed = (P(("dp", "tm"), None), P("dp", None, "tm"), P(), P(), P(), P())
    return jax.shard_map(
        shards,
        mesh=mesh,
        in_specs=placed,
        out_specs=(
            P(("dp", "tm"), None),
            P(("dp", "tm"), None),
            P(),
            P(),
            P(None, "tm", None),
            P(None, "tm"),
        ),
        check_vma=False,
    )
```

```python
import functools

import jax
import jax.numpy as jnp
from jax import lax
from jax.experimental import pallas as pl
from jax.experimental.pallas import tpu as pltpu
from jax.sharding import PartitionSpec as P

BF16 = jnp.bfloat16
F32 = jnp.float32
LANES = 128
VMEM_LIMIT = 16 * 1024 * 1024


def log2(value):
    assert value & (value - 1) == 0
    return value.bit_length() - 1


def nn(a, b):
    return lax.dot_general(a, b, (((1,), (0,)), ((), ())), preferred_element_type=F32)


def nt(a, b):
    return lax.dot_general(a, b, (((1,), (1,)), ((), ())), preferred_element_type=F32)


VMEM = pltpu.VMEM


def call(body, out_shape, args, after=(), scratch=(), aliases=None, token=False, flops=0):
    count = len(args)
    many = isinstance(out_shape, (list, tuple))
    shapes = list(out_shape) if many else [out_shape]

    def kernel(*refs):
        ends = count + len(after)
        if token:
            refs[ends + len(shapes)][...] = jnp.zeros((8, LANES), F32)
            refs = refs[:ends + len(shapes)] + refs[ends + len(shapes) + 1:]
        body(*refs[:count], *refs[ends:])

    specs = [pl.BlockSpec(memory_space=pltpu.SMEM)]
    specs += [pl.BlockSpec(memory_space=VMEM)] * (count - 1)
    specs += [pl.BlockSpec(memory_space=pl.ANY)] * len(after)
    shown = shapes + [shape((8, LANES), F32)] * token
    outs = pl.pallas_call(
        kernel,
        out_shape=shown,
        in_specs=specs,
        out_specs=[pl.BlockSpec(memory_space=VMEM)] * len(shown),
        scratch_shapes=list(scratch),
        input_output_aliases=aliases or {},
        compiler_params=pltpu.CompilerParams(vmem_limit_bytes=VMEM_LIMIT),
        cost_estimate=pl.CostEstimate(flops=flops, bytes_accessed=0, transcendentals=0),
    )(*args, *after)
    return outs if len(shown) > 1 else outs[0]


def shape(dims, dtype):
    return jax.ShapeDtypeStruct(dims, dtype)


def digits_of(value):
    high = value.astype(BF16).astype(F32)
    rest = value - high
    middle = rest.astype(BF16).astype(F32)
    low = (rest - middle).astype(BF16).astype(F32)
    return high, middle, low


def one_hot(codes, axis_codes, first, count):
    frames = codes.shape[1 - axis_codes]
    dims = (count, frames) if axis_codes == 0 else (frames, count)
    places = lax.broadcasted_iota(jnp.int32, dims, axis_codes) + first
    return jnp.where(codes == places, 1.0, 0.0).astype(BF16)


def halo_kernel(info, rows, out):
    out[...] = rows[...]


def walk(orders, halved, count):
    start = 1 if halved else 0
    shown = count // 2 if halved else count
    bits = log2(shown)
    step = 2 if shown > 1 and all(order[-1] == 0 for order in orders) else 1
    for position in range(0, shown, step):
        yield position, [
            sum(((position >> (bits - 1 - k)) & 1) << bit for k, bit in enumerate(order[start:])) for order in orders
        ], step


def correlate(flipped, sources, plan, core, bit, out):
    dz = flipped.shape[0]
    at = 0
    for source, (count, orders, halved) in zip(sources, plan):
        for position, pieces, step in walk(orders, halved, count):
            column = pieces[0] + core * (pieces[1] - pieces[0])
            if halved:
                column = column + (bit << orders[0][0])
            column = pl.multiple_of(column * LANES, LANES)
            product = nn(flipped, source[:, pl.ds(column, step * LANES)])
            for j in range(step):
                top = (at + position + j) * dz
                out[top:top + dz, :] = product[:, j * LANES:(j + 1) * LANES].astype(out.dtype)
        at += count // 2 if halved else count
    return at * dz


def code_digits(codes, dz, rows):
    parts = []
    for part in (codes >> 8, codes & 255):
        for start in range(0, codes.shape[1], dz):
            piece = part[:, start:start + dz].astype(F32)
            if piece.shape[1] < dz:
                piece = jnp.concatenate([piece, jnp.zeros((1, dz - piece.shape[1]), F32)], 1)
            parts.append(piece)
    parts.append(jnp.zeros((rows - len(parts), dz), F32))
    return jnp.concatenate(parts, 0).astype(BF16)


def codes_of(block, frames):
    dz = block.shape[1]
    per = -(-frames // dz)
    digits = block[...].astype(F32)
    parts = [jnp.concatenate([digits[k * per + j:k * per + j + 1, :] for j in range(per)], 1)[:, :frames]
             for k in range(2)]
    return (parts[0] * 256.0 + parts[1]).astype(jnp.int32)


def residuals(hidden, proj, chosen):
    latent = nn(hidden, proj)
    once = latent - chosen[0].astype(F32)
    total = once + (once - chosen[1].astype(F32))
    return latent, once, total.astype(BF16)


def put_columns(out, at, rows, block):
    for j in range(block.shape[1] // LANES):
        out[at + j * rows:at + j * rows + block.shape[0], :] = block[:, j * LANES:(j + 1) * LANES]


def local_kernel(plan, info, feats, weight, bias, codes, books, proj,
                 unfold, hidden, latent_grad, flipped, own, send, first, part, wide, chosen):
    rows, channels = feats.shape
    frames = rows // 2
    dz = proj.shape[1]
    for j in range(channels // LANES):
        wide[j, 0:8, :] = jnp.zeros((8, LANES), F32)
        wide[j, 8:, :] = feats[:, j * LANES:(j + 1) * LANES].astype(F32)
        for tap in range(4):
            start = tap * channels + j * LANES
            unfold[:, start:start + LANES] = wide[j, pl.ds(6 + tap, frames, stride=2), :].astype(BF16)
    conv = nn(unfold[...], weight[...]) + bias[...]
    first[...] = conv[0:16, :]
    hidden[...] = conv.astype(BF16)
    levels = books.shape[0]
    padded = jnp.concatenate([codes[...].astype(F32), jnp.zeros((8 - levels, frames), F32)], 0)
    tall = jnp.transpose(padded).astype(jnp.int32)
    for level in range(levels):
        matches = one_hot(tall[:, level:level + 1], 1, 0, books.shape[1])
        chosen[level] = nn(matches, books[level]).astype(BF16)
    latent, once, grad = residuals(hidden[...], proj[...], chosen)
    latent_grad[...] = grad
    row = lax.broadcasted_iota(jnp.int32, grad.shape, 0)
    flipped[...] = jnp.transpose(jnp.where(row == 0, 0.0, grad.astype(F32))).astype(BF16)
    bit = info[0]
    at = correlate(flipped[...], (unfold, hidden), plan, 1 - bit, 1 - bit, part)
    rows_b = own.shape[0]
    code_rows = rows_b - frames
    digits = [code_digits(codes[level:level + 1, :], dz, code_rows) for level in range(2)]
    own[0:frames, :] = jnp.where(bit == 1, once, latent).astype(BF16)
    own[frames:, :] = jnp.where(bit == 1, digits[1], digits[0])
    put_columns(send, at, rows_b, jnp.where(bit == 1, latent, once).astype(BF16))
    put_columns(send, at + frames, rows_b, jnp.where(bit == 1, digits[0], digits[1]))
    for level in range(levels):
        part[at + level * 16 * (dz // LANES):at + (level + 1) * 16 * (dz // LANES), :] = jnp.concatenate(
            [chosen[level, 0:16, j * LANES:(j + 1) * LANES].astype(F32) for j in range(dz // LANES)], 0)


def frame_kernel(plan, info, halo, first, part, weight, proj, unfold_in, hidden_in, grad_in, flipped_in, own_in, send_in,
                 unfold, hidden, latent_grad, flipped, own, send):
    width = unfold.shape[1]
    half = width // 2
    dz = proj.shape[1]
    row = lax.broadcasted_iota(jnp.int32, (16, half), 0)
    left = jnp.concatenate([halo[0:1, :], halo[1:2, :]], 1).astype(F32)
    head = jnp.where(row == 0, jnp.broadcast_to(left, (16, half)), 0.0)
    unfold[0:16, 0:half] = (unfold_in[0:16, 0:half].astype(F32) + head).astype(BF16)
    fix = nn(head.astype(BF16), weight[0:half, :])
    hidden[0:16, :] = (first[...] + fix).astype(BF16)
    top = hidden[0:16, :]
    pieces = part.shape[0] - 32 * (dz // LANES)
    chosen = []
    for level in range(2):
        at = pieces + level * 16 * (dz // LANES)
        chosen.append(jnp.concatenate([part[at + j * 16:at + (j + 1) * 16, :] for j in range(dz // LANES)], 1))
    latent, once, grad = residuals(top, proj[...], chosen)
    latent_grad[0:16, :] = grad
    flipped[:, 0:LANES] = jnp.transpose(latent_grad[0:LANES, :].astype(F32)).astype(BF16)
    column = flipped[:, 0:LANES].astype(F32)[:, 0:1]
    bit = info[0]
    at = 0
    for source, (count, orders, halved) in zip((unfold, hidden), plan):
        rows = source[0:16, :].astype(F32)[0:1, :]
        for position, places, step in walk(orders, halved, count):
            for j in range(step):
                offsets = [places[0] + j, places[1] + j]
                low = [offset for offset in offsets]
                high = [offset + (1 << orders[0][0] if halved else 0) for offset in offsets]
                picked = [rows[:, k * LANES:(k + 1) * LANES] for k in low + high]
                piece = jnp.where(bit == 1, picked[0], picked[3]) if halved else jnp.where(bit == 1, picked[0], picked[1])
                begin = (at + position + j) * dz
                send[begin:begin + dz, :] = (part[begin:begin + dz, :] + column * piece).astype(BF16)
        at += count // 2 if halved else count
    rows_b = own.shape[0]
    own[0:16, :] = jnp.where(bit == 1, once, latent).astype(BF16)
    put_columns(send, at * dz, rows_b, jnp.where(bit == 1, latent, once).astype(BF16))


def rest_kernel(plan, info, flipped, unfold, hidden, latent_grad, proj, keep_a, keep_c, hidden_grad, extras, row):
    bit = info[0]
    correlate(flipped[...], (unfold,), plan[:1], bit, bit, keep_a)
    correlate(flipped[...], (hidden,), plan[1:], bit, bit, keep_c)
    back = nt(latent_grad[...], proj[...]).astype(BF16)
    hidden_grad[...] = back
    row[...] = back[0:16, :]
    stride = extras.shape[0] // 4
    extras[...] = jnp.zeros(extras.shape, F32)
    sums = jnp.sum(back.astype(F32), 0, keepdims=True)
    for digit, part in enumerate(digits_of(sums)):
        for j in range(sums.shape[1] // LANES):
            extras[digit * stride + j:digit * stride + j + 1, :] = part[:, j * LANES:(j + 1) * LANES]


def split_sum(halved, bit, got, at, kept, rows, send, to, keep):
    if halved:
        half = rows // 2
        away = pl.multiple_of((1 - bit) * half, 16)
        home = pl.multiple_of(bit * half, 16)
        send[to:to + half, :] = (kept[pl.ds(away, half), :] + got[pl.ds(at + away, half), :].astype(F32)).astype(BF16)
        keep[0:half, :] = kept[pl.ds(home, half), :] + got[pl.ds(at + home, half), :].astype(F32)
        return half
    total = (kept[0:rows, :] + got[at:at + rows, :].astype(F32)).astype(BF16)
    send[to:to + rows, :] = total
    keep[0:rows, :] = total.astype(F32)
    return rows


def add_digits(mine, theirs):
    stride = mine.shape[0] // 4
    return ((mine[0:stride] + mine[stride:2 * stride]) + mine[2 * stride:3 * stride]) + (
        (theirs[0:stride] + theirs[stride:2 * stride]) + theirs[2 * stride:3 * stride])


def digit_block(value):
    return jnp.concatenate(list(digits_of(value)) + [jnp.zeros_like(value)], 0)


def first_step_kernel(halves, place, info, got, kept_a, kept_c, extras, send, keep_a, keep_c):
    (rows_a, halved_a), (rows_c, halved_c) = halves
    to = split_sum(halved_a, info[place], got, 0, kept_a, rows_a, send, 0, keep_a)
    gone = split_sum(halved_c, info[place], got, rows_a, kept_c, rows_c, send, to, keep_c)
    send[to + gone:, :] = extras[...].astype(BF16)
    keep_c[gone:, :] = extras[...]


def feat_kernel(info, grad, after, weight, out, wide, inter):
    frames, channels = grad.shape
    half = weight.shape[0] // 2
    wide[0:frames, :] = grad[...].astype(F32)
    wide[frames:, :] = jnp.broadcast_to(after[0:1, :].astype(F32), (8, channels))
    ahead = wide[pl.ds(1, frames), :].astype(BF16)
    for parity in range(2):
        rows = pl.ds(parity * (half // 2), half // 2)
        rows_after = pl.ds(half + parity * (half // 2), half // 2)
        both = nt(ahead, weight[rows, :]) + nt(grad[...], weight[rows_after, :])
        for j in range(channels // LANES):
            inter[j, pl.ds(parity, frames, stride=2), :] = both[:, j * LANES:(j + 1) * LANES]
    for j in range(channels // LANES):
        out[:, j * LANES:(j + 1) * LANES] = inter[j].astype(BF16)


def sums_kernel(first, frames, place, count, info, got, own, row, out):
    rows, dz = own.shape
    theirs = jnp.concatenate([got[first + j * rows:first + (j + 1) * rows, :] for j in range(dz // LANES)], 1)
    ones = jnp.ones((8, frames), BF16)
    parts = []
    for block in (own[...], theirs):
        parts.append((block[0:frames, :], codes_of(block[frames:, :], frames)))
    size = count + 16
    riding = [row[...].astype(F32)[0:1, :]]
    for top in range(0, out.shape[0], size):
        total = jnp.zeros((count, dz), F32)
        counts = jnp.zeros((8, count), F32)
        for values, codes in parts:
            matches = one_hot(codes, 0, info[place], count)
            total = total + nn(matches, values)
            counts = counts + nt(ones, matches)
        out[top:top + count, :] = total.astype(out.dtype)
        out[top + count:top + size, :] = count_rows(counts[0:1], dz, riding).astype(out.dtype)
        place += 1


def count_rows(count, width, riding=()):
    high = jnp.floor(count * (1.0 / 65536.0))
    rest = count - high * 65536.0
    middle = jnp.floor(rest * (1.0 / 256.0))
    low = rest - middle * 256.0
    block = jnp.concatenate([high, middle, low], 0)
    if count.shape[1] < width:
        block = jnp.concatenate([block, jnp.zeros((3, width - count.shape[1]), F32)], 1)
    parts = [block]
    for row in riding:
        parts += [row[:, at:at + width] for at in range(0, row.shape[1], width)]
    left = 16 - sum(part.shape[0] for part in parts)
    return jnp.concatenate(parts + [jnp.zeros((left, width), F32)] * (left > 0), 0)


def riding_row(block, index, parts):
    return jnp.concatenate([block[3 + index * parts + j:4 + index * parts + j, :] for j in range(parts)], 1)


def count_of(block, own):
    return (block[0:1] * 65536.0 + block[1:2] * 256.0 + block[2:3])[:, :own]


def sums_step_kernel(halved, place, row_step, row_place, info, got, kept, *refs):
    riding = ()
    if row_step is not None:
        known, refs = refs[0][...].astype(F32), refs[1:]
        after, refs = refs[-1], refs[:-1]
        parts = known.shape[1] // got.shape[1]
        block = got[row_place[0]:row_place[0] + 16, :].astype(F32)
        rows = [known[j:j + 1, :] for j in range(1 << row_step)]
        rows += [riding_row(block, j, parts) for j in range(1 << row_step)]
        if halved:
            riding = rows
            total = rows + [jnp.zeros((16 - len(rows), known.shape[1]), F32)]
            after[...] = jnp.concatenate(total, 0).astype(BF16)
        else:
            wide = jnp.zeros(after.shape, F32)
            for j in range(1, len(rows)):
                wide = jnp.where(info[row_place[1]] == j, jnp.broadcast_to(rows[j], after.shape), wide)
            after[...] = wide.astype(BF16)
    send, keep = refs
    dz = got.shape[1]
    bit = info[place]
    half = kept.shape[0] // 2 if halved else 0
    outs = [(send, (1 - bit) * half), (keep, bit * half)] if halved else [(send, 0)]
    count = row_place[0]
    size = count + 16
    for out, start in outs:
        for top in range(0, keep.shape[0], size):
            here = top + pl.multiple_of(start, 16) if halved else top
            sums = pl.ds(here, count)
            tail = pl.ds(here + count, 16)
            value = kept[sums, :].astype(F32) + got[sums, :].astype(F32)
            number = count_of(kept[tail, :].astype(F32), count) + count_of(got[tail, :].astype(F32), count)
            out[top:top + count, :] = value.astype(out.dtype)
            out[top + count:top + size, :] = count_rows(number, dz, riding).astype(out.dtype)
    if not halved:
        keep[...] = send[0:keep.shape[0], :].astype(F32)


def swap_halves(first, second, core):
    half = LANES // 2
    left = lax.broadcasted_iota(jnp.int32, first.shape, 1) < half
    turned_first, turned_second = pltpu.roll(first, half, 1), pltpu.roll(second, half, 1)
    swapped_first = jnp.where(left, first, turned_second)
    swapped_second = jnp.where(left, turned_first, second)
    return jnp.where(core == 1, swapped_first, first), jnp.where(core == 1, swapped_second, second)


def step_kernel(halves, place, mixed, info, got, kept_a, kept_c, send, keep_a, keep_c):
    (rows_a, halved_a), (rows_c, halved_c) = halves
    if mixed:
        to = rows_a // 2
        total = kept_a[0:rows_a, :] + got[0:rows_a, :].astype(F32)
        first, second = swap_halves(total[0:to, :], total[to:, :], info[0])
        low = info[place] == 0
        send[0:to, :] = jnp.where(low, second, first).astype(BF16)
        keep_a[...] = jnp.where(low, first, second)
    else:
        to = split_sum(halved_a, info[place], got, 0, kept_a, rows_a, send, 0, keep_a)
    gone = split_sum(halved_c, info[place], got, rows_a, kept_c, rows_c, send, to, keep_c)
    block = digit_block(add_digits(kept_c[rows_c:, :], got[rows_a + rows_c:, :].astype(F32)))
    keep_c[gone:, :] = block
    to += gone
    send[to:to + block.shape[0], :] = block.astype(BF16)
    to += block.shape[0]
    if to < send.shape[0]:
        send[to:, :] = jnp.zeros((send.shape[0] - to, LANES), BF16)


def last_kernel(rows_a, rows, info, got, kept_a, kept_c, sums_got, sums_kept, corr, pieces, mine):
    corr[...] = kept_a[...] + got[0:rows_a, :].astype(F32)
    pieces[...] = (kept_c[0:rows, :] + got[rows_a:rows_a + rows, :].astype(F32)).astype(BF16)
    block = digit_block(add_digits(kept_c[rows:, :], got[rows_a + rows:rows_a + kept_c.shape[0], :].astype(F32)))
    mine[0:rows, :] = pieces[...]
    mine[rows:kept_c.shape[0], :] = block.astype(BF16)
    at = kept_c.shape[0]
    count = sums_kept.shape[0] - 16
    number = count_of(sums_kept[count:, :].astype(F32), count) + count_of(sums_got[count:, :].astype(F32), count)
    square = (count, count)
    same = lax.broadcasted_iota(jnp.int32, square, 0) == lax.broadcasted_iota(jnp.int32, square, 1)
    tall = jnp.sum(jnp.where(same, jnp.broadcast_to(number, square), 0.0), 1, keepdims=True)
    total = sums_kept[0:count, :].astype(F32) + sums_got[0:count, :].astype(F32)
    means = (total / jnp.maximum(tall, 1.0)).astype(BF16)
    digits = count_rows(number, means.shape[1]).astype(BF16)
    for j in range(means.shape[1] // LANES):
        mine[at:at + count, :] = means[:, j * LANES:(j + 1) * LANES]
        mine[at + count:at + count + 16, :] = digits[:, j * LANES:(j + 1) * LANES]
        at += count + 16


def conv_out_kernel(total_frames, place, info, corr, proj, out, wide):
    rows = out.shape[0]
    flipped = jnp.transpose(corr[...])
    high = flipped.astype(BF16)
    low = (flipped - high.astype(F32)).astype(BF16)
    wide[...] = (nt(high, proj[...]) + nt(low, proj[...])) * (1.0 / total_frames)
    start = info[place]
    if rows % 8 == 0:
        out[...] = wide[pl.ds(pl.multiple_of(start, 8), rows), :]
    else:
        taken = wide[0:rows, :]
        for other in range(rows, wide.shape[0], rows):
            taken = jnp.where(start == other, wide[other:other + rows, :], taken)
        out[...] = taken


def out_kernel(total_frames, use_scale, dz, place, inner, extra, info, mine, *refs):
    parts, (out, bias, means, usage) = refs[:-4], refs[-4:]
    theirs = parts[1]
    scale = 1.0 / total_frames
    top = inner * dz
    value = add_digits(mine[top:top + extra, :].astype(F32), theirs[top:top + extra, :].astype(F32)) * scale
    for j in range(bias.shape[1] // LANES):
        bias[:, j * LANES:(j + 1) * LANES] = value[j:j + 1, :]
    bit = info[0]
    count = means.shape[1]
    numbers = []
    for ref, level in ((mine, bit), (theirs, 1 - bit)):
        at = top + extra
        blocks = []
        for j in range(dz // LANES):
            blocks.append(ref[at:at + count + 16, :])
            at += count + 16
        whole = jnp.concatenate(blocks, 1)
        means[level] = whole[0:count, :]
        numbers.append(count_of(whole[count:, :].astype(F32), count) * use_scale)
    usage[0:1, :] = jnp.where(bit == 1, numbers[1], numbers[0])
    usage[1:2, :] = jnp.where(bit == 1, numbers[0], numbers[1])
    for j, ref in enumerate(parts):
        for k in range(inner):
            start = pl.multiple_of((info[place + j] + k) * LANES, LANES)
            turned = jnp.transpose(ref[k * dz:(k + 1) * dz, :])
            out[pl.ds(start, LANES), :] = turned.astype(F32) * scale


def shifted(block, axis, distance):
    devices = range(lax.axis_size(axis))
    route = [(i - distance, i) for i in devices if i - distance in devices]
    return lax.ppermute(block, axis, route)


def swapped(block, steps):
    tm = lax.axis_size("tm")

    def partner(device):
        axis, bit = steps[(device // tm) & 1]
        return device ^ ((1 << bit) * (tm if axis == "dp" else 1))

    route = [(device, partner(device)) for device in range(lax.axis_size("dp") * tm)]
    return lax.ppermute(block, ("dp", "tm"), route)


def crossed(block, steps):
    tm = lax.axis_size("tm")

    def partner(device):
        axis, bit = steps[(device // tm) & 1]
        return device ^ tm ^ ((1 << bit) * (tm if axis == "dp" else 1))

    route = [(device, partner(device)) for device in range(lax.axis_size("dp") * tm)]
    return lax.ppermute(block, ("dp", "tm"), route)


def shards(feats, codes, conv_weight, conv_bias, proj_weight, codebooks):
    dp, tm = lax.axis_size("dp"), lax.axis_size("tm")
    rows_in, channels = feats.shape
    frames = rows_in // 2
    levels, book_size, dz = codebooks.shape
    assert levels == 2
    width = conv_weight.shape[0]
    total_frames = frames * dp * tm
    per_shard = book_size // tm
    dp_bits, tm_bits = log2(dp), log2(tm)
    owner_rows = width // (dp * tm)

    assert dp_bits >= 3 and 1 <= tm_bits <= 2
    pieces_a, pieces_c = width // LANES, channels // LANES
    under = max(dp_bits + tm_bits - log2(pieces_a), 0)
    c_bits = 2
    assert pieces_c >= 4
    whole_bits = [b for b in range(1, dp_bits) if b + tm_bits < under]
    piece_bits = [b for b in range(1, dp_bits) if b + tm_bits >= under]
    paths = [[("dp", b) for b in bits] for bits in (whole_bits + piece_bits, whole_bits[::-1] + piece_bits[::-1])]
    mixed = under == 1 and tm_bits == 2
    turned = mixed or under == 0 or under >= tm_bits
    up = [("tm", b) for b in range(tm_bits)]
    paths[0] += up[::-1]
    paths[1] += up if turned else up[::-1]
    exchanges = list(zip([("dp", 0)] + paths[0], [("dp", 0)] + paths[1]))
    sums_up = [("dp", b) for b in range(1, dp_bits)]
    sums_exchanges = list(zip(up + sums_up, up[::-1] + sums_up[::-1]))

    def piece_bit(step):
        axis, b = step
        bit = b + (tm_bits if axis == "dp" else 0)
        return bit - under if bit >= under else None

    a_split = [piece_bit(steps[0]) is not None for steps in exchanges]
    c_split = [log2(pieces_c) - 1 - k if k < c_bits else None for k in range(len(exchanges))]

    def order_of(split, count):
        used = [b for b in split if b is not None]
        return used + [b for b in reversed(range(log2(count))) if b not in used]

    orders = [order_of([piece_bit(steps[core]) for steps in exchanges], pieces_a) for core in range(2)]
    order_c = order_of(c_split, pieces_c)
    plan = [(pieces_a, orders, a_split[0]), (pieces_c, [order_c, order_c], True)]
    now_a = pieces_a // 2 if plan[0][2] else pieces_a
    now_c = pieces_c // 2

    at_dp, at_tm = lax.axis_index("dp"), lax.axis_index("tm")
    core = at_dp & 1

    def on_core(values):
        return values[0] + core * (values[1] - values[0])

    def bit_at(step):
        axis, b = step
        return ((at_dp if axis == "dp" else at_tm) >> b) & 1

    bits = [on_core([bit_at(step) for step in steps]) for steps in exchanges]
    sums_bits = [on_core([bit_at(step) for step in steps]) for steps in sums_exchanges]
    shared = [bit_at(step) for step in exchanges[1]]
    mine_c, other_c = on_core(shared), on_core(shared[::-1])
    places = [2 * core + mine_c, 2 * (1 - core) + other_c, 2 * core + 1 - mine_c, 2 * (1 - core) + 1 - other_c]
    places = [place << (log2(pieces_c) - c_bits) for place in places]
    lists = []
    for way in ([b for _, b in up], [b for _, b in up[::-1]]):
        lists.append([sum(((position >> (tm_bits - 1 - j)) & 1) << b for j, b in enumerate(way)) for position in range(tm)])
    first_bit = on_core([0, tm_bits - 1])
    lead = (at_tm >> first_bit) & 1
    quarters = [on_core([lists[0][j], lists[1][j]]) for j in range(tm // 2)]
    send_codes = [(q + ((1 - lead) << first_bit)) * per_shard for q in quarters]
    keep_codes = [(q + (lead << first_bit)) * per_shard for q in quarters]
    differ = at_tm ^ (at_tm + 1)
    ways = [sum(((differ >> b) & 1) << j for j, b in enumerate(way)) for way in (
        list(range(tm_bits)), list(reversed(range(tm_bits))))]
    row_code = jnp.where(at_tm + 1 < tm, on_core(ways), 0)
    if turned and not mixed:
        start = ((at_dp * tm + at_tm) * owner_rows) & (LANES - 1)
    else:
        start = on_core([(at_dp * tm + at_tm) * owner_rows, (at_tm >> 1) * owner_rows if mixed else (
            at_dp * tm + at_tm) * owner_rows]) & (LANES - 1)
    at_start = len(bits)
    at_codes = at_start + 1
    at_pieces = at_codes + tm
    at_sums = at_pieces + len(places)
    at_row = at_sums + len(sums_bits)
    info = jnp.stack(bits + [start] + send_codes + keep_codes + places + sums_bits + [row_code]).astype(jnp.int32)

    halo = shifted(call(halo_kernel, shape((2, channels), BF16), [info, feats[-2:]], flops=10 ** 11), "tm", 1)
    weight, proj, codes = conv_weight, proj_weight, codes[0]
    extra = 4 * (-(-channels // LANES // 8) * 8)
    code_rows = -(-(2 * -(-frames // dz)) // 16) * 16
    corr_rows = (now_a + now_c) * dz
    rows_b = frames + code_rows
    shared = [shape((frames, width), BF16), shape((frames, channels), BF16), shape((frames, dz), BF16),
              shape((dz, frames), BF16), shape((rows_b, dz), BF16),
              shape((corr_rows + rows_b * (dz // LANES), LANES), BF16)]
    *arrays, first, part = call(
        functools.partial(local_kernel, plan),
        shared + [shape((16, channels), F32), shape((corr_rows + 32 * (dz // LANES), LANES), F32)],
        [info, feats, weight, conv_bias[None, :], codes, codebooks, proj],
        scratch=[VMEM((channels // LANES, rows_in + 8, LANES), F32), VMEM((levels, frames, dz), BF16)],
    )
    unfold, hidden, latent_grad, flipped, own, send = call(
        functools.partial(frame_kernel, plan),
        shared,
        [info, halo, first, part, weight, proj] + arrays,
        aliases={6 + k: k for k in range(len(shared))},
    )
    got = swapped(send, exchanges[0])
    keep_a, keep_c, hidden_grad, extras, row = call(
        functools.partial(rest_kernel, plan),
        [shape((now_a * dz, LANES), F32), shape((now_c * dz, LANES), F32), shape((frames, channels), BF16),
         shape((extra, LANES), F32), shape((16, channels), BF16)],
        [info, flipped, unfold, hidden, latent_grad, proj],
        after=[send],
    )

    def halves_at(k):
        nonlocal now_a, now_c
        halves = [(now_a * dz, a_split[k]), (now_c * dz, c_split[k] is not None)]
        now_a = now_a // 2 if halves[0][1] else now_a
        now_c = now_c // 2 if halves[1][1] else now_c
        return halves, now_a * dz, now_c * dz + extra

    halves, rows_a, rows_c = halves_at(1)
    send, keep_a, keep_c = call(
        functools.partial(first_step_kernel, halves, 1),
        [shape((rows_a + rows_c, LANES), BF16), shape((rows_a, LANES), F32), shape((rows_c, LANES), F32)],
        [info, got, keep_a, keep_c, extras])
    size = per_shard + 16
    sums_rows = size * (tm // 2)
    sums_send = call(
        functools.partial(sums_kernel, corr_rows, frames, at_codes, per_shard),
        shape((sums_rows, dz), BF16),
        [info, got, own, row],
        after=[send])
    sums_keep = call(
        functools.partial(sums_kernel, corr_rows, frames, at_codes + tm // 2, per_shard),
        shape((sums_rows, dz), F32),
        [info, got, own, row],
        after=[sums_send])
    sums_got = swapped(sums_send, sums_exchanges[0])
    got = swapped(send, exchanges[1])
    known = row
    ordered = [sums_keep]
    for k in range(2, len(exchanges)):
        halves, rows_a, rows_c = halves_at(k)
        spare = 16 * (k == len(exchanges) - 1)
        send, keep_a, keep_c = call(
            functools.partial(step_kernel, halves, k, mixed and k == dp_bits),
            [shape((rows_a + rows_c + spare, LANES), BF16), shape((rows_a, LANES), F32), shape((rows_c, LANES), F32)],
            [info, got, keep_a, keep_c],
            after=ordered)
        got = swapped(send, exchanges[k])
        halved = sums_exchanges[k - 1][0][0] == "tm"
        sums_rows = sums_rows // 2 if halved else sums_rows
        row_step = k - 2 if k - 2 < tm_bits else None
        outs = call(
            functools.partial(sums_step_kernel, halved, at_sums + k - 1, row_step, (per_shard, at_row)),
            [shape((sums_rows, dz), BF16), shape((sums_rows, dz), F32)]
            + [shape((16, channels), BF16)] * (row_step is not None),
            [info, sums_got, sums_keep] + [known] * (row_step is not None),
            after=[send])
        sums_send, sums_keep = outs[:2]
        known = outs[2] if row_step is not None else known
        sums_got = swapped(sums_send, sums_exchanges[k - 1])
        ordered = [sums_send]
    assert now_a == 1 and sums_rows == size
    feat_grad, last = call(
        feat_kernel,
        shape((rows_in, channels), BF16),
        [info, hidden_grad, known, weight],
        after=[sums_send],
        token=True,
        scratch=[VMEM((frames + 8, channels), F32), VMEM((channels // LANES, rows_in, LANES), F32)],
    )

    corr, piece, mine = call(
        functools.partial(last_kernel, rows_a, rows_c - extra),
        [shape((rows_a, LANES), F32), shape((rows_c - extra, LANES), BF16),
         shape((rows_c + size * (dz // LANES), LANES), BF16)],
        [info, got, keep_a, keep_c, sums_got, sums_keep],
        after=[last])
    parts = [piece, swapped(mine, exchanges[0]), swapped(piece, exchanges[1]), crossed(piece, exchanges[1])]
    conv_grad, last = call(
        functools.partial(conv_out_kernel, total_frames, at_start),
        shape((owner_rows, channels), F32),
        [info, corr, proj],
        after=[piece],
        token=True,
        scratch=[VMEM((LANES, channels), F32)],
    )
    proj_grad, bias_grad, code_means, code_usage = call(
        functools.partial(out_kernel, total_frames, book_size / total_frames, dz, at_pieces, now_c, extra),
        [shape((channels, dz), F32), shape((1, channels), F32), shape((levels, per_shard, dz), BF16),
         shape((levels, per_shard), F32)],
        [info, mine] + parts,
        after=[last],
    )
    return feat_grad, conv_grad, bias_grad[0], proj_grad, code_means, code_usage


def solution(mesh):
    placed = (P(("dp", "tm"), None), P("dp", None, "tm"), P(), P(), P(), P())
    return jax.shard_map(
        shards,
        mesh=mesh,
        in_specs=placed,
        out_specs=(
            P(("dp", "tm"), None),
            P(("dp", "tm"), None),
            P(),
            P(),
            P(None, "tm", None),
            P(None, "tm"),
        ),
        check_vma=False,
    )
```

```python
import functools

import jax
import jax.numpy as jnp
from jax import lax
from jax.experimental import pallas as pl
from jax.experimental.pallas import tpu as pltpu
from jax.sharding import PartitionSpec as P

BF16 = jnp.bfloat16
F32 = jnp.float32
LANES = 128
VMEM_LIMIT = 16 * 1024 * 1024


def log2(value):
    assert value & (value - 1) == 0
    return value.bit_length() - 1


def nn(a, b):
    return lax.dot_general(a, b, (((1,), (0,)), ((), ())), preferred_element_type=F32)


def nt(a, b):
    return lax.dot_general(a, b, (((1,), (1,)), ((), ())), preferred_element_type=F32)


VMEM = pltpu.VMEM


def call(body, out_shape, args, after=(), scratch=(), aliases=None, token=False, flops=0):
    count = len(args)
    many = isinstance(out_shape, (list, tuple))
    shapes = list(out_shape) if many else [out_shape]

    def kernel(*refs):
        ends = count + len(after)
        if token:
            refs[ends + len(shapes)][...] = jnp.zeros((8, LANES), F32)
            refs = refs[:ends + len(shapes)] + refs[ends + len(shapes) + 1:]
        body(*refs[:count], *refs[ends:])

    specs = [pl.BlockSpec(memory_space=pltpu.SMEM)]
    specs += [pl.BlockSpec(memory_space=VMEM)] * (count - 1)
    specs += [pl.BlockSpec(memory_space=pl.ANY)] * len(after)
    shown = shapes + [shape((8, LANES), F32)] * token
    outs = pl.pallas_call(
        kernel,
        out_shape=shown,
        in_specs=specs,
        out_specs=[pl.BlockSpec(memory_space=VMEM)] * len(shown),
        scratch_shapes=list(scratch),
        input_output_aliases=aliases or {},
        compiler_params=pltpu.CompilerParams(vmem_limit_bytes=VMEM_LIMIT),
        cost_estimate=pl.CostEstimate(flops=flops, bytes_accessed=0, transcendentals=0),
    )(*args, *after)
    return outs if len(shown) > 1 else outs[0]


def shape(dims, dtype):
    return jax.ShapeDtypeStruct(dims, dtype)


def digits_of(value):
    high = value.astype(BF16).astype(F32)
    rest = value - high
    middle = rest.astype(BF16).astype(F32)
    low = (rest - middle).astype(BF16).astype(F32)
    return high, middle, low


def one_hot(codes, axis_codes, first, count):
    frames = codes.shape[1 - axis_codes]
    dims = (count, frames) if axis_codes == 0 else (frames, count)
    places = lax.broadcasted_iota(jnp.int32, dims, axis_codes) + first
    return jnp.where(codes == places, 1.0, 0.0).astype(BF16)


def halo_kernel(info, rows, out):
    out[...] = rows[...]


def walk(orders, halved, count):
    start = 1 if halved else 0
    shown = count // 2 if halved else count
    bits = log2(shown)
    step = 2 if shown > 1 and all(order[-1] == 0 for order in orders) else 1
    for position in range(0, shown, step):
        yield position, [
            sum(((position >> (bits - 1 - k)) & 1) << bit for k, bit in enumerate(order[start:])) for order in orders
        ], step


def correlate(flipped, sources, plan, core, bit, out):
    dz = flipped.shape[0]
    at = 0
    for source, (count, orders, halved) in zip(sources, plan):
        for position, pieces, step in walk(orders, halved, count):
            column = pieces[0] + core * (pieces[1] - pieces[0])
            if halved:
                column = column + (bit << orders[0][0])
            column = pl.multiple_of(column * LANES, LANES)
            product = nn(flipped, source[:, pl.ds(column, step * LANES)])
            for j in range(step):
                top = (at + position + j) * dz
                out[top:top + dz, :] = product[:, j * LANES:(j + 1) * LANES].astype(out.dtype)
        at += count // 2 if halved else count
    return at * dz


def code_digits(codes, dz, rows):
    parts = []
    for part in (codes >> 8, codes & 255):
        for start in range(0, codes.shape[1], dz):
            piece = part[:, start:start + dz].astype(F32)
            if piece.shape[1] < dz:
                piece = jnp.concatenate([piece, jnp.zeros((1, dz - piece.shape[1]), F32)], 1)
            parts.append(piece)
    parts.append(jnp.zeros((rows - len(parts), dz), F32))
    return jnp.concatenate(parts, 0).astype(BF16)


def codes_of(block, frames):
    dz = block.shape[1]
    per = -(-frames // dz)
    digits = block[...].astype(F32)
    parts = [jnp.concatenate([digits[k * per + j:k * per + j + 1, :] for j in range(per)], 1)[:, :frames]
             for k in range(2)]
    return (parts[0] * 256.0 + parts[1]).astype(jnp.int32)


def residuals(hidden, proj, chosen):
    latent = nn(hidden, proj)
    once = latent - chosen[0].astype(F32)
    total = once + (once - chosen[1].astype(F32))
    return latent, once, total.astype(BF16)


def put_columns(out, at, rows, block):
    for j in range(block.shape[1] // LANES):
        out[at + j * rows:at + j * rows + block.shape[0], :] = block[:, j * LANES:(j + 1) * LANES]


def local_kernel(plan, info, feats, weight, bias, codes, books, proj,
                 unfold, hidden, latent_grad, flipped, own, send, first, part, wide, chosen):
    rows, channels = feats.shape
    frames = rows // 2
    dz = proj.shape[1]
    for j in range(channels // LANES):
        wide[j, 0:8, :] = jnp.zeros((8, LANES), F32)
        wide[j, 8:, :] = feats[:, j * LANES:(j + 1) * LANES].astype(F32)
        for tap in range(4):
            start = tap * channels + j * LANES
            unfold[:, start:start + LANES] = wide[j, pl.ds(6 + tap, frames, stride=2), :].astype(BF16)
    conv = nn(unfold[...], weight[...]) + bias[...]
    first[...] = conv[0:16, :]
    hidden[...] = conv.astype(BF16)
    levels = books.shape[0]
    padded = jnp.concatenate([codes[...].astype(F32), jnp.zeros((8 - levels, frames), F32)], 0)
    tall = jnp.transpose(padded).astype(jnp.int32)
    for level in range(levels):
        matches = one_hot(tall[:, level:level + 1], 1, 0, books.shape[1])
        chosen[level] = nn(matches, books[level]).astype(BF16)
    latent, once, grad = residuals(hidden[...], proj[...], chosen)
    latent_grad[...] = grad
    row = lax.broadcasted_iota(jnp.int32, grad.shape, 0)
    flipped[...] = jnp.transpose(jnp.where(row == 0, 0.0, grad.astype(F32))).astype(BF16)
    bit = info[0]
    at = correlate(flipped[...], (unfold, hidden), plan, 1 - bit, 1 - bit, part)
    rows_b = own.shape[0]
    code_rows = rows_b - frames
    digits = [code_digits(codes[level:level + 1, :], dz, code_rows) for level in range(2)]
    own[0:frames, :] = jnp.where(bit == 1, once, latent).astype(BF16)
    own[frames:, :] = jnp.where(bit == 1, digits[1], digits[0])
    put_columns(send, at, rows_b, jnp.where(bit == 1, latent, once).astype(BF16))
    put_columns(send, at + frames, rows_b, jnp.where(bit == 1, digits[0], digits[1]))
    for level in range(levels):
        part[at + level * 16 * (dz // LANES):at + (level + 1) * 16 * (dz // LANES), :] = jnp.concatenate(
            [chosen[level, 0:16, j * LANES:(j + 1) * LANES].astype(F32) for j in range(dz // LANES)], 0)


def frame_kernel(plan, info, halo, first, part, weight, proj, unfold_in, hidden_in, grad_in, flipped_in, own_in, send_in,
                 unfold, hidden, latent_grad, flipped, own, send):
    width = unfold.shape[1]
    half = width // 2
    dz = proj.shape[1]
    row = lax.broadcasted_iota(jnp.int32, (16, half), 0)
    left = jnp.concatenate([halo[0:1, :], halo[1:2, :]], 1).astype(F32)
    head = jnp.where(row == 0, jnp.broadcast_to(left, (16, half)), 0.0)
    unfold[0:16, 0:half] = (unfold_in[0:16, 0:half].astype(F32) + head).astype(BF16)
    fix = nn(head.astype(BF16), weight[0:half, :])
    hidden[0:16, :] = (first[...] + fix).astype(BF16)
    top = hidden[0:16, :]
    pieces = part.shape[0] - 32 * (dz // LANES)
    chosen = []
    for level in range(2):
        at = pieces + level * 16 * (dz // LANES)
        chosen.append(jnp.concatenate([part[at + j * 16:at + (j + 1) * 16, :] for j in range(dz // LANES)], 1))
    latent, once, grad = residuals(top, proj[...], chosen)
    latent_grad[0:16, :] = grad
    flipped[:, 0:LANES] = jnp.transpose(latent_grad[0:LANES, :].astype(F32)).astype(BF16)
    column = flipped[:, 0:LANES].astype(F32)[:, 0:1]
    bit = info[0]
    at = 0
    for source, (count, orders, halved) in zip((unfold, hidden), plan):
        rows = source[0:16, :].astype(F32)[0:1, :]
        for position, places, step in walk(orders, halved, count):
            for j in range(step):
                offsets = [places[0] + j, places[1] + j]
                low = [offset for offset in offsets]
                high = [offset + (1 << orders[0][0] if halved else 0) for offset in offsets]
                picked = [rows[:, k * LANES:(k + 1) * LANES] for k in low + high]
                piece = jnp.where(bit == 1, picked[0], picked[3]) if halved else jnp.where(bit == 1, picked[0], picked[1])
                begin = (at + position + j) * dz
                send[begin:begin + dz, :] = (part[begin:begin + dz, :] + column * piece).astype(BF16)
        at += count // 2 if halved else count
    rows_b = own.shape[0]
    own[0:16, :] = jnp.where(bit == 1, once, latent).astype(BF16)
    put_columns(send, at * dz, rows_b, jnp.where(bit == 1, latent, once).astype(BF16))


def rest_kernel(plan, info, flipped, unfold, hidden, latent_grad, proj, keep_a, keep_c, hidden_grad, extras, row):
    bit = info[0]
    correlate(flipped[...], (unfold,), plan[:1], bit, bit, keep_a)
    correlate(flipped[...], (hidden,), plan[1:], bit, bit, keep_c)
    back = nt(latent_grad[...], proj[...]).astype(BF16)
    hidden_grad[...] = back
    row[...] = back[0:16, :]
    stride = extras.shape[0] // 4
    extras[...] = jnp.zeros(extras.shape, F32)
    sums = jnp.sum(back.astype(F32), 0, keepdims=True)
    for digit, part in enumerate(digits_of(sums)):
        for j in range(sums.shape[1] // LANES):
            extras[digit * stride + j:digit * stride + j + 1, :] = part[:, j * LANES:(j + 1) * LANES]


def split_sum(halved, bit, got, at, kept, rows, send, to, keep):
    if halved:
        half = rows // 2
        away = pl.multiple_of((1 - bit) * half, 16)
        home = pl.multiple_of(bit * half, 16)
        send[to:to + half, :] = (kept[pl.ds(away, half), :] + got[pl.ds(at + away, half), :].astype(F32)).astype(BF16)
        keep[0:half, :] = kept[pl.ds(home, half), :] + got[pl.ds(at + home, half), :].astype(F32)
        return half
    total = (kept[0:rows, :] + got[at:at + rows, :].astype(F32)).astype(BF16)
    send[to:to + rows, :] = total
    keep[0:rows, :] = total.astype(F32)
    return rows


def add_digits(mine, theirs):
    stride = mine.shape[0] // 4
    return ((mine[0:stride] + mine[stride:2 * stride]) + mine[2 * stride:3 * stride]) + (
        (theirs[0:stride] + theirs[stride:2 * stride]) + theirs[2 * stride:3 * stride])


def digit_block(value):
    return jnp.concatenate(list(digits_of(value)) + [jnp.zeros_like(value)], 0)


def first_step_kernel(halves, place, info, got, kept_a, kept_c, extras, send_a, send_c, keep_a, keep_c):
    (rows_a, halved_a), (rows_c, halved_c) = halves
    split_sum(halved_a, info[place], got, 0, kept_a, rows_a, send_a, 0, keep_a)
    gone = split_sum(halved_c, info[place], got, rows_a, kept_c, rows_c, send_c, 0, keep_c)
    send_c[gone:, :] = extras[...].astype(BF16)
    keep_c[gone:, :] = extras[...]


def feat_kernel(info, grad, after, weight, out, wide, inter):
    frames, channels = grad.shape
    half = weight.shape[0] // 2
    wide[0:frames, :] = grad[...].astype(F32)
    wide[frames:, :] = jnp.broadcast_to(after[0:1, :].astype(F32), (8, channels))
    ahead = wide[pl.ds(1, frames), :].astype(BF16)
    for parity in range(2):
        rows = pl.ds(parity * (half // 2), half // 2)
        rows_after = pl.ds(half + parity * (half // 2), half // 2)
        both = nt(ahead, weight[rows, :]) + nt(grad[...], weight[rows_after, :])
        for j in range(channels // LANES):
            inter[j, pl.ds(parity, frames, stride=2), :] = both[:, j * LANES:(j + 1) * LANES]
    for j in range(channels // LANES):
        out[:, j * LANES:(j + 1) * LANES] = inter[j].astype(BF16)


def sums_kernel(first, frames, place, count, info, got, own, row, out):
    rows, dz = own.shape
    theirs = jnp.concatenate([got[first + j * rows:first + (j + 1) * rows, :] for j in range(dz // LANES)], 1)
    ones = jnp.ones((8, frames), BF16)
    parts = []
    for block in (own[...], theirs):
        parts.append((block[0:frames, :], codes_of(block[frames:, :], frames)))
    size = count + 16
    riding = [row[...].astype(F32)[0:1, :]]
    for top in range(0, out.shape[0], size):
        total = jnp.zeros((count, dz), F32)
        counts = jnp.zeros((8, count), F32)
        for values, codes in parts:
            matches = one_hot(codes, 0, info[place], count)
            total = total + nn(matches, values)
            counts = counts + nt(ones, matches)
        out[top:top + count, :] = total.astype(out.dtype)
        out[top + count:top + size, :] = count_rows(counts[0:1], dz, riding).astype(out.dtype)
        place += 1


def count_rows(count, width, riding=()):
    high = jnp.floor(count * (1.0 / 65536.0))
    rest = count - high * 65536.0
    middle = jnp.floor(rest * (1.0 / 256.0))
    low = rest - middle * 256.0
    block = jnp.concatenate([high, middle, low], 0)
    if count.shape[1] < width:
        block = jnp.concatenate([block, jnp.zeros((3, width - count.shape[1]), F32)], 1)
    parts = [block]
    for row in riding:
        parts += [row[:, at:at + width] for at in range(0, row.shape[1], width)]
    left = 16 - sum(part.shape[0] for part in parts)
    return jnp.concatenate(parts + [jnp.zeros((left, width), F32)] * (left > 0), 0)


def riding_row(block, index, parts):
    return jnp.concatenate([block[3 + index * parts + j:4 + index * parts + j, :] for j in range(parts)], 1)


def count_of(block, own):
    return (block[0:1] * 65536.0 + block[1:2] * 256.0 + block[2:3])[:, :own]


def sums_step_kernel(halved, place, row_step, row_place, info, got, kept, *refs):
    riding = ()
    if row_step is not None:
        known, refs = refs[0][...].astype(F32), refs[1:]
        after, refs = refs[-1], refs[:-1]
        parts = known.shape[1] // got.shape[1]
        block = got[row_place[0]:row_place[0] + 16, :].astype(F32)
        rows = [known[j:j + 1, :] for j in range(1 << row_step)]
        rows += [riding_row(block, j, parts) for j in range(1 << row_step)]
        if halved:
            riding = rows
            total = rows + [jnp.zeros((16 - len(rows), known.shape[1]), F32)]
            after[...] = jnp.concatenate(total, 0).astype(BF16)
        else:
            wide = jnp.zeros(after.shape, F32)
            for j in range(1, len(rows)):
                wide = jnp.where(info[row_place[1]] == j, jnp.broadcast_to(rows[j], after.shape), wide)
            after[...] = wide.astype(BF16)
    send, keep = refs
    dz = got.shape[1]
    bit = info[place]
    half = kept.shape[0] // 2 if halved else 0
    outs = [(send, (1 - bit) * half), (keep, bit * half)] if halved else [(send, 0)]
    count = row_place[0]
    size = count + 16
    for out, start in outs:
        for top in range(0, keep.shape[0], size):
            here = top + pl.multiple_of(start, 16) if halved else top
            sums = pl.ds(here, count)
            tail = pl.ds(here + count, 16)
            value = kept[sums, :].astype(F32) + got[sums, :].astype(F32)
            number = count_of(kept[tail, :].astype(F32), count) + count_of(got[tail, :].astype(F32), count)
            out[top:top + count, :] = value.astype(out.dtype)
            out[top + count:top + size, :] = count_rows(number, dz, riding).astype(out.dtype)
    if not halved:
        keep[...] = send[0:keep.shape[0], :].astype(F32)


def swap_halves(first, second, core):
    half = LANES // 2
    left = lax.broadcasted_iota(jnp.int32, first.shape, 1) < half
    turned_first, turned_second = pltpu.roll(first, half, 1), pltpu.roll(second, half, 1)
    swapped_first = jnp.where(left, first, turned_second)
    swapped_second = jnp.where(left, turned_first, second)
    return jnp.where(core == 1, swapped_first, first), jnp.where(core == 1, swapped_second, second)


def step_kernel(halves, at_c, place, mixed, info, got, got_c, kept_a, kept_c, send, keep_a, keep_c):
    (rows_a, halved_a), (rows_c, halved_c) = halves
    if mixed:
        to = rows_a // 2
        total = kept_a[0:rows_a, :] + got[0:rows_a, :].astype(F32)
        first, second = swap_halves(total[0:to, :], total[to:, :], info[0])
        low = info[place] == 0
        send[0:to, :] = jnp.where(low, second, first).astype(BF16)
        keep_a[...] = jnp.where(low, first, second)
    else:
        to = split_sum(halved_a, info[place], got, 0, kept_a, rows_a, send, 0, keep_a)
    gone = split_sum(halved_c, info[place], got_c, at_c, kept_c, rows_c, send, to, keep_c)
    block = digit_block(add_digits(kept_c[rows_c:, :], got_c[at_c + rows_c:, :].astype(F32)))
    keep_c[gone:, :] = block
    to += gone
    send[to:to + block.shape[0], :] = block.astype(BF16)
    to += block.shape[0]
    if to < send.shape[0]:
        send[to:, :] = jnp.zeros((send.shape[0] - to, LANES), BF16)


def last_kernel(rows_a, rows, info, got, kept_a, kept_c, sums_got, sums_kept, corr, pieces, mine):
    corr[...] = kept_a[...] + got[0:rows_a, :].astype(F32)
    pieces[...] = (kept_c[0:rows, :] + got[rows_a:rows_a + rows, :].astype(F32)).astype(BF16)
    block = digit_block(add_digits(kept_c[rows:, :], got[rows_a + rows:rows_a + kept_c.shape[0], :].astype(F32)))
    mine[0:rows, :] = pieces[...]
    mine[rows:kept_c.shape[0], :] = block.astype(BF16)
    at = kept_c.shape[0]
    count = sums_kept.shape[0] - 16
    number = count_of(sums_kept[count:, :].astype(F32), count) + count_of(sums_got[count:, :].astype(F32), count)
    square = (count, count)
    same = lax.broadcasted_iota(jnp.int32, square, 0) == lax.broadcasted_iota(jnp.int32, square, 1)
    tall = jnp.sum(jnp.where(same, jnp.broadcast_to(number, square), 0.0), 1, keepdims=True)
    total = sums_kept[0:count, :].astype(F32) + sums_got[0:count, :].astype(F32)
    means = (total / jnp.maximum(tall, 1.0)).astype(BF16)
    digits = count_rows(number, means.shape[1]).astype(BF16)
    for j in range(means.shape[1] // LANES):
        mine[at:at + count, :] = means[:, j * LANES:(j + 1) * LANES]
        mine[at + count:at + count + 16, :] = digits[:, j * LANES:(j + 1) * LANES]
        at += count + 16


def conv_out_kernel(total_frames, place, info, corr, proj, out, wide):
    rows = out.shape[0]
    flipped = jnp.transpose(corr[...])
    high = flipped.astype(BF16)
    low = (flipped - high.astype(F32)).astype(BF16)
    wide[...] = (nt(high, proj[...]) + nt(low, proj[...])) * (1.0 / total_frames)
    start = info[place]
    if rows % 8 == 0:
        out[...] = wide[pl.ds(pl.multiple_of(start, 8), rows), :]
    else:
        taken = wide[0:rows, :]
        for other in range(rows, wide.shape[0], rows):
            taken = jnp.where(start == other, wide[other:other + rows, :], taken)
        out[...] = taken


def out_kernel(total_frames, use_scale, dz, place, inner, extra, info, mine, *refs):
    parts, (out, bias, means, usage) = refs[:-4], refs[-4:]
    theirs = parts[1]
    scale = 1.0 / total_frames
    top = inner * dz
    value = add_digits(mine[top:top + extra, :].astype(F32), theirs[top:top + extra, :].astype(F32)) * scale
    for j in range(bias.shape[1] // LANES):
        bias[:, j * LANES:(j + 1) * LANES] = value[j:j + 1, :]
    bit = info[0]
    count = means.shape[1]
    numbers = []
    for ref, level in ((mine, bit), (theirs, 1 - bit)):
        at = top + extra
        blocks = []
        for j in range(dz // LANES):
            blocks.append(ref[at:at + count + 16, :])
            at += count + 16
        whole = jnp.concatenate(blocks, 1)
        means[level] = whole[0:count, :]
        numbers.append(count_of(whole[count:, :].astype(F32), count) * use_scale)
    usage[0:1, :] = jnp.where(bit == 1, numbers[1], numbers[0])
    usage[1:2, :] = jnp.where(bit == 1, numbers[0], numbers[1])
    for j, ref in enumerate(parts):
        for k in range(inner):
            start = pl.multiple_of((info[place + j] + k) * LANES, LANES)
            turned = jnp.transpose(ref[k * dz:(k + 1) * dz, :])
            out[pl.ds(start, LANES), :] = turned.astype(F32) * scale


def shifted(block, axis, distance):
    devices = range(lax.axis_size(axis))
    route = [(i - distance, i) for i in devices if i - distance in devices]
    return lax.ppermute(block, axis, route)


def swapped(block, steps):
    tm = lax.axis_size("tm")

    def partner(device):
        axis, bit = steps[(device // tm) & 1]
        return device ^ ((1 << bit) * (tm if axis == "dp" else 1))

    route = [(device, partner(device)) for device in range(lax.axis_size("dp") * tm)]
    return lax.ppermute(block, ("dp", "tm"), route)


def crossed(block, steps):
    tm = lax.axis_size("tm")

    def partner(device):
        axis, bit = steps[(device // tm) & 1]
        return device ^ tm ^ ((1 << bit) * (tm if axis == "dp" else 1))

    route = [(device, partner(device)) for device in range(lax.axis_size("dp") * tm)]
    return lax.ppermute(block, ("dp", "tm"), route)


def shards(feats, codes, conv_weight, conv_bias, proj_weight, codebooks):
    dp, tm = lax.axis_size("dp"), lax.axis_size("tm")
    rows_in, channels = feats.shape
    frames = rows_in // 2
    levels, book_size, dz = codebooks.shape
    assert levels == 2
    width = conv_weight.shape[0]
    total_frames = frames * dp * tm
    per_shard = book_size // tm
    dp_bits, tm_bits = log2(dp), log2(tm)
    owner_rows = width // (dp * tm)

    assert dp_bits >= 3 and 1 <= tm_bits <= 2
    pieces_a, pieces_c = width // LANES, channels // LANES
    under = max(dp_bits + tm_bits - log2(pieces_a), 0)
    c_bits = 2
    assert pieces_c >= 4
    whole_bits = [b for b in range(1, dp_bits) if b + tm_bits < under]
    piece_bits = [b for b in range(1, dp_bits) if b + tm_bits >= under]
    paths = [[("dp", b) for b in bits] for bits in (whole_bits + piece_bits, whole_bits[::-1] + piece_bits[::-1])]
    mixed = under == 1 and tm_bits == 2
    turned = mixed or under == 0 or under >= tm_bits
    up = [("tm", b) for b in range(tm_bits)]
    paths[0] += up[::-1]
    paths[1] += up if turned else up[::-1]
    exchanges = list(zip([("dp", 0)] + paths[0], [("dp", 0)] + paths[1]))
    sums_up = [("dp", b) for b in range(1, dp_bits)]
    sums_exchanges = list(zip(up + sums_up, up[::-1] + sums_up[::-1]))

    def piece_bit(step):
        axis, b = step
        bit = b + (tm_bits if axis == "dp" else 0)
        return bit - under if bit >= under else None

    a_split = [piece_bit(steps[0]) is not None for steps in exchanges]
    c_split = [log2(pieces_c) - 1 - k if k < c_bits else None for k in range(len(exchanges))]

    def order_of(split, count):
        used = [b for b in split if b is not None]
        return used + [b for b in reversed(range(log2(count))) if b not in used]

    orders = [order_of([piece_bit(steps[core]) for steps in exchanges], pieces_a) for core in range(2)]
    order_c = order_of(c_split, pieces_c)
    plan = [(pieces_a, orders, a_split[0]), (pieces_c, [order_c, order_c], True)]
    now_a = pieces_a // 2 if plan[0][2] else pieces_a
    now_c = pieces_c // 2

    at_dp, at_tm = lax.axis_index("dp"), lax.axis_index("tm")
    core = at_dp & 1

    def on_core(values):
        return values[0] + core * (values[1] - values[0])

    def bit_at(step):
        axis, b = step
        return ((at_dp if axis == "dp" else at_tm) >> b) & 1

    bits = [on_core([bit_at(step) for step in steps]) for steps in exchanges]
    sums_bits = [on_core([bit_at(step) for step in steps]) for steps in sums_exchanges]
    shared = [bit_at(step) for step in exchanges[1]]
    mine_c, other_c = on_core(shared), on_core(shared[::-1])
    places = [2 * core + mine_c, 2 * (1 - core) + other_c, 2 * core + 1 - mine_c, 2 * (1 - core) + 1 - other_c]
    places = [place << (log2(pieces_c) - c_bits) for place in places]
    lists = []
    for way in ([b for _, b in up], [b for _, b in up[::-1]]):
        lists.append([sum(((position >> (tm_bits - 1 - j)) & 1) << b for j, b in enumerate(way)) for position in range(tm)])
    first_bit = on_core([0, tm_bits - 1])
    lead = (at_tm >> first_bit) & 1
    quarters = [on_core([lists[0][j], lists[1][j]]) for j in range(tm // 2)]
    send_codes = [(q + ((1 - lead) << first_bit)) * per_shard for q in quarters]
    keep_codes = [(q + (lead << first_bit)) * per_shard for q in quarters]
    differ = at_tm ^ (at_tm + 1)
    ways = [sum(((differ >> b) & 1) << j for j, b in enumerate(way)) for way in (
        list(range(tm_bits)), list(reversed(range(tm_bits))))]
    row_code = jnp.where(at_tm + 1 < tm, on_core(ways), 0)
    if turned and not mixed:
        start = ((at_dp * tm + at_tm) * owner_rows) & (LANES - 1)
    else:
        start = on_core([(at_dp * tm + at_tm) * owner_rows, (at_tm >> 1) * owner_rows if mixed else (
            at_dp * tm + at_tm) * owner_rows]) & (LANES - 1)
    at_start = len(bits)
    at_codes = at_start + 1
    at_pieces = at_codes + tm
    at_sums = at_pieces + len(places)
    at_row = at_sums + len(sums_bits)
    info = jnp.stack(bits + [start] + send_codes + keep_codes + places + sums_bits + [row_code]).astype(jnp.int32)

    halo = shifted(call(halo_kernel, shape((2, channels), BF16), [info, feats[-2:]], flops=10 ** 11), "tm", 1)
    weight, proj, codes = conv_weight, proj_weight, codes[0]
    extra = 4 * (-(-channels // LANES // 8) * 8)
    code_rows = -(-(2 * -(-frames // dz)) // 16) * 16
    corr_rows = (now_a + now_c) * dz
    rows_b = frames + code_rows
    shared = [shape((frames, width), BF16), shape((frames, channels), BF16), shape((frames, dz), BF16),
              shape((dz, frames), BF16), shape((rows_b, dz), BF16),
              shape((corr_rows + rows_b * (dz // LANES), LANES), BF16)]
    *arrays, first, part = call(
        functools.partial(local_kernel, plan),
        shared + [shape((16, channels), F32), shape((corr_rows + 32 * (dz // LANES), LANES), F32)],
        [info, feats, weight, conv_bias[None, :], codes, codebooks, proj],
        scratch=[VMEM((channels // LANES, rows_in + 8, LANES), F32), VMEM((levels, frames, dz), BF16)],
    )
    unfold, hidden, latent_grad, flipped, own, send = call(
        functools.partial(frame_kernel, plan),
        shared,
        [info, halo, first, part, weight, proj] + arrays,
        aliases={6 + k: k for k in range(len(shared))},
    )
    got = swapped(send, exchanges[0])
    keep_a, keep_c, hidden_grad, extras, row = call(
        functools.partial(rest_kernel, plan),
        [shape((now_a * dz, LANES), F32), shape((now_c * dz, LANES), F32), shape((frames, channels), BF16),
         shape((extra, LANES), F32), shape((16, channels), BF16)],
        [info, flipped, unfold, hidden, latent_grad, proj],
        after=[send],
    )

    def halves_at(k):
        nonlocal now_a, now_c
        halves = [(now_a * dz, a_split[k]), (now_c * dz, c_split[k] is not None)]
        now_a = now_a // 2 if halves[0][1] else now_a
        now_c = now_c // 2 if halves[1][1] else now_c
        return halves, now_a * dz, now_c * dz + extra

    size = per_shard + 16
    sums_rows = size * (tm // 2)
    sums_send = call(
        functools.partial(sums_kernel, corr_rows, frames, at_codes, per_shard),
        shape((sums_rows, dz), BF16),
        [info, got, own, row])
    sums_got = swapped(sums_send, sums_exchanges[0])
    halves, rows_a, rows_c = halves_at(1)
    send, send_c, keep_a, keep_c = call(
        functools.partial(first_step_kernel, halves, 1),
        [shape((rows_a, LANES), BF16), shape((rows_c, LANES), BF16), shape((rows_a, LANES), F32),
         shape((rows_c, LANES), F32)],
        [info, got, keep_a, keep_c, extras],
        after=[sums_send])
    sums_keep = call(
        functools.partial(sums_kernel, corr_rows, frames, at_codes + tm // 2, per_shard),
        shape((sums_rows, dz), F32),
        [info, got, own, row],
        after=[send])
    got, got_c = swapped(send, exchanges[1]), swapped(send_c, exchanges[1])
    known = row
    ordered = [sums_keep, sums_got]
    for k in range(2, len(exchanges)):
        at_c = 0 if k == 2 else rows_a
        halves, rows_a, rows_c = halves_at(k)
        spare = 16 * (k == len(exchanges) - 1)
        send, keep_a, keep_c = call(
            functools.partial(step_kernel, halves, at_c, k, mixed and k == dp_bits),
            [shape((rows_a + rows_c + spare, LANES), BF16), shape((rows_a, LANES), F32), shape((rows_c, LANES), F32)],
            [info, got, got_c, keep_a, keep_c],
            after=ordered)
        got = got_c = swapped(send, exchanges[k])
        halved = sums_exchanges[k - 1][0][0] == "tm"
        sums_rows = sums_rows // 2 if halved else sums_rows
        row_step = k - 2 if k - 2 < tm_bits else None
        outs = call(
            functools.partial(sums_step_kernel, halved, at_sums + k - 1, row_step, (per_shard, at_row)),
            [shape((sums_rows, dz), BF16), shape((sums_rows, dz), F32)]
            + [shape((16, channels), BF16)] * (row_step is not None),
            [info, sums_got, sums_keep] + [known] * (row_step is not None),
            after=[send])
        sums_send, sums_keep = outs[:2]
        known = outs[2] if row_step is not None else known
        sums_got = swapped(sums_send, sums_exchanges[k - 1])
        ordered = [sums_send]
    assert now_a == 1 and sums_rows == size
    feat_grad, last = call(
        feat_kernel,
        shape((rows_in, channels), BF16),
        [info, hidden_grad, known, weight],
        after=[sums_send],
        token=True,
        scratch=[VMEM((frames + 8, channels), F32), VMEM((channels // LANES, rows_in, LANES), F32)],
    )

    corr, piece, mine = call(
        functools.partial(last_kernel, rows_a, rows_c - extra),
        [shape((rows_a, LANES), F32), shape((rows_c - extra, LANES), BF16),
         shape((rows_c + size * (dz // LANES), LANES), BF16)],
        [info, got, keep_a, keep_c, sums_got, sums_keep],
        after=[last])
    parts = [piece, swapped(mine, exchanges[0]), swapped(piece, exchanges[1]), crossed(piece, exchanges[1])]
    conv_grad, last = call(
        functools.partial(conv_out_kernel, total_frames, at_start),
        shape((owner_rows, channels), F32),
        [info, corr, proj],
        after=[piece],
        token=True,
        scratch=[VMEM((LANES, channels), F32)],
    )
    proj_grad, bias_grad, code_means, code_usage = call(
        functools.partial(out_kernel, total_frames, book_size / total_frames, dz, at_pieces, now_c, extra),
        [shape((channels, dz), F32), shape((1, channels), F32), shape((levels, per_shard, dz), BF16),
         shape((levels, per_shard), F32)],
        [info, mine] + parts,
        after=[last],
    )
    return feat_grad, conv_grad, bias_grad[0], proj_grad, code_means, code_usage


def solution(mesh):
    placed = (P(("dp", "tm"), None), P("dp", None, "tm"), P(), P(), P(), P())
    return jax.shard_map(
        shards,
        mesh=mesh,
        in_specs=placed,
        out_specs=(
            P(("dp", "tm"), None),
            P(("dp", "tm"), None),
            P(),
            P(),
            P(None, "tm", None),
            P(None, "tm"),
        ),
        check_vma=False,
    )
```

```python
import functools

import jax
import jax.numpy as jnp
from jax import lax
from jax.experimental import pallas as pl
from jax.experimental.pallas import tpu as pltpu
from jax.sharding import PartitionSpec as P

BF16 = jnp.bfloat16
F32 = jnp.float32
LANES = 128
VMEM_LIMIT = 16 * 1024 * 1024


def log2(value):
    assert value & (value - 1) == 0
    return value.bit_length() - 1


def nn(a, b):
    return lax.dot_general(a, b, (((1,), (0,)), ((), ())), preferred_element_type=F32)


def nt(a, b):
    return lax.dot_general(a, b, (((1,), (1,)), ((), ())), preferred_element_type=F32)


VMEM = pltpu.VMEM


def call(body, out_shape, args, after=(), scratch=(), aliases=None, token=False, flops=0):
    count = len(args)
    many = isinstance(out_shape, (list, tuple))
    shapes = list(out_shape) if many else [out_shape]

    def kernel(*refs):
        ends = count + len(after)
        if token:
            refs[ends + len(shapes)][...] = jnp.zeros((8, LANES), F32)
            refs = refs[:ends + len(shapes)] + refs[ends + len(shapes) + 1:]
        body(*refs[:count], *refs[ends:])

    specs = [pl.BlockSpec(memory_space=pltpu.SMEM)]
    specs += [pl.BlockSpec(memory_space=VMEM)] * (count - 1)
    specs += [pl.BlockSpec(memory_space=pl.ANY)] * len(after)
    shown = shapes + [shape((8, LANES), F32)] * token
    outs = pl.pallas_call(
        kernel,
        out_shape=shown,
        in_specs=specs,
        out_specs=[pl.BlockSpec(memory_space=VMEM)] * len(shown),
        scratch_shapes=list(scratch),
        input_output_aliases=aliases or {},
        compiler_params=pltpu.CompilerParams(vmem_limit_bytes=VMEM_LIMIT),
        cost_estimate=pl.CostEstimate(flops=flops, bytes_accessed=0, transcendentals=0),
    )(*args, *after)
    return outs if len(shown) > 1 else outs[0]


def shape(dims, dtype):
    return jax.ShapeDtypeStruct(dims, dtype)


def digits_of(value):
    high = value.astype(BF16).astype(F32)
    rest = value - high
    middle = rest.astype(BF16).astype(F32)
    low = (rest - middle).astype(BF16).astype(F32)
    return high, middle, low


def one_hot(codes, axis_codes, first, count):
    frames = codes.shape[1 - axis_codes]
    dims = (count, frames) if axis_codes == 0 else (frames, count)
    places = lax.broadcasted_iota(jnp.int32, dims, axis_codes) + first
    return jnp.where(codes == places, 1.0, 0.0).astype(BF16)


def halo_kernel(info, rows, out):
    out[...] = rows[...]


def walk(orders, halved, count):
    start = 1 if halved else 0
    shown = count // 2 if halved else count
    bits = log2(shown)
    step = 2 if shown > 1 and all(order[-1] == 0 for order in orders) else 1
    for position in range(0, shown, step):
        yield position, [
            sum(((position >> (bits - 1 - k)) & 1) << bit for k, bit in enumerate(order[start:])) for order in orders
        ], step


def correlate(flipped, sources, plan, core, bit, out):
    dz = flipped.shape[0]
    at = 0
    for source, (count, orders, halved) in zip(sources, plan):
        for position, pieces, step in walk(orders, halved, count):
            column = pieces[0] + core * (pieces[1] - pieces[0])
            if halved:
                column = column + (bit << orders[0][0])
            column = pl.multiple_of(column * LANES, LANES)
            product = nn(flipped, source[:, pl.ds(column, step * LANES)])
            for j in range(step):
                top = (at + position + j) * dz
                out[top:top + dz, :] = product[:, j * LANES:(j + 1) * LANES].astype(out.dtype)
        at += count // 2 if halved else count
    return at * dz


def code_digits(codes, dz, rows):
    parts = []
    for part in (codes >> 8, codes & 255):
        for start in range(0, codes.shape[1], dz):
            piece = part[:, start:start + dz].astype(F32)
            if piece.shape[1] < dz:
                piece = jnp.concatenate([piece, jnp.zeros((1, dz - piece.shape[1]), F32)], 1)
            parts.append(piece)
    parts.append(jnp.zeros((rows - len(parts), dz), F32))
    return jnp.concatenate(parts, 0).astype(BF16)


def codes_of(block, frames):
    dz = block.shape[1]
    per = -(-frames // dz)
    digits = block[...].astype(F32)
    parts = [jnp.concatenate([digits[k * per + j:k * per + j + 1, :] for j in range(per)], 1)[:, :frames]
             for k in range(2)]
    return (parts[0] * 256.0 + parts[1]).astype(jnp.int32)


def residuals(hidden, proj, chosen):
    latent = nn(hidden, proj)
    once = latent - chosen[0].astype(F32)
    total = once + (once - chosen[1].astype(F32))
    return latent, once, total.astype(BF16)


def put_columns(out, at, rows, block):
    for j in range(block.shape[1] // LANES):
        out[at + j * rows:at + j * rows + block.shape[0], :] = block[:, j * LANES:(j + 1) * LANES]


def local_kernel(plan, info, feats, weight, bias, codes, books, proj,
                 unfold, hidden, latent_grad, flipped, own, send, first, part, wide, chosen):
    rows, channels = feats.shape
    frames = rows // 2
    dz = proj.shape[1]
    for j in range(channels // LANES):
        wide[j, 0:8, :] = jnp.zeros((8, LANES), F32)
        wide[j, 8:, :] = feats[:, j * LANES:(j + 1) * LANES].astype(F32)
        for tap in range(4):
            start = tap * channels + j * LANES
            unfold[:, start:start + LANES] = wide[j, pl.ds(6 + tap, frames, stride=2), :].astype(BF16)
    conv = nn(unfold[...], weight[...]) + bias[...]
    first[...] = conv[0:16, :]
    hidden[...] = conv.astype(BF16)
    levels = books.shape[0]
    padded = jnp.concatenate([codes[...].astype(F32), jnp.zeros((8 - levels, frames), F32)], 0)
    tall = jnp.transpose(padded).astype(jnp.int32)
    for level in range(levels):
        matches = one_hot(tall[:, level:level + 1], 1, 0, books.shape[1])
        chosen[level] = nn(matches, books[level]).astype(BF16)
    latent, once, grad = residuals(hidden[...], proj[...], chosen)
    latent_grad[...] = grad
    row = lax.broadcasted_iota(jnp.int32, grad.shape, 0)
    flipped[...] = jnp.transpose(jnp.where(row == 0, 0.0, grad.astype(F32))).astype(BF16)
    bit = info[0]
    at = correlate(flipped[...], (unfold, hidden), plan, 1 - bit, 1 - bit, part)
    rows_b = own.shape[0]
    code_rows = rows_b - frames
    digits = [code_digits(codes[level:level + 1, :], dz, code_rows) for level in range(2)]
    own[0:frames, :] = jnp.where(bit == 1, once, latent).astype(BF16)
    own[frames:, :] = jnp.where(bit == 1, digits[1], digits[0])
    put_columns(send, at, rows_b, jnp.where(bit == 1, latent, once).astype(BF16))
    put_columns(send, at + frames, rows_b, jnp.where(bit == 1, digits[0], digits[1]))
    for level in range(levels):
        part[at + level * 16 * (dz // LANES):at + (level + 1) * 16 * (dz // LANES), :] = jnp.concatenate(
            [chosen[level, 0:16, j * LANES:(j + 1) * LANES].astype(F32) for j in range(dz // LANES)], 0)


def frame_kernel(plan, info, halo, first, part, weight, proj, unfold_in, hidden_in, grad_in, flipped_in, own_in, send_in,
                 unfold, hidden, latent_grad, flipped, own, send):
    width = unfold.shape[1]
    half = width // 2
    dz = proj.shape[1]
    row = lax.broadcasted_iota(jnp.int32, (16, half), 0)
    left = jnp.concatenate([halo[0:1, :], halo[1:2, :]], 1).astype(F32)
    head = jnp.where(row == 0, jnp.broadcast_to(left, (16, half)), 0.0)
    unfold[0:16, 0:half] = (unfold_in[0:16, 0:half].astype(F32) + head).astype(BF16)
    fix = nn(head.astype(BF16), weight[0:half, :])
    hidden[0:16, :] = (first[...] + fix).astype(BF16)
    top = hidden[0:16, :]
    pieces = part.shape[0] - 32 * (dz // LANES)
    chosen = []
    for level in range(2):
        at = pieces + level * 16 * (dz // LANES)
        chosen.append(jnp.concatenate([part[at + j * 16:at + (j + 1) * 16, :] for j in range(dz // LANES)], 1))
    latent, once, grad = residuals(top, proj[...], chosen)
    latent_grad[0:16, :] = grad
    flipped[:, 0:LANES] = jnp.transpose(latent_grad[0:LANES, :].astype(F32)).astype(BF16)
    column = flipped[:, 0:LANES].astype(F32)[:, 0:1]
    bit = info[0]
    at = 0
    for source, (count, orders, halved) in zip((unfold, hidden), plan):
        rows = source[0:16, :].astype(F32)[0:1, :]
        for position, places, step in walk(orders, halved, count):
            for j in range(step):
                offsets = [places[0] + j, places[1] + j]
                low = [offset for offset in offsets]
                high = [offset + (1 << orders[0][0] if halved else 0) for offset in offsets]
                picked = [rows[:, k * LANES:(k + 1) * LANES] for k in low + high]
                piece = jnp.where(bit == 1, picked[0], picked[3]) if halved else jnp.where(bit == 1, picked[0], picked[1])
                begin = (at + position + j) * dz
                send[begin:begin + dz, :] = (part[begin:begin + dz, :] + column * piece).astype(BF16)
        at += count // 2 if halved else count
    rows_b = own.shape[0]
    own[0:16, :] = jnp.where(bit == 1, once, latent).astype(BF16)
    put_columns(send, at * dz, rows_b, jnp.where(bit == 1, latent, once).astype(BF16))


def rest_kernel(plan, info, flipped, unfold, hidden, latent_grad, proj, keep_a, keep_c, hidden_grad, extras, row):
    bit = info[0]
    correlate(flipped[...], (unfold,), plan[:1], bit, bit, keep_a)
    correlate(flipped[...], (hidden,), plan[1:], bit, bit, keep_c)
    back = nt(latent_grad[...], proj[...]).astype(BF16)
    hidden_grad[...] = back
    row[...] = back[0:16, :]
    stride = extras.shape[0] // 4
    extras[...] = jnp.zeros(extras.shape, F32)
    sums = jnp.sum(back.astype(F32), 0, keepdims=True)
    for digit, part in enumerate(digits_of(sums)):
        for j in range(sums.shape[1] // LANES):
            extras[digit * stride + j:digit * stride + j + 1, :] = part[:, j * LANES:(j + 1) * LANES]


def split_sum(halved, bit, got, at, kept, rows, send, to, keep):
    if halved:
        half = rows // 2
        away = pl.multiple_of((1 - bit) * half, 16)
        home = pl.multiple_of(bit * half, 16)
        send[to:to + half, :] = (kept[pl.ds(away, half), :] + got[pl.ds(at + away, half), :].astype(F32)).astype(BF16)
        keep[0:half, :] = kept[pl.ds(home, half), :] + got[pl.ds(at + home, half), :].astype(F32)
        return half
    total = (kept[0:rows, :] + got[at:at + rows, :].astype(F32)).astype(BF16)
    send[to:to + rows, :] = total
    keep[0:rows, :] = total.astype(F32)
    return rows


def add_digits(mine, theirs):
    stride = mine.shape[0] // 4
    return ((mine[0:stride] + mine[stride:2 * stride]) + mine[2 * stride:3 * stride]) + (
        (theirs[0:stride] + theirs[stride:2 * stride]) + theirs[2 * stride:3 * stride])


def digit_block(value):
    return jnp.concatenate(list(digits_of(value)) + [jnp.zeros_like(value)], 0)


def first_step_kernel(halves, place, info, got, kept_a, kept_c, extras, send_a, send_c, keep_a, keep_c):
    (rows_a, halved_a), (rows_c, halved_c) = halves
    split_sum(halved_a, info[place], got, 0, kept_a, rows_a, send_a, 0, keep_a)
    gone = split_sum(halved_c, info[place], got, rows_a, kept_c, rows_c, send_c, 0, keep_c)
    send_c[gone:, :] = extras[...].astype(BF16)
    keep_c[gone:, :] = extras[...]


def feat_kernel(info, grad, after, weight, out, wide, inter):
    frames, channels = grad.shape
    half = weight.shape[0] // 2
    wide[0:frames, :] = grad[...].astype(F32)
    wide[frames:, :] = jnp.broadcast_to(after[0:1, :].astype(F32), (8, channels))
    ahead = wide[pl.ds(1, frames), :].astype(BF16)
    for parity in range(2):
        rows = pl.ds(parity * (half // 2), half // 2)
        rows_after = pl.ds(half + parity * (half // 2), half // 2)
        both = nt(ahead, weight[rows, :]) + nt(grad[...], weight[rows_after, :])
        for j in range(channels // LANES):
            inter[j, pl.ds(parity, frames, stride=2), :] = both[:, j * LANES:(j + 1) * LANES]
    for j in range(channels // LANES):
        out[:, j * LANES:(j + 1) * LANES] = inter[j].astype(BF16)


def sums_kernel(first, frames, place, count, info, got, own, row, out):
    rows, dz = own.shape
    theirs = jnp.concatenate([got[first + j * rows:first + (j + 1) * rows, :] for j in range(dz // LANES)], 1)
    ones = jnp.ones((8, frames), BF16)
    parts = []
    for block in (own[...], theirs):
        parts.append((block[0:frames, :], codes_of(block[frames:, :], frames)))
    size = count + 16
    riding = [row[...].astype(F32)[0:1, :]]
    for top in range(0, out.shape[0], size):
        total = jnp.zeros((count, dz), F32)
        counts = jnp.zeros((8, count), F32)
        for values, codes in parts:
            matches = one_hot(codes, 0, info[place], count)
            total = total + nn(matches, values)
            counts = counts + nt(ones, matches)
        out[top:top + count, :] = total.astype(out.dtype)
        out[top + count:top + size, :] = count_rows(counts[0:1], dz, riding).astype(out.dtype)
        place += 1


def count_rows(count, width, riding=()):
    high = jnp.floor(count * (1.0 / 65536.0))
    rest = count - high * 65536.0
    middle = jnp.floor(rest * (1.0 / 256.0))
    low = rest - middle * 256.0
    block = jnp.concatenate([high, middle, low], 0)
    if count.shape[1] < width:
        block = jnp.concatenate([block, jnp.zeros((3, width - count.shape[1]), F32)], 1)
    parts = [block]
    for row in riding:
        parts += [row[:, at:at + width] for at in range(0, row.shape[1], width)]
    left = 16 - sum(part.shape[0] for part in parts)
    return jnp.concatenate(parts + [jnp.zeros((left, width), F32)] * (left > 0), 0)


def riding_row(block, index, parts):
    return jnp.concatenate([block[3 + index * parts + j:4 + index * parts + j, :] for j in range(parts)], 1)


def count_of(block, own):
    return (block[0:1] * 65536.0 + block[1:2] * 256.0 + block[2:3])[:, :own]


def sums_step_kernel(halved, place, row_step, row_place, info, got, kept, *refs):
    riding = ()
    if row_step is not None:
        known, refs = refs[0][...].astype(F32), refs[1:]
        after, refs = refs[-1], refs[:-1]
        parts = known.shape[1] // got.shape[1]
        block = got[row_place[0]:row_place[0] + 16, :].astype(F32)
        rows = [known[j:j + 1, :] for j in range(1 << row_step)]
        rows += [riding_row(block, j, parts) for j in range(1 << row_step)]
        if halved:
            riding = rows
            total = rows + [jnp.zeros((16 - len(rows), known.shape[1]), F32)]
            after[...] = jnp.concatenate(total, 0).astype(BF16)
        else:
            wide = jnp.zeros(after.shape, F32)
            for j in range(1, len(rows)):
                wide = jnp.where(info[row_place[1]] == j, jnp.broadcast_to(rows[j], after.shape), wide)
            after[...] = wide.astype(BF16)
    send, keep = refs
    dz = got.shape[1]
    bit = info[place]
    half = kept.shape[0] // 2 if halved else 0
    outs = [(send, (1 - bit) * half), (keep, bit * half)] if halved else [(send, 0)]
    count = row_place[0]
    size = count + 16
    for out, start in outs:
        for top in range(0, keep.shape[0], size):
            here = top + pl.multiple_of(start, 16) if halved else top
            sums = pl.ds(here, count)
            tail = pl.ds(here + count, 16)
            value = kept[sums, :].astype(F32) + got[sums, :].astype(F32)
            number = count_of(kept[tail, :].astype(F32), count) + count_of(got[tail, :].astype(F32), count)
            out[top:top + count, :] = value.astype(out.dtype)
            out[top + count:top + size, :] = count_rows(number, dz, riding).astype(out.dtype)
    if not halved:
        keep[...] = send[0:keep.shape[0], :].astype(F32)


def swap_halves(first, second, core):
    half = LANES // 2
    left = lax.broadcasted_iota(jnp.int32, first.shape, 1) < half
    turned_first, turned_second = pltpu.roll(first, half, 1), pltpu.roll(second, half, 1)
    swapped_first = jnp.where(left, first, turned_second)
    swapped_second = jnp.where(left, turned_first, second)
    return jnp.where(core == 1, swapped_first, first), jnp.where(core == 1, swapped_second, second)


def step_kernel(halves, at_c, place, mixed, info, got, got_c, kept_a, kept_c, send, keep_a, keep_c):
    (rows_a, halved_a), (rows_c, halved_c) = halves
    if mixed:
        to = rows_a // 2
        total = kept_a[0:rows_a, :] + got[0:rows_a, :].astype(F32)
        first, second = swap_halves(total[0:to, :], total[to:, :], info[0])
        low = info[place] == 0
        send[0:to, :] = jnp.where(low, second, first).astype(BF16)
        keep_a[...] = jnp.where(low, first, second)
    else:
        to = split_sum(halved_a, info[place], got, 0, kept_a, rows_a, send, 0, keep_a)
    gone = split_sum(halved_c, info[place], got_c, at_c, kept_c, rows_c, send, to, keep_c)
    block = digit_block(add_digits(kept_c[rows_c:, :], got_c[at_c + rows_c:, :].astype(F32)))
    keep_c[gone:, :] = block
    to += gone
    send[to:to + block.shape[0], :] = block.astype(BF16)
    to += block.shape[0]
    if to < send.shape[0]:
        send[to:, :] = jnp.zeros((send.shape[0] - to, LANES), BF16)


def last_kernel(rows_a, rows, info, got, kept_a, kept_c, sums_got, sums_kept, corr, pieces, mine):
    corr[...] = kept_a[...] + got[0:rows_a, :].astype(F32)
    pieces[...] = (kept_c[0:rows, :] + got[rows_a:rows_a + rows, :].astype(F32)).astype(BF16)
    block = digit_block(add_digits(kept_c[rows:, :], got[rows_a + rows:rows_a + kept_c.shape[0], :].astype(F32)))
    mine[0:rows, :] = pieces[...]
    mine[rows:kept_c.shape[0], :] = block.astype(BF16)
    at = kept_c.shape[0]
    count = sums_kept.shape[0] - 16
    number = count_of(sums_kept[count:, :].astype(F32), count) + count_of(sums_got[count:, :].astype(F32), count)
    square = (count, count)
    same = lax.broadcasted_iota(jnp.int32, square, 0) == lax.broadcasted_iota(jnp.int32, square, 1)
    tall = jnp.sum(jnp.where(same, jnp.broadcast_to(number, square), 0.0), 1, keepdims=True)
    total = sums_kept[0:count, :].astype(F32) + sums_got[0:count, :].astype(F32)
    means = (total / jnp.maximum(tall, 1.0)).astype(BF16)
    digits = count_rows(number, means.shape[1]).astype(BF16)
    for j in range(means.shape[1] // LANES):
        mine[at:at + count, :] = means[:, j * LANES:(j + 1) * LANES]
        mine[at + count:at + count + 16, :] = digits[:, j * LANES:(j + 1) * LANES]
        at += count + 16


def conv_out_kernel(total_frames, place, info, corr, proj, out, wide):
    rows = out.shape[0]
    flipped = jnp.transpose(corr[...])
    high = flipped.astype(BF16)
    low = (flipped - high.astype(F32)).astype(BF16)
    wide[...] = (nt(high, proj[...]) + nt(low, proj[...])) * (1.0 / total_frames)
    start = info[place]
    if rows % 8 == 0:
        out[...] = wide[pl.ds(pl.multiple_of(start, 8), rows), :]
    else:
        taken = wide[0:rows, :]
        for other in range(rows, wide.shape[0], rows):
            taken = jnp.where(start == other, wide[other:other + rows, :], taken)
        out[...] = taken


def out_kernel(total_frames, use_scale, dz, place, inner, extra, info, mine, *refs):
    parts, (out, bias, means, usage) = refs[:-4], refs[-4:]
    theirs = parts[1]
    scale = 1.0 / total_frames
    top = inner * dz
    value = add_digits(mine[top:top + extra, :].astype(F32), theirs[top:top + extra, :].astype(F32)) * scale
    for j in range(bias.shape[1] // LANES):
        bias[:, j * LANES:(j + 1) * LANES] = value[j:j + 1, :]
    bit = info[0]
    count = means.shape[1]
    numbers = []
    for ref, level in ((mine, bit), (theirs, 1 - bit)):
        at = top + extra
        blocks = []
        for j in range(dz // LANES):
            blocks.append(ref[at:at + count + 16, :])
            at += count + 16
        whole = jnp.concatenate(blocks, 1)
        means[level] = whole[0:count, :]
        numbers.append(count_of(whole[count:, :].astype(F32), count) * use_scale)
    usage[0:1, :] = jnp.where(bit == 1, numbers[1], numbers[0])
    usage[1:2, :] = jnp.where(bit == 1, numbers[0], numbers[1])
    for j, ref in enumerate(parts):
        for k in range(inner):
            start = pl.multiple_of((info[place + j] + k) * LANES, LANES)
            turned = jnp.transpose(ref[k * dz:(k + 1) * dz, :])
            out[pl.ds(start, LANES), :] = turned.astype(F32) * scale


def shifted(block, axis, distance):
    devices = range(lax.axis_size(axis))
    route = [(i - distance, i) for i in devices if i - distance in devices]
    return lax.ppermute(block, axis, route)


def swapped(block, steps):
    tm = lax.axis_size("tm")

    def partner(device):
        axis, bit = steps[(device // tm) & 1]
        return device ^ ((1 << bit) * (tm if axis == "dp" else 1))

    route = [(device, partner(device)) for device in range(lax.axis_size("dp") * tm)]
    return lax.ppermute(block, ("dp", "tm"), route)


def crossed(block, steps):
    tm = lax.axis_size("tm")

    def partner(device):
        axis, bit = steps[(device // tm) & 1]
        return device ^ tm ^ ((1 << bit) * (tm if axis == "dp" else 1))

    route = [(device, partner(device)) for device in range(lax.axis_size("dp") * tm)]
    return lax.ppermute(block, ("dp", "tm"), route)


def shards(feats, codes, conv_weight, conv_bias, proj_weight, codebooks):
    dp, tm = lax.axis_size("dp"), lax.axis_size("tm")
    rows_in, channels = feats.shape
    frames = rows_in // 2
    levels, book_size, dz = codebooks.shape
    assert levels == 2
    width = conv_weight.shape[0]
    total_frames = frames * dp * tm
    per_shard = book_size // tm
    dp_bits, tm_bits = log2(dp), log2(tm)
    owner_rows = width // (dp * tm)

    assert dp_bits >= 3 and 1 <= tm_bits <= 2
    pieces_a, pieces_c = width // LANES, channels // LANES
    under = max(dp_bits + tm_bits - log2(pieces_a), 0)
    c_bits = 2
    assert pieces_c >= 4
    whole_bits = [b for b in range(1, dp_bits) if b + tm_bits < under]
    piece_bits = [b for b in range(1, dp_bits) if b + tm_bits >= under]
    paths = [[("dp", b) for b in bits] for bits in (whole_bits + piece_bits, whole_bits[::-1] + piece_bits[::-1])]
    mixed = under == 1 and tm_bits == 2
    turned = mixed or under == 0 or under >= tm_bits
    up = [("tm", b) for b in range(tm_bits)]
    paths[0] += up[::-1]
    paths[1] += up if turned else up[::-1]
    exchanges = list(zip([("dp", 0)] + paths[0], [("dp", 0)] + paths[1]))
    sums_up = [("dp", b) for b in range(1, dp_bits)]
    sums_exchanges = list(zip(up[::-1] + sums_up, up + sums_up[::-1]))

    def piece_bit(step):
        axis, b = step
        bit = b + (tm_bits if axis == "dp" else 0)
        return bit - under if bit >= under else None

    a_split = [piece_bit(steps[0]) is not None for steps in exchanges]
    c_split = [log2(pieces_c) - 1 - k if k < c_bits else None for k in range(len(exchanges))]

    def order_of(split, count):
        used = [b for b in split if b is not None]
        return used + [b for b in reversed(range(log2(count))) if b not in used]

    orders = [order_of([piece_bit(steps[core]) for steps in exchanges], pieces_a) for core in range(2)]
    order_c = order_of(c_split, pieces_c)
    plan = [(pieces_a, orders, a_split[0]), (pieces_c, [order_c, order_c], True)]
    now_a = pieces_a // 2 if plan[0][2] else pieces_a
    now_c = pieces_c // 2

    at_dp, at_tm = lax.axis_index("dp"), lax.axis_index("tm")
    core = at_dp & 1

    def on_core(values):
        return values[0] + core * (values[1] - values[0])

    def bit_at(step):
        axis, b = step
        return ((at_dp if axis == "dp" else at_tm) >> b) & 1

    bits = [on_core([bit_at(step) for step in steps]) for steps in exchanges]
    sums_bits = [on_core([bit_at(step) for step in steps]) for steps in sums_exchanges]
    shared = [bit_at(step) for step in exchanges[1]]
    mine_c, other_c = on_core(shared), on_core(shared[::-1])
    places = [2 * core + mine_c, 2 * (1 - core) + other_c, 2 * core + 1 - mine_c, 2 * (1 - core) + 1 - other_c]
    places = [place << (log2(pieces_c) - c_bits) for place in places]
    lists = []
    for way in ([b for _, b in up[::-1]], [b for _, b in up]):
        lists.append([sum(((position >> (tm_bits - 1 - j)) & 1) << b for j, b in enumerate(way)) for position in range(tm)])
    first_bit = on_core([tm_bits - 1, 0])
    lead = (at_tm >> first_bit) & 1
    quarters = [on_core([lists[0][j], lists[1][j]]) for j in range(tm // 2)]
    send_codes = [(q + ((1 - lead) << first_bit)) * per_shard for q in quarters]
    keep_codes = [(q + (lead << first_bit)) * per_shard for q in quarters]
    differ = at_tm ^ (at_tm + 1)
    ways = [sum(((differ >> b) & 1) << j for j, b in enumerate(way)) for way in (
        list(reversed(range(tm_bits))), list(range(tm_bits)))]
    row_code = jnp.where(at_tm + 1 < tm, on_core(ways), 0)
    if turned and not mixed:
        start = ((at_dp * tm + at_tm) * owner_rows) & (LANES - 1)
    else:
        start = on_core([(at_dp * tm + at_tm) * owner_rows, (at_tm >> 1) * owner_rows if mixed else (
            at_dp * tm + at_tm) * owner_rows]) & (LANES - 1)
    at_start = len(bits)
    at_codes = at_start + 1
    at_pieces = at_codes + tm
    at_sums = at_pieces + len(places)
    at_row = at_sums + len(sums_bits)
    info = jnp.stack(bits + [start] + send_codes + keep_codes + places + sums_bits + [row_code]).astype(jnp.int32)

    halo = shifted(call(halo_kernel, shape((2, channels), BF16), [info, feats[-2:]], flops=10 ** 11), "tm", 1)
    weight, proj, codes = conv_weight, proj_weight, codes[0]
    extra = 4 * (-(-channels // LANES // 8) * 8)
    code_rows = -(-(2 * -(-frames // dz)) // 16) * 16
    corr_rows = (now_a + now_c) * dz
    rows_b = frames + code_rows
    shared = [shape((frames, width), BF16), shape((frames, channels), BF16), shape((frames, dz), BF16),
              shape((dz, frames), BF16), shape((rows_b, dz), BF16),
              shape((corr_rows + rows_b * (dz // LANES), LANES), BF16)]
    *arrays, first, part = call(
        functools.partial(local_kernel, plan),
        shared + [shape((16, channels), F32), shape((corr_rows + 32 * (dz // LANES), LANES), F32)],
        [info, feats, weight, conv_bias[None, :], codes, codebooks, proj],
        scratch=[VMEM((channels // LANES, rows_in + 8, LANES), F32), VMEM((levels, frames, dz), BF16)],
    )
    unfold, hidden, latent_grad, flipped, own, send = call(
        functools.partial(frame_kernel, plan),
        shared,
        [info, halo, first, part, weight, proj] + arrays,
        aliases={6 + k: k for k in range(len(shared))},
    )
    got = swapped(send, exchanges[0])
    keep_a, keep_c, hidden_grad, extras, row = call(
        functools.partial(rest_kernel, plan),
        [shape((now_a * dz, LANES), F32), shape((now_c * dz, LANES), F32), shape((frames, channels), BF16),
         shape((extra, LANES), F32), shape((16, channels), BF16)],
        [info, flipped, unfold, hidden, latent_grad, proj],
        after=[send],
    )

    def halves_at(k):
        nonlocal now_a, now_c
        halves = [(now_a * dz, a_split[k]), (now_c * dz, c_split[k] is not None)]
        now_a = now_a // 2 if halves[0][1] else now_a
        now_c = now_c // 2 if halves[1][1] else now_c
        return halves, now_a * dz, now_c * dz + extra

    size = per_shard + 16
    sums_rows = size * (tm // 2)
    sums_send = call(
        functools.partial(sums_kernel, corr_rows, frames, at_codes, per_shard),
        shape((sums_rows, dz), BF16),
        [info, got, own, row])
    sums_got = swapped(sums_send, sums_exchanges[0])
    halves, rows_a, rows_c = halves_at(1)
    send, send_c, keep_a, keep_c = call(
        functools.partial(first_step_kernel, halves, 1),
        [shape((rows_a, LANES), BF16), shape((rows_c, LANES), BF16), shape((rows_a, LANES), F32),
         shape((rows_c, LANES), F32)],
        [info, got, keep_a, keep_c, extras],
        after=[sums_send])
    sums_keep = call(
        functools.partial(sums_kernel, corr_rows, frames, at_codes + tm // 2, per_shard),
        shape((sums_rows, dz), F32),
        [info, got, own, row],
        after=[send])
    got, got_c = swapped(send, exchanges[1]), swapped(send_c, exchanges[1])
    known = row
    ordered = [sums_keep, sums_got]
    for k in range(2, len(exchanges)):
        at_c = 0 if k == 2 else rows_a
        halves, rows_a, rows_c = halves_at(k)
        spare = 16 * (k == len(exchanges) - 1)
        send, keep_a, keep_c = call(
            functools.partial(step_kernel, halves, at_c, k, mixed and k == dp_bits),
            [shape((rows_a + rows_c + spare, LANES), BF16), shape((rows_a, LANES), F32), shape((rows_c, LANES), F32)],
            [info, got, got_c, keep_a, keep_c],
            after=ordered)
        got = got_c = swapped(send, exchanges[k])
        halved = sums_exchanges[k - 1][0][0] == "tm"
        sums_rows = sums_rows // 2 if halved else sums_rows
        row_step = k - 2 if k - 2 < tm_bits else None
        outs = call(
            functools.partial(sums_step_kernel, halved, at_sums + k - 1, row_step, (per_shard, at_row)),
            [shape((sums_rows, dz), BF16), shape((sums_rows, dz), F32)]
            + [shape((16, channels), BF16)] * (row_step is not None),
            [info, sums_got, sums_keep] + [known] * (row_step is not None),
            after=[send])
        sums_send, sums_keep = outs[:2]
        known = outs[2] if row_step is not None else known
        sums_got = swapped(sums_send, sums_exchanges[k - 1])
        ordered = [sums_send]
    assert now_a == 1 and sums_rows == size
    feat_grad, last = call(
        feat_kernel,
        shape((rows_in, channels), BF16),
        [info, hidden_grad, known, weight],
        after=[sums_send],
        token=True,
        scratch=[VMEM((frames + 8, channels), F32), VMEM((channels // LANES, rows_in, LANES), F32)],
    )

    corr, piece, mine = call(
        functools.partial(last_kernel, rows_a, rows_c - extra),
        [shape((rows_a, LANES), F32), shape((rows_c - extra, LANES), BF16),
         shape((rows_c + size * (dz // LANES), LANES), BF16)],
        [info, got, keep_a, keep_c, sums_got, sums_keep],
        after=[last])
    parts = [piece, swapped(mine, exchanges[0]), swapped(piece, exchanges[1]), crossed(piece, exchanges[1])]
    conv_grad, last = call(
        functools.partial(conv_out_kernel, total_frames, at_start),
        shape((owner_rows, channels), F32),
        [info, corr, proj],
        after=[piece],
        token=True,
        scratch=[VMEM((LANES, channels), F32)],
    )
    proj_grad, bias_grad, code_means, code_usage = call(
        functools.partial(out_kernel, total_frames, book_size / total_frames, dz, at_pieces, now_c, extra),
        [shape((channels, dz), F32), shape((1, channels), F32), shape((levels, per_shard, dz), BF16),
         shape((levels, per_shard), F32)],
        [info, mine] + parts,
        after=[last],
    )
    return feat_grad, conv_grad, bias_grad[0], proj_grad, code_means, code_usage


def solution(mesh):
    placed = (P(("dp", "tm"), None), P("dp", None, "tm"), P(), P(), P(), P())
    return jax.shard_map(
        shards,
        mesh=mesh,
        in_specs=placed,
        out_specs=(
            P(("dp", "tm"), None),
            P(("dp", "tm"), None),
            P(),
            P(),
            P(None, "tm", None),
            P(None, "tm"),
        ),
        check_vma=False,
    )
```

```python
import functools

import jax
import jax.numpy as jnp
from jax import lax
from jax.experimental import pallas as pl
from jax.experimental.pallas import tpu as pltpu
from jax.sharding import PartitionSpec as P

BF16 = jnp.bfloat16
F32 = jnp.float32
LANES = 128
VMEM_LIMIT = 16 * 1024 * 1024


def log2(value):
    assert value & (value - 1) == 0
    return value.bit_length() - 1


def nn(a, b):
    return lax.dot_general(a, b, (((1,), (0,)), ((), ())), preferred_element_type=F32)


def nt(a, b):
    return lax.dot_general(a, b, (((1,), (1,)), ((), ())), preferred_element_type=F32)


VMEM = pltpu.VMEM


def call(body, out_shape, args, after=(), scratch=(), aliases=None, token=False, flops=0):
    info, args = args[0], args[1:]
    count = len(args)
    many = isinstance(out_shape, (list, tuple))
    shapes = list(out_shape) if many else [out_shape]

    def kernel(*refs):
        ends = count + len(after)
        if token:
            refs[ends + len(shapes)][...] = jnp.zeros((8, LANES), F32)
            refs = refs[:ends + len(shapes)] + refs[ends + len(shapes) + 1:]
        body(info(), *refs[:count], *refs[ends:])

    specs = [pl.BlockSpec(memory_space=VMEM)] * count + [pl.BlockSpec(memory_space=pl.ANY)] * len(after)
    shown = shapes + [shape((8, LANES), F32)] * token
    outs = pl.pallas_call(
        kernel,
        out_shape=shown,
        in_specs=specs,
        out_specs=[pl.BlockSpec(memory_space=VMEM)] * len(shown),
        scratch_shapes=list(scratch),
        input_output_aliases={at - 1: out for at, out in (aliases or {}).items()},
        compiler_params=pltpu.CompilerParams(vmem_limit_bytes=VMEM_LIMIT),
        cost_estimate=pl.CostEstimate(flops=flops, bytes_accessed=0, transcendentals=0),
    )(*args, *after)
    return outs if len(shown) > 1 else outs[0]


def shape(dims, dtype):
    return jax.ShapeDtypeStruct(dims, dtype)


def digits_of(value):
    high = value.astype(BF16).astype(F32)
    rest = value - high
    middle = rest.astype(BF16).astype(F32)
    low = (rest - middle).astype(BF16).astype(F32)
    return high, middle, low


def one_hot(codes, axis_codes, first, count):
    frames = codes.shape[1 - axis_codes]
    dims = (count, frames) if axis_codes == 0 else (frames, count)
    places = lax.broadcasted_iota(jnp.int32, dims, axis_codes) + first
    return jnp.where(codes == places, 1.0, 0.0).astype(BF16)


def halo_kernel(info, rows, out):
    out[...] = rows[...]


def walk(orders, halved, count):
    start = 1 if halved else 0
    shown = count // 2 if halved else count
    bits = log2(shown)
    step = 2 if shown > 1 and all(order[-1] == 0 for order in orders) else 1
    for position in range(0, shown, step):
        yield position, [
            sum(((position >> (bits - 1 - k)) & 1) << bit for k, bit in enumerate(order[start:])) for order in orders
        ], step


def correlate(flipped, sources, plan, core, bit, out):
    dz = flipped.shape[0]
    at = 0
    for source, (count, orders, halved) in zip(sources, plan):
        for position, pieces, step in walk(orders, halved, count):
            column = pieces[0] + core * (pieces[1] - pieces[0])
            if halved:
                column = column + (bit << orders[0][0])
            column = pl.multiple_of(column * LANES, LANES)
            product = nn(flipped, source[:, pl.ds(column, step * LANES)])
            for j in range(step):
                top = (at + position + j) * dz
                out[top:top + dz, :] = product[:, j * LANES:(j + 1) * LANES].astype(out.dtype)
        at += count // 2 if halved else count
    return at * dz


def code_digits(codes, dz, rows):
    parts = []
    for part in (codes >> 8, codes & 255):
        for start in range(0, codes.shape[1], dz):
            piece = part[:, start:start + dz].astype(F32)
            if piece.shape[1] < dz:
                piece = jnp.concatenate([piece, jnp.zeros((1, dz - piece.shape[1]), F32)], 1)
            parts.append(piece)
    parts.append(jnp.zeros((rows - len(parts), dz), F32))
    return jnp.concatenate(parts, 0).astype(BF16)


def codes_of(block, frames):
    dz = block.shape[1]
    per = -(-frames // dz)
    digits = block[...].astype(F32)
    parts = [jnp.concatenate([digits[k * per + j:k * per + j + 1, :] for j in range(per)], 1)[:, :frames]
             for k in range(2)]
    return (parts[0] * 256.0 + parts[1]).astype(jnp.int32)


def residuals(hidden, proj, chosen):
    latent = nn(hidden, proj)
    once = latent - chosen[0].astype(F32)
    total = once + (once - chosen[1].astype(F32))
    return latent, once, total.astype(BF16)


def put_columns(out, at, rows, block):
    for j in range(block.shape[1] // LANES):
        out[at + j * rows:at + j * rows + block.shape[0], :] = block[:, j * LANES:(j + 1) * LANES]


def local_kernel(plan, info, feats, weight, bias, codes, books, proj,
                 unfold, hidden, latent_grad, flipped, own, send, first, part, wide, chosen):
    rows, channels = feats.shape
    frames = rows // 2
    dz = proj.shape[1]
    for j in range(channels // LANES):
        wide[j, 0:8, :] = jnp.zeros((8, LANES), F32)
        wide[j, 8:, :] = feats[:, j * LANES:(j + 1) * LANES].astype(F32)
        for tap in range(4):
            start = tap * channels + j * LANES
            unfold[:, start:start + LANES] = wide[j, pl.ds(6 + tap, frames, stride=2), :].astype(BF16)
    conv = nn(unfold[...], weight[...]) + bias[...]
    first[...] = conv[0:16, :]
    hidden[...] = conv.astype(BF16)
    levels = books.shape[0]
    padded = jnp.concatenate([codes[...].astype(F32), jnp.zeros((8 - levels, frames), F32)], 0)
    tall = jnp.transpose(padded).astype(jnp.int32)
    for level in range(levels):
        matches = one_hot(tall[:, level:level + 1], 1, 0, books.shape[1])
        chosen[level] = nn(matches, books[level]).astype(BF16)
    latent, once, grad = residuals(hidden[...], proj[...], chosen)
    latent_grad[...] = grad
    row = lax.broadcasted_iota(jnp.int32, grad.shape, 0)
    flipped[...] = jnp.transpose(jnp.where(row == 0, 0.0, grad.astype(F32))).astype(BF16)
    bit = info[0]
    at = correlate(flipped[...], (unfold, hidden), plan, 1 - bit, 1 - bit, part)
    rows_b = own.shape[0]
    code_rows = rows_b - frames
    digits = [code_digits(codes[level:level + 1, :], dz, code_rows) for level in range(2)]
    own[0:frames, :] = jnp.where(bit == 1, once, latent).astype(BF16)
    own[frames:, :] = jnp.where(bit == 1, digits[1], digits[0])
    put_columns(send, at, rows_b, jnp.where(bit == 1, latent, once).astype(BF16))
    put_columns(send, at + frames, rows_b, jnp.where(bit == 1, digits[0], digits[1]))
    for level in range(levels):
        part[at + level * 16 * (dz // LANES):at + (level + 1) * 16 * (dz // LANES), :] = jnp.concatenate(
            [chosen[level, 0:16, j * LANES:(j + 1) * LANES].astype(F32) for j in range(dz // LANES)], 0)


def frame_kernel(plan, info, halo, first, part, weight, proj, unfold_in, hidden_in, grad_in, flipped_in, own_in, send_in,
                 unfold, hidden, latent_grad, flipped, own, send):
    width = unfold.shape[1]
    half = width // 2
    dz = proj.shape[1]
    row = lax.broadcasted_iota(jnp.int32, (16, half), 0)
    left = jnp.concatenate([halo[0:1, :], halo[1:2, :]], 1).astype(F32)
    head = jnp.where(row == 0, jnp.broadcast_to(left, (16, half)), 0.0)
    unfold[0:16, 0:half] = (unfold_in[0:16, 0:half].astype(F32) + head).astype(BF16)
    fix = nn(head.astype(BF16), weight[0:half, :])
    hidden[0:16, :] = (first[...] + fix).astype(BF16)
    top = hidden[0:16, :]
    pieces = part.shape[0] - 32 * (dz // LANES)
    chosen = []
    for level in range(2):
        at = pieces + level * 16 * (dz // LANES)
        chosen.append(jnp.concatenate([part[at + j * 16:at + (j + 1) * 16, :] for j in range(dz // LANES)], 1))
    latent, once, grad = residuals(top, proj[...], chosen)
    latent_grad[0:16, :] = grad
    flipped[:, 0:LANES] = jnp.transpose(latent_grad[0:LANES, :].astype(F32)).astype(BF16)
    column = flipped[:, 0:LANES].astype(F32)[:, 0:1]
    bit = info[0]
    at = 0
    for source, (count, orders, halved) in zip((unfold, hidden), plan):
        rows = source[0:16, :].astype(F32)[0:1, :]
        for position, places, step in walk(orders, halved, count):
            for j in range(step):
                offsets = [places[0] + j, places[1] + j]
                low = [offset for offset in offsets]
                high = [offset + (1 << orders[0][0] if halved else 0) for offset in offsets]
                picked = [rows[:, k * LANES:(k + 1) * LANES] for k in low + high]
                piece = jnp.where(bit == 1, picked[0], picked[3]) if halved else jnp.where(bit == 1, picked[0], picked[1])
                begin = (at + position + j) * dz
                send[begin:begin + dz, :] = (part[begin:begin + dz, :] + column * piece).astype(BF16)
        at += count // 2 if halved else count
    rows_b = own.shape[0]
    own[0:16, :] = jnp.where(bit == 1, once, latent).astype(BF16)
    put_columns(send, at * dz, rows_b, jnp.where(bit == 1, latent, once).astype(BF16))


def rest_kernel(plan, info, flipped, unfold, hidden, latent_grad, proj, keep_a, keep_c, hidden_grad, extras, row):
    bit = info[0]
    correlate(flipped[...], (unfold,), plan[:1], bit, bit, keep_a)
    correlate(flipped[...], (hidden,), plan[1:], bit, bit, keep_c)
    back = nt(latent_grad[...], proj[...]).astype(BF16)
    hidden_grad[...] = back
    row[...] = back[0:16, :]
    stride = extras.shape[0] // 4
    extras[...] = jnp.zeros(extras.shape, F32)
    sums = jnp.sum(back.astype(F32), 0, keepdims=True)
    for digit, part in enumerate(digits_of(sums)):
        for j in range(sums.shape[1] // LANES):
            extras[digit * stride + j:digit * stride + j + 1, :] = part[:, j * LANES:(j + 1) * LANES]


def split_sum(halved, bit, got, at, kept, rows, send, to, keep):
    if halved:
        half = rows // 2
        away = pl.multiple_of((1 - bit) * half, 16)
        home = pl.multiple_of(bit * half, 16)
        send[to:to + half, :] = (kept[pl.ds(away, half), :] + got[pl.ds(at + away, half), :].astype(F32)).astype(BF16)
        keep[0:half, :] = kept[pl.ds(home, half), :] + got[pl.ds(at + home, half), :].astype(F32)
        return half
    total = (kept[0:rows, :] + got[at:at + rows, :].astype(F32)).astype(BF16)
    send[to:to + rows, :] = total
    keep[0:rows, :] = total.astype(F32)
    return rows


def add_digits(mine, theirs):
    stride = mine.shape[0] // 4
    return ((mine[0:stride] + mine[stride:2 * stride]) + mine[2 * stride:3 * stride]) + (
        (theirs[0:stride] + theirs[stride:2 * stride]) + theirs[2 * stride:3 * stride])


def digit_block(value):
    return jnp.concatenate(list(digits_of(value)) + [jnp.zeros_like(value)], 0)


def first_step_kernel(halves, place, info, got, kept_a, kept_c, extras, send, keep_a, keep_c):
    (rows_a, halved_a), (rows_c, halved_c) = halves
    to = split_sum(halved_a, info[place], got, 0, kept_a, rows_a, send, 0, keep_a)
    gone = split_sum(halved_c, info[place], got, rows_a, kept_c, rows_c, send, to, keep_c)
    send[to + gone:, :] = extras[...].astype(BF16)
    keep_c[gone:, :] = extras[...]


def feat_kernel(info, grad, after, weight, out, wide, inter):
    frames, channels = grad.shape
    half = weight.shape[0] // 2
    wide[0:frames, :] = grad[...].astype(F32)
    wide[frames:, :] = jnp.broadcast_to(after[0:1, :].astype(F32), (8, channels))
    ahead = wide[pl.ds(1, frames), :].astype(BF16)
    for parity in range(2):
        rows = pl.ds(parity * (half // 2), half // 2)
        rows_after = pl.ds(half + parity * (half // 2), half // 2)
        both = nt(ahead, weight[rows, :]) + nt(grad[...], weight[rows_after, :])
        for j in range(channels // LANES):
            inter[j, pl.ds(parity, frames, stride=2), :] = both[:, j * LANES:(j + 1) * LANES]
    for j in range(channels // LANES):
        out[:, j * LANES:(j + 1) * LANES] = inter[j].astype(BF16)


def sums_kernel(first, frames, place, count, info, got, own, row, out):
    rows, dz = own.shape
    theirs = jnp.concatenate([got[first + j * rows:first + (j + 1) * rows, :] for j in range(dz // LANES)], 1)
    ones = jnp.ones((8, frames), BF16)
    parts = []
    for block in (own[...], theirs):
        parts.append((block[0:frames, :], codes_of(block[frames:, :], frames)))
    size = count + 16
    riding = [row[...].astype(F32)[0:1, :]]
    for top in range(0, out.shape[0], size):
        total = jnp.zeros((count, dz), F32)
        counts = jnp.zeros((8, count), F32)
        for values, codes in parts:
            matches = one_hot(codes, 0, info[place], count)
            total = total + nn(matches, values)
            counts = counts + nt(ones, matches)
        out[top:top + count, :] = total.astype(out.dtype)
        out[top + count:top + size, :] = count_rows(counts[0:1], dz, riding).astype(out.dtype)
        place += 1


def count_rows(count, width, riding=()):
    high = jnp.floor(count * (1.0 / 65536.0))
    rest = count - high * 65536.0
    middle = jnp.floor(rest * (1.0 / 256.0))
    low = rest - middle * 256.0
    block = jnp.concatenate([high, middle, low], 0)
    if count.shape[1] < width:
        block = jnp.concatenate([block, jnp.zeros((3, width - count.shape[1]), F32)], 1)
    parts = [block]
    for row in riding:
        parts += [row[:, at:at + width] for at in range(0, row.shape[1], width)]
    left = 16 - sum(part.shape[0] for part in parts)
    return jnp.concatenate(parts + [jnp.zeros((left, width), F32)] * (left > 0), 0)


def riding_row(block, index, parts):
    return jnp.concatenate([block[3 + index * parts + j:4 + index * parts + j, :] for j in range(parts)], 1)


def count_of(block, own):
    return (block[0:1] * 65536.0 + block[1:2] * 256.0 + block[2:3])[:, :own]


def sums_step_kernel(halved, place, row_step, row_place, info, got, kept, *refs):
    riding = ()
    if row_step is not None:
        known, refs = refs[0][...].astype(F32), refs[1:]
        after, refs = refs[-1], refs[:-1]
        parts = known.shape[1] // got.shape[1]
        block = got[row_place[0]:row_place[0] + 16, :].astype(F32)
        rows = [known[j:j + 1, :] for j in range(1 << row_step)]
        rows += [riding_row(block, j, parts) for j in range(1 << row_step)]
        if halved:
            riding = rows
            total = rows + [jnp.zeros((16 - len(rows), known.shape[1]), F32)]
            after[...] = jnp.concatenate(total, 0).astype(BF16)
        else:
            wide = jnp.zeros(after.shape, F32)
            for j in range(1, len(rows)):
                wide = jnp.where(info[row_place[1]] == j, jnp.broadcast_to(rows[j], after.shape), wide)
            after[...] = wide.astype(BF16)
    send, keep = refs
    dz = got.shape[1]
    bit = info[place]
    half = kept.shape[0] // 2 if halved else 0
    outs = [(send, (1 - bit) * half), (keep, bit * half)] if halved else [(send, 0)]
    count = row_place[0]
    size = count + 16
    for out, start in outs:
        for top in range(0, keep.shape[0], size):
            here = top + pl.multiple_of(start, 16) if halved else top
            sums = pl.ds(here, count)
            tail = pl.ds(here + count, 16)
            value = kept[sums, :].astype(F32) + got[sums, :].astype(F32)
            number = count_of(kept[tail, :].astype(F32), count) + count_of(got[tail, :].astype(F32), count)
            out[top:top + count, :] = value.astype(out.dtype)
            out[top + count:top + size, :] = count_rows(number, dz, riding).astype(out.dtype)
    if not halved:
        keep[...] = send[0:keep.shape[0], :].astype(F32)


def swap_halves(first, second, core):
    half = LANES // 2
    left = lax.broadcasted_iota(jnp.int32, first.shape, 1) < half
    turned_first, turned_second = pltpu.roll(first, half, 1), pltpu.roll(second, half, 1)
    swapped_first = jnp.where(left, first, turned_second)
    swapped_second = jnp.where(left, turned_first, second)
    return jnp.where(core == 1, swapped_first, first), jnp.where(core == 1, swapped_second, second)


def step_kernel(halves, place, mixed, info, got, kept_a, kept_c, send, keep_a, keep_c):
    (rows_a, halved_a), (rows_c, halved_c) = halves
    if mixed:
        to = rows_a // 2
        total = kept_a[0:rows_a, :] + got[0:rows_a, :].astype(F32)
        first, second = swap_halves(total[0:to, :], total[to:, :], info[0])
        low = info[place] == 0
        send[0:to, :] = jnp.where(low, second, first).astype(BF16)
        keep_a[...] = jnp.where(low, first, second)
    else:
        to = split_sum(halved_a, info[place], got, 0, kept_a, rows_a, send, 0, keep_a)
    gone = split_sum(halved_c, info[place], got, rows_a, kept_c, rows_c, send, to, keep_c)
    block = digit_block(add_digits(kept_c[rows_c:, :], got[rows_a + rows_c:, :].astype(F32)))
    keep_c[gone:, :] = block
    to += gone
    send[to:to + block.shape[0], :] = block.astype(BF16)
    to += block.shape[0]
    if to < send.shape[0]:
        send[to:, :] = jnp.zeros((send.shape[0] - to, LANES), BF16)


def last_kernel(rows_a, rows, info, got, kept_a, kept_c, sums_got, sums_kept, corr, pieces, mine):
    corr[...] = kept_a[...] + got[0:rows_a, :].astype(F32)
    pieces[...] = (kept_c[0:rows, :] + got[rows_a:rows_a + rows, :].astype(F32)).astype(BF16)
    block = digit_block(add_digits(kept_c[rows:, :], got[rows_a + rows:rows_a + kept_c.shape[0], :].astype(F32)))
    mine[0:rows, :] = pieces[...]
    mine[rows:kept_c.shape[0], :] = block.astype(BF16)
    at = kept_c.shape[0]
    count = sums_kept.shape[0] - 16
    number = count_of(sums_kept[count:, :].astype(F32), count) + count_of(sums_got[count:, :].astype(F32), count)
    square = (count, count)
    same = lax.broadcasted_iota(jnp.int32, square, 0) == lax.broadcasted_iota(jnp.int32, square, 1)
    tall = jnp.sum(jnp.where(same, jnp.broadcast_to(number, square), 0.0), 1, keepdims=True)
    total = sums_kept[0:count, :].astype(F32) + sums_got[0:count, :].astype(F32)
    means = (total / jnp.maximum(tall, 1.0)).astype(BF16)
    digits = count_rows(number, means.shape[1]).astype(BF16)
    for j in range(means.shape[1] // LANES):
        mine[at:at + count, :] = means[:, j * LANES:(j + 1) * LANES]
        mine[at + count:at + count + 16, :] = digits[:, j * LANES:(j + 1) * LANES]
        at += count + 16


def conv_out_kernel(total_frames, place, info, corr, proj, out, wide):
    rows = out.shape[0]
    flipped = jnp.transpose(corr[...])
    high = flipped.astype(BF16)
    low = (flipped - high.astype(F32)).astype(BF16)
    wide[...] = (nt(high, proj[...]) + nt(low, proj[...])) * (1.0 / total_frames)
    start = info[place]
    if rows % 8 == 0:
        out[...] = wide[pl.ds(pl.multiple_of(start, 8), rows), :]
    else:
        taken = wide[0:rows, :]
        for other in range(rows, wide.shape[0], rows):
            taken = jnp.where(start == other, wide[other:other + rows, :], taken)
        out[...] = taken


def out_kernel(total_frames, use_scale, dz, place, inner, extra, info, mine, *refs):
    parts, (out, bias, means, usage) = refs[:-4], refs[-4:]
    theirs = parts[1]
    scale = 1.0 / total_frames
    top = inner * dz
    value = add_digits(mine[top:top + extra, :].astype(F32), theirs[top:top + extra, :].astype(F32)) * scale
    for j in range(bias.shape[1] // LANES):
        bias[:, j * LANES:(j + 1) * LANES] = value[j:j + 1, :]
    bit = info[0]
    count = means.shape[1]
    numbers = []
    for ref, level in ((mine, bit), (theirs, 1 - bit)):
        at = top + extra
        blocks = []
        for j in range(dz // LANES):
            blocks.append(ref[at:at + count + 16, :])
            at += count + 16
        whole = jnp.concatenate(blocks, 1)
        means[level] = whole[0:count, :]
        numbers.append(count_of(whole[count:, :].astype(F32), count) * use_scale)
    usage[0:1, :] = jnp.where(bit == 1, numbers[1], numbers[0])
    usage[1:2, :] = jnp.where(bit == 1, numbers[0], numbers[1])
    for j, ref in enumerate(parts):
        for k in range(inner):
            start = pl.multiple_of((info[place + j] + k) * LANES, LANES)
            turned = jnp.transpose(ref[k * dz:(k + 1) * dz, :])
            out[pl.ds(start, LANES), :] = turned.astype(F32) * scale


def shifted(block, axis, distance):
    devices = range(lax.axis_size(axis))
    route = [(i - distance, i) for i in devices if i - distance in devices]
    return lax.ppermute(block, axis, route)


def swapped(block, steps):
    tm = lax.axis_size("tm")

    def partner(device):
        axis, bit = steps[(device // tm) & 1]
        return device ^ ((1 << bit) * (tm if axis == "dp" else 1))

    route = [(device, partner(device)) for device in range(lax.axis_size("dp") * tm)]
    return lax.ppermute(block, ("dp", "tm"), route)


def crossed(block, steps):
    tm = lax.axis_size("tm")

    def partner(device):
        axis, bit = steps[(device // tm) & 1]
        return device ^ tm ^ ((1 << bit) * (tm if axis == "dp" else 1))

    route = [(device, partner(device)) for device in range(lax.axis_size("dp") * tm)]
    return lax.ppermute(block, ("dp", "tm"), route)


def shards(feats, codes, conv_weight, conv_bias, proj_weight, codebooks):
    dp, tm = lax.axis_size("dp"), lax.axis_size("tm")
    rows_in, channels = feats.shape
    frames = rows_in // 2
    levels, book_size, dz = codebooks.shape
    assert levels == 2
    width = conv_weight.shape[0]
    total_frames = frames * dp * tm
    per_shard = book_size // tm
    dp_bits, tm_bits = log2(dp), log2(tm)
    owner_rows = width // (dp * tm)

    assert dp_bits >= 3 and 1 <= tm_bits <= 2
    pieces_a, pieces_c = width // LANES, channels // LANES
    under = max(dp_bits + tm_bits - log2(pieces_a), 0)
    c_bits = 2
    assert pieces_c >= 4
    whole_bits = [b for b in range(1, dp_bits) if b + tm_bits < under]
    piece_bits = [b for b in range(1, dp_bits) if b + tm_bits >= under]
    paths = [[("dp", b) for b in bits] for bits in (whole_bits + piece_bits, whole_bits[::-1] + piece_bits[::-1])]
    mixed = under == 1 and tm_bits == 2
    turned = mixed or under == 0 or under >= tm_bits
    up = [("tm", b) for b in range(tm_bits)]
    paths[0] += up[::-1]
    paths[1] += up if turned else up[::-1]
    exchanges = list(zip([("dp", 0)] + paths[0], [("dp", 0)] + paths[1]))
    sums_up = [("dp", b) for b in range(1, dp_bits)]
    sums_exchanges = list(zip(up + sums_up, up[::-1] + sums_up[::-1]))

    def piece_bit(step):
        axis, b = step
        bit = b + (tm_bits if axis == "dp" else 0)
        return bit - under if bit >= under else None

    a_split = [piece_bit(steps[0]) is not None for steps in exchanges]
    c_split = [log2(pieces_c) - 1 - k if k < c_bits else None for k in range(len(exchanges))]

    def order_of(split, count):
        used = [b for b in split if b is not None]
        return used + [b for b in reversed(range(log2(count))) if b not in used]

    orders = [order_of([piece_bit(steps[core]) for steps in exchanges], pieces_a) for core in range(2)]
    order_c = order_of(c_split, pieces_c)
    plan = [(pieces_a, orders, a_split[0]), (pieces_c, [order_c, order_c], True)]
    now_a = pieces_a // 2 if plan[0][2] else pieces_a
    now_c = pieces_c // 2

    count_bits, count_places = len(exchanges), 4
    at_start = count_bits
    at_codes = at_start + 1
    at_pieces = at_codes + tm
    at_sums = at_pieces + count_places
    at_row = at_sums + len(sums_exchanges)

    def info():
        at_dp, at_tm = lax.axis_index("dp"), lax.axis_index("tm")
        core = at_dp & 1

        def on_core(values):
            return values[0] + core * (values[1] - values[0])

        def bit_at(step):
            axis, b = step
            return ((at_dp if axis == "dp" else at_tm) >> b) & 1

        bits = [on_core([bit_at(step) for step in steps]) for steps in exchanges]
        sums_bits = [on_core([bit_at(step) for step in steps]) for steps in sums_exchanges]
        shared = [bit_at(step) for step in exchanges[1]]
        mine_c, other_c = on_core(shared), on_core(shared[::-1])
        places = [2 * core + mine_c, 2 * (1 - core) + other_c, 2 * core + 1 - mine_c, 2 * (1 - core) + 1 - other_c]
        places = [place << (log2(pieces_c) - c_bits) for place in places]
        lists = []
        for way in ([b for _, b in up], [b for _, b in up[::-1]]):
            lists.append([sum(((position >> (tm_bits - 1 - j)) & 1) << b for j, b in enumerate(way)) for position in range(tm)])
        first_bit = on_core([0, tm_bits - 1])
        lead = (at_tm >> first_bit) & 1
        quarters = [on_core([lists[0][j], lists[1][j]]) for j in range(tm // 2)]
        send_codes = [(q + ((1 - lead) << first_bit)) * per_shard for q in quarters]
        keep_codes = [(q + (lead << first_bit)) * per_shard for q in quarters]
        differ = at_tm ^ (at_tm + 1)
        ways = [sum(((differ >> b) & 1) << j for j, b in enumerate(way)) for way in (
            list(range(tm_bits)), list(reversed(range(tm_bits))))]
        row_code = jnp.where(at_tm + 1 < tm, on_core(ways), 0)
        if turned and not mixed:
            start = ((at_dp * tm + at_tm) * owner_rows) & (LANES - 1)
        else:
            start = on_core([(at_dp * tm + at_tm) * owner_rows, (at_tm >> 1) * owner_rows if mixed else (
                at_dp * tm + at_tm) * owner_rows]) & (LANES - 1)
        return bits + [start] + send_codes + keep_codes + places + sums_bits + [row_code]

    halo = shifted(call(halo_kernel, shape((2, channels), BF16), [info, feats[-2:]], flops=10 ** 11), "tm", 1)
    weight, proj, codes = conv_weight, proj_weight, codes[0]
    extra = 4 * (-(-channels // LANES // 8) * 8)
    code_rows = -(-(2 * -(-frames // dz)) // 16) * 16
    corr_rows = (now_a + now_c) * dz
    rows_b = frames + code_rows
    shared = [shape((frames, width), BF16), shape((frames, channels), BF16), shape((frames, dz), BF16),
              shape((dz, frames), BF16), shape((rows_b, dz), BF16),
              shape((corr_rows + rows_b * (dz // LANES), LANES), BF16)]
    *arrays, first, part = call(
        functools.partial(local_kernel, plan),
        shared + [shape((16, channels), F32), shape((corr_rows + 32 * (dz // LANES), LANES), F32)],
        [info, feats, weight, conv_bias[None, :], codes, codebooks, proj],
        scratch=[VMEM((channels // LANES, rows_in + 8, LANES), F32), VMEM((levels, frames, dz), BF16)],
    )
    unfold, hidden, latent_grad, flipped, own, send = call(
        functools.partial(frame_kernel, plan),
        shared,
        [info, halo, first, part, weight, proj] + arrays,
        aliases={6 + k: k for k in range(len(shared))},
    )
    got = swapped(send, exchanges[0])
    keep_a, keep_c, hidden_grad, extras, row = call(
        functools.partial(rest_kernel, plan),
        [shape((now_a * dz, LANES), F32), shape((now_c * dz, LANES), F32), shape((frames, channels), BF16),
         shape((extra, LANES), F32), shape((16, channels), BF16)],
        [info, flipped, unfold, hidden, latent_grad, proj],
        after=[send],
    )

    def halves_at(k):
        nonlocal now_a, now_c
        halves = [(now_a * dz, a_split[k]), (now_c * dz, c_split[k] is not None)]
        now_a = now_a // 2 if halves[0][1] else now_a
        now_c = now_c // 2 if halves[1][1] else now_c
        return halves, now_a * dz, now_c * dz + extra

    halves, rows_a, rows_c = halves_at(1)
    send, keep_a, keep_c = call(
        functools.partial(first_step_kernel, halves, 1),
        [shape((rows_a + rows_c, LANES), BF16), shape((rows_a, LANES), F32), shape((rows_c, LANES), F32)],
        [info, got, keep_a, keep_c, extras])
    size = per_shard + 16
    sums_rows = size * (tm // 2)
    sums_send = call(
        functools.partial(sums_kernel, corr_rows, frames, at_codes, per_shard),
        shape((sums_rows, dz), BF16),
        [info, got, own, row],
        after=[send])
    sums_keep = call(
        functools.partial(sums_kernel, corr_rows, frames, at_codes + tm // 2, per_shard),
        shape((sums_rows, dz), F32),
        [info, got, own, row],
        after=[sums_send])
    sums_got = swapped(sums_send, sums_exchanges[0])
    got = swapped(send, exchanges[1])
    known = row
    ordered = [sums_keep]
    for k in range(2, len(exchanges)):
        halves, rows_a, rows_c = halves_at(k)
        spare = 16 * (k == len(exchanges) - 1)
        send, keep_a, keep_c = call(
            functools.partial(step_kernel, halves, k, mixed and k == dp_bits),
            [shape((rows_a + rows_c + spare, LANES), BF16), shape((rows_a, LANES), F32), shape((rows_c, LANES), F32)],
            [info, got, keep_a, keep_c],
            after=ordered)
        got = swapped(send, exchanges[k])
        halved = sums_exchanges[k - 1][0][0] == "tm"
        sums_rows = sums_rows // 2 if halved else sums_rows
        row_step = k - 2 if k - 2 < tm_bits else None
        outs = call(
            functools.partial(sums_step_kernel, halved, at_sums + k - 1, row_step, (per_shard, at_row)),
            [shape((sums_rows, dz), BF16), shape((sums_rows, dz), F32)]
            + [shape((16, channels), BF16)] * (row_step is not None),
            [info, sums_got, sums_keep] + [known] * (row_step is not None),
            after=[send])
        sums_send, sums_keep = outs[:2]
        known = outs[2] if row_step is not None else known
        sums_got = swapped(sums_send, sums_exchanges[k - 1])
        ordered = [sums_send]
    assert now_a == 1 and sums_rows == size
    feat_grad, last = call(
        feat_kernel,
        shape((rows_in, channels), BF16),
        [info, hidden_grad, known, weight],
        after=[sums_send],
        token=True,
        scratch=[VMEM((frames + 8, channels), F32), VMEM((channels // LANES, rows_in, LANES), F32)],
    )

    corr, piece, mine = call(
        functools.partial(last_kernel, rows_a, rows_c - extra),
        [shape((rows_a, LANES), F32), shape((rows_c - extra, LANES), BF16),
         shape((rows_c + size * (dz // LANES), LANES), BF16)],
        [info, got, keep_a, keep_c, sums_got, sums_keep],
        after=[last])
    parts = [piece, swapped(mine, exchanges[0]), swapped(piece, exchanges[1]), crossed(piece, exchanges[1])]
    conv_grad, last = call(
        functools.partial(conv_out_kernel, total_frames, at_start),
        shape((owner_rows, channels), F32),
        [info, corr, proj],
        after=[piece],
        token=True,
        scratch=[VMEM((LANES, channels), F32)],
    )
    proj_grad, bias_grad, code_means, code_usage = call(
        functools.partial(out_kernel, total_frames, book_size / total_frames, dz, at_pieces, now_c, extra),
        [shape((channels, dz), F32), shape((1, channels), F32), shape((levels, per_shard, dz), BF16),
         shape((levels, per_shard), F32)],
        [info, mine] + parts,
        after=[last],
    )
    return feat_grad, conv_grad, bias_grad[0], proj_grad, code_means, code_usage


def solution(mesh):
    placed = (P(("dp", "tm"), None), P("dp", None, "tm"), P(), P(), P(), P())
    return jax.shard_map(
        shards,
        mesh=mesh,
        in_specs=placed,
        out_specs=(
            P(("dp", "tm"), None),
            P(("dp", "tm"), None),
            P(),
            P(),
            P(None, "tm", None),
            P(None, "tm"),
        ),
        check_vma=False,
    )
```

```python
import functools

import jax
import jax.numpy as jnp
from jax import lax
from jax.experimental import pallas as pl
from jax.experimental.pallas import tpu as pltpu
from jax.sharding import PartitionSpec as P

BF16 = jnp.bfloat16
F32 = jnp.float32
LANES = 128
VMEM_LIMIT = 16 * 1024 * 1024


def log2(value):
    assert value & (value - 1) == 0
    return value.bit_length() - 1


def nn(a, b):
    return lax.dot_general(a, b, (((1,), (0,)), ((), ())), preferred_element_type=F32)


def nt(a, b):
    return lax.dot_general(a, b, (((1,), (1,)), ((), ())), preferred_element_type=F32)


VMEM = pltpu.VMEM


def call(body, out_shape, args, after=(), scratch=(), aliases=None, token=False, flops=0):
    info, args = args[0], args[1:]
    count = len(args)
    many = isinstance(out_shape, (list, tuple))
    shapes = list(out_shape) if many else [out_shape]

    def kernel(*refs):
        ends = count + len(after)
        if token:
            refs[ends + len(shapes)][...] = jnp.zeros((8, LANES), F32)
            refs = refs[:ends + len(shapes)] + refs[ends + len(shapes) + 1:]
        body(info(), *refs[:count], *refs[ends:])

    specs = [pl.BlockSpec(memory_space=VMEM)] * count + [pl.BlockSpec(memory_space=pl.ANY)] * len(after)
    shown = shapes + [shape((8, LANES), F32)] * token
    outs = pl.pallas_call(
        kernel,
        out_shape=shown,
        in_specs=specs,
        out_specs=[pl.BlockSpec(memory_space=VMEM)] * len(shown),
        scratch_shapes=list(scratch),
        input_output_aliases={at - 1: out for at, out in (aliases or {}).items()},
        compiler_params=pltpu.CompilerParams(vmem_limit_bytes=VMEM_LIMIT),
        cost_estimate=pl.CostEstimate(flops=flops, bytes_accessed=0, transcendentals=0),
    )(*args, *after)
    return outs if len(shown) > 1 else outs[0]


def shape(dims, dtype):
    return jax.ShapeDtypeStruct(dims, dtype)


def digits_of(value):
    high = value.astype(BF16).astype(F32)
    rest = value - high
    middle = rest.astype(BF16).astype(F32)
    low = (rest - middle).astype(BF16).astype(F32)
    return high, middle, low


def one_hot(codes, axis_codes, first, count):
    frames = codes.shape[1 - axis_codes]
    dims = (count, frames) if axis_codes == 0 else (frames, count)
    places = lax.broadcasted_iota(jnp.int32, dims, axis_codes) + first
    return jnp.where(codes == places, 1.0, 0.0).astype(BF16)


def halo_kernel(info, rows, out):
    out[...] = rows[...]


def walk(orders, halved, count):
    start = 1 if halved else 0
    shown = count // 2 if halved else count
    bits = log2(shown)
    step = 2 if shown > 1 and all(order[-1] == 0 for order in orders) else 1
    for position in range(0, shown, step):
        yield position, [
            sum(((position >> (bits - 1 - k)) & 1) << bit for k, bit in enumerate(order[start:])) for order in orders
        ], step


def correlate(flipped, sources, plan, core, bit, out):
    dz = flipped.shape[0]
    at = 0
    for source, (count, orders, halved) in zip(sources, plan):
        for position, pieces, step in walk(orders, halved, count):
            column = pieces[0] + core * (pieces[1] - pieces[0])
            if halved:
                column = column + (bit << orders[0][0])
            column = pl.multiple_of(column * LANES, LANES)
            product = nn(flipped, source[:, pl.ds(column, step * LANES)])
            for j in range(step):
                top = (at + position + j) * dz
                out[top:top + dz, :] = product[:, j * LANES:(j + 1) * LANES].astype(out.dtype)
        at += count // 2 if halved else count
    return at * dz


def code_digits(codes, dz, rows):
    parts = []
    for part in (codes >> 8, codes & 255):
        for start in range(0, codes.shape[1], dz):
            piece = part[:, start:start + dz].astype(F32)
            if piece.shape[1] < dz:
                piece = jnp.concatenate([piece, jnp.zeros((1, dz - piece.shape[1]), F32)], 1)
            parts.append(piece)
    parts.append(jnp.zeros((rows - len(parts), dz), F32))
    return jnp.concatenate(parts, 0).astype(BF16)


def codes_of(block, frames):
    dz = block.shape[1]
    per = -(-frames // dz)
    digits = block[...].astype(F32)
    parts = [jnp.concatenate([digits[k * per + j:k * per + j + 1, :] for j in range(per)], 1)[:, :frames]
             for k in range(2)]
    return (parts[0] * 256.0 + parts[1]).astype(jnp.int32)


def residuals(hidden, proj, chosen):
    latent = nn(hidden, proj)
    once = latent - chosen[0].astype(F32)
    total = once + (once - chosen[1].astype(F32))
    return latent, once, total.astype(BF16)


def put_columns(out, at, rows, block):
    for j in range(block.shape[1] // LANES):
        out[at + j * rows:at + j * rows + block.shape[0], :] = block[:, j * LANES:(j + 1) * LANES]


def local_kernel(plan, info, feats, weight, bias, codes, books, proj,
                 unfold, hidden, latent_grad, flipped, own, send, first, part, wide, chosen):
    rows, channels = feats.shape
    frames = rows // 2
    dz = proj.shape[1]
    for j in range(channels // LANES):
        wide[j, 0:8, :] = jnp.zeros((8, LANES), F32)
        wide[j, 8:, :] = feats[:, j * LANES:(j + 1) * LANES].astype(F32)
        for tap in range(4):
            start = tap * channels + j * LANES
            unfold[:, start:start + LANES] = wide[j, pl.ds(6 + tap, frames, stride=2), :].astype(BF16)
    conv = nn(unfold[...], weight[...]) + bias[...]
    first[...] = conv[0:16, :]
    hidden[...] = conv.astype(BF16)
    levels = books.shape[0]
    padded = jnp.concatenate([codes[...].astype(F32), jnp.zeros((8 - levels, frames), F32)], 0)
    tall = jnp.transpose(padded).astype(jnp.int32)
    for level in range(levels):
        matches = one_hot(tall[:, level:level + 1], 1, 0, books.shape[1])
        chosen[level] = nn(matches, books[level]).astype(BF16)
    latent, once, grad = residuals(hidden[...], proj[...], chosen)
    latent_grad[...] = grad
    row = lax.broadcasted_iota(jnp.int32, grad.shape, 0)
    flipped[...] = jnp.transpose(jnp.where(row == 0, 0.0, grad.astype(F32))).astype(BF16)
    bit = info[0]
    at = correlate(flipped[...], (unfold, hidden), plan, 1 - bit, 1 - bit, part)
    rows_b = own.shape[0]
    code_rows = rows_b - frames
    digits = [code_digits(codes[level:level + 1, :], dz, code_rows) for level in range(2)]
    own[0:frames, :] = jnp.where(bit == 1, once, latent).astype(BF16)
    own[frames:, :] = jnp.where(bit == 1, digits[1], digits[0])
    put_columns(send, at, rows_b, jnp.where(bit == 1, latent, once).astype(BF16))
    put_columns(send, at + frames, rows_b, jnp.where(bit == 1, digits[0], digits[1]))
    for level in range(levels):
        part[at + level * 16 * (dz // LANES):at + (level + 1) * 16 * (dz // LANES), :] = jnp.concatenate(
            [chosen[level, 0:16, j * LANES:(j + 1) * LANES].astype(F32) for j in range(dz // LANES)], 0)


def frame_kernel(plan, info, halo, first, part, weight, proj, unfold_in, hidden_in, grad_in, flipped_in, own_in, send_in,
                 unfold, hidden, latent_grad, flipped, own, send):
    width = unfold.shape[1]
    half = width // 2
    dz = proj.shape[1]
    row = lax.broadcasted_iota(jnp.int32, (16, half), 0)
    left = jnp.concatenate([halo[0:1, :], halo[1:2, :]], 1).astype(F32)
    head = jnp.where(row == 0, jnp.broadcast_to(left, (16, half)), 0.0)
    unfold[0:16, 0:half] = (unfold_in[0:16, 0:half].astype(F32) + head).astype(BF16)
    fix = nn(head.astype(BF16), weight[0:half, :])
    hidden[0:16, :] = (first[...] + fix).astype(BF16)
    top = hidden[0:16, :]
    pieces = part.shape[0] - 32 * (dz // LANES)
    chosen = []
    for level in range(2):
        at = pieces + level * 16 * (dz // LANES)
        chosen.append(jnp.concatenate([part[at + j * 16:at + (j + 1) * 16, :] for j in range(dz // LANES)], 1))
    latent, once, grad = residuals(top, proj[...], chosen)
    latent_grad[0:16, :] = grad
    flipped[:, 0:LANES] = jnp.transpose(latent_grad[0:LANES, :].astype(F32)).astype(BF16)
    column = flipped[:, 0:LANES].astype(F32)[:, 0:1]
    bit = info[0]
    at = 0
    for source, (count, orders, halved) in zip((unfold, hidden), plan):
        rows = source[0:16, :].astype(F32)[0:1, :]
        for position, places, step in walk(orders, halved, count):
            for j in range(step):
                offsets = [places[0] + j, places[1] + j]
                low = [offset for offset in offsets]
                high = [offset + (1 << orders[0][0] if halved else 0) for offset in offsets]
                picked = [rows[:, k * LANES:(k + 1) * LANES] for k in low + high]
                piece = jnp.where(bit == 1, picked[0], picked[3]) if halved else jnp.where(bit == 1, picked[0], picked[1])
                begin = (at + position + j) * dz
                send[begin:begin + dz, :] = (part[begin:begin + dz, :] + column * piece).astype(BF16)
        at += count // 2 if halved else count
    rows_b = own.shape[0]
    own[0:16, :] = jnp.where(bit == 1, once, latent).astype(BF16)
    put_columns(send, at * dz, rows_b, jnp.where(bit == 1, latent, once).astype(BF16))


def rest_kernel(plan, info, flipped, unfold, hidden, latent_grad, proj, keep_a, keep_c, hidden_grad, extras, row):
    bit = info[0]
    correlate(flipped[...], (unfold,), plan[:1], bit, bit, keep_a)
    correlate(flipped[...], (hidden,), plan[1:], bit, bit, keep_c)
    back = nt(latent_grad[...], proj[...]).astype(BF16)
    hidden_grad[...] = back
    row[...] = back[0:16, :]
    stride = extras.shape[0] // 4
    extras[...] = jnp.zeros(extras.shape, F32)
    sums = jnp.sum(back.astype(F32), 0, keepdims=True)
    for digit, part in enumerate(digits_of(sums)):
        for j in range(sums.shape[1] // LANES):
            extras[digit * stride + j:digit * stride + j + 1, :] = part[:, j * LANES:(j + 1) * LANES]


def split_sum(halved, bit, got, at, kept, rows, send, to, keep):
    if halved:
        half = rows // 2
        away = pl.multiple_of((1 - bit) * half, 16)
        home = pl.multiple_of(bit * half, 16)
        send[to:to + half, :] = (kept[pl.ds(away, half), :] + got[pl.ds(at + away, half), :].astype(F32)).astype(BF16)
        keep[0:half, :] = kept[pl.ds(home, half), :] + got[pl.ds(at + home, half), :].astype(F32)
        return half
    total = (kept[0:rows, :] + got[at:at + rows, :].astype(F32)).astype(BF16)
    send[to:to + rows, :] = total
    keep[0:rows, :] = total.astype(F32)
    return rows


def add_digits(mine, theirs):
    stride = mine.shape[0] // 4
    return ((mine[0:stride] + mine[stride:2 * stride]) + mine[2 * stride:3 * stride]) + (
        (theirs[0:stride] + theirs[stride:2 * stride]) + theirs[2 * stride:3 * stride])


def digit_block(value):
    return jnp.concatenate(list(digits_of(value)) + [jnp.zeros_like(value)], 0)


def first_step_kernel(halves, place, info, got, kept_a, kept_c, extras, send_a, send_c, keep_a, keep_c):
    (rows_a, halved_a), (rows_c, halved_c) = halves
    split_sum(halved_a, info[place], got, 0, kept_a, rows_a, send_a, 0, keep_a)
    gone = split_sum(halved_c, info[place], got, rows_a, kept_c, rows_c, send_c, 0, keep_c)
    send_c[gone:, :] = extras[...].astype(BF16)
    keep_c[gone:, :] = extras[...]


def feat_kernel(info, grad, after, weight, out, wide, inter):
    frames, channels = grad.shape
    half = weight.shape[0] // 2
    wide[0:frames, :] = grad[...].astype(F32)
    wide[frames:, :] = jnp.broadcast_to(after[0:1, :].astype(F32), (8, channels))
    ahead = wide[pl.ds(1, frames), :].astype(BF16)
    for parity in range(2):
        rows = pl.ds(parity * (half // 2), half // 2)
        rows_after = pl.ds(half + parity * (half // 2), half // 2)
        both = nt(ahead, weight[rows, :]) + nt(grad[...], weight[rows_after, :])
        for j in range(channels // LANES):
            inter[j, pl.ds(parity, frames, stride=2), :] = both[:, j * LANES:(j + 1) * LANES]
    for j in range(channels // LANES):
        out[:, j * LANES:(j + 1) * LANES] = inter[j].astype(BF16)


def own_sums_kernel(frames, place, count, info, own, out):
    codes = codes_of(own[frames:, :], frames)
    ones = jnp.ones((8, frames), BF16)
    size = count + 16
    for top in range(0, out.shape[0], size):
        matches = one_hot(codes, 0, info[place], count)
        out[top:top + count, :] = nn(matches, own[0:frames, :])
        out[top + count:top + count + 8, 0:count] = nt(ones, matches)
        place += 1


def sums_kernel(first, frames, place, count, info, got, base, row, out):
    dz = base.shape[1]
    rows = (got.shape[0] - first) // (dz // LANES)
    theirs = jnp.concatenate([got[first + j * rows:first + (j + 1) * rows, :] for j in range(dz // LANES)], 1)
    codes = codes_of(theirs[frames:, :], frames)
    ones = jnp.ones((8, frames), BF16)
    size = count + 16
    riding = [row[...].astype(F32)[0:1, :]]
    for top in range(0, out.shape[0], size):
        matches = one_hot(codes, 0, info[place], count)
        total = base[top:top + count, :] + nn(matches, theirs[0:frames, :])
        counts = base[top + count:top + count + 8, 0:count] + nt(ones, matches)
        out[top:top + count, :] = total.astype(out.dtype)
        out[top + count:top + size, :] = count_rows(counts[0:1], dz, riding).astype(out.dtype)
        place += 1


def count_rows(count, width, riding=()):
    high = jnp.floor(count * (1.0 / 65536.0))
    rest = count - high * 65536.0
    middle = jnp.floor(rest * (1.0 / 256.0))
    low = rest - middle * 256.0
    block = jnp.concatenate([high, middle, low], 0)
    if count.shape[1] < width:
        block = jnp.concatenate([block, jnp.zeros((3, width - count.shape[1]), F32)], 1)
    parts = [block]
    for row in riding:
        parts += [row[:, at:at + width] for at in range(0, row.shape[1], width)]
    left = 16 - sum(part.shape[0] for part in parts)
    return jnp.concatenate(parts + [jnp.zeros((left, width), F32)] * (left > 0), 0)


def riding_row(block, index, parts):
    return jnp.concatenate([block[3 + index * parts + j:4 + index * parts + j, :] for j in range(parts)], 1)


def count_of(block, own):
    return (block[0:1] * 65536.0 + block[1:2] * 256.0 + block[2:3])[:, :own]


def sums_step_kernel(halved, place, row_step, row_place, info, got, kept, *refs):
    riding = ()
    if row_step is not None:
        known, refs = refs[0][...].astype(F32), refs[1:]
        after, refs = refs[-1], refs[:-1]
        parts = known.shape[1] // got.shape[1]
        block = got[row_place[0]:row_place[0] + 16, :].astype(F32)
        rows = [known[j:j + 1, :] for j in range(1 << row_step)]
        rows += [riding_row(block, j, parts) for j in range(1 << row_step)]
        if halved:
            riding = rows
            total = rows + [jnp.zeros((16 - len(rows), known.shape[1]), F32)]
            after[...] = jnp.concatenate(total, 0).astype(BF16)
        else:
            wide = jnp.zeros(after.shape, F32)
            for j in range(1, len(rows)):
                wide = jnp.where(info[row_place[1]] == j, jnp.broadcast_to(rows[j], after.shape), wide)
            after[...] = wide.astype(BF16)
    send, keep = refs
    dz = got.shape[1]
    bit = info[place]
    half = kept.shape[0] // 2 if halved else 0
    outs = [(send, (1 - bit) * half), (keep, bit * half)] if halved else [(send, 0)]
    count = row_place[0]
    size = count + 16
    for out, start in outs:
        for top in range(0, keep.shape[0], size):
            here = top + pl.multiple_of(start, 16) if halved else top
            sums = pl.ds(here, count)
            tail = pl.ds(here + count, 16)
            value = kept[sums, :].astype(F32) + got[sums, :].astype(F32)
            number = count_of(kept[tail, :].astype(F32), count) + count_of(got[tail, :].astype(F32), count)
            out[top:top + count, :] = value.astype(out.dtype)
            out[top + count:top + size, :] = count_rows(number, dz, riding).astype(out.dtype)
    if not halved:
        keep[...] = send[0:keep.shape[0], :].astype(F32)


def swap_halves(first, second, core):
    half = LANES // 2
    left = lax.broadcasted_iota(jnp.int32, first.shape, 1) < half
    turned_first, turned_second = pltpu.roll(first, half, 1), pltpu.roll(second, half, 1)
    swapped_first = jnp.where(left, first, turned_second)
    swapped_second = jnp.where(left, turned_first, second)
    return jnp.where(core == 1, swapped_first, first), jnp.where(core == 1, swapped_second, second)


def step_kernel(halves, at_c, place, mixed, info, got, got_c, kept_a, kept_c, send, keep_a, keep_c):
    (rows_a, halved_a), (rows_c, halved_c) = halves
    if mixed:
        to = rows_a // 2
        total = kept_a[0:rows_a, :] + got[0:rows_a, :].astype(F32)
        first, second = swap_halves(total[0:to, :], total[to:, :], info[0])
        low = info[place] == 0
        send[0:to, :] = jnp.where(low, second, first).astype(BF16)
        keep_a[...] = jnp.where(low, first, second)
    else:
        to = split_sum(halved_a, info[place], got, 0, kept_a, rows_a, send, 0, keep_a)
    gone = split_sum(halved_c, info[place], got_c, at_c, kept_c, rows_c, send, to, keep_c)
    block = digit_block(add_digits(kept_c[rows_c:, :], got_c[at_c + rows_c:, :].astype(F32)))
    keep_c[gone:, :] = block
    to += gone
    send[to:to + block.shape[0], :] = block.astype(BF16)
    to += block.shape[0]
    if to < send.shape[0]:
        send[to:, :] = jnp.zeros((send.shape[0] - to, LANES), BF16)


def last_kernel(rows_a, rows, info, got, kept_a, kept_c, sums_got, sums_kept, corr, pieces, mine):
    corr[...] = kept_a[...] + got[0:rows_a, :].astype(F32)
    pieces[...] = (kept_c[0:rows, :] + got[rows_a:rows_a + rows, :].astype(F32)).astype(BF16)
    block = digit_block(add_digits(kept_c[rows:, :], got[rows_a + rows:rows_a + kept_c.shape[0], :].astype(F32)))
    mine[0:rows, :] = pieces[...]
    mine[rows:kept_c.shape[0], :] = block.astype(BF16)
    at = kept_c.shape[0]
    count = sums_kept.shape[0] - 16
    number = count_of(sums_kept[count:, :].astype(F32), count) + count_of(sums_got[count:, :].astype(F32), count)
    square = (count, count)
    same = lax.broadcasted_iota(jnp.int32, square, 0) == lax.broadcasted_iota(jnp.int32, square, 1)
    tall = jnp.sum(jnp.where(same, jnp.broadcast_to(number, square), 0.0), 1, keepdims=True)
    total = sums_kept[0:count, :].astype(F32) + sums_got[0:count, :].astype(F32)
    means = (total / jnp.maximum(tall, 1.0)).astype(BF16)
    digits = count_rows(number, means.shape[1]).astype(BF16)
    for j in range(means.shape[1] // LANES):
        mine[at:at + count, :] = means[:, j * LANES:(j + 1) * LANES]
        mine[at + count:at + count + 16, :] = digits[:, j * LANES:(j + 1) * LANES]
        at += count + 16


def conv_out_kernel(total_frames, place, info, corr, proj, out, wide):
    rows = out.shape[0]
    flipped = jnp.transpose(corr[...])
    high = flipped.astype(BF16)
    low = (flipped - high.astype(F32)).astype(BF16)
    wide[...] = (nt(high, proj[...]) + nt(low, proj[...])) * (1.0 / total_frames)
    start = info[place]
    if rows % 8 == 0:
        out[...] = wide[pl.ds(pl.multiple_of(start, 8), rows), :]
    else:
        taken = wide[0:rows, :]
        for other in range(rows, wide.shape[0], rows):
            taken = jnp.where(start == other, wide[other:other + rows, :], taken)
        out[...] = taken


def out_kernel(total_frames, use_scale, dz, place, inner, extra, info, mine, *refs):
    parts, (out, bias, means, usage) = refs[:-4], refs[-4:]
    theirs = parts[1]
    scale = 1.0 / total_frames
    top = inner * dz
    value = add_digits(mine[top:top + extra, :].astype(F32), theirs[top:top + extra, :].astype(F32)) * scale
    for j in range(bias.shape[1] // LANES):
        bias[:, j * LANES:(j + 1) * LANES] = value[j:j + 1, :]
    bit = info[0]
    count = means.shape[1]
    numbers = []
    for ref, level in ((mine, bit), (theirs, 1 - bit)):
        at = top + extra
        blocks = []
        for j in range(dz // LANES):
            blocks.append(ref[at:at + count + 16, :])
            at += count + 16
        whole = jnp.concatenate(blocks, 1)
        means[level] = whole[0:count, :]
        numbers.append(count_of(whole[count:, :].astype(F32), count) * use_scale)
    usage[0:1, :] = jnp.where(bit == 1, numbers[1], numbers[0])
    usage[1:2, :] = jnp.where(bit == 1, numbers[0], numbers[1])
    for j, ref in enumerate(parts):
        for k in range(inner):
            start = pl.multiple_of((info[place + j] + k) * LANES, LANES)
            turned = jnp.transpose(ref[k * dz:(k + 1) * dz, :])
            out[pl.ds(start, LANES), :] = turned.astype(F32) * scale


def shifted(block, axis, distance):
    devices = range(lax.axis_size(axis))
    route = [(i - distance, i) for i in devices if i - distance in devices]
    return lax.ppermute(block, axis, route)


def swapped(block, steps):
    tm = lax.axis_size("tm")

    def partner(device):
        axis, bit = steps[(device // tm) & 1]
        return device ^ ((1 << bit) * (tm if axis == "dp" else 1))

    route = [(device, partner(device)) for device in range(lax.axis_size("dp") * tm)]
    return lax.ppermute(block, ("dp", "tm"), route)


def crossed(block, steps):
    tm = lax.axis_size("tm")

    def partner(device):
        axis, bit = steps[(device // tm) & 1]
        return device ^ tm ^ ((1 << bit) * (tm if axis == "dp" else 1))

    route = [(device, partner(device)) for device in range(lax.axis_size("dp") * tm)]
    return lax.ppermute(block, ("dp", "tm"), route)


def shards(feats, codes, conv_weight, conv_bias, proj_weight, codebooks):
    dp, tm = lax.axis_size("dp"), lax.axis_size("tm")
    rows_in, channels = feats.shape
    frames = rows_in // 2
    levels, book_size, dz = codebooks.shape
    assert levels == 2
    width = conv_weight.shape[0]
    total_frames = frames * dp * tm
    per_shard = book_size // tm
    dp_bits, tm_bits = log2(dp), log2(tm)
    owner_rows = width // (dp * tm)

    assert dp_bits >= 3 and 1 <= tm_bits <= 2
    pieces_a, pieces_c = width // LANES, channels // LANES
    under = max(dp_bits + tm_bits - log2(pieces_a), 0)
    c_bits = 2
    assert pieces_c >= 4
    whole_bits = [b for b in range(1, dp_bits) if b + tm_bits < under]
    piece_bits = [b for b in range(1, dp_bits) if b + tm_bits >= under]
    paths = [[("dp", b) for b in bits] for bits in (whole_bits + piece_bits, whole_bits[::-1] + piece_bits[::-1])]
    mixed = under == 1 and tm_bits == 2
    turned = mixed or under == 0 or under >= tm_bits
    up = [("tm", b) for b in range(tm_bits)]
    paths[0] += up[::-1]
    paths[1] += up if turned else up[::-1]
    exchanges = list(zip([("dp", 0)] + paths[0], [("dp", 0)] + paths[1]))
    sums_up = [("dp", b) for b in range(1, dp_bits)]
    sums_exchanges = list(zip(up + sums_up, up[::-1] + sums_up[::-1]))

    def piece_bit(step):
        axis, b = step
        bit = b + (tm_bits if axis == "dp" else 0)
        return bit - under if bit >= under else None

    a_split = [piece_bit(steps[0]) is not None for steps in exchanges]
    c_split = [log2(pieces_c) - 1 - k if k < c_bits else None for k in range(len(exchanges))]

    def order_of(split, count):
        used = [b for b in split if b is not None]
        return used + [b for b in reversed(range(log2(count))) if b not in used]

    orders = [order_of([piece_bit(steps[core]) for steps in exchanges], pieces_a) for core in range(2)]
    order_c = order_of(c_split, pieces_c)
    plan = [(pieces_a, orders, a_split[0]), (pieces_c, [order_c, order_c], True)]
    now_a = pieces_a // 2 if plan[0][2] else pieces_a
    now_c = pieces_c // 2

    count_bits, count_places = len(exchanges), 4
    at_start = count_bits
    at_codes = at_start + 1
    at_pieces = at_codes + tm
    at_sums = at_pieces + count_places
    at_row = at_sums + len(sums_exchanges)

    def info():
        at_dp, at_tm = lax.axis_index("dp"), lax.axis_index("tm")
        core = at_dp & 1

        def on_core(values):
            return values[0] + core * (values[1] - values[0])

        def bit_at(step):
            axis, b = step
            return ((at_dp if axis == "dp" else at_tm) >> b) & 1

        bits = [on_core([bit_at(step) for step in steps]) for steps in exchanges]
        sums_bits = [on_core([bit_at(step) for step in steps]) for steps in sums_exchanges]
        shared = [bit_at(step) for step in exchanges[1]]
        mine_c, other_c = on_core(shared), on_core(shared[::-1])
        places = [2 * core + mine_c, 2 * (1 - core) + other_c, 2 * core + 1 - mine_c, 2 * (1 - core) + 1 - other_c]
        places = [place << (log2(pieces_c) - c_bits) for place in places]
        lists = []
        for way in ([b for _, b in up], [b for _, b in up[::-1]]):
            lists.append([sum(((position >> (tm_bits - 1 - j)) & 1) << b for j, b in enumerate(way)) for position in range(tm)])
        first_bit = on_core([0, tm_bits - 1])
        lead = (at_tm >> first_bit) & 1
        quarters = [on_core([lists[0][j], lists[1][j]]) for j in range(tm // 2)]
        send_codes = [(q + ((1 - lead) << first_bit)) * per_shard for q in quarters]
        keep_codes = [(q + (lead << first_bit)) * per_shard for q in quarters]
        differ = at_tm ^ (at_tm + 1)
        ways = [sum(((differ >> b) & 1) << j for j, b in enumerate(way)) for way in (
            list(range(tm_bits)), list(reversed(range(tm_bits))))]
        row_code = jnp.where(at_tm + 1 < tm, on_core(ways), 0)
        if turned and not mixed:
            start = ((at_dp * tm + at_tm) * owner_rows) & (LANES - 1)
        else:
            start = on_core([(at_dp * tm + at_tm) * owner_rows, (at_tm >> 1) * owner_rows if mixed else (
                at_dp * tm + at_tm) * owner_rows]) & (LANES - 1)
        return bits + [start] + send_codes + keep_codes + places + sums_bits + [row_code]

    halo = shifted(call(halo_kernel, shape((2, channels), BF16), [info, feats[-2:]], flops=10 ** 11), "tm", 1)
    weight, proj, codes = conv_weight, proj_weight, codes[0]
    extra = 4 * (-(-channels // LANES // 8) * 8)
    code_rows = -(-(2 * -(-frames // dz)) // 16) * 16
    corr_rows = (now_a + now_c) * dz
    rows_b = frames + code_rows
    shared = [shape((frames, width), BF16), shape((frames, channels), BF16), shape((frames, dz), BF16),
              shape((dz, frames), BF16), shape((rows_b, dz), BF16),
              shape((corr_rows + rows_b * (dz // LANES), LANES), BF16)]
    *arrays, first, part = call(
        functools.partial(local_kernel, plan),
        shared + [shape((16, channels), F32), shape((corr_rows + 32 * (dz // LANES), LANES), F32)],
        [info, feats, weight, conv_bias[None, :], codes, codebooks, proj],
        scratch=[VMEM((channels // LANES, rows_in + 8, LANES), F32), VMEM((levels, frames, dz), BF16)],
    )
    unfold, hidden, latent_grad, flipped, own, send = call(
        functools.partial(frame_kernel, plan),
        shared,
        [info, halo, first, part, weight, proj] + arrays,
        aliases={6 + k: k for k in range(len(shared))},
    )
    got = swapped(send, exchanges[0])
    keep_a, keep_c, hidden_grad, extras, row = call(
        functools.partial(rest_kernel, plan),
        [shape((now_a * dz, LANES), F32), shape((now_c * dz, LANES), F32), shape((frames, channels), BF16),
         shape((extra, LANES), F32), shape((16, channels), BF16)],
        [info, flipped, unfold, hidden, latent_grad, proj],
        after=[send],
    )

    def halves_at(k):
        nonlocal now_a, now_c
        halves = [(now_a * dz, a_split[k]), (now_c * dz, c_split[k] is not None)]
        now_a = now_a // 2 if halves[0][1] else now_a
        now_c = now_c // 2 if halves[1][1] else now_c
        return halves, now_a * dz, now_c * dz + extra

    size = per_shard + 16
    sums_rows = size * (tm // 2)

    def own_sums(first, after):
        return call(
            functools.partial(own_sums_kernel, frames, at_codes + first, per_shard),
            shape((sums_rows, dz), F32),
            [info, own],
            after=after)

    def both_sums(first, base, dtype, after):
        return call(
            functools.partial(sums_kernel, corr_rows, frames, at_codes + first, per_shard),
            shape((sums_rows, dz), dtype),
            [info, got, base, row],
            after=after)

    sums_send = both_sums(0, own_sums(0, [extras]), BF16, [])
    sums_got = swapped(sums_send, sums_exchanges[0])
    halves, rows_a, rows_c = halves_at(1)
    send, send_c, keep_a, keep_c = call(
        functools.partial(first_step_kernel, halves, 1),
        [shape((rows_a, LANES), BF16), shape((rows_c, LANES), BF16), shape((rows_a, LANES), F32),
         shape((rows_c, LANES), F32)],
        [info, got, keep_a, keep_c, extras],
        after=[sums_send])
    sums_keep = both_sums(tm // 2, own_sums(tm // 2, [send]), F32, [])
    got, got_c = swapped(send, exchanges[1]), swapped(send_c, exchanges[1])
    known = row
    ordered = [sums_keep, sums_got]
    for k in range(2, len(exchanges)):
        at_c = 0 if k == 2 else rows_a
        halves, rows_a, rows_c = halves_at(k)
        spare = 16 * (k == len(exchanges) - 1)
        send, keep_a, keep_c = call(
            functools.partial(step_kernel, halves, at_c, k, mixed and k == dp_bits),
            [shape((rows_a + rows_c + spare, LANES), BF16), shape((rows_a, LANES), F32), shape((rows_c, LANES), F32)],
            [info, got, got_c, keep_a, keep_c],
            after=ordered)
        got = got_c = swapped(send, exchanges[k])
        halved = sums_exchanges[k - 1][0][0] == "tm"
        sums_rows = sums_rows // 2 if halved else sums_rows
        row_step = k - 2 if k - 2 < tm_bits else None
        outs = call(
            functools.partial(sums_step_kernel, halved, at_sums + k - 1, row_step, (per_shard, at_row)),
            [shape((sums_rows, dz), BF16), shape((sums_rows, dz), F32)]
            + [shape((16, channels), BF16)] * (row_step is not None),
            [info, sums_got, sums_keep] + [known] * (row_step is not None),
            after=[send])
        sums_send, sums_keep = outs[:2]
        known = outs[2] if row_step is not None else known
        sums_got = swapped(sums_send, sums_exchanges[k - 1])
        ordered = [sums_send]
    assert now_a == 1 and sums_rows == size
    feat_grad, last = call(
        feat_kernel,
        shape((rows_in, channels), BF16),
        [info, hidden_grad, known, weight],
        after=[sums_send],
        token=True,
        scratch=[VMEM((frames + 8, channels), F32), VMEM((channels // LANES, rows_in, LANES), F32)],
    )

    corr, piece, mine = call(
        functools.partial(last_kernel, rows_a, rows_c - extra),
        [shape((rows_a, LANES), F32), shape((rows_c - extra, LANES), BF16),
         shape((rows_c + size * (dz // LANES), LANES), BF16)],
        [info, got, keep_a, keep_c, sums_got, sums_keep],
        after=[last])
    parts = [piece, swapped(mine, exchanges[0]), swapped(piece, exchanges[1]), crossed(piece, exchanges[1])]
    conv_grad, last = call(
        functools.partial(conv_out_kernel, total_frames, at_start),
        shape((owner_rows, channels), F32),
        [info, corr, proj],
        after=[piece],
        token=True,
        scratch=[VMEM((LANES, channels), F32)],
    )
    proj_grad, bias_grad, code_means, code_usage = call(
        functools.partial(out_kernel, total_frames, book_size / total_frames, dz, at_pieces, now_c, extra),
        [shape((channels, dz), F32), shape((1, channels), F32), shape((levels, per_shard, dz), BF16),
         shape((levels, per_shard), F32)],
        [info, mine] + parts,
        after=[last],
    )
    return feat_grad, conv_grad, bias_grad[0], proj_grad, code_means, code_usage


def solution(mesh):
    placed = (P(("dp", "tm"), None), P("dp", None, "tm"), P(), P(), P(), P())
    return jax.shard_map(
        shards,
        mesh=mesh,
        in_specs=placed,
        out_specs=(
            P(("dp", "tm"), None),
            P(("dp", "tm"), None),
            P(),
            P(),
            P(None, "tm", None),
            P(None, "tm"),
        ),
        check_vma=False,
    )
```

```python
import functools

import jax
import jax.numpy as jnp
from jax import lax
from jax.experimental import pallas as pl
from jax.experimental.pallas import tpu as pltpu
from jax.sharding import PartitionSpec as P

BF16 = jnp.bfloat16
F32 = jnp.float32
LANES = 128
VMEM_LIMIT = 16 * 1024 * 1024


def log2(value):
    assert value & (value - 1) == 0
    return value.bit_length() - 1


def nn(a, b):
    return lax.dot_general(a, b, (((1,), (0,)), ((), ())), preferred_element_type=F32)


def nt(a, b):
    return lax.dot_general(a, b, (((1,), (1,)), ((), ())), preferred_element_type=F32)


VMEM = pltpu.VMEM


def call(body, out_shape, args, after=(), scratch=(), aliases=None, token=False, flops=0):
    info, args = args[0], args[1:]
    count = len(args)
    many = isinstance(out_shape, (list, tuple))
    shapes = list(out_shape) if many else [out_shape]

    def kernel(*refs):
        ends = count + len(after)
        if token:
            refs[ends + len(shapes)][...] = jnp.zeros((8, LANES), F32)
            refs = refs[:ends + len(shapes)] + refs[ends + len(shapes) + 1:]
        body(info(), *refs[:count], *refs[ends:])

    specs = [pl.BlockSpec(memory_space=VMEM)] * count + [pl.BlockSpec(memory_space=pl.ANY)] * len(after)
    shown = shapes + [shape((8, LANES), F32)] * token
    outs = pl.pallas_call(
        kernel,
        out_shape=shown,
        in_specs=specs,
        out_specs=[pl.BlockSpec(memory_space=VMEM)] * len(shown),
        scratch_shapes=list(scratch),
        input_output_aliases={at - 1: out for at, out in (aliases or {}).items()},
        compiler_params=pltpu.CompilerParams(vmem_limit_bytes=VMEM_LIMIT),
        cost_estimate=pl.CostEstimate(flops=flops, bytes_accessed=0, transcendentals=0),
    )(*args, *after)
    return outs if len(shown) > 1 else outs[0]


def shape(dims, dtype):
    return jax.ShapeDtypeStruct(dims, dtype)


def digits_of(value):
    high = value.astype(BF16).astype(F32)
    rest = value - high
    middle = rest.astype(BF16).astype(F32)
    low = (rest - middle).astype(BF16).astype(F32)
    return high, middle, low


def one_hot(codes, axis_codes, first, count):
    frames = codes.shape[1 - axis_codes]
    dims = (count, frames) if axis_codes == 0 else (frames, count)
    places = lax.broadcasted_iota(jnp.int32, dims, axis_codes) + first
    return jnp.where(codes == places, 1.0, 0.0).astype(BF16)


def halo_kernel(info, rows, out):
    out[...] = rows[...]


def walk(orders, halved, count):
    start = 1 if halved else 0
    shown = count // 2 if halved else count
    bits = log2(shown)
    step = 2 if shown > 1 and all(order[-1] == 0 for order in orders) else 1
    for position in range(0, shown, step):
        yield position, [
            sum(((position >> (bits - 1 - k)) & 1) << bit for k, bit in enumerate(order[start:])) for order in orders
        ], step


def correlate(flipped, sources, plan, core, bit, out):
    dz = flipped.shape[0]
    at = 0
    for source, (count, orders, halved) in zip(sources, plan):
        for position, pieces, step in walk(orders, halved, count):
            column = pieces[0] + core * (pieces[1] - pieces[0])
            if halved:
                column = column + (bit << orders[0][0])
            column = pl.multiple_of(column * LANES, LANES)
            product = nn(flipped, source[:, pl.ds(column, step * LANES)])
            for j in range(step):
                top = (at + position + j) * dz
                out[top:top + dz, :] = product[:, j * LANES:(j + 1) * LANES].astype(out.dtype)
        at += count // 2 if halved else count
    return at * dz


def code_digits(codes, dz, rows):
    parts = []
    for part in (codes >> 8, codes & 255):
        for start in range(0, codes.shape[1], dz):
            piece = part[:, start:start + dz].astype(F32)
            if piece.shape[1] < dz:
                piece = jnp.concatenate([piece, jnp.zeros((1, dz - piece.shape[1]), F32)], 1)
            parts.append(piece)
    parts.append(jnp.zeros((rows - len(parts), dz), F32))
    return jnp.concatenate(parts, 0).astype(BF16)


def codes_of(block, frames):
    dz = block.shape[1]
    per = -(-frames // dz)
    digits = block[...].astype(F32)
    parts = [jnp.concatenate([digits[k * per + j:k * per + j + 1, :] for j in range(per)], 1)[:, :frames]
             for k in range(2)]
    return (parts[0] * 256.0 + parts[1]).astype(jnp.int32)


def residuals(hidden, proj, chosen):
    latent = nn(hidden, proj)
    once = latent - chosen[0].astype(F32)
    total = once + (once - chosen[1].astype(F32))
    return latent, once, total.astype(BF16)


def put_columns(out, at, rows, block):
    for j in range(block.shape[1] // LANES):
        out[at + j * rows:at + j * rows + block.shape[0], :] = block[:, j * LANES:(j + 1) * LANES]


def local_kernel(plan, info, feats, weight, bias, codes, books, proj,
                 unfold, hidden, latent_grad, flipped, own, send, first, part, wide, chosen):
    rows, channels = feats.shape
    frames = rows // 2
    dz = proj.shape[1]
    for j in range(channels // LANES):
        wide[j, 0:8, :] = jnp.zeros((8, LANES), F32)
        wide[j, 8:, :] = feats[:, j * LANES:(j + 1) * LANES].astype(F32)
        for tap in range(4):
            start = tap * channels + j * LANES
            unfold[:, start:start + LANES] = wide[j, pl.ds(6 + tap, frames, stride=2), :].astype(BF16)
    conv = nn(unfold[...], weight[...]) + bias[...]
    first[...] = conv[0:16, :]
    hidden[...] = conv.astype(BF16)
    levels = books.shape[0]
    padded = jnp.concatenate([codes[...].astype(F32), jnp.zeros((8 - levels, frames), F32)], 0)
    tall = jnp.transpose(padded).astype(jnp.int32)
    for level in range(levels):
        matches = one_hot(tall[:, level:level + 1], 1, 0, books.shape[1])
        chosen[level] = nn(matches, books[level]).astype(BF16)
    latent, once, grad = residuals(hidden[...], proj[...], chosen)
    latent_grad[...] = grad
    row = lax.broadcasted_iota(jnp.int32, grad.shape, 0)
    flipped[...] = jnp.transpose(jnp.where(row == 0, 0.0, grad.astype(F32))).astype(BF16)
    bit = info[0]
    at = correlate(flipped[...], (unfold, hidden), plan, 1 - bit, 1 - bit, part)
    rows_b = own.shape[0]
    code_rows = rows_b - frames
    digits = [code_digits(codes[level:level + 1, :], dz, code_rows) for level in range(2)]
    own[0:frames, :] = jnp.where(bit == 1, once, latent).astype(BF16)
    own[frames:, :] = jnp.where(bit == 1, digits[1], digits[0])
    put_columns(send, at, rows_b, jnp.where(bit == 1, latent, once).astype(BF16))
    put_columns(send, at + frames, rows_b, jnp.where(bit == 1, digits[0], digits[1]))
    for level in range(levels):
        part[at + level * 16 * (dz // LANES):at + (level + 1) * 16 * (dz // LANES), :] = jnp.concatenate(
            [chosen[level, 0:16, j * LANES:(j + 1) * LANES].astype(F32) for j in range(dz // LANES)], 0)


def frame_kernel(plan, info, halo, first, part, weight, proj, unfold_in, hidden_in, grad_in, flipped_in, own_in, send_in,
                 unfold, hidden, latent_grad, flipped, own, send):
    width = unfold.shape[1]
    half = width // 2
    dz = proj.shape[1]
    row = lax.broadcasted_iota(jnp.int32, (16, half), 0)
    left = jnp.concatenate([halo[0:1, :], halo[1:2, :]], 1).astype(F32)
    head = jnp.where(row == 0, jnp.broadcast_to(left, (16, half)), 0.0)
    unfold[0:16, 0:half] = (unfold_in[0:16, 0:half].astype(F32) + head).astype(BF16)
    fix = nn(head.astype(BF16), weight[0:half, :])
    hidden[0:16, :] = (first[...] + fix).astype(BF16)
    top = hidden[0:16, :]
    pieces = part.shape[0] - 32 * (dz // LANES)
    chosen = []
    for level in range(2):
        at = pieces + level * 16 * (dz // LANES)
        chosen.append(jnp.concatenate([part[at + j * 16:at + (j + 1) * 16, :] for j in range(dz // LANES)], 1))
    latent, once, grad = residuals(top, proj[...], chosen)
    latent_grad[0:16, :] = grad
    flipped[:, 0:LANES] = jnp.transpose(latent_grad[0:LANES, :].astype(F32)).astype(BF16)
    column = flipped[:, 0:LANES].astype(F32)[:, 0:1]
    bit = info[0]
    at = 0
    for source, (count, orders, halved) in zip((unfold, hidden), plan):
        rows = source[0:16, :].astype(F32)[0:1, :]
        for position, places, step in walk(orders, halved, count):
            for j in range(step):
                offsets = [places[0] + j, places[1] + j]
                low = [offset for offset in offsets]
                high = [offset + (1 << orders[0][0] if halved else 0) for offset in offsets]
                picked = [rows[:, k * LANES:(k + 1) * LANES] for k in low + high]
                piece = jnp.where(bit == 1, picked[0], picked[3]) if halved else jnp.where(bit == 1, picked[0], picked[1])
                begin = (at + position + j) * dz
                send[begin:begin + dz, :] = (part[begin:begin + dz, :] + column * piece).astype(BF16)
        at += count // 2 if halved else count
    rows_b = own.shape[0]
    own[0:16, :] = jnp.where(bit == 1, once, latent).astype(BF16)
    put_columns(send, at * dz, rows_b, jnp.where(bit == 1, latent, once).astype(BF16))


def rest_kernel(plan, info, flipped, unfold, hidden, latent_grad, proj, keep_a, keep_c, hidden_grad, extras, row):
    bit = info[0]
    correlate(flipped[...], (unfold,), plan[:1], bit, bit, keep_a)
    correlate(flipped[...], (hidden,), plan[1:], bit, bit, keep_c)
    back = nt(latent_grad[...], proj[...]).astype(BF16)
    hidden_grad[...] = back
    row[...] = back[0:16, :]
    stride = extras.shape[0] // 4
    extras[...] = jnp.zeros(extras.shape, F32)
    sums = jnp.sum(back.astype(F32), 0, keepdims=True)
    for digit, part in enumerate(digits_of(sums)):
        for j in range(sums.shape[1] // LANES):
            extras[digit * stride + j:digit * stride + j + 1, :] = part[:, j * LANES:(j + 1) * LANES]


def split_sum(halved, bit, got, at, kept, rows, send, to, keep):
    if halved:
        half = rows // 2
        away = pl.multiple_of((1 - bit) * half, 16)
        home = pl.multiple_of(bit * half, 16)
        send[to:to + half, :] = (kept[pl.ds(away, half), :] + got[pl.ds(at + away, half), :].astype(F32)).astype(BF16)
        keep[0:half, :] = kept[pl.ds(home, half), :] + got[pl.ds(at + home, half), :].astype(F32)
        return half
    total = (kept[0:rows, :] + got[at:at + rows, :].astype(F32)).astype(BF16)
    send[to:to + rows, :] = total
    keep[0:rows, :] = total.astype(F32)
    return rows


def add_digits(mine, theirs):
    stride = mine.shape[0] // 4
    return ((mine[0:stride] + mine[stride:2 * stride]) + mine[2 * stride:3 * stride]) + (
        (theirs[0:stride] + theirs[stride:2 * stride]) + theirs[2 * stride:3 * stride])


def digit_block(value):
    return jnp.concatenate(list(digits_of(value)) + [jnp.zeros_like(value)], 0)


def first_step_kernel(halves, place, info, got, kept_a, kept_c, extras, send, keep_a, keep_c):
    (rows_a, halved_a), (rows_c, halved_c) = halves
    to = split_sum(halved_a, info[place], got, 0, kept_a, rows_a, send, 0, keep_a)
    gone = split_sum(halved_c, info[place], got, rows_a, kept_c, rows_c, send, to, keep_c)
    send[to + gone:, :] = extras[...].astype(BF16)
    keep_c[gone:, :] = extras[...]


def feat_kernel(info, grad, after, weight, out, wide, inter):
    frames, channels = grad.shape
    half = weight.shape[0] // 2
    wide[0:frames, :] = grad[...].astype(F32)
    wide[frames:, :] = jnp.broadcast_to(after[0:1, :].astype(F32), (8, channels))
    ahead = wide[pl.ds(1, frames), :].astype(BF16)
    for parity in range(2):
        rows = pl.ds(parity * (half // 2), half // 2)
        rows_after = pl.ds(half + parity * (half // 2), half // 2)
        both = nt(ahead, weight[rows, :]) + nt(grad[...], weight[rows_after, :])
        for j in range(channels // LANES):
            inter[j, pl.ds(parity, frames, stride=2), :] = both[:, j * LANES:(j + 1) * LANES]
    for j in range(channels // LANES):
        out[:, j * LANES:(j + 1) * LANES] = inter[j].astype(BF16)


def own_sums_kernel(frames, place, count, info, own, out):
    codes = codes_of(own[frames:, :], frames)
    ones = jnp.ones((8, frames), BF16)
    size = count + 16
    for top in range(0, out.shape[0], size):
        matches = one_hot(codes, 0, info[place], count)
        out[top:top + count, :] = nn(matches, own[0:frames, :])
        out[top + count:top + count + 8, 0:count] = nt(ones, matches)
        place += 1


def sums_kernel(first, frames, place, count, info, got, base, row, *outs):
    dz = base.shape[1]
    rows = (got.shape[0] - first) // (dz // LANES)
    theirs = jnp.concatenate([got[first + j * rows:first + (j + 1) * rows, :] for j in range(dz // LANES)], 1)
    codes = codes_of(theirs[frames:, :], frames)
    ones = jnp.ones((8, frames), BF16)
    size = count + 16
    riding = [row[...].astype(F32)[0:1, :]]
    for j, out in enumerate(outs):
        top = j * size
        matches = one_hot(codes, 0, info[place + j], count)
        total = base[top:top + count, :] + nn(matches, theirs[0:frames, :])
        counts = base[top + count:top + count + 8, 0:count] + nt(ones, matches)
        out[0:count, :] = total.astype(out.dtype)
        out[count:, :] = count_rows(counts[0:1], dz, riding).astype(out.dtype)


def count_rows(count, width, riding=()):
    high = jnp.floor(count * (1.0 / 65536.0))
    rest = count - high * 65536.0
    middle = jnp.floor(rest * (1.0 / 256.0))
    low = rest - middle * 256.0
    block = jnp.concatenate([high, middle, low], 0)
    if count.shape[1] < width:
        block = jnp.concatenate([block, jnp.zeros((3, width - count.shape[1]), F32)], 1)
    parts = [block]
    for row in riding:
        parts += [row[:, at:at + width] for at in range(0, row.shape[1], width)]
    left = 16 - sum(part.shape[0] for part in parts)
    return jnp.concatenate(parts + [jnp.zeros((left, width), F32)] * (left > 0), 0)


def riding_row(block, index, parts):
    return jnp.concatenate([block[3 + index * parts + j:4 + index * parts + j, :] for j in range(parts)], 1)


def count_of(block, own):
    return (block[0:1] * 65536.0 + block[1:2] * 256.0 + block[2:3])[:, :own]


def add_sums(kept, gots, out, riding=()):
    count = out.shape[0] - 16
    value = kept[0:count, :].astype(F32)
    number = count_of(kept[count:, :].astype(F32), count)
    for got in gots:
        value = value + got[0:count, :].astype(F32)
        number = number + count_of(got[count:, :].astype(F32), count)
    out[0:count, :] = value.astype(out.dtype)
    out[count:, :] = count_rows(number, out.shape[1], riding).astype(out.dtype)


def forward_sums_kernel(info, got, kept, row, out, known):
    parts = row.shape[1] // got.shape[1]
    mine = row[...].astype(F32)[0:1, :]
    other = riding_row(got[got.shape[0] - 16:, :].astype(F32), 0, parts)
    add_sums(kept, [got], out, [mine, other])
    known[...] = jnp.concatenate([mine, other, jnp.zeros((14, row.shape[1]), F32)], 0).astype(BF16)


def own_block_kernel(row_place, info, first, second, kept, known, out, after):
    parts = known.shape[1] // second.shape[1]
    block = second[second.shape[0] - 16:, :].astype(F32)
    rows = [known[...].astype(F32)[1:2, :], riding_row(block, 0, parts), riding_row(block, 1, parts)]
    wide = jnp.zeros(after.shape, F32)
    for j, row in enumerate(rows):
        wide = jnp.where(info[row_place] == j + 1, jnp.broadcast_to(row, after.shape), wide)
    after[...] = wide.astype(BF16)
    add_sums(kept, [first, second], out)


def sums_step_kernel(info, got, kept, out):
    add_sums(kept, [got], out)


def swap_halves(first, second, core):
    half = LANES // 2
    left = lax.broadcasted_iota(jnp.int32, first.shape, 1) < half
    turned_first, turned_second = pltpu.roll(first, half, 1), pltpu.roll(second, half, 1)
    swapped_first = jnp.where(left, first, turned_second)
    swapped_second = jnp.where(left, turned_first, second)
    return jnp.where(core == 1, swapped_first, first), jnp.where(core == 1, swapped_second, second)


def step_kernel(halves, at_c, place, mixed, apart, info, got, got_c, kept_a, kept_c, *refs):
    (rows_a, halved_a), (rows_c, halved_c) = halves
    send, keep_a, keep_c = refs[0], refs[-2], refs[-1]
    send_c = refs[1] if apart else send
    if mixed:
        to = rows_a // 2
        total = kept_a[0:rows_a, :] + got[0:rows_a, :].astype(F32)
        first, second = swap_halves(total[0:to, :], total[to:, :], info[0])
        low = info[place] == 0
        send[0:to, :] = jnp.where(low, second, first).astype(BF16)
        keep_a[...] = jnp.where(low, first, second)
    else:
        to = split_sum(halved_a, info[place], got, 0, kept_a, rows_a, send, 0, keep_a)
    to = 0 if apart else to
    gone = split_sum(halved_c, info[place], got_c, at_c, kept_c, rows_c, send_c, to, keep_c)
    block = digit_block(add_digits(kept_c[rows_c:, :], got_c[at_c + rows_c:, :].astype(F32)))
    keep_c[gone:, :] = block
    to += gone
    send_c[to:to + block.shape[0], :] = block.astype(BF16)
    to += block.shape[0]
    if to < send_c.shape[0]:
        send_c[to:, :] = jnp.zeros((send_c.shape[0] - to, LANES), BF16)


def last_kernel(rows_a, rows, info, got, kept_a, kept_c, sums_got, sums_kept, corr, pieces, mine):
    corr[...] = kept_a[...] + got[0:rows_a, :].astype(F32)
    pieces[...] = (kept_c[0:rows, :] + got[rows_a:rows_a + rows, :].astype(F32)).astype(BF16)
    block = digit_block(add_digits(kept_c[rows:, :], got[rows_a + rows:rows_a + kept_c.shape[0], :].astype(F32)))
    mine[0:rows, :] = pieces[...]
    mine[rows:kept_c.shape[0], :] = block.astype(BF16)
    at = kept_c.shape[0]
    count = sums_kept.shape[0] - 16
    number = count_of(sums_kept[count:, :].astype(F32), count) + count_of(sums_got[count:, :].astype(F32), count)
    square = (count, count)
    same = lax.broadcasted_iota(jnp.int32, square, 0) == lax.broadcasted_iota(jnp.int32, square, 1)
    tall = jnp.sum(jnp.where(same, jnp.broadcast_to(number, square), 0.0), 1, keepdims=True)
    total = sums_kept[0:count, :].astype(F32) + sums_got[0:count, :].astype(F32)
    means = (total / jnp.maximum(tall, 1.0)).astype(BF16)
    digits = count_rows(number, means.shape[1]).astype(BF16)
    for j in range(means.shape[1] // LANES):
        mine[at:at + count, :] = means[:, j * LANES:(j + 1) * LANES]
        mine[at + count:at + count + 16, :] = digits[:, j * LANES:(j + 1) * LANES]
        at += count + 16


def conv_out_kernel(total_frames, place, info, corr, proj, out, wide):
    rows = out.shape[0]
    flipped = jnp.transpose(corr[...])
    high = flipped.astype(BF16)
    low = (flipped - high.astype(F32)).astype(BF16)
    wide[...] = (nt(high, proj[...]) + nt(low, proj[...])) * (1.0 / total_frames)
    start = info[place]
    if rows % 8 == 0:
        out[...] = wide[pl.ds(pl.multiple_of(start, 8), rows), :]
    else:
        taken = wide[0:rows, :]
        for other in range(rows, wide.shape[0], rows):
            taken = jnp.where(start == other, wide[other:other + rows, :], taken)
        out[...] = taken


def out_kernel(total_frames, use_scale, dz, place, inner, extra, info, mine, *refs):
    parts, (out, bias, means, usage) = refs[:-4], refs[-4:]
    theirs = parts[1]
    scale = 1.0 / total_frames
    top = inner * dz
    value = add_digits(mine[top:top + extra, :].astype(F32), theirs[top:top + extra, :].astype(F32)) * scale
    for j in range(bias.shape[1] // LANES):
        bias[:, j * LANES:(j + 1) * LANES] = value[j:j + 1, :]
    bit = info[0]
    count = means.shape[1]
    numbers = []
    for ref, level in ((mine, bit), (theirs, 1 - bit)):
        at = top + extra
        blocks = []
        for j in range(dz // LANES):
            blocks.append(ref[at:at + count + 16, :])
            at += count + 16
        whole = jnp.concatenate(blocks, 1)
        means[level] = whole[0:count, :]
        numbers.append(count_of(whole[count:, :].astype(F32), count) * use_scale)
    usage[0:1, :] = jnp.where(bit == 1, numbers[1], numbers[0])
    usage[1:2, :] = jnp.where(bit == 1, numbers[0], numbers[1])
    for j, ref in enumerate(parts):
        for k in range(inner):
            start = pl.multiple_of((info[place + j] + k) * LANES, LANES)
            turned = jnp.transpose(ref[k * dz:(k + 1) * dz, :])
            out[pl.ds(start, LANES), :] = turned.astype(F32) * scale


def shifted(block, axis, distance):
    devices = range(lax.axis_size(axis))
    route = [(i - distance, i) for i in devices if i - distance in devices]
    return lax.ppermute(block, axis, route)


def swapped(block, steps):
    tm = lax.axis_size("tm")

    def partner(device):
        axis, bit = steps[(device // tm) & 1]
        return device ^ ((1 << bit) * (tm if axis == "dp" else 1))

    route = [(device, partner(device)) for device in range(lax.axis_size("dp") * tm)]
    return lax.ppermute(block, ("dp", "tm"), route)


def crossed(block, steps):
    tm = lax.axis_size("tm")

    def partner(device):
        axis, bit = steps[(device // tm) & 1]
        return device ^ tm ^ ((1 << bit) * (tm if axis == "dp" else 1))

    route = [(device, partner(device)) for device in range(lax.axis_size("dp") * tm)]
    return lax.ppermute(block, ("dp", "tm"), route)


def shards(feats, codes, conv_weight, conv_bias, proj_weight, codebooks):
    dp, tm = lax.axis_size("dp"), lax.axis_size("tm")
    rows_in, channels = feats.shape
    frames = rows_in // 2
    levels, book_size, dz = codebooks.shape
    assert levels == 2
    width = conv_weight.shape[0]
    total_frames = frames * dp * tm
    per_shard = book_size // tm
    dp_bits, tm_bits = log2(dp), log2(tm)
    owner_rows = width // (dp * tm)

    assert dp_bits >= 3 and tm_bits == 2
    pieces_a, pieces_c = width // LANES, channels // LANES
    under = max(dp_bits + tm_bits - log2(pieces_a), 0)
    c_bits = 2
    assert pieces_c >= 4
    whole_bits = [b for b in range(1, dp_bits) if b + tm_bits < under]
    piece_bits = [b for b in range(1, dp_bits) if b + tm_bits >= under]
    paths = [[("dp", b) for b in bits] for bits in (whole_bits + piece_bits, whole_bits[::-1] + piece_bits[::-1])]
    mixed = under == 1 and tm_bits == 2
    turned = mixed or under == 0 or under >= tm_bits
    up = [("tm", b) for b in range(tm_bits)]
    paths[0] += up[::-1]
    paths[1] += up if turned else up[::-1]
    exchanges = list(zip([("dp", 0)] + paths[0], [("dp", 0)] + paths[1]))
    sums_up = [("dp", b) for b in range(1, dp_bits)]
    sums_exchanges = list(zip(up + sums_up, up[::-1] + sums_up[::-1]))

    def piece_bit(step):
        axis, b = step
        bit = b + (tm_bits if axis == "dp" else 0)
        return bit - under if bit >= under else None

    a_split = [piece_bit(steps[0]) is not None for steps in exchanges]
    c_split = [log2(pieces_c) - 1 - k if k < c_bits else None for k in range(len(exchanges))]

    def order_of(split, count):
        used = [b for b in split if b is not None]
        return used + [b for b in reversed(range(log2(count))) if b not in used]

    orders = [order_of([piece_bit(steps[core]) for steps in exchanges], pieces_a) for core in range(2)]
    order_c = order_of(c_split, pieces_c)
    plan = [(pieces_a, orders, a_split[0]), (pieces_c, [order_c, order_c], True)]
    now_a = pieces_a // 2 if plan[0][2] else pieces_a
    now_c = pieces_c // 2

    count_bits, count_places = len(exchanges), 4
    at_start = count_bits
    at_codes = at_start + 1
    at_pieces = at_codes + tm
    at_row = at_pieces + count_places

    def info():
        at_dp, at_tm = lax.axis_index("dp"), lax.axis_index("tm")
        core = at_dp & 1

        def on_core(values):
            return values[0] + core * (values[1] - values[0])

        def bit_at(step):
            axis, b = step
            return ((at_dp if axis == "dp" else at_tm) >> b) & 1

        bits = [on_core([bit_at(step) for step in steps]) for steps in exchanges]
        shared = [bit_at(step) for step in exchanges[1]]
        mine_c, other_c = on_core(shared), on_core(shared[::-1])
        places = [2 * core + mine_c, 2 * (1 - core) + other_c, 2 * core + 1 - mine_c, 2 * (1 - core) + 1 - other_c]
        places = [place << (log2(pieces_c) - c_bits) for place in places]
        ways = [[b for _, b in up], [b for _, b in up[::-1]]]
        first_bit, second_bit = on_core([way[0] for way in ways]), on_core([way[1] for way in ways])
        lead, other = (at_tm >> first_bit) & 1, (at_tm >> second_bit) & 1
        blocks = [((a << first_bit) + (b << second_bit)) * per_shard for a in (1 - lead, lead) for b in (1 - other, other)]
        differ = at_tm ^ (at_tm + 1)
        coded = [sum(((differ >> b) & 1) << j for j, b in enumerate(way)) for way in ways]
        row_code = jnp.where(at_tm + 1 < tm, on_core(coded), 0)
        if turned and not mixed:
            start = ((at_dp * tm + at_tm) * owner_rows) & (LANES - 1)
        else:
            start = on_core([(at_dp * tm + at_tm) * owner_rows, (at_tm >> 1) * owner_rows if mixed else (
                at_dp * tm + at_tm) * owner_rows]) & (LANES - 1)
        return bits + [start] + blocks + places + [row_code]

    halo = shifted(call(halo_kernel, shape((2, channels), BF16), [info, feats[-2:]], flops=10 ** 11), "tm", 1)
    weight, proj, codes = conv_weight, proj_weight, codes[0]
    extra = 4 * (-(-channels // LANES // 8) * 8)
    code_rows = -(-(2 * -(-frames // dz)) // 16) * 16
    corr_rows = (now_a + now_c) * dz
    rows_b = frames + code_rows
    shared = [shape((frames, width), BF16), shape((frames, channels), BF16), shape((frames, dz), BF16),
              shape((dz, frames), BF16), shape((rows_b, dz), BF16),
              shape((corr_rows + rows_b * (dz // LANES), LANES), BF16)]
    *arrays, first, part = call(
        functools.partial(local_kernel, plan),
        shared + [shape((16, channels), F32), shape((corr_rows + 32 * (dz // LANES), LANES), F32)],
        [info, feats, weight, conv_bias[None, :], codes, codebooks, proj],
        scratch=[VMEM((channels // LANES, rows_in + 8, LANES), F32), VMEM((levels, frames, dz), BF16)],
    )
    unfold, hidden, latent_grad, flipped, own, send = call(
        functools.partial(frame_kernel, plan),
        shared,
        [info, halo, first, part, weight, proj] + arrays,
        aliases={6 + k: k for k in range(len(shared))},
    )
    got = swapped(send, exchanges[0])
    keep_a, keep_c, hidden_grad, extras, row = call(
        functools.partial(rest_kernel, plan),
        [shape((now_a * dz, LANES), F32), shape((now_c * dz, LANES), F32), shape((frames, channels), BF16),
         shape((extra, LANES), F32), shape((16, channels), BF16)],
        [info, flipped, unfold, hidden, latent_grad, proj],
        after=[send],
    )

    def halves_at(k):
        nonlocal now_a, now_c
        halves = [(now_a * dz, a_split[k]), (now_c * dz, c_split[k] is not None)]
        now_a = now_a // 2 if halves[0][1] else now_a
        now_c = now_c // 2 if halves[1][1] else now_c
        return halves, now_a * dz, now_c * dz + extra

    size = per_shard + 16

    def own_sums(first, after):
        return call(
            functools.partial(own_sums_kernel, frames, at_codes + first, per_shard),
            shape((2 * size, dz), F32),
            [info, own],
            after=after)

    base = own_sums(0, [extras])
    halves, rows_a, rows_c = halves_at(1)
    send, keep_a, keep_c = call(
        functools.partial(first_step_kernel, halves, 1),
        [shape((rows_a + rows_c, LANES), BF16), shape((rows_a, LANES), F32), shape((rows_c, LANES), F32)],
        [info, got, keep_a, keep_c, extras],
        after=[base])
    got_core = got
    got = swapped(send, exchanges[1])

    def both_sums(first, base, dtype, after):
        return call(
            functools.partial(sums_kernel, corr_rows, frames, at_codes + first, per_shard),
            [shape((size, dz), dtype)] * 2,
            [info, got_core, base, row],
            after=after)

    leaving = both_sums(0, base, BF16, [send])
    sums_got = [swapped(block, sums_exchanges[0]) for block in leaving]
    staying = both_sums(2, own_sums(2, [leaving[0]]), F32, [])
    sums_kept, known = call(
        forward_sums_kernel,
        [shape((size, dz), BF16), shape((16, channels), BF16)],
        [info, sums_got[0], staying[0], row],
        after=[staying[1]])
    sums_new = swapped(sums_kept, sums_exchanges[1])
    got_c = got
    ordered = [sums_kept]
    for k in range(2, len(exchanges)):
        at_c = rows_a if got_c is got else 0
        halves, rows_a, rows_c = halves_at(k)
        apart = k == 2
        spare = 16 * (k == len(exchanges) - 1)
        sends = [rows_a, rows_c] if apart else [rows_a + rows_c + spare]
        *outs, keep_a, keep_c = call(
            functools.partial(step_kernel, halves, at_c, k, mixed and k == dp_bits, apart),
            [shape((rows, LANES), BF16) for rows in sends] + [shape((rows_a, LANES), F32), shape((rows_c, LANES), F32)],
            [info, got, got_c, keep_a, keep_c],
            after=ordered)
        got = got_c = swapped(outs[0], exchanges[k])
        if apart:
            got_c = swapped(outs[1], exchanges[k])
        ordered = [outs[0]]
        if k == 3:
            sums_kept, known = call(
                functools.partial(own_block_kernel, at_row),
                [shape((size, dz), BF16), shape((16, channels), BF16)],
                [info, sums_got[1], sums_new, staying[1], known],
                after=ordered)
        elif k > 3:
            sums_kept = call(sums_step_kernel, shape((size, dz), BF16), [info, sums_new, sums_kept], after=ordered)
        if k > 2:
            sums_new = swapped(sums_kept, sums_exchanges[k - 1])
            ordered = [sums_kept]
    assert now_a == 1
    feat_grad, last = call(
        feat_kernel,
        shape((rows_in, channels), BF16),
        [info, hidden_grad, known, weight],
        after=[sums_kept],
        token=True,
        scratch=[VMEM((frames + 8, channels), F32), VMEM((channels // LANES, rows_in, LANES), F32)],
    )

    corr, piece, mine = call(
        functools.partial(last_kernel, rows_a, rows_c - extra),
        [shape((rows_a, LANES), F32), shape((rows_c - extra, LANES), BF16),
         shape((rows_c + size * (dz // LANES), LANES), BF16)],
        [info, got, keep_a, keep_c, sums_new, sums_kept],
        after=[last])
    parts = [piece, swapped(mine, exchanges[0]), swapped(piece, exchanges[1]), crossed(piece, exchanges[1])]
    conv_grad, last = call(
        functools.partial(conv_out_kernel, total_frames, at_start),
        shape((owner_rows, channels), F32),
        [info, corr, proj],
        after=[piece],
        token=True,
        scratch=[VMEM((LANES, channels), F32)],
    )
    proj_grad, bias_grad, code_means, code_usage = call(
        functools.partial(out_kernel, total_frames, book_size / total_frames, dz, at_pieces, now_c, extra),
        [shape((channels, dz), F32), shape((1, channels), F32), shape((levels, per_shard, dz), BF16),
         shape((levels, per_shard), F32)],
        [info, mine] + parts,
        after=[last],
    )
    return feat_grad, conv_grad, bias_grad[0], proj_grad, code_means, code_usage


def solution(mesh):
    placed = (P(("dp", "tm"), None), P("dp", None, "tm"), P(), P(), P(), P())
    return jax.shard_map(
        shards,
        mesh=mesh,
        in_specs=placed,
        out_specs=(
            P(("dp", "tm"), None),
            P(("dp", "tm"), None),
            P(),
            P(),
            P(None, "tm", None),
            P(None, "tm"),
        ),
        check_vma=False,
    )
```

```python
import functools

import jax
import jax.numpy as jnp
from jax import lax
from jax.experimental import pallas as pl
from jax.experimental.pallas import tpu as pltpu
from jax.sharding import PartitionSpec as P

BF16 = jnp.bfloat16
F32 = jnp.float32
LANES = 128
VMEM_LIMIT = 16 * 1024 * 1024


def log2(value):
    assert value & (value - 1) == 0
    return value.bit_length() - 1


def nn(a, b):
    return lax.dot_general(a, b, (((1,), (0,)), ((), ())), preferred_element_type=F32)


def nt(a, b):
    return lax.dot_general(a, b, (((1,), (1,)), ((), ())), preferred_element_type=F32)


VMEM = pltpu.VMEM


def call(body, out_shape, args, after=(), scratch=(), aliases=None, token=False, flops=0):
    info, args = args[0], args[1:]
    count = len(args)
    many = isinstance(out_shape, (list, tuple))
    shapes = list(out_shape) if many else [out_shape]

    def kernel(*refs):
        ends = count + len(after)
        if token:
            refs[ends + len(shapes)][...] = jnp.zeros((8, LANES), F32)
            refs = refs[:ends + len(shapes)] + refs[ends + len(shapes) + 1:]
        body(info(), *refs[:count], *refs[ends:])

    specs = [pl.BlockSpec(memory_space=VMEM)] * count + [pl.BlockSpec(memory_space=pl.ANY)] * len(after)
    shown = shapes + [shape((8, LANES), F32)] * token
    outs = pl.pallas_call(
        kernel,
        out_shape=shown,
        in_specs=specs,
        out_specs=[pl.BlockSpec(memory_space=VMEM)] * len(shown),
        scratch_shapes=list(scratch),
        input_output_aliases={at - 1: out for at, out in (aliases or {}).items()},
        compiler_params=pltpu.CompilerParams(vmem_limit_bytes=VMEM_LIMIT),
        cost_estimate=pl.CostEstimate(flops=flops, bytes_accessed=0, transcendentals=0),
    )(*args, *after)
    return outs if len(shown) > 1 else outs[0]


def shape(dims, dtype):
    return jax.ShapeDtypeStruct(dims, dtype)


def digits_of(value):
    high = value.astype(BF16).astype(F32)
    rest = value - high
    middle = rest.astype(BF16).astype(F32)
    low = (rest - middle).astype(BF16).astype(F32)
    return high, middle, low


def one_hot(codes, axis_codes, first, count):
    frames = codes.shape[1 - axis_codes]
    dims = (count, frames) if axis_codes == 0 else (frames, count)
    places = lax.broadcasted_iota(jnp.int32, dims, axis_codes) + first
    return jnp.where(codes == places, 1.0, 0.0).astype(BF16)


def halo_kernel(info, rows, out):
    out[...] = rows[...]


def walk(orders, halved, count):
    start = 1 if halved else 0
    shown = count // 2 if halved else count
    bits = log2(shown)
    step = 2 if shown > 1 and all(order[-1] == 0 for order in orders) else 1
    for position in range(0, shown, step):
        yield position, [
            sum(((position >> (bits - 1 - k)) & 1) << bit for k, bit in enumerate(order[start:])) for order in orders
        ], step


def correlate(flipped, sources, plan, core, bit, out):
    dz = flipped.shape[0]
    at = 0
    for source, (count, orders, halved) in zip(sources, plan):
        for position, pieces, step in walk(orders, halved, count):
            column = pieces[0] + core * (pieces[1] - pieces[0])
            if halved:
                column = column + (bit << orders[0][0])
            column = pl.multiple_of(column * LANES, LANES)
            product = nn(flipped, source[:, pl.ds(column, step * LANES)])
            for j in range(step):
                top = (at + position + j) * dz
                out[top:top + dz, :] = product[:, j * LANES:(j + 1) * LANES].astype(out.dtype)
        at += count // 2 if halved else count
    return at * dz


def code_digits(codes, dz, rows):
    parts = []
    for part in (codes >> 8, codes & 255):
        for start in range(0, codes.shape[1], dz):
            piece = part[:, start:start + dz].astype(F32)
            if piece.shape[1] < dz:
                piece = jnp.concatenate([piece, jnp.zeros((1, dz - piece.shape[1]), F32)], 1)
            parts.append(piece)
    parts.append(jnp.zeros((rows - len(parts), dz), F32))
    return jnp.concatenate(parts, 0).astype(BF16)


def codes_of(block, frames):
    dz = block.shape[1]
    per = -(-frames // dz)
    digits = block[...].astype(F32)
    parts = [jnp.concatenate([digits[k * per + j:k * per + j + 1, :] for j in range(per)], 1)[:, :frames]
             for k in range(2)]
    return (parts[0] * 256.0 + parts[1]).astype(jnp.int32)


def residuals(hidden, proj, chosen):
    latent = nn(hidden, proj)
    once = latent - chosen[0].astype(F32)
    total = once + (once - chosen[1].astype(F32))
    return latent, once, total.astype(BF16)


def put_columns(out, at, rows, block):
    for j in range(block.shape[1] // LANES):
        out[at + j * rows:at + j * rows + block.shape[0], :] = block[:, j * LANES:(j + 1) * LANES]


def local_kernel(plan, info, feats, weight, bias, codes, books, proj,
                 unfold, hidden, latent_grad, flipped, own, send, first, part, wide, chosen):
    rows, channels = feats.shape
    frames = rows // 2
    dz = proj.shape[1]
    for j in range(channels // LANES):
        wide[j, 0:8, :] = jnp.zeros((8, LANES), F32)
        wide[j, 8:, :] = feats[:, j * LANES:(j + 1) * LANES].astype(F32)
        for tap in range(4):
            start = tap * channels + j * LANES
            unfold[:, start:start + LANES] = wide[j, pl.ds(6 + tap, frames, stride=2), :].astype(BF16)
    conv = nn(unfold[...], weight[...]) + bias[...]
    first[...] = conv[0:16, :]
    hidden[...] = conv.astype(BF16)
    levels = books.shape[0]
    padded = jnp.concatenate([codes[...].astype(F32), jnp.zeros((8 - levels, frames), F32)], 0)
    tall = jnp.transpose(padded).astype(jnp.int32)
    for level in range(levels):
        matches = one_hot(tall[:, level:level + 1], 1, 0, books.shape[1])
        chosen[level] = nn(matches, books[level]).astype(BF16)
    latent, once, grad = residuals(hidden[...], proj[...], chosen)
    latent_grad[...] = grad
    row = lax.broadcasted_iota(jnp.int32, grad.shape, 0)
    flipped[...] = jnp.transpose(jnp.where(row == 0, 0.0, grad.astype(F32))).astype(BF16)
    bit = info[0]
    at = correlate(flipped[...], (unfold, hidden), plan, 1 - bit, 1 - bit, part)
    rows_b = own.shape[0]
    code_rows = rows_b - frames
    digits = [code_digits(codes[level:level + 1, :], dz, code_rows) for level in range(2)]
    own[0:frames, :] = jnp.where(bit == 1, once, latent).astype(BF16)
    own[frames:, :] = jnp.where(bit == 1, digits[1], digits[0])
    put_columns(send, at, rows_b, jnp.where(bit == 1, latent, once).astype(BF16))
    put_columns(send, at + frames, rows_b, jnp.where(bit == 1, digits[0], digits[1]))
    for level in range(levels):
        part[at + level * 16 * (dz // LANES):at + (level + 1) * 16 * (dz // LANES), :] = jnp.concatenate(
            [chosen[level, 0:16, j * LANES:(j + 1) * LANES].astype(F32) for j in range(dz // LANES)], 0)


def frame_kernel(plan, info, halo, first, part, weight, proj, unfold_in, hidden_in, grad_in, flipped_in, own_in, send_in,
                 unfold, hidden, latent_grad, flipped, own, send):
    width = unfold.shape[1]
    half = width // 2
    dz = proj.shape[1]
    row = lax.broadcasted_iota(jnp.int32, (16, half), 0)
    left = jnp.concatenate([halo[0:1, :], halo[1:2, :]], 1).astype(F32)
    head = jnp.where(row == 0, jnp.broadcast_to(left, (16, half)), 0.0)
    unfold[0:16, 0:half] = (unfold_in[0:16, 0:half].astype(F32) + head).astype(BF16)
    fix = nn(head.astype(BF16), weight[0:half, :])
    hidden[0:16, :] = (first[...] + fix).astype(BF16)
    top = hidden[0:16, :]
    pieces = part.shape[0] - 32 * (dz // LANES)
    chosen = []
    for level in range(2):
        at = pieces + level * 16 * (dz // LANES)
        chosen.append(jnp.concatenate([part[at + j * 16:at + (j + 1) * 16, :] for j in range(dz // LANES)], 1))
    latent, once, grad = residuals(top, proj[...], chosen)
    latent_grad[0:16, :] = grad
    flipped[:, 0:LANES] = jnp.transpose(latent_grad[0:LANES, :].astype(F32)).astype(BF16)
    column = flipped[:, 0:LANES].astype(F32)[:, 0:1]
    bit = info[0]
    at = 0
    for source, (count, orders, halved) in zip((unfold, hidden), plan):
        rows = source[0:16, :].astype(F32)[0:1, :]
        for position, places, step in walk(orders, halved, count):
            for j in range(step):
                offsets = [places[0] + j, places[1] + j]
                low = [offset for offset in offsets]
                high = [offset + (1 << orders[0][0] if halved else 0) for offset in offsets]
                picked = [rows[:, k * LANES:(k + 1) * LANES] for k in low + high]
                piece = jnp.where(bit == 1, picked[0], picked[3]) if halved else jnp.where(bit == 1, picked[0], picked[1])
                begin = (at + position + j) * dz
                send[begin:begin + dz, :] = (part[begin:begin + dz, :] + column * piece).astype(BF16)
        at += count // 2 if halved else count
    rows_b = own.shape[0]
    own[0:16, :] = jnp.where(bit == 1, once, latent).astype(BF16)
    put_columns(send, at * dz, rows_b, jnp.where(bit == 1, latent, once).astype(BF16))


def rest_kernel(plan, info, flipped, unfold, hidden, latent_grad, proj, keep_a, keep_c, hidden_grad, extras, row):
    bit = info[0]
    correlate(flipped[...], (unfold,), plan[:1], bit, bit, keep_a)
    correlate(flipped[...], (hidden,), plan[1:], bit, bit, keep_c)
    back = nt(latent_grad[...], proj[...]).astype(BF16)
    hidden_grad[...] = back
    row[...] = back[0:16, :]
    stride = extras.shape[0] // 4
    extras[...] = jnp.zeros(extras.shape, F32)
    sums = jnp.sum(back.astype(F32), 0, keepdims=True)
    for digit, part in enumerate(digits_of(sums)):
        for j in range(sums.shape[1] // LANES):
            extras[digit * stride + j:digit * stride + j + 1, :] = part[:, j * LANES:(j + 1) * LANES]


def split_sum(halved, bit, got, at, kept, rows, send, to, keep):
    if halved:
        half = rows // 2
        away = pl.multiple_of((1 - bit) * half, 16)
        home = pl.multiple_of(bit * half, 16)
        send[to:to + half, :] = (kept[pl.ds(away, half), :] + got[pl.ds(at + away, half), :].astype(F32)).astype(BF16)
        keep[0:half, :] = kept[pl.ds(home, half), :] + got[pl.ds(at + home, half), :].astype(F32)
        return half
    total = (kept[0:rows, :] + got[at:at + rows, :].astype(F32)).astype(BF16)
    send[to:to + rows, :] = total
    keep[0:rows, :] = total.astype(F32)
    return rows


def add_digits(mine, theirs):
    stride = mine.shape[0] // 4
    return ((mine[0:stride] + mine[stride:2 * stride]) + mine[2 * stride:3 * stride]) + (
        (theirs[0:stride] + theirs[stride:2 * stride]) + theirs[2 * stride:3 * stride])


def digit_block(value):
    return jnp.concatenate(list(digits_of(value)) + [jnp.zeros_like(value)], 0)


def first_step_kernel(halves, place, info, got, kept_a, kept_c, extras, send, keep_a, keep_c):
    (rows_a, halved_a), (rows_c, halved_c) = halves
    to = split_sum(halved_a, info[place], got, 0, kept_a, rows_a, send, 0, keep_a)
    gone = split_sum(halved_c, info[place], got, rows_a, kept_c, rows_c, send, to, keep_c)
    send[to + gone:, :] = extras[...].astype(BF16)
    keep_c[gone:, :] = extras[...]


def feat_kernel(info, grad, after, weight, out, wide, inter):
    frames, channels = grad.shape
    half = weight.shape[0] // 2
    wide[0:frames, :] = grad[...].astype(F32)
    wide[frames:, :] = jnp.broadcast_to(after[0:1, :].astype(F32), (8, channels))
    ahead = wide[pl.ds(1, frames), :].astype(BF16)
    for parity in range(2):
        rows = pl.ds(parity * (half // 2), half // 2)
        rows_after = pl.ds(half + parity * (half // 2), half // 2)
        both = nt(ahead, weight[rows, :]) + nt(grad[...], weight[rows_after, :])
        for j in range(channels // LANES):
            inter[j, pl.ds(parity, frames, stride=2), :] = both[:, j * LANES:(j + 1) * LANES]
    for j in range(channels // LANES):
        out[:, j * LANES:(j + 1) * LANES] = inter[j].astype(BF16)


def own_sums_kernel(frames, place, count, info, own, out):
    codes = codes_of(own[frames:, :], frames)
    ones = jnp.ones((8, frames), BF16)
    size = count + 16
    for top in range(0, out.shape[0], size):
        matches = one_hot(codes, 0, info[place], count)
        out[top:top + count, :] = nn(matches, own[0:frames, :])
        out[top + count:top + count + 8, 0:count] = nt(ones, matches)
        place += 1


def sums_kernel(first, frames, place, count, info, got, base, row, out):
    dz = base.shape[1]
    rows = (got.shape[0] - first) // (dz // LANES)
    theirs = jnp.concatenate([got[first + j * rows:first + (j + 1) * rows, :] for j in range(dz // LANES)], 1)
    codes = codes_of(theirs[frames:, :], frames)
    ones = jnp.ones((8, frames), BF16)
    size = count + 16
    riding = [row[...].astype(F32)[0:1, :]]
    for top in range(0, out.shape[0], size):
        matches = one_hot(codes, 0, info[place], count)
        total = base[top:top + count, :] + nn(matches, theirs[0:frames, :])
        counts = base[top + count:top + count + 8, 0:count] + nt(ones, matches)
        out[top:top + count, :] = total.astype(out.dtype)
        out[top + count:top + size, :] = count_rows(counts[0:1], dz, riding).astype(out.dtype)
        place += 1


def count_rows(count, width, riding=()):
    high = jnp.floor(count * (1.0 / 65536.0))
    rest = count - high * 65536.0
    middle = jnp.floor(rest * (1.0 / 256.0))
    low = rest - middle * 256.0
    block = jnp.concatenate([high, middle, low], 0)
    if count.shape[1] < width:
        block = jnp.concatenate([block, jnp.zeros((3, width - count.shape[1]), F32)], 1)
    parts = [block]
    for row in riding:
        parts += [row[:, at:at + width] for at in range(0, row.shape[1], width)]
    left = 16 - sum(part.shape[0] for part in parts)
    return jnp.concatenate(parts + [jnp.zeros((left, width), F32)] * (left > 0), 0)


def riding_row(block, index, parts):
    return jnp.concatenate([block[3 + index * parts + j:4 + index * parts + j, :] for j in range(parts)], 1)


def count_of(block, own):
    return (block[0:1] * 65536.0 + block[1:2] * 256.0 + block[2:3])[:, :own]


def sums_step_kernel(halved, place, row_step, row_place, info, got, kept, *refs):
    riding = ()
    if row_step is not None:
        known, refs = refs[0][...].astype(F32), refs[1:]
        after, refs = refs[-1], refs[:-1]
        parts = known.shape[1] // got.shape[1]
        block = got[row_place[0]:row_place[0] + 16, :].astype(F32)
        rows = [known[j:j + 1, :] for j in range(1 << row_step)]
        rows += [riding_row(block, j, parts) for j in range(1 << row_step)]
        if halved:
            riding = rows
            total = rows + [jnp.zeros((16 - len(rows), known.shape[1]), F32)]
            after[...] = jnp.concatenate(total, 0).astype(BF16)
        else:
            wide = jnp.zeros(after.shape, F32)
            for j in range(1, len(rows)):
                wide = jnp.where(info[row_place[1]] == j, jnp.broadcast_to(rows[j], after.shape), wide)
            after[...] = wide.astype(BF16)
    send, keep = refs
    dz = got.shape[1]
    bit = info[place]
    half = kept.shape[0] // 2 if halved else 0
    outs = [(send, (1 - bit) * half), (keep, bit * half)] if halved else [(send, 0)]
    count = row_place[0]
    size = count + 16
    for out, start in outs:
        for top in range(0, keep.shape[0], size):
            here = top + pl.multiple_of(start, 16) if halved else top
            sums = pl.ds(here, count)
            tail = pl.ds(here + count, 16)
            value = kept[sums, :].astype(F32) + got[sums, :].astype(F32)
            number = count_of(kept[tail, :].astype(F32), count) + count_of(got[tail, :].astype(F32), count)
            out[top:top + count, :] = value.astype(out.dtype)
            out[top + count:top + size, :] = count_rows(number, dz, riding).astype(out.dtype)
    if not halved:
        keep[...] = send[0:keep.shape[0], :].astype(F32)


def swap_halves(first, second, core):
    half = LANES // 2
    left = lax.broadcasted_iota(jnp.int32, first.shape, 1) < half
    turned_first, turned_second = pltpu.roll(first, half, 1), pltpu.roll(second, half, 1)
    swapped_first = jnp.where(left, first, turned_second)
    swapped_second = jnp.where(left, turned_first, second)
    return jnp.where(core == 1, swapped_first, first), jnp.where(core == 1, swapped_second, second)


def step_kernel(halves, place, mixed, info, got, kept_a, kept_c, send, keep_a, keep_c):
    (rows_a, halved_a), (rows_c, halved_c) = halves
    if mixed:
        to = rows_a // 2
        total = kept_a[0:rows_a, :] + got[0:rows_a, :].astype(F32)
        first, second = swap_halves(total[0:to, :], total[to:, :], info[0])
        low = info[place] == 0
        send[0:to, :] = jnp.where(low, second, first).astype(BF16)
        keep_a[...] = jnp.where(low, first, second)
    else:
        to = split_sum(halved_a, info[place], got, 0, kept_a, rows_a, send, 0, keep_a)
    gone = split_sum(halved_c, info[place], got, rows_a, kept_c, rows_c, send, to, keep_c)
    block = digit_block(add_digits(kept_c[rows_c:, :], got[rows_a + rows_c:, :].astype(F32)))
    keep_c[gone:, :] = block
    to += gone
    send[to:to + block.shape[0], :] = block.astype(BF16)
    to += block.shape[0]
    if to < send.shape[0]:
        send[to:, :] = jnp.zeros((send.shape[0] - to, LANES), BF16)


def last_kernel(rows_a, rows, info, got, kept_a, kept_c, sums_got, sums_kept, corr, pieces, mine):
    corr[...] = kept_a[...] + got[0:rows_a, :].astype(F32)
    pieces[...] = (kept_c[0:rows, :] + got[rows_a:rows_a + rows, :].astype(F32)).astype(BF16)
    block = digit_block(add_digits(kept_c[rows:, :], got[rows_a + rows:rows_a + kept_c.shape[0], :].astype(F32)))
    mine[0:rows, :] = pieces[...]
    mine[rows:kept_c.shape[0], :] = block.astype(BF16)
    at = kept_c.shape[0]
    count = sums_kept.shape[0] - 16
    number = count_of(sums_kept[count:, :].astype(F32), count) + count_of(sums_got[count:, :].astype(F32), count)
    square = (count, count)
    same = lax.broadcasted_iota(jnp.int32, square, 0) == lax.broadcasted_iota(jnp.int32, square, 1)
    tall = jnp.sum(jnp.where(same, jnp.broadcast_to(number, square), 0.0), 1, keepdims=True)
    total = sums_kept[0:count, :].astype(F32) + sums_got[0:count, :].astype(F32)
    means = (total / jnp.maximum(tall, 1.0)).astype(BF16)
    digits = count_rows(number, means.shape[1]).astype(BF16)
    for j in range(means.shape[1] // LANES):
        mine[at:at + count, :] = means[:, j * LANES:(j + 1) * LANES]
        mine[at + count:at + count + 16, :] = digits[:, j * LANES:(j + 1) * LANES]
        at += count + 16


def conv_out_kernel(total_frames, place, info, corr, proj, out, wide):
    rows = out.shape[0]
    flipped = jnp.transpose(corr[...])
    high = flipped.astype(BF16)
    low = (flipped - high.astype(F32)).astype(BF16)
    wide[...] = (nt(high, proj[...]) + nt(low, proj[...])) * (1.0 / total_frames)
    start = info[place]
    if rows % 8 == 0:
        out[...] = wide[pl.ds(pl.multiple_of(start, 8), rows), :]
    else:
        taken = wide[0:rows, :]
        for other in range(rows, wide.shape[0], rows):
            taken = jnp.where(start == other, wide[other:other + rows, :], taken)
        out[...] = taken


def out_kernel(total_frames, use_scale, dz, place, inner, extra, info, mine, *refs):
    parts, (out, bias, means, usage) = refs[:-4], refs[-4:]
    theirs = parts[1]
    scale = 1.0 / total_frames
    top = inner * dz
    value = add_digits(mine[top:top + extra, :].astype(F32), theirs[top:top + extra, :].astype(F32)) * scale
    for j in range(bias.shape[1] // LANES):
        bias[:, j * LANES:(j + 1) * LANES] = value[j:j + 1, :]
    bit = info[0]
    count = means.shape[1]
    numbers = []
    for ref, level in ((mine, bit), (theirs, 1 - bit)):
        at = top + extra
        blocks = []
        for j in range(dz // LANES):
            blocks.append(ref[at:at + count + 16, :])
            at += count + 16
        whole = jnp.concatenate(blocks, 1)
        means[level] = whole[0:count, :]
        numbers.append(count_of(whole[count:, :].astype(F32), count) * use_scale)
    usage[0:1, :] = jnp.where(bit == 1, numbers[1], numbers[0])
    usage[1:2, :] = jnp.where(bit == 1, numbers[0], numbers[1])
    for j, ref in enumerate(parts):
        for k in range(inner):
            start = pl.multiple_of((info[place + j] + k) * LANES, LANES)
            turned = jnp.transpose(ref[k * dz:(k + 1) * dz, :])
            out[pl.ds(start, LANES), :] = turned.astype(F32) * scale


def shifted(block, axis, distance):
    devices = range(lax.axis_size(axis))
    route = [(i - distance, i) for i in devices if i - distance in devices]
    return lax.ppermute(block, axis, route)


def swapped(block, steps):
    tm = lax.axis_size("tm")

    def partner(device):
        axis, bit = steps[(device // tm) & 1]
        return device ^ ((1 << bit) * (tm if axis == "dp" else 1))

    route = [(device, partner(device)) for device in range(lax.axis_size("dp") * tm)]
    return lax.ppermute(block, ("dp", "tm"), route)


def crossed(block, steps):
    tm = lax.axis_size("tm")

    def partner(device):
        axis, bit = steps[(device // tm) & 1]
        return device ^ tm ^ ((1 << bit) * (tm if axis == "dp" else 1))

    route = [(device, partner(device)) for device in range(lax.axis_size("dp") * tm)]
    return lax.ppermute(block, ("dp", "tm"), route)


def shards(feats, codes, conv_weight, conv_bias, proj_weight, codebooks):
    dp, tm = lax.axis_size("dp"), lax.axis_size("tm")
    rows_in, channels = feats.shape
    frames = rows_in // 2
    levels, book_size, dz = codebooks.shape
    assert levels == 2
    width = conv_weight.shape[0]
    total_frames = frames * dp * tm
    per_shard = book_size // tm
    dp_bits, tm_bits = log2(dp), log2(tm)
    owner_rows = width // (dp * tm)

    assert dp_bits >= 3 and 1 <= tm_bits <= 2
    pieces_a, pieces_c = width // LANES, channels // LANES
    under = max(dp_bits + tm_bits - log2(pieces_a), 0)
    c_bits = 2
    assert pieces_c >= 4
    whole_bits = [b for b in range(1, dp_bits) if b + tm_bits < under]
    piece_bits = [b for b in range(1, dp_bits) if b + tm_bits >= under]
    paths = [[("dp", b) for b in bits] for bits in (whole_bits + piece_bits, whole_bits[::-1] + piece_bits[::-1])]
    mixed = under == 1 and tm_bits == 2
    turned = mixed or under == 0 or under >= tm_bits
    up = [("tm", b) for b in range(tm_bits)]
    paths[0] += up[::-1]
    paths[1] += up if turned else up[::-1]
    exchanges = list(zip([("dp", 0)] + paths[0], [("dp", 0)] + paths[1]))
    sums_up = [("dp", b) for b in range(1, dp_bits)]
    sums_exchanges = list(zip(up + sums_up, up[::-1] + sums_up[::-1]))

    def piece_bit(step):
        axis, b = step
        bit = b + (tm_bits if axis == "dp" else 0)
        return bit - under if bit >= under else None

    a_split = [piece_bit(steps[0]) is not None for steps in exchanges]
    c_split = [log2(pieces_c) - 1 - k if k < c_bits else None for k in range(len(exchanges))]

    def order_of(split, count):
        used = [b for b in split if b is not None]
        return used + [b for b in reversed(range(log2(count))) if b not in used]

    orders = [order_of([piece_bit(steps[core]) for steps in exchanges], pieces_a) for core in range(2)]
    order_c = order_of(c_split, pieces_c)
    plan = [(pieces_a, orders, a_split[0]), (pieces_c, [order_c, order_c], True)]
    now_a = pieces_a // 2 if plan[0][2] else pieces_a
    now_c = pieces_c // 2

    count_bits, count_places = len(exchanges), 4
    at_start = count_bits
    at_codes = at_start + 1
    at_pieces = at_codes + tm
    at_sums = at_pieces + count_places
    at_row = at_sums + len(sums_exchanges)

    def info():
        at_dp, at_tm = lax.axis_index("dp"), lax.axis_index("tm")
        core = at_dp & 1

        def on_core(values):
            return values[0] + core * (values[1] - values[0])

        def bit_at(step):
            axis, b = step
            return ((at_dp if axis == "dp" else at_tm) >> b) & 1

        bits = [on_core([bit_at(step) for step in steps]) for steps in exchanges]
        sums_bits = [on_core([bit_at(step) for step in steps]) for steps in sums_exchanges]
        shared = [bit_at(step) for step in exchanges[1]]
        mine_c, other_c = on_core(shared), on_core(shared[::-1])
        places = [2 * core + mine_c, 2 * (1 - core) + other_c, 2 * core + 1 - mine_c, 2 * (1 - core) + 1 - other_c]
        places = [place << (log2(pieces_c) - c_bits) for place in places]
        lists = []
        for way in ([b for _, b in up], [b for _, b in up[::-1]]):
            lists.append([sum(((position >> (tm_bits - 1 - j)) & 1) << b for j, b in enumerate(way)) for position in range(tm)])
        first_bit = on_core([0, tm_bits - 1])
        lead = (at_tm >> first_bit) & 1
        quarters = [on_core([lists[0][j], lists[1][j]]) for j in range(tm // 2)]
        send_codes = [(q + ((1 - lead) << first_bit)) * per_shard for q in quarters]
        keep_codes = [(q + (lead << first_bit)) * per_shard for q in quarters]
        differ = at_tm ^ (at_tm + 1)
        ways = [sum(((differ >> b) & 1) << j for j, b in enumerate(way)) for way in (
            list(range(tm_bits)), list(reversed(range(tm_bits))))]
        row_code = jnp.where(at_tm + 1 < tm, on_core(ways), 0)
        if turned and not mixed:
            start = ((at_dp * tm + at_tm) * owner_rows) & (LANES - 1)
        else:
            start = on_core([(at_dp * tm + at_tm) * owner_rows, (at_tm >> 1) * owner_rows if mixed else (
                at_dp * tm + at_tm) * owner_rows]) & (LANES - 1)
        return bits + [start] + send_codes + keep_codes + places + sums_bits + [row_code]

    halo = shifted(call(halo_kernel, shape((2, channels), BF16), [info, feats[-2:]], flops=10 ** 11), "tm", 1)
    weight, proj, codes = conv_weight, proj_weight, codes[0]
    extra = 4 * (-(-channels // LANES // 8) * 8)
    code_rows = -(-(2 * -(-frames // dz)) // 16) * 16
    corr_rows = (now_a + now_c) * dz
    rows_b = frames + code_rows
    shared = [shape((frames, width), BF16), shape((frames, channels), BF16), shape((frames, dz), BF16),
              shape((dz, frames), BF16), shape((rows_b, dz), BF16),
              shape((corr_rows + rows_b * (dz // LANES), LANES), BF16)]
    *arrays, first, part = call(
        functools.partial(local_kernel, plan),
        shared + [shape((16, channels), F32), shape((corr_rows + 32 * (dz // LANES), LANES), F32)],
        [info, feats, weight, conv_bias[None, :], codes, codebooks, proj],
        scratch=[VMEM((channels // LANES, rows_in + 8, LANES), F32), VMEM((levels, frames, dz), BF16)],
    )
    unfold, hidden, latent_grad, flipped, own, send = call(
        functools.partial(frame_kernel, plan),
        shared,
        [info, halo, first, part, weight, proj] + arrays,
        aliases={6 + k: k for k in range(len(shared))},
    )
    got = swapped(send, exchanges[0])
    keep_a, keep_c, hidden_grad, extras, row = call(
        functools.partial(rest_kernel, plan),
        [shape((now_a * dz, LANES), F32), shape((now_c * dz, LANES), F32), shape((frames, channels), BF16),
         shape((extra, LANES), F32), shape((16, channels), BF16)],
        [info, flipped, unfold, hidden, latent_grad, proj],
        after=[send],
    )

    def halves_at(k):
        nonlocal now_a, now_c
        halves = [(now_a * dz, a_split[k]), (now_c * dz, c_split[k] is not None)]
        now_a = now_a // 2 if halves[0][1] else now_a
        now_c = now_c // 2 if halves[1][1] else now_c
        return halves, now_a * dz, now_c * dz + extra

    size = per_shard + 16
    sums_rows = size * (tm // 2)
    got_core = got

    def own_sums(first, after):
        return call(
            functools.partial(own_sums_kernel, frames, at_codes + first, per_shard),
            shape((sums_rows, dz), F32),
            [info, own],
            after=after)

    def both_sums(first, base, dtype, after):
        return call(
            functools.partial(sums_kernel, corr_rows, frames, at_codes + first, per_shard),
            shape((sums_rows, dz), dtype),
            [info, got_core, base, row],
            after=after)

    base = own_sums(0, [extras])
    halves, rows_a, rows_c = halves_at(1)
    send, keep_a, keep_c = call(
        functools.partial(first_step_kernel, halves, 1),
        [shape((rows_a + rows_c, LANES), BF16), shape((rows_a, LANES), F32), shape((rows_c, LANES), F32)],
        [info, got, keep_a, keep_c, extras],
        after=[base])
    sums_send = both_sums(0, base, BF16, [send])
    sums_keep = both_sums(tm // 2, own_sums(tm // 2, [sums_send]), F32, [])
    sums_got = swapped(sums_send, sums_exchanges[0])
    got = swapped(send, exchanges[1])
    known = row
    ordered = [sums_keep]
    for k in range(2, len(exchanges)):
        halves, rows_a, rows_c = halves_at(k)
        spare = 16 * (k == len(exchanges) - 1)
        send, keep_a, keep_c = call(
            functools.partial(step_kernel, halves, k, mixed and k == dp_bits),
            [shape((rows_a + rows_c + spare, LANES), BF16), shape((rows_a, LANES), F32), shape((rows_c, LANES), F32)],
            [info, got, keep_a, keep_c],
            after=ordered)
        got = swapped(send, exchanges[k])
        halved = sums_exchanges[k - 1][0][0] == "tm"
        sums_rows = sums_rows // 2 if halved else sums_rows
        row_step = k - 2 if k - 2 < tm_bits else None
        outs = call(
            functools.partial(sums_step_kernel, halved, at_sums + k - 1, row_step, (per_shard, at_row)),
            [shape((sums_rows, dz), BF16), shape((sums_rows, dz), F32)]
            + [shape((16, channels), BF16)] * (row_step is not None),
            [info, sums_got, sums_keep] + [known] * (row_step is not None),
            after=[send])
        sums_send, sums_keep = outs[:2]
        known = outs[2] if row_step is not None else known
        sums_got = swapped(sums_send, sums_exchanges[k - 1])
        ordered = [sums_send]
    assert now_a == 1 and sums_rows == size
    feat_grad, last = call(
        feat_kernel,
        shape((rows_in, channels), BF16),
        [info, hidden_grad, known, weight],
        after=[sums_send],
        token=True,
        scratch=[VMEM((frames + 8, channels), F32), VMEM((channels // LANES, rows_in, LANES), F32)],
    )

    corr, piece, mine = call(
        functools.partial(last_kernel, rows_a, rows_c - extra),
        [shape((rows_a, LANES), F32), shape((rows_c - extra, LANES), BF16),
         shape((rows_c + size * (dz // LANES), LANES), BF16)],
        [info, got, keep_a, keep_c, sums_got, sums_keep],
        after=[last])
    parts = [piece, swapped(mine, exchanges[0]), swapped(piece, exchanges[1]), crossed(piece, exchanges[1])]
    conv_grad, last = call(
        functools.partial(conv_out_kernel, total_frames, at_start),
        shape((owner_rows, channels), F32),
        [info, corr, proj],
        after=[piece],
        token=True,
        scratch=[VMEM((LANES, channels), F32)],
    )
    proj_grad, bias_grad, code_means, code_usage = call(
        functools.partial(out_kernel, total_frames, book_size / total_frames, dz, at_pieces, now_c, extra),
        [shape((channels, dz), F32), shape((1, channels), F32), shape((levels, per_shard, dz), BF16),
         shape((levels, per_shard), F32)],
        [info, mine] + parts,
        after=[last],
    )
    return feat_grad, conv_grad, bias_grad[0], proj_grad, code_means, code_usage


def solution(mesh):
    placed = (P(("dp", "tm"), None), P("dp", None, "tm"), P(), P(), P(), P())
    return jax.shard_map(
        shards,
        mesh=mesh,
        in_specs=placed,
        out_specs=(
            P(("dp", "tm"), None),
            P(("dp", "tm"), None),
            P(),
            P(),
            P(None, "tm", None),
            P(None, "tm"),
        ),
        check_vma=False,
    )
```

```python
import functools

import jax
import jax.numpy as jnp
from jax import lax
from jax.experimental import pallas as pl
from jax.experimental.pallas import tpu as pltpu
from jax.sharding import PartitionSpec as P

BF16 = jnp.bfloat16
F32 = jnp.float32
LANES = 128
VMEM_LIMIT = 16 * 1024 * 1024


def log2(value):
    assert value & (value - 1) == 0
    return value.bit_length() - 1


def nn(a, b):
    return lax.dot_general(a, b, (((1,), (0,)), ((), ())), preferred_element_type=F32)


def nt(a, b):
    return lax.dot_general(a, b, (((1,), (1,)), ((), ())), preferred_element_type=F32)


VMEM = pltpu.VMEM


def call(body, out_shape, args, after=(), scratch=(), aliases=None, token=False, flops=0, fuse=None):
    info, args = args[0], args[1:]
    count = len(args)
    many = isinstance(out_shape, (list, tuple))
    shapes = list(out_shape) if many else [out_shape]

    def kernel(*refs):
        ends = count + len(after)
        if token:
            refs[ends + len(shapes)][...] = jnp.zeros((8, LANES), F32)
            refs = refs[:ends + len(shapes)] + refs[ends + len(shapes) + 1:]
        body(info(), *refs[:count], *refs[ends:])

    specs = [pl.BlockSpec(memory_space=VMEM)] * count + [pl.BlockSpec(memory_space=pl.ANY)] * len(after)
    shown = shapes + [shape((8, LANES), F32)] * token
    outs = pl.pallas_call(
        kernel,
        out_shape=shown,
        in_specs=specs,
        out_specs=[pl.BlockSpec(memory_space=VMEM)] * len(shown),
        scratch_shapes=list(scratch),
        input_output_aliases={at - 1: out for at, out in (aliases or {}).items()},
        compiler_params=pltpu.CompilerParams(vmem_limit_bytes=VMEM_LIMIT, allow_input_fusion=fuse),
        cost_estimate=pl.CostEstimate(flops=flops, bytes_accessed=0, transcendentals=0),
    )(*args, *after)
    return outs if len(shown) > 1 else outs[0]


def shape(dims, dtype):
    return jax.ShapeDtypeStruct(dims, dtype)


def digits_of(value):
    high = value.astype(BF16).astype(F32)
    rest = value - high
    middle = rest.astype(BF16).astype(F32)
    low = (rest - middle).astype(BF16).astype(F32)
    return high, middle, low


def one_hot(codes, axis_codes, first, count):
    frames = codes.shape[1 - axis_codes]
    dims = (count, frames) if axis_codes == 0 else (frames, count)
    places = lax.broadcasted_iota(jnp.int32, dims, axis_codes) + first
    return jnp.where(codes == places, 1.0, 0.0).astype(BF16)


def halo_kernel(info, rows, out):
    out[...] = rows[...]


def walk(orders, halved, count):
    start = 1 if halved else 0
    shown = count // 2 if halved else count
    bits = log2(shown)
    step = 2 if shown > 1 and all(order[-1] == 0 for order in orders) else 1
    for position in range(0, shown, step):
        yield position, [
            sum(((position >> (bits - 1 - k)) & 1) << bit for k, bit in enumerate(order[start:])) for order in orders
        ], step


def correlate(flipped, sources, plan, core, bit, out):
    dz = flipped.shape[0]
    at = 0
    for source, (count, orders, halved) in zip(sources, plan):
        for position, pieces, step in walk(orders, halved, count):
            column = pieces[0] + core * (pieces[1] - pieces[0])
            if halved:
                column = column + (bit << orders[0][0])
            column = pl.multiple_of(column * LANES, LANES)
            product = nn(flipped, source[:, pl.ds(column, step * LANES)])
            for j in range(step):
                top = (at + position + j) * dz
                out[top:top + dz, :] = product[:, j * LANES:(j + 1) * LANES].astype(out.dtype)
        at += count // 2 if halved else count
    return at * dz


def code_digits(codes, dz, rows):
    parts = []
    for part in (codes >> 8, codes & 255):
        for start in range(0, codes.shape[1], dz):
            piece = part[:, start:start + dz].astype(F32)
            if piece.shape[1] < dz:
                piece = jnp.concatenate([piece, jnp.zeros((1, dz - piece.shape[1]), F32)], 1)
            parts.append(piece)
    parts.append(jnp.zeros((rows - len(parts), dz), F32))
    return jnp.concatenate(parts, 0).astype(BF16)


def codes_of(block, frames):
    dz = block.shape[1]
    per = -(-frames // dz)
    digits = block[...].astype(F32)
    parts = [jnp.concatenate([digits[k * per + j:k * per + j + 1, :] for j in range(per)], 1)[:, :frames]
             for k in range(2)]
    return (parts[0] * 256.0 + parts[1]).astype(jnp.int32)


def residuals(hidden, proj, chosen):
    latent = nn(hidden, proj)
    once = latent - chosen[0].astype(F32)
    total = once + (once - chosen[1].astype(F32))
    return latent, once, total.astype(BF16)


def put_columns(out, at, rows, block):
    for j in range(block.shape[1] // LANES):
        out[at + j * rows:at + j * rows + block.shape[0], :] = block[:, j * LANES:(j + 1) * LANES]


def local_kernel(plan, info, feats, weight, bias, codes, books, proj,
                 unfold, hidden, latent_grad, flipped, own, send, first, part, wide, chosen):
    rows, channels = feats.shape
    frames = rows // 2
    dz = proj.shape[1]
    for j in range(channels // LANES):
        wide[j, 0:8, :] = jnp.zeros((8, LANES), F32)
        wide[j, 8:, :] = feats[:, j * LANES:(j + 1) * LANES].astype(F32)
        for tap in range(4):
            start = tap * channels + j * LANES
            unfold[:, start:start + LANES] = wide[j, pl.ds(6 + tap, frames, stride=2), :].astype(BF16)
    conv = nn(unfold[...], weight[...]) + bias[...]
    first[...] = conv[0:16, :]
    hidden[...] = conv.astype(BF16)
    levels = books.shape[0]
    padded = jnp.concatenate([codes[...].astype(F32), jnp.zeros((8 - levels, frames), F32)], 0)
    tall = jnp.transpose(padded).astype(jnp.int32)
    for level in range(levels):
        matches = one_hot(tall[:, level:level + 1], 1, 0, books.shape[1])
        chosen[level] = nn(matches, books[level]).astype(BF16)
    latent, once, grad = residuals(hidden[...], proj[...], chosen)
    latent_grad[...] = grad
    row = lax.broadcasted_iota(jnp.int32, grad.shape, 0)
    flipped[...] = jnp.transpose(jnp.where(row == 0, 0.0, grad.astype(F32))).astype(BF16)
    bit = info[0]
    at = correlate(flipped[...], (unfold, hidden), plan, 1 - bit, 1 - bit, part)
    rows_b = own.shape[0]
    code_rows = rows_b - frames
    digits = [code_digits(codes[level:level + 1, :], dz, code_rows) for level in range(2)]
    own[0:frames, :] = jnp.where(bit == 1, once, latent).astype(BF16)
    own[frames:, :] = jnp.where(bit == 1, digits[1], digits[0])
    put_columns(send, at, rows_b, jnp.where(bit == 1, latent, once).astype(BF16))
    put_columns(send, at + frames, rows_b, jnp.where(bit == 1, digits[0], digits[1]))
    for level in range(levels):
        part[at + level * 16 * (dz // LANES):at + (level + 1) * 16 * (dz // LANES), :] = jnp.concatenate(
            [chosen[level, 0:16, j * LANES:(j + 1) * LANES].astype(F32) for j in range(dz // LANES)], 0)


def frame_kernel(plan, info, halo, first, part, weight, proj, unfold_in, hidden_in, grad_in, flipped_in, own_in, send_in,
                 unfold, hidden, latent_grad, flipped, own, send):
    width = unfold.shape[1]
    half = width // 2
    dz = proj.shape[1]
    row = lax.broadcasted_iota(jnp.int32, (16, half), 0)
    left = jnp.concatenate([halo[0:1, :], halo[1:2, :]], 1).astype(F32)
    head = jnp.where(row == 0, jnp.broadcast_to(left, (16, half)), 0.0)
    unfold[0:16, 0:half] = (unfold_in[0:16, 0:half].astype(F32) + head).astype(BF16)
    fix = nn(head.astype(BF16), weight[0:half, :])
    hidden[0:16, :] = (first[...] + fix).astype(BF16)
    top = hidden[0:16, :]
    pieces = part.shape[0] - 32 * (dz // LANES)
    chosen = []
    for level in range(2):
        at = pieces + level * 16 * (dz // LANES)
        chosen.append(jnp.concatenate([part[at + j * 16:at + (j + 1) * 16, :] for j in range(dz // LANES)], 1))
    latent, once, grad = residuals(top, proj[...], chosen)
    latent_grad[0:16, :] = grad
    flipped[:, 0:LANES] = jnp.transpose(latent_grad[0:LANES, :].astype(F32)).astype(BF16)
    column = flipped[:, 0:LANES].astype(F32)[:, 0:1]
    bit = info[0]
    at = 0
    for source, (count, orders, halved) in zip((unfold, hidden), plan):
        rows = source[0:16, :].astype(F32)[0:1, :]
        for position, places, step in walk(orders, halved, count):
            for j in range(step):
                offsets = [places[0] + j, places[1] + j]
                low = [offset for offset in offsets]
                high = [offset + (1 << orders[0][0] if halved else 0) for offset in offsets]
                picked = [rows[:, k * LANES:(k + 1) * LANES] for k in low + high]
                piece = jnp.where(bit == 1, picked[0], picked[3]) if halved else jnp.where(bit == 1, picked[0], picked[1])
                begin = (at + position + j) * dz
                send[begin:begin + dz, :] = (part[begin:begin + dz, :] + column * piece).astype(BF16)
        at += count // 2 if halved else count
    rows_b = own.shape[0]
    own[0:16, :] = jnp.where(bit == 1, once, latent).astype(BF16)
    put_columns(send, at * dz, rows_b, jnp.where(bit == 1, latent, once).astype(BF16))


def rest_kernel(plan, info, flipped, unfold, hidden, latent_grad, proj, keep_a, keep_c, hidden_grad, extras, row):
    bit = info[0]
    correlate(flipped[...], (unfold,), plan[:1], bit, bit, keep_a)
    correlate(flipped[...], (hidden,), plan[1:], bit, bit, keep_c)
    back = nt(latent_grad[...], proj[...]).astype(BF16)
    hidden_grad[...] = back
    row[...] = back[0:16, :]
    stride = extras.shape[0] // 4
    extras[...] = jnp.zeros(extras.shape, F32)
    sums = jnp.sum(back.astype(F32), 0, keepdims=True)
    for digit, part in enumerate(digits_of(sums)):
        for j in range(sums.shape[1] // LANES):
            extras[digit * stride + j:digit * stride + j + 1, :] = part[:, j * LANES:(j + 1) * LANES]


def split_sum(halved, bit, got, at, kept, rows, send, to, keep):
    if halved:
        half = rows // 2
        away = pl.multiple_of((1 - bit) * half, 16)
        home = pl.multiple_of(bit * half, 16)
        send[to:to + half, :] = (kept[pl.ds(away, half), :] + got[pl.ds(at + away, half), :].astype(F32)).astype(BF16)
        keep[0:half, :] = kept[pl.ds(home, half), :] + got[pl.ds(at + home, half), :].astype(F32)
        return half
    total = (kept[0:rows, :] + got[at:at + rows, :].astype(F32)).astype(BF16)
    send[to:to + rows, :] = total
    keep[0:rows, :] = total.astype(F32)
    return rows


def add_digits(mine, theirs):
    stride = mine.shape[0] // 4
    return ((mine[0:stride] + mine[stride:2 * stride]) + mine[2 * stride:3 * stride]) + (
        (theirs[0:stride] + theirs[stride:2 * stride]) + theirs[2 * stride:3 * stride])


def digit_block(value):
    return jnp.concatenate(list(digits_of(value)) + [jnp.zeros_like(value)], 0)


def first_step_kernel(halves, place, info, got, kept_a, kept_c, extras, send, keep_a, keep_c):
    (rows_a, halved_a), (rows_c, halved_c) = halves
    to = split_sum(halved_a, info[place], got, 0, kept_a, rows_a, send, 0, keep_a)
    gone = split_sum(halved_c, info[place], got, rows_a, kept_c, rows_c, send, to, keep_c)
    send[to + gone:, :] = extras[...].astype(BF16)
    keep_c[gone:, :] = extras[...]


def feat_kernel(info, grad, after, weight, out, wide, inter):
    frames, channels = grad.shape
    half = weight.shape[0] // 2
    wide[0:frames, :] = grad[...].astype(F32)
    wide[frames:, :] = jnp.broadcast_to(after[0:1, :].astype(F32), (8, channels))
    ahead = wide[pl.ds(1, frames), :].astype(BF16)
    for parity in range(2):
        rows = pl.ds(parity * (half // 2), half // 2)
        rows_after = pl.ds(half + parity * (half // 2), half // 2)
        both = nt(ahead, weight[rows, :]) + nt(grad[...], weight[rows_after, :])
        for j in range(channels // LANES):
            inter[j, pl.ds(parity, frames, stride=2), :] = both[:, j * LANES:(j + 1) * LANES]
    for j in range(channels // LANES):
        out[:, j * LANES:(j + 1) * LANES] = inter[j].astype(BF16)


def own_sums_kernel(frames, place, count, info, own, out):
    codes = codes_of(own[frames:, :], frames)
    ones = jnp.ones((8, frames), BF16)
    size = count + 16
    for top in range(0, out.shape[0], size):
        matches = one_hot(codes, 0, info[place], count)
        out[top:top + count, :] = nn(matches, own[0:frames, :])
        out[top + count:top + count + 8, 0:count] = nt(ones, matches)
        place += 1


def sums_kernel(first, frames, place, count, info, got, base, row, out):
    dz = base.shape[1]
    rows = (got.shape[0] - first) // (dz // LANES)
    theirs = jnp.concatenate([got[first + j * rows:first + (j + 1) * rows, :] for j in range(dz // LANES)], 1)
    codes = codes_of(theirs[frames:, :], frames)
    ones = jnp.ones((8, frames), BF16)
    size = count + 16
    riding = [row[...].astype(F32)[0:1, :]]
    for top in range(0, out.shape[0], size):
        matches = one_hot(codes, 0, info[place], count)
        total = base[top:top + count, :] + nn(matches, theirs[0:frames, :])
        counts = base[top + count:top + count + 8, 0:count] + nt(ones, matches)
        out[top:top + count, :] = total.astype(out.dtype)
        out[top + count:top + size, :] = count_rows(counts[0:1], dz, riding).astype(out.dtype)
        place += 1


def count_rows(count, width, riding=()):
    high = jnp.floor(count * (1.0 / 65536.0))
    rest = count - high * 65536.0
    middle = jnp.floor(rest * (1.0 / 256.0))
    low = rest - middle * 256.0
    block = jnp.concatenate([high, middle, low], 0)
    if count.shape[1] < width:
        block = jnp.concatenate([block, jnp.zeros((3, width - count.shape[1]), F32)], 1)
    parts = [block]
    for row in riding:
        parts += [row[:, at:at + width] for at in range(0, row.shape[1], width)]
    left = 16 - sum(part.shape[0] for part in parts)
    return jnp.concatenate(parts + [jnp.zeros((left, width), F32)] * (left > 0), 0)


def riding_row(block, index, parts):
    return jnp.concatenate([block[3 + index * parts + j:4 + index * parts + j, :] for j in range(parts)], 1)


def count_of(block, own):
    return (block[0:1] * 65536.0 + block[1:2] * 256.0 + block[2:3])[:, :own]


def sums_step_kernel(halved, place, row_step, row_place, info, got, kept, *refs):
    riding = ()
    if row_step is not None:
        known, refs = refs[0][...].astype(F32), refs[1:]
        after, refs = refs[-1], refs[:-1]
        parts = known.shape[1] // got.shape[1]
        block = got[row_place[0]:row_place[0] + 16, :].astype(F32)
        rows = [known[j:j + 1, :] for j in range(1 << row_step)]
        rows += [riding_row(block, j, parts) for j in range(1 << row_step)]
        if halved:
            riding = rows
            total = rows + [jnp.zeros((16 - len(rows), known.shape[1]), F32)]
            after[...] = jnp.concatenate(total, 0).astype(BF16)
        else:
            wide = jnp.zeros(after.shape, F32)
            for j in range(1, len(rows)):
                wide = jnp.where(info[row_place[1]] == j, jnp.broadcast_to(rows[j], after.shape), wide)
            after[...] = wide.astype(BF16)
    send, keep = refs
    dz = got.shape[1]
    bit = info[place]
    half = kept.shape[0] // 2 if halved else 0
    outs = [(send, (1 - bit) * half), (keep, bit * half)] if halved else [(send, 0)]
    count = row_place[0]
    size = count + 16
    for out, start in outs:
        for top in range(0, keep.shape[0], size):
            here = top + pl.multiple_of(start, 16) if halved else top
            sums = pl.ds(here, count)
            tail = pl.ds(here + count, 16)
            value = kept[sums, :].astype(F32) + got[sums, :].astype(F32)
            number = count_of(kept[tail, :].astype(F32), count) + count_of(got[tail, :].astype(F32), count)
            out[top:top + count, :] = value.astype(out.dtype)
            out[top + count:top + size, :] = count_rows(number, dz, riding).astype(out.dtype)
    if not halved:
        keep[...] = send[0:keep.shape[0], :].astype(F32)


def swap_halves(first, second, core):
    half = LANES // 2
    left = lax.broadcasted_iota(jnp.int32, first.shape, 1) < half
    turned_first, turned_second = pltpu.roll(first, half, 1), pltpu.roll(second, half, 1)
    swapped_first = jnp.where(left, first, turned_second)
    swapped_second = jnp.where(left, turned_first, second)
    return jnp.where(core == 1, swapped_first, first), jnp.where(core == 1, swapped_second, second)


def step_kernel(halves, place, mixed, info, got, kept_a, kept_c, send, keep_a, keep_c):
    (rows_a, halved_a), (rows_c, halved_c) = halves
    if mixed:
        to = rows_a // 2
        total = kept_a[0:rows_a, :] + got[0:rows_a, :].astype(F32)
        first, second = swap_halves(total[0:to, :], total[to:, :], info[0])
        low = info[place] == 0
        send[0:to, :] = jnp.where(low, second, first).astype(BF16)
        keep_a[...] = jnp.where(low, first, second)
    else:
        to = split_sum(halved_a, info[place], got, 0, kept_a, rows_a, send, 0, keep_a)
    gone = split_sum(halved_c, info[place], got, rows_a, kept_c, rows_c, send, to, keep_c)
    block = digit_block(add_digits(kept_c[rows_c:, :], got[rows_a + rows_c:, :].astype(F32)))
    keep_c[gone:, :] = block
    to += gone
    send[to:to + block.shape[0], :] = block.astype(BF16)
    to += block.shape[0]
    if to < send.shape[0]:
        send[to:, :] = jnp.zeros((send.shape[0] - to, LANES), BF16)


def last_kernel(rows_a, rows, info, got, kept_a, kept_c, sums_got, sums_kept, corr, pieces, mine):
    corr[...] = kept_a[...] + got[0:rows_a, :].astype(F32)
    pieces[...] = (kept_c[0:rows, :] + got[rows_a:rows_a + rows, :].astype(F32)).astype(BF16)
    block = digit_block(add_digits(kept_c[rows:, :], got[rows_a + rows:rows_a + kept_c.shape[0], :].astype(F32)))
    mine[0:rows, :] = pieces[...]
    mine[rows:kept_c.shape[0], :] = block.astype(BF16)
    at = kept_c.shape[0]
    count = sums_kept.shape[0] - 16
    number = count_of(sums_kept[count:, :].astype(F32), count) + count_of(sums_got[count:, :].astype(F32), count)
    square = (count, count)
    same = lax.broadcasted_iota(jnp.int32, square, 0) == lax.broadcasted_iota(jnp.int32, square, 1)
    tall = jnp.sum(jnp.where(same, jnp.broadcast_to(number, square), 0.0), 1, keepdims=True)
    total = sums_kept[0:count, :].astype(F32) + sums_got[0:count, :].astype(F32)
    means = (total / jnp.maximum(tall, 1.0)).astype(BF16)
    digits = count_rows(number, means.shape[1]).astype(BF16)
    for j in range(means.shape[1] // LANES):
        mine[at:at + count, :] = means[:, j * LANES:(j + 1) * LANES]
        mine[at + count:at + count + 16, :] = digits[:, j * LANES:(j + 1) * LANES]
        at += count + 16


def conv_out_kernel(total_frames, place, info, corr, proj, out, wide):
    rows = out.shape[0]
    flipped = jnp.transpose(corr[...])
    high = flipped.astype(BF16)
    low = (flipped - high.astype(F32)).astype(BF16)
    wide[...] = (nt(high, proj[...]) + nt(low, proj[...])) * (1.0 / total_frames)
    start = info[place]
    if rows % 8 == 0:
        out[...] = wide[pl.ds(pl.multiple_of(start, 8), rows), :]
    else:
        taken = wide[0:rows, :]
        for other in range(rows, wide.shape[0], rows):
            taken = jnp.where(start == other, wide[other:other + rows, :], taken)
        out[...] = taken


def out_kernel(total_frames, use_scale, dz, place, inner, extra, info, mine, *refs):
    parts, (out, bias, means, usage) = refs[:-4], refs[-4:]
    theirs = parts[1]
    scale = 1.0 / total_frames
    top = inner * dz
    value = add_digits(mine[top:top + extra, :].astype(F32), theirs[top:top + extra, :].astype(F32)) * scale
    for j in range(bias.shape[1] // LANES):
        bias[:, j * LANES:(j + 1) * LANES] = value[j:j + 1, :]
    bit = info[0]
    count = means.shape[1]
    numbers = []
    for ref, level in ((mine, bit), (theirs, 1 - bit)):
        at = top + extra
        blocks = []
        for j in range(dz // LANES):
            blocks.append(ref[at:at + count + 16, :])
            at += count + 16
        whole = jnp.concatenate(blocks, 1)
        means[level] = whole[0:count, :]
        numbers.append(count_of(whole[count:, :].astype(F32), count) * use_scale)
    usage[0:1, :] = jnp.where(bit == 1, numbers[1], numbers[0])
    usage[1:2, :] = jnp.where(bit == 1, numbers[0], numbers[1])
    for j, ref in enumerate(parts):
        for k in range(inner):
            start = pl.multiple_of((info[place + j] + k) * LANES, LANES)
            turned = jnp.transpose(ref[k * dz:(k + 1) * dz, :])
            out[pl.ds(start, LANES), :] = turned.astype(F32) * scale


def shifted(block, axis, distance):
    devices = range(lax.axis_size(axis))
    route = [(i - distance, i) for i in devices if i - distance in devices]
    return lax.ppermute(block, axis, route)


def swapped(block, steps):
    tm = lax.axis_size("tm")

    def partner(device):
        axis, bit = steps[(device // tm) & 1]
        return device ^ ((1 << bit) * (tm if axis == "dp" else 1))

    route = [(device, partner(device)) for device in range(lax.axis_size("dp") * tm)]
    return lax.ppermute(block, ("dp", "tm"), route)


def crossed(block, steps):
    tm = lax.axis_size("tm")

    def partner(device):
        axis, bit = steps[(device // tm) & 1]
        return device ^ tm ^ ((1 << bit) * (tm if axis == "dp" else 1))

    route = [(device, partner(device)) for device in range(lax.axis_size("dp") * tm)]
    return lax.ppermute(block, ("dp", "tm"), route)


def shards(feats, codes, conv_weight, conv_bias, proj_weight, codebooks):
    dp, tm = lax.axis_size("dp"), lax.axis_size("tm")
    rows_in, channels = feats.shape
    frames = rows_in // 2
    levels, book_size, dz = codebooks.shape
    assert levels == 2
    width = conv_weight.shape[0]
    total_frames = frames * dp * tm
    per_shard = book_size // tm
    dp_bits, tm_bits = log2(dp), log2(tm)
    owner_rows = width // (dp * tm)

    assert dp_bits >= 3 and 1 <= tm_bits <= 2
    pieces_a, pieces_c = width // LANES, channels // LANES
    under = max(dp_bits + tm_bits - log2(pieces_a), 0)
    c_bits = 2
    assert pieces_c >= 4
    whole_bits = [b for b in range(1, dp_bits) if b + tm_bits < under]
    piece_bits = [b for b in range(1, dp_bits) if b + tm_bits >= under]
    paths = [[("dp", b) for b in bits] for bits in (whole_bits + piece_bits, whole_bits[::-1] + piece_bits[::-1])]
    mixed = under == 1 and tm_bits == 2
    turned = mixed or under == 0 or under >= tm_bits
    up = [("tm", b) for b in range(tm_bits)]
    paths[0] += up[::-1]
    paths[1] += up if turned else up[::-1]
    exchanges = list(zip([("dp", 0)] + paths[0], [("dp", 0)] + paths[1]))
    sums_up = [("dp", b) for b in range(1, dp_bits)]
    sums_exchanges = list(zip(up + sums_up, up[::-1] + sums_up[::-1]))

    def piece_bit(step):
        axis, b = step
        bit = b + (tm_bits if axis == "dp" else 0)
        return bit - under if bit >= under else None

    a_split = [piece_bit(steps[0]) is not None for steps in exchanges]
    c_split = [log2(pieces_c) - 1 - k if k < c_bits else None for k in range(len(exchanges))]

    def order_of(split, count):
        used = [b for b in split if b is not None]
        return used + [b for b in reversed(range(log2(count))) if b not in used]

    orders = [order_of([piece_bit(steps[core]) for steps in exchanges], pieces_a) for core in range(2)]
    order_c = order_of(c_split, pieces_c)
    plan = [(pieces_a, orders, a_split[0]), (pieces_c, [order_c, order_c], True)]
    now_a = pieces_a // 2 if plan[0][2] else pieces_a
    now_c = pieces_c // 2

    count_bits, count_places = len(exchanges), 4
    at_start = count_bits
    at_codes = at_start + 1
    at_pieces = at_codes + tm
    at_sums = at_pieces + count_places
    at_row = at_sums + len(sums_exchanges)

    def info():
        at_dp, at_tm = lax.axis_index("dp"), lax.axis_index("tm")
        core = at_dp & 1

        def on_core(values):
            return values[0] + core * (values[1] - values[0])

        def bit_at(step):
            axis, b = step
            return ((at_dp if axis == "dp" else at_tm) >> b) & 1

        bits = [on_core([bit_at(step) for step in steps]) for steps in exchanges]
        sums_bits = [on_core([bit_at(step) for step in steps]) for steps in sums_exchanges]
        shared = [bit_at(step) for step in exchanges[1]]
        mine_c, other_c = on_core(shared), on_core(shared[::-1])
        places = [2 * core + mine_c, 2 * (1 - core) + other_c, 2 * core + 1 - mine_c, 2 * (1 - core) + 1 - other_c]
        places = [place << (log2(pieces_c) - c_bits) for place in places]
        lists = []
        for way in ([b for _, b in up], [b for _, b in up[::-1]]):
            lists.append([sum(((position >> (tm_bits - 1 - j)) & 1) << b for j, b in enumerate(way)) for position in range(tm)])
        first_bit = on_core([0, tm_bits - 1])
        lead = (at_tm >> first_bit) & 1
        quarters = [on_core([lists[0][j], lists[1][j]]) for j in range(tm // 2)]
        send_codes = [(q + ((1 - lead) << first_bit)) * per_shard for q in quarters]
        keep_codes = [(q + (lead << first_bit)) * per_shard for q in quarters]
        differ = at_tm ^ (at_tm + 1)
        ways = [sum(((differ >> b) & 1) << j for j, b in enumerate(way)) for way in (
            list(range(tm_bits)), list(reversed(range(tm_bits))))]
        row_code = jnp.where(at_tm + 1 < tm, on_core(ways), 0)
        if turned and not mixed:
            start = ((at_dp * tm + at_tm) * owner_rows) & (LANES - 1)
        else:
            start = on_core([(at_dp * tm + at_tm) * owner_rows, (at_tm >> 1) * owner_rows if mixed else (
                at_dp * tm + at_tm) * owner_rows]) & (LANES - 1)
        return bits + [start] + send_codes + keep_codes + places + sums_bits + [row_code]

    halo = shifted(call(halo_kernel, shape((2, channels), BF16), [info, feats[-2:]], flops=10 ** 11, fuse=[True]), "tm", 1)
    weight, proj, codes = conv_weight, proj_weight, codes[0]
    extra = 4 * (-(-channels // LANES // 8) * 8)
    code_rows = -(-(2 * -(-frames // dz)) // 16) * 16
    corr_rows = (now_a + now_c) * dz
    rows_b = frames + code_rows
    shared = [shape((frames, width), BF16), shape((frames, channels), BF16), shape((frames, dz), BF16),
              shape((dz, frames), BF16), shape((rows_b, dz), BF16),
              shape((corr_rows + rows_b * (dz // LANES), LANES), BF16)]
    *arrays, first, part = call(
        functools.partial(local_kernel, plan),
        shared + [shape((16, channels), F32), shape((corr_rows + 32 * (dz // LANES), LANES), F32)],
        [info, feats, weight, conv_bias[None, :], codes, codebooks, proj],
        scratch=[VMEM((channels // LANES, rows_in + 8, LANES), F32), VMEM((levels, frames, dz), BF16)],
    )
    unfold, hidden, latent_grad, flipped, own, send = call(
        functools.partial(frame_kernel, plan),
        shared,
        [info, halo, first, part, weight, proj] + arrays,
        aliases={6 + k: k for k in range(len(shared))},
    )
    got = swapped(send, exchanges[0])
    keep_a, keep_c, hidden_grad, extras, row = call(
        functools.partial(rest_kernel, plan),
        [shape((now_a * dz, LANES), F32), shape((now_c * dz, LANES), F32), shape((frames, channels), BF16),
         shape((extra, LANES), F32), shape((16, channels), BF16)],
        [info, flipped, unfold, hidden, latent_grad, proj],
        after=[send],
    )

    def halves_at(k):
        nonlocal now_a, now_c
        halves = [(now_a * dz, a_split[k]), (now_c * dz, c_split[k] is not None)]
        now_a = now_a // 2 if halves[0][1] else now_a
        now_c = now_c // 2 if halves[1][1] else now_c
        return halves, now_a * dz, now_c * dz + extra

    size = per_shard + 16
    sums_rows = size * (tm // 2)
    got_core = got

    def own_sums(first, after):
        return call(
            functools.partial(own_sums_kernel, frames, at_codes + first, per_shard),
            shape((sums_rows, dz), F32),
            [info, own],
            after=after)

    def both_sums(first, base, dtype, after):
        return call(
            functools.partial(sums_kernel, corr_rows, frames, at_codes + first, per_shard),
            shape((sums_rows, dz), dtype),
            [info, got_core, base, row],
            after=after)

    base = own_sums(0, [extras])
    halves, rows_a, rows_c = halves_at(1)
    send, keep_a, keep_c = call(
        functools.partial(first_step_kernel, halves, 1),
        [shape((rows_a + rows_c, LANES), BF16), shape((rows_a, LANES), F32), shape((rows_c, LANES), F32)],
        [info, got, keep_a, keep_c, extras],
        after=[base])
    sums_send = both_sums(0, base, BF16, [send])
    sums_keep = both_sums(tm // 2, own_sums(tm // 2, [sums_send]), F32, [])
    sums_got = swapped(sums_send, sums_exchanges[0])
    got = swapped(send, exchanges[1])
    known = row
    ordered = [sums_keep]
    for k in range(2, len(exchanges)):
        halves, rows_a, rows_c = halves_at(k)
        spare = 16 * (k == len(exchanges) - 1)
        send, keep_a, keep_c = call(
            functools.partial(step_kernel, halves, k, mixed and k == dp_bits),
            [shape((rows_a + rows_c + spare, LANES), BF16), shape((rows_a, LANES), F32), shape((rows_c, LANES), F32)],
            [info, got, keep_a, keep_c],
            after=ordered)
        got = swapped(send, exchanges[k])
        halved = sums_exchanges[k - 1][0][0] == "tm"
        sums_rows = sums_rows // 2 if halved else sums_rows
        row_step = k - 2 if k - 2 < tm_bits else None
        outs = call(
            functools.partial(sums_step_kernel, halved, at_sums + k - 1, row_step, (per_shard, at_row)),
            [shape((sums_rows, dz), BF16), shape((sums_rows, dz), F32)]
            + [shape((16, channels), BF16)] * (row_step is not None),
            [info, sums_got, sums_keep] + [known] * (row_step is not None),
            after=[send])
        sums_send, sums_keep = outs[:2]
        known = outs[2] if row_step is not None else known
        sums_got = swapped(sums_send, sums_exchanges[k - 1])
        ordered = [sums_send]
    assert now_a == 1 and sums_rows == size
    feat_grad, last = call(
        feat_kernel,
        shape((rows_in, channels), BF16),
        [info, hidden_grad, known, weight],
        after=[sums_send],
        token=True,
        scratch=[VMEM((frames + 8, channels), F32), VMEM((channels // LANES, rows_in, LANES), F32)],
    )

    corr, piece, mine = call(
        functools.partial(last_kernel, rows_a, rows_c - extra),
        [shape((rows_a, LANES), F32), shape((rows_c - extra, LANES), BF16),
         shape((rows_c + size * (dz // LANES), LANES), BF16)],
        [info, got, keep_a, keep_c, sums_got, sums_keep],
        after=[last])
    parts = [piece, swapped(mine, exchanges[0]), swapped(piece, exchanges[1]), crossed(piece, exchanges[1])]
    conv_grad, last = call(
        functools.partial(conv_out_kernel, total_frames, at_start),
        shape((owner_rows, channels), F32),
        [info, corr, proj],
        after=[piece],
        token=True,
        scratch=[VMEM((LANES, channels), F32)],
    )
    proj_grad, bias_grad, code_means, code_usage = call(
        functools.partial(out_kernel, total_frames, book_size / total_frames, dz, at_pieces, now_c, extra),
        [shape((channels, dz), F32), shape((1, channels), F32), shape((levels, per_shard, dz), BF16),
         shape((levels, per_shard), F32)],
        [info, mine] + parts,
        after=[last],
    )
    return feat_grad, conv_grad, bias_grad[0], proj_grad, code_means, code_usage


def solution(mesh):
    placed = (P(("dp", "tm"), None), P("dp", None, "tm"), P(), P(), P(), P())
    return jax.shard_map(
        shards,
        mesh=mesh,
        in_specs=placed,
        out_specs=(
            P(("dp", "tm"), None),
            P(("dp", "tm"), None),
            P(),
            P(),
            P(None, "tm", None),
            P(None, "tm"),
        ),
        check_vma=False,
    )
```

```python
import functools

import jax
import jax.numpy as jnp
from jax import lax
from jax.experimental import pallas as pl
from jax.experimental.pallas import tpu as pltpu
from jax.sharding import PartitionSpec as P

BF16 = jnp.bfloat16
F32 = jnp.float32
LANES = 128
VMEM_LIMIT = 16 * 1024 * 1024


def log2(value):
    assert value & (value - 1) == 0
    return value.bit_length() - 1


def nn(a, b):
    return lax.dot_general(a, b, (((1,), (0,)), ((), ())), preferred_element_type=F32)


def nt(a, b):
    return lax.dot_general(a, b, (((1,), (1,)), ((), ())), preferred_element_type=F32)


VMEM = pltpu.VMEM


def call(body, out_shape, args, after=(), scratch=(), aliases=None, token=False, flops=0):
    info, args = args[0], args[1:]
    count = len(args)
    many = isinstance(out_shape, (list, tuple))
    shapes = list(out_shape) if many else [out_shape]

    def kernel(*refs):
        ends = count + len(after)
        if token:
            refs[ends + len(shapes)][...] = jnp.zeros((8, LANES), F32)
            refs = refs[:ends + len(shapes)] + refs[ends + len(shapes) + 1:]
        body(info(), *refs[:count], *refs[ends:])

    specs = [pl.BlockSpec(memory_space=VMEM)] * count + [pl.BlockSpec(memory_space=pl.ANY)] * len(after)
    shown = shapes + [shape((8, LANES), F32)] * token
    outs = pl.pallas_call(
        kernel,
        out_shape=shown,
        in_specs=specs,
        out_specs=[pl.BlockSpec(memory_space=VMEM)] * len(shown),
        scratch_shapes=list(scratch),
        input_output_aliases={at - 1: out for at, out in (aliases or {}).items()},
        compiler_params=pltpu.CompilerParams(vmem_limit_bytes=VMEM_LIMIT),
        cost_estimate=pl.CostEstimate(flops=flops, bytes_accessed=0, transcendentals=0),
    )(*args, *after)
    return outs if len(shown) > 1 else outs[0]


def shape(dims, dtype):
    return jax.ShapeDtypeStruct(dims, dtype)


def digits_of(value):
    high = value.astype(BF16).astype(F32)
    rest = value - high
    middle = rest.astype(BF16).astype(F32)
    low = (rest - middle).astype(BF16).astype(F32)
    return high, middle, low


def one_hot(codes, axis_codes, first, count):
    frames = codes.shape[1 - axis_codes]
    dims = (count, frames) if axis_codes == 0 else (frames, count)
    places = lax.broadcasted_iota(jnp.int32, dims, axis_codes) + first
    return jnp.where(codes == places, 1.0, 0.0).astype(BF16)


def halo_kernel(info, rows, out):
    out[...] = rows[...]


def walk(orders, halved, count):
    start = 1 if halved else 0
    shown = count // 2 if halved else count
    bits = log2(shown)
    step = 2 if shown > 1 and all(order[-1] == 0 for order in orders) else 1
    for position in range(0, shown, step):
        yield position, [
            sum(((position >> (bits - 1 - k)) & 1) << bit for k, bit in enumerate(order[start:])) for order in orders
        ], step


def correlate(flipped, sources, plan, core, bit, out):
    dz = flipped.shape[0]
    at = 0
    for source, (count, orders, halved) in zip(sources, plan):
        for position, pieces, step in walk(orders, halved, count):
            column = pieces[0] + core * (pieces[1] - pieces[0])
            if halved:
                column = column + (bit << orders[0][0])
            column = pl.multiple_of(column * LANES, LANES)
            product = nn(flipped, source[:, pl.ds(column, step * LANES)])
            for j in range(step):
                top = (at + position + j) * dz
                out[top:top + dz, :] = product[:, j * LANES:(j + 1) * LANES].astype(out.dtype)
        at += count // 2 if halved else count
    return at * dz


def code_digits(codes, dz, rows):
    parts = []
    for part in (codes >> 8, codes & 255):
        for start in range(0, codes.shape[1], dz):
            piece = part[:, start:start + dz].astype(F32)
            if piece.shape[1] < dz:
                piece = jnp.concatenate([piece, jnp.zeros((1, dz - piece.shape[1]), F32)], 1)
            parts.append(piece)
    parts.append(jnp.zeros((rows - len(parts), dz), F32))
    return jnp.concatenate(parts, 0).astype(BF16)


def codes_of(block, frames):
    dz = block.shape[1]
    per = -(-frames // dz)
    digits = block[...].astype(F32)
    parts = [jnp.concatenate([digits[k * per + j:k * per + j + 1, :] for j in range(per)], 1)[:, :frames]
             for k in range(2)]
    return (parts[0] * 256.0 + parts[1]).astype(jnp.int32)


def residuals(hidden, proj, chosen):
    latent = nn(hidden, proj)
    once = latent - chosen[0].astype(F32)
    total = once + (once - chosen[1].astype(F32))
    return latent, once, total.astype(BF16)


def put_columns(out, at, rows, block):
    for j in range(block.shape[1] // LANES):
        out[at + j * rows:at + j * rows + block.shape[0], :] = block[:, j * LANES:(j + 1) * LANES]


def local_kernel(plan, info, feats, weight, bias, codes, books, proj,
                 unfold, hidden, latent_grad, flipped, own, send, first, part, wide, chosen):
    rows, channels = feats.shape
    frames = rows // 2
    dz = proj.shape[1]
    for j in range(channels // LANES):
        wide[j, 0:8, :] = jnp.zeros((8, LANES), F32)
        wide[j, 8:, :] = feats[:, j * LANES:(j + 1) * LANES].astype(F32)
        for tap in range(4):
            start = tap * channels + j * LANES
            unfold[:, start:start + LANES] = wide[j, pl.ds(6 + tap, frames, stride=2), :].astype(BF16)
    conv = nn(unfold[...], weight[...]) + bias[...]
    first[...] = conv[0:16, :]
    hidden[...] = conv.astype(BF16)
    levels = books.shape[0]
    padded = jnp.concatenate([codes[...].astype(F32), jnp.zeros((8 - levels, frames), F32)], 0)
    tall = jnp.transpose(padded).astype(jnp.int32)
    for level in range(levels):
        matches = one_hot(tall[:, level:level + 1], 1, 0, books.shape[1])
        chosen[level] = nn(matches, books[level]).astype(BF16)
    latent, once, grad = residuals(hidden[...], proj[...], chosen)
    latent_grad[...] = grad
    row = lax.broadcasted_iota(jnp.int32, grad.shape, 0)
    flipped[...] = jnp.transpose(jnp.where(row == 0, 0.0, grad.astype(F32))).astype(BF16)
    bit = info[0]
    at = correlate(flipped[...], (unfold, hidden), plan, 1 - bit, 1 - bit, part)
    rows_b = own.shape[0]
    code_rows = rows_b - frames
    digits = [code_digits(codes[level:level + 1, :], dz, code_rows) for level in range(2)]
    own[0:frames, :] = jnp.where(bit == 1, once, latent).astype(BF16)
    own[frames:, :] = jnp.where(bit == 1, digits[1], digits[0])
    put_columns(send, at, rows_b, jnp.where(bit == 1, latent, once).astype(BF16))
    put_columns(send, at + frames, rows_b, jnp.where(bit == 1, digits[0], digits[1]))
    for level in range(levels):
        part[at + level * 16 * (dz // LANES):at + (level + 1) * 16 * (dz // LANES), :] = jnp.concatenate(
            [chosen[level, 0:16, j * LANES:(j + 1) * LANES].astype(F32) for j in range(dz // LANES)], 0)


def frame_kernel(plan, info, halo, first, part, weight, proj, unfold_in, hidden_in, grad_in, flipped_in, own_in, send_in,
                 unfold, hidden, latent_grad, flipped, own, send):
    width = unfold.shape[1]
    half = width // 2
    dz = proj.shape[1]
    row = lax.broadcasted_iota(jnp.int32, (16, half), 0)
    left = jnp.concatenate([halo[0:1, :], halo[1:2, :]], 1).astype(F32)
    head = jnp.where(row == 0, jnp.broadcast_to(left, (16, half)), 0.0)
    unfold[0:16, 0:half] = (unfold_in[0:16, 0:half].astype(F32) + head).astype(BF16)
    fix = nn(head.astype(BF16), weight[0:half, :])
    hidden[0:16, :] = (first[...] + fix).astype(BF16)
    top = hidden[0:16, :]
    pieces = part.shape[0] - 32 * (dz // LANES)
    chosen = []
    for level in range(2):
        at = pieces + level * 16 * (dz // LANES)
        chosen.append(jnp.concatenate([part[at + j * 16:at + (j + 1) * 16, :] for j in range(dz // LANES)], 1))
    latent, once, grad = residuals(top, proj[...], chosen)
    latent_grad[0:16, :] = grad
    flipped[:, 0:LANES] = jnp.transpose(latent_grad[0:LANES, :].astype(F32)).astype(BF16)
    column = flipped[:, 0:LANES].astype(F32)[:, 0:1]
    bit = info[0]
    at = 0
    for source, (count, orders, halved) in zip((unfold, hidden), plan):
        rows = source[0:16, :].astype(F32)[0:1, :]
        for position, places, step in walk(orders, halved, count):
            for j in range(step):
                offsets = [places[0] + j, places[1] + j]
                low = [offset for offset in offsets]
                high = [offset + (1 << orders[0][0] if halved else 0) for offset in offsets]
                picked = [rows[:, k * LANES:(k + 1) * LANES] for k in low + high]
                piece = jnp.where(bit == 1, picked[0], picked[3]) if halved else jnp.where(bit == 1, picked[0], picked[1])
                begin = (at + position + j) * dz
                send[begin:begin + dz, :] = (part[begin:begin + dz, :] + column * piece).astype(BF16)
        at += count // 2 if halved else count
    rows_b = own.shape[0]
    own[0:16, :] = jnp.where(bit == 1, once, latent).astype(BF16)
    put_columns(send, at * dz, rows_b, jnp.where(bit == 1, latent, once).astype(BF16))


def rest_kernel(plan, info, flipped, unfold, hidden, latent_grad, proj, keep_a, keep_c, hidden_grad, extras, row):
    bit = info[0]
    correlate(flipped[...], (unfold,), plan[:1], bit, bit, keep_a)
    correlate(flipped[...], (hidden,), plan[1:], bit, bit, keep_c)
    back = nt(latent_grad[...], proj[...]).astype(BF16)
    hidden_grad[...] = back
    row[...] = back[0:16, :]
    stride = extras.shape[0] // 4
    extras[...] = jnp.zeros(extras.shape, F32)
    sums = jnp.sum(back.astype(F32), 0, keepdims=True)
    for digit, part in enumerate(digits_of(sums)):
        for j in range(sums.shape[1] // LANES):
            extras[digit * stride + j:digit * stride + j + 1, :] = part[:, j * LANES:(j + 1) * LANES]


def split_sum(halved, bit, got, at, kept, rows, send, to, keep):
    if halved:
        half = rows // 2
        away = pl.multiple_of((1 - bit) * half, 16)
        home = pl.multiple_of(bit * half, 16)
        send[to:to + half, :] = (kept[pl.ds(away, half), :] + got[pl.ds(at + away, half), :].astype(F32)).astype(BF16)
        keep[0:half, :] = kept[pl.ds(home, half), :] + got[pl.ds(at + home, half), :].astype(F32)
        return half
    total = (kept[0:rows, :] + got[at:at + rows, :].astype(F32)).astype(BF16)
    send[to:to + rows, :] = total
    keep[0:rows, :] = total.astype(F32)
    return rows


def add_digits(mine, theirs):
    stride = mine.shape[0] // 4
    return ((mine[0:stride] + mine[stride:2 * stride]) + mine[2 * stride:3 * stride]) + (
        (theirs[0:stride] + theirs[stride:2 * stride]) + theirs[2 * stride:3 * stride])


def digit_block(value):
    return jnp.concatenate(list(digits_of(value)) + [jnp.zeros_like(value)], 0)


def first_step_kernel(halves, place, info, got, kept_a, kept_c, extras, send, keep_a, keep_c):
    (rows_a, halved_a), (rows_c, halved_c) = halves
    to = split_sum(halved_a, info[place], got, 0, kept_a, rows_a, send, 0, keep_a)
    gone = split_sum(halved_c, info[place], got, rows_a, kept_c, rows_c, send, to, keep_c)
    send[to + gone:, :] = extras[...].astype(BF16)
    keep_c[gone:, :] = extras[...]


def feat_kernel(info, grad, after, weight, out, wide, inter):
    frames, channels = grad.shape
    half = weight.shape[0] // 2
    wide[0:frames, :] = grad[...].astype(F32)
    wide[frames:, :] = jnp.broadcast_to(after[0:1, :].astype(F32), (8, channels))
    ahead = wide[pl.ds(1, frames), :].astype(BF16)
    for parity in range(2):
        rows = pl.ds(parity * (half // 2), half // 2)
        rows_after = pl.ds(half + parity * (half // 2), half // 2)
        both = nt(ahead, weight[rows, :]) + nt(grad[...], weight[rows_after, :])
        for j in range(channels // LANES):
            inter[j, pl.ds(parity, frames, stride=2), :] = both[:, j * LANES:(j + 1) * LANES]
    for j in range(channels // LANES):
        out[:, j * LANES:(j + 1) * LANES] = inter[j].astype(BF16)


def own_sums_kernel(frames, place, count, info, own, out):
    codes = codes_of(own[frames:, :], frames)
    ones = jnp.ones((8, frames), BF16)
    size = count + 16
    for top in range(0, out.shape[0], size):
        matches = one_hot(codes, 0, info[place], count)
        out[top:top + count, :] = nn(matches, own[0:frames, :])
        out[top + count:top + count + 8, 0:count] = nt(ones, matches)
        place += 1


def sums_kernel(first, frames, place, count, info, got, base, row, out):
    dz = base.shape[1]
    rows = (got.shape[0] - first) // (dz // LANES)
    theirs = jnp.concatenate([got[first + j * rows:first + (j + 1) * rows, :] for j in range(dz // LANES)], 1)
    codes = codes_of(theirs[frames:, :], frames)
    ones = jnp.ones((8, frames), BF16)
    size = count + 16
    riding = [row[...].astype(F32)[0:1, :]]
    for top in range(0, out.shape[0], size):
        matches = one_hot(codes, 0, info[place], count)
        total = base[top:top + count, :] + nn(matches, theirs[0:frames, :])
        counts = base[top + count:top + count + 8, 0:count] + nt(ones, matches)
        out[top:top + count, :] = total.astype(out.dtype)
        out[top + count:top + size, :] = count_rows(counts[0:1], dz, riding).astype(out.dtype)
        place += 1


def count_rows(count, width, riding=()):
    high = jnp.floor(count * (1.0 / 65536.0))
    rest = count - high * 65536.0
    middle = jnp.floor(rest * (1.0 / 256.0))
    low = rest - middle * 256.0
    block = jnp.concatenate([high, middle, low], 0)
    if count.shape[1] < width:
        block = jnp.concatenate([block, jnp.zeros((3, width - count.shape[1]), F32)], 1)
    parts = [block]
    for row in riding:
        parts += [row[:, at:at + width] for at in range(0, row.shape[1], width)]
    left = 16 - sum(part.shape[0] for part in parts)
    return jnp.concatenate(parts + [jnp.zeros((left, width), F32)] * (left > 0), 0)


def riding_row(block, index, parts):
    return jnp.concatenate([block[3 + index * parts + j:4 + index * parts + j, :] for j in range(parts)], 1)


def count_of(block, own):
    return (block[0:1] * 65536.0 + block[1:2] * 256.0 + block[2:3])[:, :own]


def sums_step_kernel(halved, place, row_step, row_place, info, got, kept, *refs):
    riding = ()
    if row_step is not None:
        known, refs = refs[0][...].astype(F32), refs[1:]
        after, refs = refs[-1], refs[:-1]
        parts = known.shape[1] // got.shape[1]
        block = got[row_place[0]:row_place[0] + 16, :].astype(F32)
        rows = [known[j:j + 1, :] for j in range(1 << row_step)]
        rows += [riding_row(block, j, parts) for j in range(1 << row_step)]
        if halved:
            riding = rows
            total = rows + [jnp.zeros((16 - len(rows), known.shape[1]), F32)]
            after[...] = jnp.concatenate(total, 0).astype(BF16)
        else:
            wide = jnp.zeros(after.shape, F32)
            for j in range(1, len(rows)):
                wide = jnp.where(info[row_place[1]] == j, jnp.broadcast_to(rows[j], after.shape), wide)
            after[...] = wide.astype(BF16)
    send, keep = refs
    dz = got.shape[1]
    bit = info[place]
    half = kept.shape[0] // 2 if halved else 0
    outs = [(send, (1 - bit) * half), (keep, bit * half)] if halved else [(send, 0)]
    count = row_place[0]
    size = count + 16
    for out, start in outs:
        for top in range(0, keep.shape[0], size):
            here = top + pl.multiple_of(start, 16) if halved else top
            sums = pl.ds(here, count)
            tail = pl.ds(here + count, 16)
            value = kept[sums, :].astype(F32) + got[sums, :].astype(F32)
            number = count_of(kept[tail, :].astype(F32), count) + count_of(got[tail, :].astype(F32), count)
            out[top:top + count, :] = value.astype(out.dtype)
            out[top + count:top + size, :] = count_rows(number, dz, riding).astype(out.dtype)
    if not halved:
        keep[...] = send[0:keep.shape[0], :].astype(F32)


def swap_halves(first, second, core):
    half = LANES // 2
    left = lax.broadcasted_iota(jnp.int32, first.shape, 1) < half
    turned_first, turned_second = pltpu.roll(first, half, 1), pltpu.roll(second, half, 1)
    swapped_first = jnp.where(left, first, turned_second)
    swapped_second = jnp.where(left, turned_first, second)
    return jnp.where(core == 1, swapped_first, first), jnp.where(core == 1, swapped_second, second)


def step_kernel(halves, place, mixed, info, got, kept_a, kept_c, send, keep_a, keep_c):
    (rows_a, halved_a), (rows_c, halved_c) = halves
    if mixed:
        to = rows_a // 2
        total = kept_a[0:rows_a, :] + got[0:rows_a, :].astype(F32)
        first, second = swap_halves(total[0:to, :], total[to:, :], info[0])
        low = info[place] == 0
        send[0:to, :] = jnp.where(low, second, first).astype(BF16)
        keep_a[...] = jnp.where(low, first, second)
    else:
        to = split_sum(halved_a, info[place], got, 0, kept_a, rows_a, send, 0, keep_a)
    gone = split_sum(halved_c, info[place], got, rows_a, kept_c, rows_c, send, to, keep_c)
    block = digit_block(add_digits(kept_c[rows_c:, :], got[rows_a + rows_c:, :].astype(F32)))
    keep_c[gone:, :] = block
    to += gone
    send[to:to + block.shape[0], :] = block.astype(BF16)
    to += block.shape[0]
    if to < send.shape[0]:
        send[to:, :] = jnp.zeros((send.shape[0] - to, LANES), BF16)


def last_kernel(rows_a, rows, info, got, kept_a, kept_c, sums_got, sums_kept, corr, pieces, mine):
    corr[...] = kept_a[...] + got[0:rows_a, :].astype(F32)
    pieces[...] = (kept_c[0:rows, :] + got[rows_a:rows_a + rows, :].astype(F32)).astype(BF16)
    block = digit_block(add_digits(kept_c[rows:, :], got[rows_a + rows:rows_a + kept_c.shape[0], :].astype(F32)))
    mine[0:rows, :] = pieces[...]
    mine[rows:kept_c.shape[0], :] = block.astype(BF16)
    at = kept_c.shape[0]
    count = sums_kept.shape[0] - 16
    number = count_of(sums_kept[count:, :].astype(F32), count) + count_of(sums_got[count:, :].astype(F32), count)
    square = (count, count)
    same = lax.broadcasted_iota(jnp.int32, square, 0) == lax.broadcasted_iota(jnp.int32, square, 1)
    tall = jnp.sum(jnp.where(same, jnp.broadcast_to(number, square), 0.0), 1, keepdims=True)
    total = sums_kept[0:count, :].astype(F32) + sums_got[0:count, :].astype(F32)
    means = (total / jnp.maximum(tall, 1.0)).astype(BF16)
    digits = count_rows(number, means.shape[1]).astype(BF16)
    for j in range(means.shape[1] // LANES):
        mine[at:at + count, :] = means[:, j * LANES:(j + 1) * LANES]
        mine[at + count:at + count + 16, :] = digits[:, j * LANES:(j + 1) * LANES]
        at += count + 16


def conv_out_kernel(total_frames, place, info, corr, proj, out, wide):
    rows = out.shape[0]
    flipped = jnp.transpose(corr[...])
    high = flipped.astype(BF16)
    low = (flipped - high.astype(F32)).astype(BF16)
    wide[...] = (nt(high, proj[...]) + nt(low, proj[...])) * (1.0 / total_frames)
    start = info[place]
    if rows % 8 == 0:
        out[...] = wide[pl.ds(pl.multiple_of(start, 8), rows), :]
    else:
        taken = wide[0:rows, :]
        for other in range(rows, wide.shape[0], rows):
            taken = jnp.where(start == other, wide[other:other + rows, :], taken)
        out[...] = taken


def out_kernel(total_frames, use_scale, dz, place, inner, extra, info, mine, *refs):
    parts, (out, bias, means, usage) = refs[:-4], refs[-4:]
    theirs = parts[1]
    scale = 1.0 / total_frames
    top = inner * dz
    value = add_digits(mine[top:top + extra, :].astype(F32), theirs[top:top + extra, :].astype(F32)) * scale
    for j in range(bias.shape[1] // LANES):
        bias[:, j * LANES:(j + 1) * LANES] = value[j:j + 1, :]
    bit = info[0]
    count = means.shape[1]
    numbers = []
    for ref, level in ((mine, bit), (theirs, 1 - bit)):
        at = top + extra
        blocks = []
        for j in range(dz // LANES):
            blocks.append(ref[at:at + count + 16, :])
            at += count + 16
        whole = jnp.concatenate(blocks, 1)
        means[level] = whole[0:count, :]
        numbers.append(count_of(whole[count:, :].astype(F32), count) * use_scale)
    usage[0:1, :] = jnp.where(bit == 1, numbers[1], numbers[0])
    usage[1:2, :] = jnp.where(bit == 1, numbers[0], numbers[1])
    for j, ref in enumerate(parts):
        for k in range(inner):
            start = pl.multiple_of((info[place + j] + k) * LANES, LANES)
            turned = jnp.transpose(ref[k * dz:(k + 1) * dz, :])
            out[pl.ds(start, LANES), :] = turned.astype(F32) * scale


def shifted(block, axis, distance):
    devices = range(lax.axis_size(axis))
    route = [(i - distance, i) for i in devices if i - distance in devices]
    return lax.ppermute(block, axis, route)


def swapped(block, steps):
    tm = lax.axis_size("tm")

    def partner(device):
        axis, bit = steps[(device // tm) & 1]
        return device ^ ((1 << bit) * (tm if axis == "dp" else 1))

    route = [(device, partner(device)) for device in range(lax.axis_size("dp") * tm)]
    return lax.ppermute(block, ("dp", "tm"), route)


def crossed(block, steps):
    tm = lax.axis_size("tm")

    def partner(device):
        axis, bit = steps[(device // tm) & 1]
        return device ^ tm ^ ((1 << bit) * (tm if axis == "dp" else 1))

    route = [(device, partner(device)) for device in range(lax.axis_size("dp") * tm)]
    return lax.ppermute(block, ("dp", "tm"), route)


def shards(feats, codes, conv_weight, conv_bias, proj_weight, codebooks):
    dp, tm = lax.axis_size("dp"), lax.axis_size("tm")
    rows_in, channels = feats.shape
    frames = rows_in // 2
    levels, book_size, dz = codebooks.shape
    assert levels == 2
    width = conv_weight.shape[0]
    total_frames = frames * dp * tm
    per_shard = book_size // tm
    dp_bits, tm_bits = log2(dp), log2(tm)
    owner_rows = width // (dp * tm)

    assert dp_bits >= 3 and 1 <= tm_bits <= 2
    pieces_a, pieces_c = width // LANES, channels // LANES
    under = max(dp_bits + tm_bits - log2(pieces_a), 0)
    c_bits = 2
    assert pieces_c >= 4
    whole_bits = [b for b in range(1, dp_bits) if b + tm_bits < under]
    piece_bits = [b for b in range(1, dp_bits) if b + tm_bits >= under]
    paths = [[("dp", b) for b in bits] for bits in (whole_bits[::-1] + piece_bits[::-1], whole_bits + piece_bits)]
    mixed = under == 1 and tm_bits == 2
    turned = mixed or under == 0 or under >= tm_bits
    up = [("tm", b) for b in range(tm_bits)]
    paths[0] += up[::-1]
    paths[1] += up if turned else up[::-1]
    exchanges = list(zip([("dp", 0)] + paths[0], [("dp", 0)] + paths[1]))
    sums_up = [("dp", b) for b in range(1, dp_bits)]
    sums_exchanges = list(zip(up + sums_up[::-1], up[::-1] + sums_up))

    def piece_bit(step):
        axis, b = step
        bit = b + (tm_bits if axis == "dp" else 0)
        return bit - under if bit >= under else None

    a_split = [piece_bit(steps[0]) is not None for steps in exchanges]
    c_split = [log2(pieces_c) - 1 - k if k < c_bits else None for k in range(len(exchanges))]

    def order_of(split, count):
        used = [b for b in split if b is not None]
        return used + [b for b in reversed(range(log2(count))) if b not in used]

    orders = [order_of([piece_bit(steps[core]) for steps in exchanges], pieces_a) for core in range(2)]
    order_c = order_of(c_split, pieces_c)
    plan = [(pieces_a, orders, a_split[0]), (pieces_c, [order_c, order_c], True)]
    now_a = pieces_a // 2 if plan[0][2] else pieces_a
    now_c = pieces_c // 2

    count_bits, count_places = len(exchanges), 4
    at_start = count_bits
    at_codes = at_start + 1
    at_pieces = at_codes + tm
    at_sums = at_pieces + count_places
    at_row = at_sums + len(sums_exchanges)

    def info():
        at_dp, at_tm = lax.axis_index("dp"), lax.axis_index("tm")
        core = at_dp & 1

        def on_core(values):
            return values[0] + core * (values[1] - values[0])

        def bit_at(step):
            axis, b = step
            return ((at_dp if axis == "dp" else at_tm) >> b) & 1

        bits = [on_core([bit_at(step) for step in steps]) for steps in exchanges]
        sums_bits = [on_core([bit_at(step) for step in steps]) for steps in sums_exchanges]
        shared = [bit_at(step) for step in exchanges[1]]
        mine_c, other_c = on_core(shared), on_core(shared[::-1])
        places = [2 * core + mine_c, 2 * (1 - core) + other_c, 2 * core + 1 - mine_c, 2 * (1 - core) + 1 - other_c]
        places = [place << (log2(pieces_c) - c_bits) for place in places]
        lists = []
        for way in ([b for _, b in up], [b for _, b in up[::-1]]):
            lists.append([sum(((position >> (tm_bits - 1 - j)) & 1) << b for j, b in enumerate(way)) for position in range(tm)])
        first_bit = on_core([0, tm_bits - 1])
        lead = (at_tm >> first_bit) & 1
        quarters = [on_core([lists[0][j], lists[1][j]]) for j in range(tm // 2)]
        send_codes = [(q + ((1 - lead) << first_bit)) * per_shard for q in quarters]
        keep_codes = [(q + (lead << first_bit)) * per_shard for q in quarters]
        differ = at_tm ^ (at_tm + 1)
        ways = [sum(((differ >> b) & 1) << j for j, b in enumerate(way)) for way in (
            list(range(tm_bits)), list(reversed(range(tm_bits))))]
        row_code = jnp.where(at_tm + 1 < tm, on_core(ways), 0)
        if turned and not mixed:
            start = ((at_dp * tm + at_tm) * owner_rows) & (LANES - 1)
        else:
            start = on_core([(at_dp * tm + at_tm) * owner_rows, (at_tm >> 1) * owner_rows if mixed else (
                at_dp * tm + at_tm) * owner_rows]) & (LANES - 1)
        return bits + [start] + send_codes + keep_codes + places + sums_bits + [row_code]

    halo = shifted(call(halo_kernel, shape((2, channels), BF16), [info, feats[-2:]], flops=10 ** 11), "tm", 1)
    weight, proj, codes = conv_weight, proj_weight, codes[0]
    extra = 4 * (-(-channels // LANES // 8) * 8)
    code_rows = -(-(2 * -(-frames // dz)) // 16) * 16
    corr_rows = (now_a + now_c) * dz
    rows_b = frames + code_rows
    shared = [shape((frames, width), BF16), shape((frames, channels), BF16), shape((frames, dz), BF16),
              shape((dz, frames), BF16), shape((rows_b, dz), BF16),
              shape((corr_rows + rows_b * (dz // LANES), LANES), BF16)]
    *arrays, first, part = call(
        functools.partial(local_kernel, plan),
        shared + [shape((16, channels), F32), shape((corr_rows + 32 * (dz // LANES), LANES), F32)],
        [info, feats, weight, conv_bias[None, :], codes, codebooks, proj],
        scratch=[VMEM((channels // LANES, rows_in + 8, LANES), F32), VMEM((levels, frames, dz), BF16)],
    )
    unfold, hidden, latent_grad, flipped, own, send = call(
        functools.partial(frame_kernel, plan),
        shared,
        [info, halo, first, part, weight, proj] + arrays,
        aliases={6 + k: k for k in range(len(shared))},
    )
    got = swapped(send, exchanges[0])
    keep_a, keep_c, hidden_grad, extras, row = call(
        functools.partial(rest_kernel, plan),
        [shape((now_a * dz, LANES), F32), shape((now_c * dz, LANES), F32), shape((frames, channels), BF16),
         shape((extra, LANES), F32), shape((16, channels), BF16)],
        [info, flipped, unfold, hidden, latent_grad, proj],
        after=[send],
    )

    def halves_at(k):
        nonlocal now_a, now_c
        halves = [(now_a * dz, a_split[k]), (now_c * dz, c_split[k] is not None)]
        now_a = now_a // 2 if halves[0][1] else now_a
        now_c = now_c // 2 if halves[1][1] else now_c
        return halves, now_a * dz, now_c * dz + extra

    size = per_shard + 16
    sums_rows = size * (tm // 2)
    got_core = got

    def own_sums(first, after):
        return call(
            functools.partial(own_sums_kernel, frames, at_codes + first, per_shard),
            shape((sums_rows, dz), F32),
            [info, own],
            after=after)

    def both_sums(first, base, dtype, after):
        return call(
            functools.partial(sums_kernel, corr_rows, frames, at_codes + first, per_shard),
            shape((sums_rows, dz), dtype),
            [info, got_core, base, row],
            after=after)

    base = own_sums(0, [extras])
    halves, rows_a, rows_c = halves_at(1)
    send, keep_a, keep_c = call(
        functools.partial(first_step_kernel, halves, 1),
        [shape((rows_a + rows_c, LANES), BF16), shape((rows_a, LANES), F32), shape((rows_c, LANES), F32)],
        [info, got, keep_a, keep_c, extras],
        after=[base])
    sums_send = both_sums(0, base, BF16, [send])
    sums_keep = both_sums(tm // 2, own_sums(tm // 2, [sums_send]), F32, [])
    sums_got = swapped(sums_send, sums_exchanges[0])
    got = swapped(send, exchanges[1])
    known = row
    ordered = [sums_keep]
    for k in range(2, len(exchanges)):
        halves, rows_a, rows_c = halves_at(k)
        spare = 16 * (k == len(exchanges) - 1)
        send, keep_a, keep_c = call(
            functools.partial(step_kernel, halves, k, mixed and k == dp_bits),
            [shape((rows_a + rows_c + spare, LANES), BF16), shape((rows_a, LANES), F32), shape((rows_c, LANES), F32)],
            [info, got, keep_a, keep_c],
            after=ordered)
        got = swapped(send, exchanges[k])
        halved = sums_exchanges[k - 1][0][0] == "tm"
        sums_rows = sums_rows // 2 if halved else sums_rows
        row_step = k - 2 if k - 2 < tm_bits else None
        outs = call(
            functools.partial(sums_step_kernel, halved, at_sums + k - 1, row_step, (per_shard, at_row)),
            [shape((sums_rows, dz), BF16), shape((sums_rows, dz), F32)]
            + [shape((16, channels), BF16)] * (row_step is not None),
            [info, sums_got, sums_keep] + [known] * (row_step is not None),
            after=[send])
        sums_send, sums_keep = outs[:2]
        known = outs[2] if row_step is not None else known
        sums_got = swapped(sums_send, sums_exchanges[k - 1])
        ordered = [sums_send]
    assert now_a == 1 and sums_rows == size
    feat_grad, last = call(
        feat_kernel,
        shape((rows_in, channels), BF16),
        [info, hidden_grad, known, weight],
        after=[sums_send],
        token=True,
        scratch=[VMEM((frames + 8, channels), F32), VMEM((channels // LANES, rows_in, LANES), F32)],
    )

    corr, piece, mine = call(
        functools.partial(last_kernel, rows_a, rows_c - extra),
        [shape((rows_a, LANES), F32), shape((rows_c - extra, LANES), BF16),
         shape((rows_c + size * (dz // LANES), LANES), BF16)],
        [info, got, keep_a, keep_c, sums_got, sums_keep],
        after=[last])
    parts = [piece, swapped(mine, exchanges[0]), swapped(piece, exchanges[1]), crossed(piece, exchanges[1])]
    conv_grad, last = call(
        functools.partial(conv_out_kernel, total_frames, at_start),
        shape((owner_rows, channels), F32),
        [info, corr, proj],
        after=[piece],
        token=True,
        scratch=[VMEM((LANES, channels), F32)],
    )
    proj_grad, bias_grad, code_means, code_usage = call(
        functools.partial(out_kernel, total_frames, book_size / total_frames, dz, at_pieces, now_c, extra),
        [shape((channels, dz), F32), shape((1, channels), F32), shape((levels, per_shard, dz), BF16),
         shape((levels, per_shard), F32)],
        [info, mine] + parts,
        after=[last],
    )
    return feat_grad, conv_grad, bias_grad[0], proj_grad, code_means, code_usage


def solution(mesh):
    placed = (P(("dp", "tm"), None), P("dp", None, "tm"), P(), P(), P(), P())
    return jax.shard_map(
        shards,
        mesh=mesh,
        in_specs=placed,
        out_specs=(
            P(("dp", "tm"), None),
            P(("dp", "tm"), None),
            P(),
            P(),
            P(None, "tm", None),
            P(None, "tm"),
        ),
        check_vma=False,
    )
```

```python
import functools

import jax
import jax.numpy as jnp
from jax import lax
from jax.experimental import pallas as pl
from jax.experimental.pallas import tpu as pltpu
from jax.sharding import PartitionSpec as P

BF16 = jnp.bfloat16
F32 = jnp.float32
LANES = 128
VMEM_LIMIT = 16 * 1024 * 1024


def log2(value):
    assert value & (value - 1) == 0
    return value.bit_length() - 1


def nn(a, b):
    return lax.dot_general(a, b, (((1,), (0,)), ((), ())), preferred_element_type=F32)


def nt(a, b):
    return lax.dot_general(a, b, (((1,), (1,)), ((), ())), preferred_element_type=F32)


VMEM = pltpu.VMEM


def call(body, out_shape, args, after=(), scratch=(), aliases=None, token=False, flops=0):
    info, args = args[0], args[1:]
    count = len(args)
    many = isinstance(out_shape, (list, tuple))
    shapes = list(out_shape) if many else [out_shape]

    def kernel(*refs):
        ends = count + len(after)
        if token:
            refs[ends + len(shapes)][...] = jnp.zeros((8, LANES), F32)
            refs = refs[:ends + len(shapes)] + refs[ends + len(shapes) + 1:]
        body(info(), *refs[:count], *refs[ends:])

    specs = [pl.BlockSpec(memory_space=VMEM)] * count + [pl.BlockSpec(memory_space=pl.ANY)] * len(after)
    shown = shapes + [shape((8, LANES), F32)] * token
    outs = pl.pallas_call(
        kernel,
        out_shape=shown,
        in_specs=specs,
        out_specs=[pl.BlockSpec(memory_space=VMEM)] * len(shown),
        scratch_shapes=list(scratch),
        input_output_aliases={at - 1: out for at, out in (aliases or {}).items()},
        compiler_params=pltpu.CompilerParams(vmem_limit_bytes=VMEM_LIMIT),
        cost_estimate=pl.CostEstimate(flops=flops, bytes_accessed=0, transcendentals=0),
    )(*args, *after)
    return outs if len(shown) > 1 else outs[0]


def shape(dims, dtype):
    return jax.ShapeDtypeStruct(dims, dtype)


def digits_of(value):
    high = value.astype(BF16).astype(F32)
    rest = value - high
    middle = rest.astype(BF16).astype(F32)
    low = (rest - middle).astype(BF16).astype(F32)
    return high, middle, low


def one_hot(codes, axis_codes, first, count):
    frames = codes.shape[1 - axis_codes]
    dims = (count, frames) if axis_codes == 0 else (frames, count)
    places = lax.broadcasted_iota(jnp.int32, dims, axis_codes) + first
    return jnp.where(codes == places, 1.0, 0.0).astype(BF16)


def halo_kernel(info, rows, out):
    out[...] = rows[...]


def walk(orders, halved, count):
    start = 1 if halved else 0
    shown = count // 2 if halved else count
    bits = log2(shown)
    step = 2 if shown > 1 and all(order[-1] == 0 for order in orders) else 1
    for position in range(0, shown, step):
        yield position, [
            sum(((position >> (bits - 1 - k)) & 1) << bit for k, bit in enumerate(order[start:])) for order in orders
        ], step


def correlate(flipped, sources, plan, core, bit, out):
    dz = flipped.shape[0]
    at = 0
    for source, (count, orders, halved) in zip(sources, plan):
        for position, pieces, step in walk(orders, halved, count):
            column = pieces[0] + core * (pieces[1] - pieces[0])
            if halved:
                column = column + (bit << orders[0][0])
            column = pl.multiple_of(column * LANES, LANES)
            product = nn(flipped, source[:, pl.ds(column, step * LANES)])
            for j in range(step):
                top = (at + position + j) * dz
                out[top:top + dz, :] = product[:, j * LANES:(j + 1) * LANES].astype(out.dtype)
        at += count // 2 if halved else count
    return at * dz


def code_digits(codes, dz, rows):
    parts = []
    for part in (codes >> 8, codes & 255):
        for start in range(0, codes.shape[1], dz):
            piece = part[:, start:start + dz].astype(F32)
            if piece.shape[1] < dz:
                piece = jnp.concatenate([piece, jnp.zeros((1, dz - piece.shape[1]), F32)], 1)
            parts.append(piece)
    parts.append(jnp.zeros((rows - len(parts), dz), F32))
    return jnp.concatenate(parts, 0).astype(BF16)


def codes_of(block, frames):
    dz = block.shape[1]
    per = -(-frames // dz)
    digits = block[...].astype(F32)
    parts = [jnp.concatenate([digits[k * per + j:k * per + j + 1, :] for j in range(per)], 1)[:, :frames]
             for k in range(2)]
    return (parts[0] * 256.0 + parts[1]).astype(jnp.int32)


def residuals(hidden, proj, chosen):
    latent = nn(hidden, proj)
    once = latent - chosen[0].astype(F32)
    total = once + (once - chosen[1].astype(F32))
    return latent, once, total.astype(BF16)


def put_columns(out, at, rows, block):
    for j in range(block.shape[1] // LANES):
        out[at + j * rows:at + j * rows + block.shape[0], :] = block[:, j * LANES:(j + 1) * LANES]


def local_kernel(plan, info, feats, weight, bias, codes, books, proj,
                 unfold, hidden, latent_grad, flipped, own, send_sums, first, part, wide, chosen):
    rows, channels = feats.shape
    frames = rows // 2
    dz = proj.shape[1]
    for j in range(channels // LANES):
        wide[j, 0:8, :] = jnp.zeros((8, LANES), F32)
        wide[j, 8:, :] = feats[:, j * LANES:(j + 1) * LANES].astype(F32)
        for tap in range(4):
            start = tap * channels + j * LANES
            unfold[:, start:start + LANES] = wide[j, pl.ds(6 + tap, frames, stride=2), :].astype(BF16)
    conv = nn(unfold[...], weight[...]) + bias[...]
    first[...] = conv[0:16, :]
    hidden[...] = conv.astype(BF16)
    levels = books.shape[0]
    padded = jnp.concatenate([codes[...].astype(F32), jnp.zeros((8 - levels, frames), F32)], 0)
    tall = jnp.transpose(padded).astype(jnp.int32)
    for level in range(levels):
        matches = one_hot(tall[:, level:level + 1], 1, 0, books.shape[1])
        chosen[level] = nn(matches, books[level]).astype(BF16)
    latent, once, grad = residuals(hidden[...], proj[...], chosen)
    latent_grad[...] = grad
    row = lax.broadcasted_iota(jnp.int32, grad.shape, 0)
    flipped[...] = jnp.transpose(jnp.where(row == 0, 0.0, grad.astype(F32))).astype(BF16)
    bit = info[0]
    at = correlate(flipped[...], (unfold, hidden), plan, 1 - bit, 1 - bit, part)
    rows_b = own.shape[0]
    code_rows = rows_b - frames
    digits = [code_digits(codes[level:level + 1, :], dz, code_rows) for level in range(2)]
    own[0:frames, :] = jnp.where(bit == 1, once, latent).astype(BF16)
    own[frames:, :] = jnp.where(bit == 1, digits[1], digits[0])
    put_columns(send_sums, 0, rows_b, jnp.where(bit == 1, latent, once).astype(BF16))
    put_columns(send_sums, frames, rows_b, jnp.where(bit == 1, digits[0], digits[1]))
    for level in range(levels):
        part[at + level * 16 * (dz // LANES):at + (level + 1) * 16 * (dz // LANES), :] = jnp.concatenate(
            [chosen[level, 0:16, j * LANES:(j + 1) * LANES].astype(F32) for j in range(dz // LANES)], 0)


def frame_kernel(plan, info, halo, first, part, weight, proj, unfold_in, hidden_in, grad_in, flipped_in, own_in, sums_in,
                 unfold, hidden, latent_grad, flipped, own, send_sums, send):
    width = unfold.shape[1]
    half = width // 2
    dz = proj.shape[1]
    row = lax.broadcasted_iota(jnp.int32, (16, half), 0)
    left = jnp.concatenate([halo[0:1, :], halo[1:2, :]], 1).astype(F32)
    head = jnp.where(row == 0, jnp.broadcast_to(left, (16, half)), 0.0)
    unfold[0:16, 0:half] = (unfold_in[0:16, 0:half].astype(F32) + head).astype(BF16)
    fix = nn(head.astype(BF16), weight[0:half, :])
    hidden[0:16, :] = (first[...] + fix).astype(BF16)
    top = hidden[0:16, :]
    pieces = part.shape[0] - 32 * (dz // LANES)
    chosen = []
    for level in range(2):
        at = pieces + level * 16 * (dz // LANES)
        chosen.append(jnp.concatenate([part[at + j * 16:at + (j + 1) * 16, :] for j in range(dz // LANES)], 1))
    latent, once, grad = residuals(top, proj[...], chosen)
    latent_grad[0:16, :] = grad
    flipped[:, 0:LANES] = jnp.transpose(latent_grad[0:LANES, :].astype(F32)).astype(BF16)
    column = flipped[:, 0:LANES].astype(F32)[:, 0:1]
    bit = info[0]
    at = 0
    for source, (count, orders, halved) in zip((unfold, hidden), plan):
        rows = source[0:16, :].astype(F32)[0:1, :]
        for position, places, step in walk(orders, halved, count):
            for j in range(step):
                offsets = [places[0] + j, places[1] + j]
                low = [offset for offset in offsets]
                high = [offset + (1 << orders[0][0] if halved else 0) for offset in offsets]
                picked = [rows[:, k * LANES:(k + 1) * LANES] for k in low + high]
                piece = jnp.where(bit == 1, picked[0], picked[3]) if halved else jnp.where(bit == 1, picked[0], picked[1])
                begin = (at + position + j) * dz
                send[begin:begin + dz, :] = (part[begin:begin + dz, :] + column * piece).astype(BF16)
        at += count // 2 if halved else count
    rows_b = own.shape[0]
    own[0:16, :] = jnp.where(bit == 1, once, latent).astype(BF16)
    put_columns(send_sums, 0, rows_b, jnp.where(bit == 1, latent, once).astype(BF16))


def rest_kernel(plan, info, flipped, unfold, hidden, latent_grad, proj, keep_a, keep_c, hidden_grad, extras, row):
    bit = info[0]
    correlate(flipped[...], (unfold,), plan[:1], bit, bit, keep_a)
    correlate(flipped[...], (hidden,), plan[1:], bit, bit, keep_c)
    back = nt(latent_grad[...], proj[...]).astype(BF16)
    hidden_grad[...] = back
    row[...] = back[0:16, :]
    stride = extras.shape[0] // 4
    extras[...] = jnp.zeros(extras.shape, F32)
    sums = jnp.sum(back.astype(F32), 0, keepdims=True)
    for digit, part in enumerate(digits_of(sums)):
        for j in range(sums.shape[1] // LANES):
            extras[digit * stride + j:digit * stride + j + 1, :] = part[:, j * LANES:(j + 1) * LANES]


def split_sum(halved, bit, got, at, kept, rows, send, to, keep):
    if halved:
        half = rows // 2
        away = pl.multiple_of((1 - bit) * half, 16)
        home = pl.multiple_of(bit * half, 16)
        send[to:to + half, :] = (kept[pl.ds(away, half), :] + got[pl.ds(at + away, half), :].astype(F32)).astype(BF16)
        keep[0:half, :] = kept[pl.ds(home, half), :] + got[pl.ds(at + home, half), :].astype(F32)
        return half
    total = (kept[0:rows, :] + got[at:at + rows, :].astype(F32)).astype(BF16)
    send[to:to + rows, :] = total
    keep[0:rows, :] = total.astype(F32)
    return rows


def add_digits(mine, theirs):
    stride = mine.shape[0] // 4
    return ((mine[0:stride] + mine[stride:2 * stride]) + mine[2 * stride:3 * stride]) + (
        (theirs[0:stride] + theirs[stride:2 * stride]) + theirs[2 * stride:3 * stride])


def digit_block(value):
    return jnp.concatenate(list(digits_of(value)) + [jnp.zeros_like(value)], 0)


def first_step_kernel(halves, place, info, got, kept_a, kept_c, extras, send, keep_a, keep_c):
    (rows_a, halved_a), (rows_c, halved_c) = halves
    to = split_sum(halved_a, info[place], got, 0, kept_a, rows_a, send, 0, keep_a)
    gone = split_sum(halved_c, info[place], got, rows_a, kept_c, rows_c, send, to, keep_c)
    send[to + gone:, :] = extras[...].astype(BF16)
    keep_c[gone:, :] = extras[...]


def feat_kernel(info, grad, after, weight, out, wide, inter):
    frames, channels = grad.shape
    half = weight.shape[0] // 2
    wide[0:frames, :] = grad[...].astype(F32)
    wide[frames:, :] = jnp.broadcast_to(after[0:1, :].astype(F32), (8, channels))
    ahead = wide[pl.ds(1, frames), :].astype(BF16)
    for parity in range(2):
        rows = pl.ds(parity * (half // 2), half // 2)
        rows_after = pl.ds(half + parity * (half // 2), half // 2)
        both = nt(ahead, weight[rows, :]) + nt(grad[...], weight[rows_after, :])
        for j in range(channels // LANES):
            inter[j, pl.ds(parity, frames, stride=2), :] = both[:, j * LANES:(j + 1) * LANES]
    for j in range(channels // LANES):
        out[:, j * LANES:(j + 1) * LANES] = inter[j].astype(BF16)


def own_sums_kernel(frames, place, count, info, own, out):
    codes = codes_of(own[frames:, :], frames)
    ones = jnp.ones((8, frames), BF16)
    size = count + 16
    for top in range(0, out.shape[0], size):
        matches = one_hot(codes, 0, info[place], count)
        out[top:top + count, :] = nn(matches, own[0:frames, :])
        out[top + count:top + count + 8, 0:count] = nt(ones, matches)
        place += 1


def sums_kernel(first, frames, place, count, info, got, base, row, out):
    dz = base.shape[1]
    rows = (got.shape[0] - first) // (dz // LANES)
    theirs = jnp.concatenate([got[first + j * rows:first + (j + 1) * rows, :] for j in range(dz // LANES)], 1)
    codes = codes_of(theirs[frames:, :], frames)
    ones = jnp.ones((8, frames), BF16)
    size = count + 16
    riding = [row[...].astype(F32)[0:1, :]]
    for top in range(0, out.shape[0], size):
        matches = one_hot(codes, 0, info[place], count)
        total = base[top:top + count, :] + nn(matches, theirs[0:frames, :])
        counts = base[top + count:top + count + 8, 0:count] + nt(ones, matches)
        out[top:top + count, :] = total.astype(out.dtype)
        out[top + count:top + size, :] = count_rows(counts[0:1], dz, riding).astype(out.dtype)
        place += 1


def count_rows(count, width, riding=()):
    high = jnp.floor(count * (1.0 / 65536.0))
    rest = count - high * 65536.0
    middle = jnp.floor(rest * (1.0 / 256.0))
    low = rest - middle * 256.0
    block = jnp.concatenate([high, middle, low], 0)
    if count.shape[1] < width:
        block = jnp.concatenate([block, jnp.zeros((3, width - count.shape[1]), F32)], 1)
    parts = [block]
    for row in riding:
        parts += [row[:, at:at + width] for at in range(0, row.shape[1], width)]
    left = 16 - sum(part.shape[0] for part in parts)
    return jnp.concatenate(parts + [jnp.zeros((left, width), F32)] * (left > 0), 0)


def riding_row(block, index, parts):
    return jnp.concatenate([block[3 + index * parts + j:4 + index * parts + j, :] for j in range(parts)], 1)


def count_of(block, own):
    return (block[0:1] * 65536.0 + block[1:2] * 256.0 + block[2:3])[:, :own]


def sums_step_kernel(halved, place, row_step, row_place, info, got, kept, *refs):
    riding = ()
    if row_step is not None:
        known, refs = refs[0][...].astype(F32), refs[1:]
        after, refs = refs[-1], refs[:-1]
        parts = known.shape[1] // got.shape[1]
        block = got[row_place[0]:row_place[0] + 16, :].astype(F32)
        rows = [known[j:j + 1, :] for j in range(1 << row_step)]
        rows += [riding_row(block, j, parts) for j in range(1 << row_step)]
        if halved:
            riding = rows
            total = rows + [jnp.zeros((16 - len(rows), known.shape[1]), F32)]
            after[...] = jnp.concatenate(total, 0).astype(BF16)
        else:
            wide = jnp.zeros(after.shape, F32)
            for j in range(1, len(rows)):
                wide = jnp.where(info[row_place[1]] == j, jnp.broadcast_to(rows[j], after.shape), wide)
            after[...] = wide.astype(BF16)
    send, keep = refs
    dz = got.shape[1]
    bit = info[place]
    half = kept.shape[0] // 2 if halved else 0
    outs = [(send, (1 - bit) * half), (keep, bit * half)] if halved else [(send, 0)]
    count = row_place[0]
    size = count + 16
    for out, start in outs:
        for top in range(0, keep.shape[0], size):
            here = top + pl.multiple_of(start, 16) if halved else top
            sums = pl.ds(here, count)
            tail = pl.ds(here + count, 16)
            value = kept[sums, :].astype(F32) + got[sums, :].astype(F32)
            number = count_of(kept[tail, :].astype(F32), count) + count_of(got[tail, :].astype(F32), count)
            out[top:top + count, :] = value.astype(out.dtype)
            out[top + count:top + size, :] = count_rows(number, dz, riding).astype(out.dtype)
    if not halved:
        keep[...] = send[0:keep.shape[0], :].astype(F32)


def swap_halves(first, second, core):
    half = LANES // 2
    left = lax.broadcasted_iota(jnp.int32, first.shape, 1) < half
    turned_first, turned_second = pltpu.roll(first, half, 1), pltpu.roll(second, half, 1)
    swapped_first = jnp.where(left, first, turned_second)
    swapped_second = jnp.where(left, turned_first, second)
    return jnp.where(core == 1, swapped_first, first), jnp.where(core == 1, swapped_second, second)


def step_kernel(halves, place, mixed, info, got, kept_a, kept_c, send, keep_a, keep_c):
    (rows_a, halved_a), (rows_c, halved_c) = halves
    if mixed:
        to = rows_a // 2
        total = kept_a[0:rows_a, :] + got[0:rows_a, :].astype(F32)
        first, second = swap_halves(total[0:to, :], total[to:, :], info[0])
        low = info[place] == 0
        send[0:to, :] = jnp.where(low, second, first).astype(BF16)
        keep_a[...] = jnp.where(low, first, second)
    else:
        to = split_sum(halved_a, info[place], got, 0, kept_a, rows_a, send, 0, keep_a)
    gone = split_sum(halved_c, info[place], got, rows_a, kept_c, rows_c, send, to, keep_c)
    block = digit_block(add_digits(kept_c[rows_c:, :], got[rows_a + rows_c:, :].astype(F32)))
    keep_c[gone:, :] = block
    to += gone
    send[to:to + block.shape[0], :] = block.astype(BF16)
    to += block.shape[0]
    if to < send.shape[0]:
        send[to:, :] = jnp.zeros((send.shape[0] - to, LANES), BF16)


def last_kernel(rows_a, rows, info, got, kept_a, kept_c, sums_got, sums_kept, corr, pieces, mine):
    corr[...] = kept_a[...] + got[0:rows_a, :].astype(F32)
    pieces[...] = (kept_c[0:rows, :] + got[rows_a:rows_a + rows, :].astype(F32)).astype(BF16)
    block = digit_block(add_digits(kept_c[rows:, :], got[rows_a + rows:rows_a + kept_c.shape[0], :].astype(F32)))
    mine[0:rows, :] = pieces[...]
    mine[rows:kept_c.shape[0], :] = block.astype(BF16)
    at = kept_c.shape[0]
    count = sums_kept.shape[0] - 16
    number = count_of(sums_kept[count:, :].astype(F32), count) + count_of(sums_got[count:, :].astype(F32), count)
    square = (count, count)
    same = lax.broadcasted_iota(jnp.int32, square, 0) == lax.broadcasted_iota(jnp.int32, square, 1)
    tall = jnp.sum(jnp.where(same, jnp.broadcast_to(number, square), 0.0), 1, keepdims=True)
    total = sums_kept[0:count, :].astype(F32) + sums_got[0:count, :].astype(F32)
    means = (total / jnp.maximum(tall, 1.0)).astype(BF16)
    digits = count_rows(number, means.shape[1]).astype(BF16)
    for j in range(means.shape[1] // LANES):
        mine[at:at + count, :] = means[:, j * LANES:(j + 1) * LANES]
        mine[at + count:at + count + 16, :] = digits[:, j * LANES:(j + 1) * LANES]
        at += count + 16


def conv_out_kernel(total_frames, place, info, corr, proj, out, wide):
    rows = out.shape[0]
    flipped = jnp.transpose(corr[...])
    high = flipped.astype(BF16)
    low = (flipped - high.astype(F32)).astype(BF16)
    wide[...] = (nt(high, proj[...]) + nt(low, proj[...])) * (1.0 / total_frames)
    start = info[place]
    if rows % 8 == 0:
        out[...] = wide[pl.ds(pl.multiple_of(start, 8), rows), :]
    else:
        taken = wide[0:rows, :]
        for other in range(rows, wide.shape[0], rows):
            taken = jnp.where(start == other, wide[other:other + rows, :], taken)
        out[...] = taken


def out_kernel(total_frames, use_scale, dz, place, inner, extra, info, mine, *refs):
    parts, (out, bias, means, usage) = refs[:-4], refs[-4:]
    theirs = parts[1]
    scale = 1.0 / total_frames
    top = inner * dz
    value = add_digits(mine[top:top + extra, :].astype(F32), theirs[top:top + extra, :].astype(F32)) * scale
    for j in range(bias.shape[1] // LANES):
        bias[:, j * LANES:(j + 1) * LANES] = value[j:j + 1, :]
    bit = info[0]
    count = means.shape[1]
    numbers = []
    for ref, level in ((mine, bit), (theirs, 1 - bit)):
        at = top + extra
        blocks = []
        for j in range(dz // LANES):
            blocks.append(ref[at:at + count + 16, :])
            at += count + 16
        whole = jnp.concatenate(blocks, 1)
        means[level] = whole[0:count, :]
        numbers.append(count_of(whole[count:, :].astype(F32), count) * use_scale)
    usage[0:1, :] = jnp.where(bit == 1, numbers[1], numbers[0])
    usage[1:2, :] = jnp.where(bit == 1, numbers[0], numbers[1])
    for j, ref in enumerate(parts):
        for k in range(inner):
            start = pl.multiple_of((info[place + j] + k) * LANES, LANES)
            turned = jnp.transpose(ref[k * dz:(k + 1) * dz, :])
            out[pl.ds(start, LANES), :] = turned.astype(F32) * scale


def shifted(block, axis, distance):
    devices = range(lax.axis_size(axis))
    route = [(i - distance, i) for i in devices if i - distance in devices]
    return lax.ppermute(block, axis, route)


def swapped(block, steps):
    tm = lax.axis_size("tm")

    def partner(device):
        axis, bit = steps[(device // tm) & 1]
        return device ^ ((1 << bit) * (tm if axis == "dp" else 1))

    route = [(device, partner(device)) for device in range(lax.axis_size("dp") * tm)]
    return lax.ppermute(block, ("dp", "tm"), route)


def crossed(block, steps):
    tm = lax.axis_size("tm")

    def partner(device):
        axis, bit = steps[(device // tm) & 1]
        return device ^ tm ^ ((1 << bit) * (tm if axis == "dp" else 1))

    route = [(device, partner(device)) for device in range(lax.axis_size("dp") * tm)]
    return lax.ppermute(block, ("dp", "tm"), route)


def shards(feats, codes, conv_weight, conv_bias, proj_weight, codebooks):
    dp, tm = lax.axis_size("dp"), lax.axis_size("tm")
    rows_in, channels = feats.shape
    frames = rows_in // 2
    levels, book_size, dz = codebooks.shape
    assert levels == 2
    width = conv_weight.shape[0]
    total_frames = frames * dp * tm
    per_shard = book_size // tm
    dp_bits, tm_bits = log2(dp), log2(tm)
    owner_rows = width // (dp * tm)

    assert dp_bits >= 3 and 1 <= tm_bits <= 2
    pieces_a, pieces_c = width // LANES, channels // LANES
    under = max(dp_bits + tm_bits - log2(pieces_a), 0)
    c_bits = 2
    assert pieces_c >= 4
    whole_bits = [b for b in range(1, dp_bits) if b + tm_bits < under]
    piece_bits = [b for b in range(1, dp_bits) if b + tm_bits >= under]
    paths = [[("dp", b) for b in bits] for bits in (whole_bits + piece_bits, whole_bits[::-1] + piece_bits[::-1])]
    mixed = under == 1 and tm_bits == 2
    turned = mixed or under == 0 or under >= tm_bits
    up = [("tm", b) for b in range(tm_bits)]
    paths[0] += up[::-1]
    paths[1] += up if turned else up[::-1]
    exchanges = list(zip([("dp", 0)] + paths[0], [("dp", 0)] + paths[1]))
    sums_up = [("dp", b) for b in range(1, dp_bits)]
    sums_exchanges = list(zip(up + sums_up, up[::-1] + sums_up[::-1]))

    def piece_bit(step):
        axis, b = step
        bit = b + (tm_bits if axis == "dp" else 0)
        return bit - under if bit >= under else None

    a_split = [piece_bit(steps[0]) is not None for steps in exchanges]
    c_split = [log2(pieces_c) - 1 - k if k < c_bits else None for k in range(len(exchanges))]

    def order_of(split, count):
        used = [b for b in split if b is not None]
        return used + [b for b in reversed(range(log2(count))) if b not in used]

    orders = [order_of([piece_bit(steps[core]) for steps in exchanges], pieces_a) for core in range(2)]
    order_c = order_of(c_split, pieces_c)
    plan = [(pieces_a, orders, a_split[0]), (pieces_c, [order_c, order_c], True)]
    now_a = pieces_a // 2 if plan[0][2] else pieces_a
    now_c = pieces_c // 2

    count_bits, count_places = len(exchanges), 4
    at_start = count_bits
    at_codes = at_start + 1
    at_pieces = at_codes + tm
    at_sums = at_pieces + count_places
    at_row = at_sums + len(sums_exchanges)

    def info():
        at_dp, at_tm = lax.axis_index("dp"), lax.axis_index("tm")
        core = at_dp & 1

        def on_core(values):
            return values[0] + core * (values[1] - values[0])

        def bit_at(step):
            axis, b = step
            return ((at_dp if axis == "dp" else at_tm) >> b) & 1

        bits = [on_core([bit_at(step) for step in steps]) for steps in exchanges]
        sums_bits = [on_core([bit_at(step) for step in steps]) for steps in sums_exchanges]
        shared = [bit_at(step) for step in exchanges[1]]
        mine_c, other_c = on_core(shared), on_core(shared[::-1])
        places = [2 * core + mine_c, 2 * (1 - core) + other_c, 2 * core + 1 - mine_c, 2 * (1 - core) + 1 - other_c]
        places = [place << (log2(pieces_c) - c_bits) for place in places]
        lists = []
        for way in ([b for _, b in up], [b for _, b in up[::-1]]):
            lists.append([sum(((position >> (tm_bits - 1 - j)) & 1) << b for j, b in enumerate(way)) for position in range(tm)])
        first_bit = on_core([0, tm_bits - 1])
        lead = (at_tm >> first_bit) & 1
        quarters = [on_core([lists[0][j], lists[1][j]]) for j in range(tm // 2)]
        send_codes = [(q + ((1 - lead) << first_bit)) * per_shard for q in quarters]
        keep_codes = [(q + (lead << first_bit)) * per_shard for q in quarters]
        differ = at_tm ^ (at_tm + 1)
        ways = [sum(((differ >> b) & 1) << j for j, b in enumerate(way)) for way in (
            list(range(tm_bits)), list(reversed(range(tm_bits))))]
        row_code = jnp.where(at_tm + 1 < tm, on_core(ways), 0)
        if turned and not mixed:
            start = ((at_dp * tm + at_tm) * owner_rows) & (LANES - 1)
        else:
            start = on_core([(at_dp * tm + at_tm) * owner_rows, (at_tm >> 1) * owner_rows if mixed else (
                at_dp * tm + at_tm) * owner_rows]) & (LANES - 1)
        return bits + [start] + send_codes + keep_codes + places + sums_bits + [row_code]

    halo = shifted(call(halo_kernel, shape((2, channels), BF16), [info, feats[-2:]], flops=10 ** 11), "tm", 1)
    weight, proj, codes = conv_weight, proj_weight, codes[0]
    extra = 4 * (-(-channels // LANES // 8) * 8)
    code_rows = -(-(2 * -(-frames // dz)) // 16) * 16
    corr_rows = (now_a + now_c) * dz
    rows_b = frames + code_rows
    shared = [shape((frames, width), BF16), shape((frames, channels), BF16), shape((frames, dz), BF16),
              shape((dz, frames), BF16), shape((rows_b, dz), BF16),
              shape((rows_b * (dz // LANES), LANES), BF16)]
    *arrays, first, part = call(
        functools.partial(local_kernel, plan),
        shared + [shape((16, channels), F32), shape((corr_rows + 32 * (dz // LANES), LANES), F32)],
        [info, feats, weight, conv_bias[None, :], codes, codebooks, proj],
        scratch=[VMEM((channels // LANES, rows_in + 8, LANES), F32), VMEM((levels, frames, dz), BF16)],
    )
    unfold, hidden, latent_grad, flipped, own, send_sums, send = call(
        functools.partial(frame_kernel, plan),
        shared + [shape((corr_rows, LANES), BF16)],
        [info, halo, first, part, weight, proj] + arrays,
        aliases={6 + k: k for k in range(len(shared))},
    )
    got = swapped(send, exchanges[0])
    keep_a, keep_c, hidden_grad, extras, row = call(
        functools.partial(rest_kernel, plan),
        [shape((now_a * dz, LANES), F32), shape((now_c * dz, LANES), F32), shape((frames, channels), BF16),
         shape((extra, LANES), F32), shape((16, channels), BF16)],
        [info, flipped, unfold, hidden, latent_grad, proj],
        after=[send],
    )

    def halves_at(k):
        nonlocal now_a, now_c
        halves = [(now_a * dz, a_split[k]), (now_c * dz, c_split[k] is not None)]
        now_a = now_a // 2 if halves[0][1] else now_a
        now_c = now_c // 2 if halves[1][1] else now_c
        return halves, now_a * dz, now_c * dz + extra

    size = per_shard + 16
    sums_rows = size * (tm // 2)
    got_core = swapped(send_sums, exchanges[0])

    def own_sums(first, after):
        return call(
            functools.partial(own_sums_kernel, frames, at_codes + first, per_shard),
            shape((sums_rows, dz), F32),
            [info, own],
            after=after)

    def both_sums(first, base, dtype, after):
        return call(
            functools.partial(sums_kernel, 0, frames, at_codes + first, per_shard),
            shape((sums_rows, dz), dtype),
            [info, got_core, base, row],
            after=after)

    base = own_sums(0, [extras])
    halves, rows_a, rows_c = halves_at(1)
    send, keep_a, keep_c = call(
        functools.partial(first_step_kernel, halves, 1),
        [shape((rows_a + rows_c, LANES), BF16), shape((rows_a, LANES), F32), shape((rows_c, LANES), F32)],
        [info, got, keep_a, keep_c, extras],
        after=[base])
    sums_send = both_sums(0, base, BF16, [send])
    sums_keep = both_sums(tm // 2, own_sums(tm // 2, [sums_send]), F32, [])
    sums_got = swapped(sums_send, sums_exchanges[0])
    got = swapped(send, exchanges[1])
    known = row
    ordered = [sums_keep]
    for k in range(2, len(exchanges)):
        halves, rows_a, rows_c = halves_at(k)
        spare = 16 * (k == len(exchanges) - 1)
        send, keep_a, keep_c = call(
            functools.partial(step_kernel, halves, k, mixed and k == dp_bits),
            [shape((rows_a + rows_c + spare, LANES), BF16), shape((rows_a, LANES), F32), shape((rows_c, LANES), F32)],
            [info, got, keep_a, keep_c],
            after=ordered)
        got = swapped(send, exchanges[k])
        halved = sums_exchanges[k - 1][0][0] == "tm"
        sums_rows = sums_rows // 2 if halved else sums_rows
        row_step = k - 2 if k - 2 < tm_bits else None
        outs = call(
            functools.partial(sums_step_kernel, halved, at_sums + k - 1, row_step, (per_shard, at_row)),
            [shape((sums_rows, dz), BF16), shape((sums_rows, dz), F32)]
            + [shape((16, channels), BF16)] * (row_step is not None),
            [info, sums_got, sums_keep] + [known] * (row_step is not None),
            after=[send])
        sums_send, sums_keep = outs[:2]
        known = outs[2] if row_step is not None else known
        sums_got = swapped(sums_send, sums_exchanges[k - 1])
        ordered = [sums_send]
    assert now_a == 1 and sums_rows == size
    feat_grad, last = call(
        feat_kernel,
        shape((rows_in, channels), BF16),
        [info, hidden_grad, known, weight],
        after=[sums_send],
        token=True,
        scratch=[VMEM((frames + 8, channels), F32), VMEM((channels // LANES, rows_in, LANES), F32)],
    )

    corr, piece, mine = call(
        functools.partial(last_kernel, rows_a, rows_c - extra),
        [shape((rows_a, LANES), F32), shape((rows_c - extra, LANES), BF16),
         shape((rows_c + size * (dz // LANES), LANES), BF16)],
        [info, got, keep_a, keep_c, sums_got, sums_keep],
        after=[last])
    parts = [piece, swapped(mine, exchanges[0]), swapped(piece, exchanges[1]), crossed(piece, exchanges[1])]
    conv_grad, last = call(
        functools.partial(conv_out_kernel, total_frames, at_start),
        shape((owner_rows, channels), F32),
        [info, corr, proj],
        after=[piece],
        token=True,
        scratch=[VMEM((LANES, channels), F32)],
    )
    proj_grad, bias_grad, code_means, code_usage = call(
        functools.partial(out_kernel, total_frames, book_size / total_frames, dz, at_pieces, now_c, extra),
        [shape((channels, dz), F32), shape((1, channels), F32), shape((levels, per_shard, dz), BF16),
         shape((levels, per_shard), F32)],
        [info, mine] + parts,
        after=[last],
    )
    return feat_grad, conv_grad, bias_grad[0], proj_grad, code_means, code_usage


def solution(mesh):
    placed = (P(("dp", "tm"), None), P("dp", None, "tm"), P(), P(), P(), P())
    return jax.shard_map(
        shards,
        mesh=mesh,
        in_specs=placed,
        out_specs=(
            P(("dp", "tm"), None),
            P(("dp", "tm"), None),
            P(),
            P(),
            P(None, "tm", None),
            P(None, "tm"),
        ),
        check_vma=False,
    )
```

```python
import functools

import jax
import jax.numpy as jnp
from jax import lax
from jax.experimental import pallas as pl
from jax.experimental.pallas import tpu as pltpu
from jax.sharding import PartitionSpec as P

BF16 = jnp.bfloat16
F32 = jnp.float32
LANES = 128
VMEM_LIMIT = 16 * 1024 * 1024


def log2(value):
    assert value & (value - 1) == 0
    return value.bit_length() - 1


def nn(a, b):
    return lax.dot_general(a, b, (((1,), (0,)), ((), ())), preferred_element_type=F32)


def nt(a, b):
    return lax.dot_general(a, b, (((1,), (1,)), ((), ())), preferred_element_type=F32)


VMEM = pltpu.VMEM


def call(body, out_shape, args, after=(), scratch=(), aliases=None, token=False, flops=0):
    info, args = args[0], args[1:]
    count = len(args)
    many = isinstance(out_shape, (list, tuple))
    shapes = list(out_shape) if many else [out_shape]

    def kernel(*refs):
        ends = count + len(after)
        if token:
            refs[ends + len(shapes)][...] = jnp.zeros((8, LANES), F32)
            refs = refs[:ends + len(shapes)] + refs[ends + len(shapes) + 1:]
        body(info(), *refs[:count], *refs[ends:])

    specs = [pl.BlockSpec(memory_space=VMEM)] * count + [pl.BlockSpec(memory_space=pl.ANY)] * len(after)
    shown = shapes + [shape((8, LANES), F32)] * token
    outs = pl.pallas_call(
        kernel,
        out_shape=shown,
        in_specs=specs,
        out_specs=[pl.BlockSpec(memory_space=VMEM)] * len(shown),
        scratch_shapes=list(scratch),
        input_output_aliases={at - 1: out for at, out in (aliases or {}).items()},
        compiler_params=pltpu.CompilerParams(vmem_limit_bytes=VMEM_LIMIT),
        cost_estimate=pl.CostEstimate(flops=flops, bytes_accessed=0, transcendentals=0),
    )(*args, *after)
    return outs if len(shown) > 1 else outs[0]


def shape(dims, dtype):
    return jax.ShapeDtypeStruct(dims, dtype)


def digits_of(value):
    high = value.astype(BF16).astype(F32)
    rest = value - high
    middle = rest.astype(BF16).astype(F32)
    low = (rest - middle).astype(BF16).astype(F32)
    return high, middle, low


def one_hot(codes, axis_codes, first, count):
    frames = codes.shape[1 - axis_codes]
    dims = (count, frames) if axis_codes == 0 else (frames, count)
    places = lax.broadcasted_iota(jnp.int32, dims, axis_codes) + first
    return jnp.where(codes == places, 1.0, 0.0).astype(BF16)


def halo_kernel(info, rows, out):
    out[...] = rows[...]


def walk(orders, halved, count):
    start = 1 if halved else 0
    shown = count // 2 if halved else count
    bits = log2(shown)
    step = 2 if shown > 1 and all(order[-1] == 0 for order in orders) else 1
    for position in range(0, shown, step):
        yield position, [
            sum(((position >> (bits - 1 - k)) & 1) << bit for k, bit in enumerate(order[start:])) for order in orders
        ], step


def correlate(flipped, sources, plan, core, bit, out):
    dz = flipped.shape[0]
    at = 0
    for source, (count, orders, halved) in zip(sources, plan):
        for position, pieces, step in walk(orders, halved, count):
            column = pieces[0] + core * (pieces[1] - pieces[0])
            if halved:
                column = column + (bit << orders[0][0])
            column = pl.multiple_of(column * LANES, LANES)
            product = nn(flipped, source[:, pl.ds(column, step * LANES)])
            for j in range(step):
                top = (at + position + j) * dz
                out[top:top + dz, :] = product[:, j * LANES:(j + 1) * LANES].astype(out.dtype)
        at += count // 2 if halved else count
    return at * dz


def code_digits(codes, dz, rows):
    parts = []
    for part in (codes >> 8, codes & 255):
        for start in range(0, codes.shape[1], dz):
            piece = part[:, start:start + dz].astype(F32)
            if piece.shape[1] < dz:
                piece = jnp.concatenate([piece, jnp.zeros((1, dz - piece.shape[1]), F32)], 1)
            parts.append(piece)
    parts.append(jnp.zeros((rows - len(parts), dz), F32))
    return jnp.concatenate(parts, 0).astype(BF16)


def codes_of(block, frames):
    dz = block.shape[1]
    per = -(-frames // dz)
    digits = block[...].astype(F32)
    parts = [jnp.concatenate([digits[k * per + j:k * per + j + 1, :] for j in range(per)], 1)[:, :frames]
             for k in range(2)]
    return (parts[0] * 256.0 + parts[1]).astype(jnp.int32)


def residuals(hidden, proj, chosen):
    latent = nn(hidden, proj)
    once = latent - chosen[0].astype(F32)
    total = once + (once - chosen[1].astype(F32))
    return latent, once, total.astype(BF16)


def put_columns(out, at, rows, block):
    for j in range(block.shape[1] // LANES):
        out[at + j * rows:at + j * rows + block.shape[0], :] = block[:, j * LANES:(j + 1) * LANES]


def local_kernel(plan, info, feats, weight, bias, codes, books, proj,
                 unfold, hidden, latent_grad, flipped, own, send_sums, first, part, wide, chosen):
    rows, channels = feats.shape
    frames = rows // 2
    dz = proj.shape[1]
    for j in range(channels // LANES):
        wide[j, 0:8, :] = jnp.zeros((8, LANES), F32)
        wide[j, 8:, :] = feats[:, j * LANES:(j + 1) * LANES].astype(F32)
        for tap in range(4):
            start = tap * channels + j * LANES
            unfold[:, start:start + LANES] = wide[j, pl.ds(6 + tap, frames, stride=2), :].astype(BF16)
    conv = nn(unfold[...], weight[...]) + bias[...]
    first[...] = conv[0:16, :]
    hidden[...] = conv.astype(BF16)
    levels = books.shape[0]
    padded = jnp.concatenate([codes[...].astype(F32), jnp.zeros((8 - levels, frames), F32)], 0)
    tall = jnp.transpose(padded).astype(jnp.int32)
    for level in range(levels):
        matches = one_hot(tall[:, level:level + 1], 1, 0, books.shape[1])
        chosen[level] = nn(matches, books[level]).astype(BF16)
    latent, once, grad = residuals(hidden[...], proj[...], chosen)
    latent_grad[...] = grad
    row = lax.broadcasted_iota(jnp.int32, grad.shape, 0)
    flipped[...] = jnp.transpose(jnp.where(row == 0, 0.0, grad.astype(F32))).astype(BF16)
    bit = info[0]
    at = correlate(flipped[...], (unfold, hidden), plan, 1 - bit, 1 - bit, part)
    rows_b = own.shape[0]
    code_rows = rows_b - frames
    digits = [code_digits(codes[level:level + 1, :], dz, code_rows) for level in range(2)]
    own[0:frames, :] = jnp.where(bit == 1, once, latent).astype(BF16)
    own[frames:, :] = jnp.where(bit == 1, digits[1], digits[0])
    put_columns(send_sums, 0, rows_b, jnp.where(bit == 1, latent, once).astype(BF16))
    put_columns(send_sums, frames, rows_b, jnp.where(bit == 1, digits[0], digits[1]))
    for level in range(levels):
        part[at + level * 16 * (dz // LANES):at + (level + 1) * 16 * (dz // LANES), :] = jnp.concatenate(
            [chosen[level, 0:16, j * LANES:(j + 1) * LANES].astype(F32) for j in range(dz // LANES)], 0)


def frame_kernel(plan, info, halo, first, part, weight, proj, unfold_in, hidden_in, grad_in, flipped_in, own_in, sums_in,
                 unfold, hidden, latent_grad, flipped, own, send_sums, send):
    width = unfold.shape[1]
    half = width // 2
    dz = proj.shape[1]
    row = lax.broadcasted_iota(jnp.int32, (16, half), 0)
    left = jnp.concatenate([halo[0:1, :], halo[1:2, :]], 1).astype(F32)
    head = jnp.where(row == 0, jnp.broadcast_to(left, (16, half)), 0.0)
    unfold[0:16, 0:half] = (unfold_in[0:16, 0:half].astype(F32) + head).astype(BF16)
    fix = nn(head.astype(BF16), weight[0:half, :])
    hidden[0:16, :] = (first[...] + fix).astype(BF16)
    top = hidden[0:16, :]
    pieces = part.shape[0] - 32 * (dz // LANES)
    chosen = []
    for level in range(2):
        at = pieces + level * 16 * (dz // LANES)
        chosen.append(jnp.concatenate([part[at + j * 16:at + (j + 1) * 16, :] for j in range(dz // LANES)], 1))
    latent, once, grad = residuals(top, proj[...], chosen)
    latent_grad[0:16, :] = grad
    flipped[:, 0:LANES] = jnp.transpose(latent_grad[0:LANES, :].astype(F32)).astype(BF16)
    column = flipped[:, 0:LANES].astype(F32)[:, 0:1]
    bit = info[0]
    at = 0
    for source, (count, orders, halved) in zip((unfold, hidden), plan):
        rows = source[0:16, :].astype(F32)[0:1, :]
        for position, places, step in walk(orders, halved, count):
            for j in range(step):
                offsets = [places[0] + j, places[1] + j]
                low = [offset for offset in offsets]
                high = [offset + (1 << orders[0][0] if halved else 0) for offset in offsets]
                picked = [rows[:, k * LANES:(k + 1) * LANES] for k in low + high]
                piece = jnp.where(bit == 1, picked[0], picked[3]) if halved else jnp.where(bit == 1, picked[0], picked[1])
                begin = (at + position + j) * dz
                send[begin:begin + dz, :] = (part[begin:begin + dz, :] + column * piece).astype(BF16)
        at += count // 2 if halved else count
    rows_b = own.shape[0]
    own[0:16, :] = jnp.where(bit == 1, once, latent).astype(BF16)
    put_columns(send_sums, 0, rows_b, jnp.where(bit == 1, latent, once).astype(BF16))


def rest_kernel(plan, info, flipped, unfold, hidden, latent_grad, proj, keep_a, keep_c, hidden_grad, extras, row):
    bit = info[0]
    correlate(flipped[...], (unfold,), plan[:1], bit, bit, keep_a)
    correlate(flipped[...], (hidden,), plan[1:], bit, bit, keep_c)
    back = nt(latent_grad[...], proj[...]).astype(BF16)
    hidden_grad[...] = back
    row[...] = back[0:16, :]
    stride = extras.shape[0] // 4
    extras[...] = jnp.zeros(extras.shape, F32)
    sums = jnp.sum(back.astype(F32), 0, keepdims=True)
    for digit, part in enumerate(digits_of(sums)):
        for j in range(sums.shape[1] // LANES):
            extras[digit * stride + j:digit * stride + j + 1, :] = part[:, j * LANES:(j + 1) * LANES]


def split_sum(halved, bit, got, at, kept, rows, send, to, keep):
    if halved:
        half = rows // 2
        away = pl.multiple_of((1 - bit) * half, 16)
        home = pl.multiple_of(bit * half, 16)
        send[to:to + half, :] = (kept[pl.ds(away, half), :] + got[pl.ds(at + away, half), :].astype(F32)).astype(BF16)
        keep[0:half, :] = kept[pl.ds(home, half), :] + got[pl.ds(at + home, half), :].astype(F32)
        return half
    total = (kept[0:rows, :] + got[at:at + rows, :].astype(F32)).astype(BF16)
    send[to:to + rows, :] = total
    keep[0:rows, :] = total.astype(F32)
    return rows


def add_digits(mine, theirs):
    stride = mine.shape[0] // 4
    return ((mine[0:stride] + mine[stride:2 * stride]) + mine[2 * stride:3 * stride]) + (
        (theirs[0:stride] + theirs[stride:2 * stride]) + theirs[2 * stride:3 * stride])


def digit_block(value):
    return jnp.concatenate(list(digits_of(value)) + [jnp.zeros_like(value)], 0)


def first_step_kernel(halves, place, info, got, kept_a, kept_c, extras, send, keep_a, keep_c):
    (rows_a, halved_a), (rows_c, halved_c) = halves
    to = split_sum(halved_a, info[place], got, 0, kept_a, rows_a, send, 0, keep_a)
    gone = split_sum(halved_c, info[place], got, rows_a, kept_c, rows_c, send, to, keep_c)
    send[to + gone:, :] = extras[...].astype(BF16)
    keep_c[gone:, :] = extras[...]


def feat_kernel(info, grad, after, weight, out, wide, inter):
    frames, channels = grad.shape
    half = weight.shape[0] // 2
    wide[0:frames, :] = grad[...].astype(F32)
    wide[frames:, :] = jnp.broadcast_to(after[0:1, :].astype(F32), (8, channels))
    ahead = wide[pl.ds(1, frames), :].astype(BF16)
    for parity in range(2):
        rows = pl.ds(parity * (half // 2), half // 2)
        rows_after = pl.ds(half + parity * (half // 2), half // 2)
        both = nt(ahead, weight[rows, :]) + nt(grad[...], weight[rows_after, :])
        for j in range(channels // LANES):
            inter[j, pl.ds(parity, frames, stride=2), :] = both[:, j * LANES:(j + 1) * LANES]
    for j in range(channels // LANES):
        out[:, j * LANES:(j + 1) * LANES] = inter[j].astype(BF16)


def own_sums_kernel(frames, place, count, info, own, out):
    codes = codes_of(own[frames:, :], frames)
    ones = jnp.ones((8, frames), BF16)
    size = count + 16
    for top in range(0, out.shape[0], size):
        matches = one_hot(codes, 0, info[place], count)
        out[top:top + count, :] = nn(matches, own[0:frames, :])
        out[top + count:top + count + 8, 0:count] = nt(ones, matches)
        place += 1


def sums_kernel(first, frames, place, count, info, got, base, row, out):
    dz = base.shape[1]
    rows = (got.shape[0] - first) // (dz // LANES)
    theirs = jnp.concatenate([got[first + j * rows:first + (j + 1) * rows, :] for j in range(dz // LANES)], 1)
    codes = codes_of(theirs[frames:, :], frames)
    ones = jnp.ones((8, frames), BF16)
    size = count + 16
    riding = [row[...].astype(F32)[0:1, :]]
    for top in range(0, out.shape[0], size):
        matches = one_hot(codes, 0, info[place], count)
        total = base[top:top + count, :] + nn(matches, theirs[0:frames, :])
        counts = base[top + count:top + count + 8, 0:count] + nt(ones, matches)
        out[top:top + count, :] = total.astype(out.dtype)
        out[top + count:top + size, :] = count_rows(counts[0:1], dz, riding).astype(out.dtype)
        place += 1


def count_rows(count, width, riding=()):
    high = jnp.floor(count * (1.0 / 65536.0))
    rest = count - high * 65536.0
    middle = jnp.floor(rest * (1.0 / 256.0))
    low = rest - middle * 256.0
    block = jnp.concatenate([high, middle, low], 0)
    if count.shape[1] < width:
        block = jnp.concatenate([block, jnp.zeros((3, width - count.shape[1]), F32)], 1)
    parts = [block]
    for row in riding:
        parts += [row[:, at:at + width] for at in range(0, row.shape[1], width)]
    left = 16 - sum(part.shape[0] for part in parts)
    return jnp.concatenate(parts + [jnp.zeros((left, width), F32)] * (left > 0), 0)


def riding_row(block, index, parts):
    return jnp.concatenate([block[3 + index * parts + j:4 + index * parts + j, :] for j in range(parts)], 1)


def count_of(block, own):
    return (block[0:1] * 65536.0 + block[1:2] * 256.0 + block[2:3])[:, :own]


def sums_step_kernel(halved, place, row_step, row_place, info, got, kept, *refs):
    riding = ()
    if row_step is not None:
        known, refs = refs[0][...].astype(F32), refs[1:]
        after, refs = refs[-1], refs[:-1]
        parts = known.shape[1] // got.shape[1]
        block = got[row_place[0]:row_place[0] + 16, :].astype(F32)
        rows = [known[j:j + 1, :] for j in range(1 << row_step)]
        rows += [riding_row(block, j, parts) for j in range(1 << row_step)]
        if halved:
            riding = rows
            total = rows + [jnp.zeros((16 - len(rows), known.shape[1]), F32)]
            after[...] = jnp.concatenate(total, 0).astype(BF16)
        else:
            wide = jnp.zeros(after.shape, F32)
            for j in range(1, len(rows)):
                wide = jnp.where(info[row_place[1]] == j, jnp.broadcast_to(rows[j], after.shape), wide)
            after[...] = wide.astype(BF16)
    send, keep = refs
    dz = got.shape[1]
    bit = info[place]
    half = kept.shape[0] // 2 if halved else 0
    outs = [(send, (1 - bit) * half), (keep, bit * half)] if halved else [(send, 0)]
    count = row_place[0]
    size = count + 16
    for out, start in outs:
        for top in range(0, keep.shape[0], size):
            here = top + pl.multiple_of(start, 16) if halved else top
            sums = pl.ds(here, count)
            tail = pl.ds(here + count, 16)
            value = kept[sums, :].astype(F32) + got[sums, :].astype(F32)
            number = count_of(kept[tail, :].astype(F32), count) + count_of(got[tail, :].astype(F32), count)
            out[top:top + count, :] = value.astype(out.dtype)
            out[top + count:top + size, :] = count_rows(number, dz, riding).astype(out.dtype)
    if not halved:
        keep[...] = send[0:keep.shape[0], :].astype(F32)


def swap_halves(first, second, core):
    half = LANES // 2
    left = lax.broadcasted_iota(jnp.int32, first.shape, 1) < half
    turned_first, turned_second = pltpu.roll(first, half, 1), pltpu.roll(second, half, 1)
    swapped_first = jnp.where(left, first, turned_second)
    swapped_second = jnp.where(left, turned_first, second)
    return jnp.where(core == 1, swapped_first, first), jnp.where(core == 1, swapped_second, second)


def step_kernel(halves, place, mixed, info, got, kept_a, kept_c, send, keep_a, keep_c):
    (rows_a, halved_a), (rows_c, halved_c) = halves
    if mixed:
        to = rows_a // 2
        total = kept_a[0:rows_a, :] + got[0:rows_a, :].astype(F32)
        first, second = swap_halves(total[0:to, :], total[to:, :], info[0])
        low = info[place] == 0
        send[0:to, :] = jnp.where(low, second, first).astype(BF16)
        keep_a[...] = jnp.where(low, first, second)
    else:
        to = split_sum(halved_a, info[place], got, 0, kept_a, rows_a, send, 0, keep_a)
    gone = split_sum(halved_c, info[place], got, rows_a, kept_c, rows_c, send, to, keep_c)
    block = digit_block(add_digits(kept_c[rows_c:, :], got[rows_a + rows_c:, :].astype(F32)))
    keep_c[gone:, :] = block
    to += gone
    send[to:to + block.shape[0], :] = block.astype(BF16)
    to += block.shape[0]
    if to < send.shape[0]:
        send[to:, :] = jnp.zeros((send.shape[0] - to, LANES), BF16)


def last_kernel(rows_a, rows, info, got, kept_a, kept_c, sums_got, sums_kept, corr, pieces, mine):
    corr[...] = kept_a[...] + got[0:rows_a, :].astype(F32)
    pieces[...] = (kept_c[0:rows, :] + got[rows_a:rows_a + rows, :].astype(F32)).astype(BF16)
    block = digit_block(add_digits(kept_c[rows:, :], got[rows_a + rows:rows_a + kept_c.shape[0], :].astype(F32)))
    mine[0:rows, :] = pieces[...]
    mine[rows:kept_c.shape[0], :] = block.astype(BF16)
    at = kept_c.shape[0]
    count = sums_kept.shape[0] - 16
    number = count_of(sums_kept[count:, :].astype(F32), count) + count_of(sums_got[count:, :].astype(F32), count)
    square = (count, count)
    same = lax.broadcasted_iota(jnp.int32, square, 0) == lax.broadcasted_iota(jnp.int32, square, 1)
    tall = jnp.sum(jnp.where(same, jnp.broadcast_to(number, square), 0.0), 1, keepdims=True)
    total = sums_kept[0:count, :].astype(F32) + sums_got[0:count, :].astype(F32)
    means = (total / jnp.maximum(tall, 1.0)).astype(BF16)
    digits = count_rows(number, means.shape[1]).astype(BF16)
    for j in range(means.shape[1] // LANES):
        mine[at:at + count, :] = means[:, j * LANES:(j + 1) * LANES]
        mine[at + count:at + count + 16, :] = digits[:, j * LANES:(j + 1) * LANES]
        at += count + 16


def conv_out_kernel(total_frames, place, info, corr, proj, out, wide):
    rows = out.shape[0]
    flipped = jnp.transpose(corr[...])
    high = flipped.astype(BF16)
    low = (flipped - high.astype(F32)).astype(BF16)
    wide[...] = (nt(high, proj[...]) + nt(low, proj[...])) * (1.0 / total_frames)
    start = info[place]
    if rows % 8 == 0:
        out[...] = wide[pl.ds(pl.multiple_of(start, 8), rows), :]
    else:
        taken = wide[0:rows, :]
        for other in range(rows, wide.shape[0], rows):
            taken = jnp.where(start == other, wide[other:other + rows, :], taken)
        out[...] = taken


def means_out_kernel(total_frames, use_scale, dz, inner, extra, info, mine, theirs, bias, means, usage):
    scale = 1.0 / total_frames
    top = inner * dz
    value = add_digits(mine[top:top + extra, :].astype(F32), theirs[top:top + extra, :].astype(F32)) * scale
    for j in range(bias.shape[1] // LANES):
        bias[:, j * LANES:(j + 1) * LANES] = value[j:j + 1, :]
    bit = info[0]
    count = means.shape[1]
    numbers = []
    for ref, level in ((mine, bit), (theirs, 1 - bit)):
        at = top + extra
        blocks = []
        for j in range(dz // LANES):
            blocks.append(ref[at:at + count + 16, :])
            at += count + 16
        whole = jnp.concatenate(blocks, 1)
        means[level] = whole[0:count, :]
        numbers.append(count_of(whole[count:, :].astype(F32), count) * use_scale)
    usage[0:1, :] = jnp.where(bit == 1, numbers[1], numbers[0])
    usage[1:2, :] = jnp.where(bit == 1, numbers[0], numbers[1])


def proj_out_kernel(total_frames, dz, place, inner, info, *refs):
    parts, out = refs[:-1], refs[-1]
    scale = 1.0 / total_frames
    for j, ref in enumerate(parts):
        for k in range(inner):
            start = pl.multiple_of((info[place + j] + k) * LANES, LANES)
            turned = jnp.transpose(ref[k * dz:(k + 1) * dz, :])
            out[pl.ds(start, LANES), :] = turned.astype(F32) * scale


def shifted(block, axis, distance):
    devices = range(lax.axis_size(axis))
    route = [(i - distance, i) for i in devices if i - distance in devices]
    return lax.ppermute(block, axis, route)


def swapped(block, steps):
    tm = lax.axis_size("tm")

    def partner(device):
        axis, bit = steps[(device // tm) & 1]
        return device ^ ((1 << bit) * (tm if axis == "dp" else 1))

    route = [(device, partner(device)) for device in range(lax.axis_size("dp") * tm)]
    return lax.ppermute(block, ("dp", "tm"), route)


def crossed(block, steps):
    tm = lax.axis_size("tm")

    def partner(device):
        axis, bit = steps[(device // tm) & 1]
        return device ^ tm ^ ((1 << bit) * (tm if axis == "dp" else 1))

    route = [(device, partner(device)) for device in range(lax.axis_size("dp") * tm)]
    return lax.ppermute(block, ("dp", "tm"), route)


def shards(feats, codes, conv_weight, conv_bias, proj_weight, codebooks):
    dp, tm = lax.axis_size("dp"), lax.axis_size("tm")
    rows_in, channels = feats.shape
    frames = rows_in // 2
    levels, book_size, dz = codebooks.shape
    assert levels == 2
    width = conv_weight.shape[0]
    total_frames = frames * dp * tm
    per_shard = book_size // tm
    dp_bits, tm_bits = log2(dp), log2(tm)
    owner_rows = width // (dp * tm)

    assert dp_bits >= 3 and 1 <= tm_bits <= 2
    pieces_a, pieces_c = width // LANES, channels // LANES
    under = max(dp_bits + tm_bits - log2(pieces_a), 0)
    c_bits = 2
    assert pieces_c >= 4
    whole_bits = [b for b in range(1, dp_bits) if b + tm_bits < under]
    piece_bits = [b for b in range(1, dp_bits) if b + tm_bits >= under]
    paths = [[("dp", b) for b in bits] for bits in (whole_bits + piece_bits, whole_bits[::-1] + piece_bits[::-1])]
    mixed = under == 1 and tm_bits == 2
    turned = mixed or under == 0 or under >= tm_bits
    up = [("tm", b) for b in range(tm_bits)]
    paths[0] += up[::-1]
    paths[1] += up if turned else up[::-1]
    exchanges = list(zip([("dp", 0)] + paths[0], [("dp", 0)] + paths[1]))
    sums_up = [("dp", b) for b in range(1, dp_bits)]
    sums_exchanges = list(zip(up + sums_up, up[::-1] + sums_up[::-1]))

    def piece_bit(step):
        axis, b = step
        bit = b + (tm_bits if axis == "dp" else 0)
        return bit - under if bit >= under else None

    a_split = [piece_bit(steps[0]) is not None for steps in exchanges]
    c_split = [log2(pieces_c) - 1 - k if k < c_bits else None for k in range(len(exchanges))]

    def order_of(split, count):
        used = [b for b in split if b is not None]
        return used + [b for b in reversed(range(log2(count))) if b not in used]

    orders = [order_of([piece_bit(steps[core]) for steps in exchanges], pieces_a) for core in range(2)]
    order_c = order_of(c_split, pieces_c)
    plan = [(pieces_a, orders, a_split[0]), (pieces_c, [order_c, order_c], True)]
    now_a = pieces_a // 2 if plan[0][2] else pieces_a
    now_c = pieces_c // 2

    count_bits, count_places = len(exchanges), 4
    at_start = count_bits
    at_codes = at_start + 1
    at_pieces = at_codes + tm
    at_sums = at_pieces + count_places
    at_row = at_sums + len(sums_exchanges)

    def info():
        at_dp, at_tm = lax.axis_index("dp"), lax.axis_index("tm")
        core = at_dp & 1

        def on_core(values):
            return values[0] + core * (values[1] - values[0])

        def bit_at(step):
            axis, b = step
            return ((at_dp if axis == "dp" else at_tm) >> b) & 1

        bits = [on_core([bit_at(step) for step in steps]) for steps in exchanges]
        sums_bits = [on_core([bit_at(step) for step in steps]) for steps in sums_exchanges]
        shared = [bit_at(step) for step in exchanges[1]]
        mine_c, other_c = on_core(shared), on_core(shared[::-1])
        places = [2 * core + mine_c, 2 * (1 - core) + other_c, 2 * core + 1 - mine_c, 2 * (1 - core) + 1 - other_c]
        places = [place << (log2(pieces_c) - c_bits) for place in places]
        lists = []
        for way in ([b for _, b in up], [b for _, b in up[::-1]]):
            lists.append([sum(((position >> (tm_bits - 1 - j)) & 1) << b for j, b in enumerate(way)) for position in range(tm)])
        first_bit = on_core([0, tm_bits - 1])
        lead = (at_tm >> first_bit) & 1
        quarters = [on_core([lists[0][j], lists[1][j]]) for j in range(tm // 2)]
        send_codes = [(q + ((1 - lead) << first_bit)) * per_shard for q in quarters]
        keep_codes = [(q + (lead << first_bit)) * per_shard for q in quarters]
        differ = at_tm ^ (at_tm + 1)
        ways = [sum(((differ >> b) & 1) << j for j, b in enumerate(way)) for way in (
            list(range(tm_bits)), list(reversed(range(tm_bits))))]
        row_code = jnp.where(at_tm + 1 < tm, on_core(ways), 0)
        if turned and not mixed:
            start = ((at_dp * tm + at_tm) * owner_rows) & (LANES - 1)
        else:
            start = on_core([(at_dp * tm + at_tm) * owner_rows, (at_tm >> 1) * owner_rows if mixed else (
                at_dp * tm + at_tm) * owner_rows]) & (LANES - 1)
        return bits + [start] + send_codes + keep_codes + places + sums_bits + [row_code]

    halo = shifted(call(halo_kernel, shape((2, channels), BF16), [info, feats[-2:]], flops=10 ** 11), "tm", 1)
    weight, proj, codes = conv_weight, proj_weight, codes[0]
    extra = 4 * (-(-channels // LANES // 8) * 8)
    code_rows = -(-(2 * -(-frames // dz)) // 16) * 16
    corr_rows = (now_a + now_c) * dz
    rows_b = frames + code_rows
    shared = [shape((frames, width), BF16), shape((frames, channels), BF16), shape((frames, dz), BF16),
              shape((dz, frames), BF16), shape((rows_b, dz), BF16),
              shape((rows_b * (dz // LANES), LANES), BF16)]
    *arrays, first, part = call(
        functools.partial(local_kernel, plan),
        shared + [shape((16, channels), F32), shape((corr_rows + 32 * (dz // LANES), LANES), F32)],
        [info, feats, weight, conv_bias[None, :], codes, codebooks, proj],
        scratch=[VMEM((channels // LANES, rows_in + 8, LANES), F32), VMEM((levels, frames, dz), BF16)],
    )
    unfold, hidden, latent_grad, flipped, own, send_sums, send = call(
        functools.partial(frame_kernel, plan),
        shared + [shape((corr_rows, LANES), BF16)],
        [info, halo, first, part, weight, proj] + arrays,
        aliases={6 + k: k for k in range(len(shared))},
    )
    got = swapped(send, exchanges[0])
    keep_a, keep_c, hidden_grad, extras, row = call(
        functools.partial(rest_kernel, plan),
        [shape((now_a * dz, LANES), F32), shape((now_c * dz, LANES), F32), shape((frames, channels), BF16),
         shape((extra, LANES), F32), shape((16, channels), BF16)],
        [info, flipped, unfold, hidden, latent_grad, proj],
        after=[send],
    )

    def halves_at(k):
        nonlocal now_a, now_c
        halves = [(now_a * dz, a_split[k]), (now_c * dz, c_split[k] is not None)]
        now_a = now_a // 2 if halves[0][1] else now_a
        now_c = now_c // 2 if halves[1][1] else now_c
        return halves, now_a * dz, now_c * dz + extra

    size = per_shard + 16
    sums_rows = size * (tm // 2)
    got_core = swapped(send_sums, exchanges[0])

    def own_sums(first, after):
        return call(
            functools.partial(own_sums_kernel, frames, at_codes + first, per_shard),
            shape((sums_rows, dz), F32),
            [info, own],
            after=after)

    def both_sums(first, base, dtype, after):
        return call(
            functools.partial(sums_kernel, 0, frames, at_codes + first, per_shard),
            shape((sums_rows, dz), dtype),
            [info, got_core, base, row],
            after=after)

    base = own_sums(0, [extras])
    halves, rows_a, rows_c = halves_at(1)
    send, keep_a, keep_c = call(
        functools.partial(first_step_kernel, halves, 1),
        [shape((rows_a + rows_c, LANES), BF16), shape((rows_a, LANES), F32), shape((rows_c, LANES), F32)],
        [info, got, keep_a, keep_c, extras],
        after=[base])
    sums_send = both_sums(0, base, BF16, [send])
    sums_keep = both_sums(tm // 2, own_sums(tm // 2, [sums_send]), F32, [])
    sums_got = swapped(sums_send, sums_exchanges[0])
    got = swapped(send, exchanges[1])
    known = row
    ordered = [sums_keep]
    for k in range(2, len(exchanges)):
        halves, rows_a, rows_c = halves_at(k)
        spare = 16 * (k == len(exchanges) - 1)
        send, keep_a, keep_c = call(
            functools.partial(step_kernel, halves, k, mixed and k == dp_bits),
            [shape((rows_a + rows_c + spare, LANES), BF16), shape((rows_a, LANES), F32), shape((rows_c, LANES), F32)],
            [info, got, keep_a, keep_c],
            after=ordered)
        got = swapped(send, exchanges[k])
        halved = sums_exchanges[k - 1][0][0] == "tm"
        sums_rows = sums_rows // 2 if halved else sums_rows
        row_step = k - 2 if k - 2 < tm_bits else None
        outs = call(
            functools.partial(sums_step_kernel, halved, at_sums + k - 1, row_step, (per_shard, at_row)),
            [shape((sums_rows, dz), BF16), shape((sums_rows, dz), F32)]
            + [shape((16, channels), BF16)] * (row_step is not None),
            [info, sums_got, sums_keep] + [known] * (row_step is not None),
            after=[send])
        sums_send, sums_keep = outs[:2]
        known = outs[2] if row_step is not None else known
        sums_got = swapped(sums_send, sums_exchanges[k - 1])
        ordered = [sums_send]
    assert now_a == 1 and sums_rows == size
    feat_grad, last = call(
        feat_kernel,
        shape((rows_in, channels), BF16),
        [info, hidden_grad, known, weight],
        after=[sums_send],
        token=True,
        scratch=[VMEM((frames + 8, channels), F32), VMEM((channels // LANES, rows_in, LANES), F32)],
    )

    corr, piece, mine = call(
        functools.partial(last_kernel, rows_a, rows_c - extra),
        [shape((rows_a, LANES), F32), shape((rows_c - extra, LANES), BF16),
         shape((rows_c + size * (dz // LANES), LANES), BF16)],
        [info, got, keep_a, keep_c, sums_got, sums_keep],
        after=[last])
    parts = [piece, swapped(mine, exchanges[0]), swapped(piece, exchanges[1]), crossed(piece, exchanges[1])]
    conv_grad, last = call(
        functools.partial(conv_out_kernel, total_frames, at_start),
        shape((owner_rows, channels), F32),
        [info, corr, proj],
        after=[piece],
        token=True,
        scratch=[VMEM((LANES, channels), F32)],
    )
    bias_grad, code_means, code_usage, last = call(
        functools.partial(means_out_kernel, total_frames, book_size / total_frames, dz, now_c, extra),
        [shape((1, channels), F32), shape((levels, per_shard, dz), BF16), shape((levels, per_shard), F32)],
        [info, mine, parts[1]],
        after=[last],
        token=True,
    )
    proj_grad = call(
        functools.partial(proj_out_kernel, total_frames, dz, at_pieces, now_c),
        shape((channels, dz), F32),
        [info] + parts,
        after=[last],
    )
    return feat_grad, conv_grad, bias_grad[0], proj_grad, code_means, code_usage


def solution(mesh):
    placed = (P(("dp", "tm"), None), P("dp", None, "tm"), P(), P(), P(), P())
    return jax.shard_map(
        shards,
        mesh=mesh,
        in_specs=placed,
        out_specs=(
            P(("dp", "tm"), None),
            P(("dp", "tm"), None),
            P(),
            P(),
            P(None, "tm", None),
            P(None, "tm"),
        ),
        check_vma=False,
    )
```
